32 devices in a mesh: replica: 2 (over x), fsdp: 16 (over z, y, core).
Axes of the slice: x: 2, y: 2, z: 4, core: 2. Of those that a mesh axis runs over, the one named last changes fastest.
Arguments:
- tokens: bfloat16 [8192, 2048], P(('replica', 'fsdp')), may hold values from -88 to 88
- doc_ids: int32 [32, 256], P(('replica', 'fsdp')), may hold values from 0 to 31, never falling along the last dimension, each value on 1 to 128 neighbouring positions
- norm_gain: bfloat16 [2048], P('fsdp'), may hold values from 0.5 to 1.5
- in_weight: bfloat16 [2048, 8192], P('fsdp'), may hold values from -0.125 to 0.125
- conv_taps: bfloat16 [4096, 4], P('fsdp'), may hold values from -3 to 3
- conv_offset: bfloat16 [4096], P('fsdp'), may hold values from -0.5 to 0.5
- select_weight: bfloat16 [4096, 160], P('fsdp'), may hold values from -0.09375 to 0.09375
- step_weight: bfloat16 [4096, 128], P('fsdp'), may hold values from -0.5 to 0.5
- step_bias: bfloat16 [4096], P('fsdp'), may hold values from -7 to -2
- decay_log: bfloat16 [4096, 16], P('fsdp'), may hold values from -3 to 2
- skip_gain: bfloat16 [4096], P('fsdp'), may hold values from 0.5 to 1.5
- out_weight: bfloat16 [4096, 2048], P('fsdp'), may hold values from -0.375 to 0.375
- cotangent: bfloat16 [8192, 2048], P(('replica', 'fsdp')), may hold values from -6 to 6
Outputs:
- layer_out: bfloat16 [8192, 2048], P(('replica', 'fsdp'))
- tokens_grad: bfloat16 [8192, 2048], P(('replica', 'fsdp'))
- grad_norm_gain: float32 [2048], P('fsdp')
- grad_in_weight: float32 [2048, 8192], P('fsdp')
- grad_conv_taps: float32 [4096, 4], P('fsdp')
- grad_conv_offset: float32 [4096], P('fsdp')
- grad_select_weight: float32 [4096, 160], P('fsdp')
- grad_step_weight: float32 [4096, 128], P('fsdp')
- grad_step_bias: float32 [4096], P('fsdp')
- grad_decay_log: float32 [4096, 16], P('fsdp')
- grad_skip_gain: float32 [4096], P('fsdp')
- grad_out_weight: float32 [4096, 2048], P('fsdp')
The draws below stay inside these ranges and needn't reach their ends.
Inputs may be any that keep to these rules, and one draw needn't show every extreme that they name: `doc_ids`: within each row of 256 tokens the ids never fall; tokens with one id in a row form one document.
All inputs are finite; a program needn't handle non-finite values.
Results may differ from the reference program's by a relative error of at most 0.014.
Values may be sent and summed in bfloat16 or wider, within the bound.
A program may use at most 384 MiB of HBM per device.

```python
import math
from functools import partial
import jax
import jax.numpy as jnp
import numpy as np
from jax import lax

D = 2048
DI = 4096
NS = 16
RK = 128
KW = 4
SEQ_LEN = 256
SEQS = 32
TOKENS = 8192


def draw_tokens(key, part):
    key = jax.random.fold_in(key, 11)
    key_bulk, key_pair, key_cols, key_sign, key_size = jax.random.split(key, 5)
    bulk = jnp.clip(jax.random.normal(key_bulk, (TOKENS, D), jnp.float32), -6.0, 6.0)
    pairing = jax.random.permutation(key_pair, SEQS)
    row_block = pairing[jnp.arange(TOKENS) // SEQ_LEN]
    col_block = jnp.arange(D) // (D // SEQS)
    paired = row_block[:, None] == col_block[None, :]
    bulk = jnp.where(paired, 4.0 * bulk, bulk)
    columns = jax.random.permutation(key_cols, D)[:2]
    chosen = jnp.any(jnp.arange(D)[:, None] == columns[None, :], axis=1)
    signs = jnp.where(jax.random.bernoulli(key_sign, 0.5, (D,)), 1.0, -1.0)
    magnitude = jax.random.uniform(key_size, (TOKENS, 1), jnp.float32, 0.8, 1.2)
    outlier = signs[None, :] * magnitude * (0.7 * math.sqrt(D))
    return jnp.where(chosen[None, :], outlier, bulk).astype(jnp.bfloat16)


def raised(array, stream_key, source, target, blocks, factor):
    def block_of(axis_at):
        return (jnp.arange(array.shape[axis_at]) // (array.shape[axis_at] // blocks)).reshape((-1,) + (1,) * (array.ndim - 1 - axis_at))

    first = jax.random.permutation(stream_key, blocks)[block_of(target)]
    second = (block_of(target) + blocks // 2) % blocks
    return jnp.where((block_of(source) == first) | (block_of(source) == second), factor * array, array)


def shard_levels(key, dims, cuts, low, high):
    gain = 1.0
    for dim, parts in cuts:
        heights = jax.random.uniform(jax.random.fold_in(jax.random.fold_in(key, 6), dim), (parts,), jnp.float32, low / len(cuts), high / len(cuts))
        gain = gain * jnp.repeat(jnp.exp(heights), dims[dim] // parts).reshape((-1,) + (1,) * (len(dims) - 1 - dim))
    return gain


def length_profile(amount, total, limit, slope):
    weights = [(1 << 20) // math.isqrt(rank ** slope) + 1 for rank in range(2, amount + 1)]
    surplus, given = total - limit - (amount - 1), [1] * (amount - 1)
    while surplus > 0:
        candidates = [i for i in range(amount - 1) if given[i] < limit]
        mass, budget = sum([weights[i] for i in candidates]), surplus
        for i in candidates:
            more = min(limit - given[i], max(1, budget * weights[i] // mass), surplus)
            given[i] = given[i] + more
            surplus = surplus - more
    return np.array([limit] + given)


def ragged_sizes(key, amount, total, most, slope):
    if amount == 2:
        one = jax.random.randint(key, (), max(1, total - most), min(most, total - 1) + 1)
        return jnp.stack([one, total - one])
    tallies = jnp.asarray(length_profile(amount, total, most, slope), jnp.int32)
    pairs = (amount - 1) // 2
    source_of, taker = tallies[1:1 + 2 * pairs:2], tallies[2:2 + 2 * pairs:2]
    margin = jnp.minimum(source_of - 1, most - taker)
    passed = jax.random.randint(jax.random.fold_in(key, 1), (pairs,), 0, 1 << 20) % (margin + 1)
    tallies = tallies.at[1:1 + 2 * pairs:2].set(source_of - passed).at[2:2 + 2 * pairs:2].set(taker + passed)
    return tallies[jax.random.permutation(jax.random.fold_in(key, 2), amount)]


def centred(own_key, extent, spread, bound, cuts=(), kind=jnp.bfloat16):
    factor_of = shard_levels(own_key, extent, cuts, -0.22, 0.18) if cuts else 1.0
    array = jax.random.normal(own_key, extent, jnp.float32) * spread * factor_of
    return jnp.minimum(jnp.maximum(array, -bound), bound).astype(kind)


def bell_draw_with(key, shape, scale, most, cuts, heavy, kind=jnp.bfloat16):
    entries = scale * jax.random.normal(key, shape, jnp.float32)
    if cuts:
        entries = entries * shard_levels(key, shape, cuts, -0.22, 0.18)
    return jnp.clip(raised(entries, jax.random.fold_in(key, 3), *heavy), -most, most).astype(kind)


def setup_inputs(seed: int = 0) -> dict:
    keys = jax.random.split(jax.random.key(seed), 14)
    return {
        "tokens": draw_tokens(jax.random.fold_in(keys[13], 71), 0),
        "doc_ids": jax.vmap(lambda own: jnp.searchsorted(jnp.cumsum(ragged_sizes(own, max(SEQ_LEN // 8, 4), SEQ_LEN, SEQ_LEN // 2, 2)), jnp.arange(SEQ_LEN), side="right"))(jax.random.split(keys[1], SEQS)).reshape((SEQS, SEQ_LEN)).astype(jnp.int32),
        "norm_gain": jnp.clip(1.0 + 0.1 * jax.random.normal(keys[2], (D,), jnp.float32), 0.5, 1.5).astype(jnp.bfloat16),
        "in_weight": centred(keys[3], (D, 2 * DI), D ** -0.5, 0.125, ((0, 16),)),
        "conv_taps": centred(keys[4], (DI, KW), KW ** -0.5, 3.0, ((0, 16),)),
        "conv_offset": jnp.clip(jax.random.uniform(keys[5], (DI,), jnp.float32, -0.5, 0.5) * shard_levels(keys[5], (DI,), ((0, 16),), -0.4, 0.0), -0.5, 0.5).astype(jnp.bfloat16),
        "select_weight": centred(keys[6], (DI, RK + 2 * NS), DI ** -0.5, 0.09375, ((0, 16),)),
        "step_weight": centred(keys[7], (DI, RK), RK ** -0.5, 0.5, ((0, 16),)),
        "step_bias": jnp.clip(-7.0 + 5.0 * jax.random.uniform(keys[8], (DI,), jnp.float32) ** shard_levels(keys[8], (DI,), ((0, 16),), -0.2, 0.2), -7.0, -2.0).astype(jnp.bfloat16),
        "decay_log": jnp.clip(-3.0 + 5.0 * jax.random.uniform(keys[9], (DI, NS), jnp.float32) ** shard_levels(keys[9], (DI, NS), ((0, 16),), -0.2, 0.2), -3.0, 2.0).astype(jnp.bfloat16),
        "skip_gain": jnp.clip(0.5 + 1.0 * jax.random.uniform(keys[10], (DI,), jnp.float32) ** shard_levels(keys[10], (DI,), ((0, 16),), -0.2, 0.2), 0.5, 1.5).astype(jnp.bfloat16),
        "out_weight": centred(keys[11], (DI, D), (DI // 16) ** -0.5, 0.375, ((0, 16),)),
        "cotangent": bell_draw_with(keys[12], (TOKENS, D), 1.0, 6.0, ((0, 32),), (0, 1, 32, 2.75)),
    }


epsilon = 1e-05
highest = lax.Precision.HIGHEST

@jax.custom_vjp
def low(v):
    return lax.optimization_barrier(v.astype(jnp.bfloat16)).astype(jnp.float32)

@jax.custom_vjp
def low_back(v):
    return v

def low_keep(v):
    return (low(v), None)

def low_pass(kept, grad):
    return (grad,)

def back_keep(v):
    return (v, None)

def back_low(kept, grad):
    return (low(grad),)
low.defvjp(low_keep, low_pass)
low_back.defvjp(back_keep, back_low)

def causal_conv(values, weights, offsets, doc_ids):
    length = values.shape[1]
    kernel_len = weights.shape[1]
    padded = jnp.pad(values, ((0, 0), (kernel_len - 1, 0), (0, 0)))
    padded_ids = jnp.pad(doc_ids, ((0, 0), (kernel_len - 1, 0)), constant_values=-1)
    result = offsets + jnp.zeros_like(values)
    for back_step in range(kernel_len):
        first_row = kernel_len - 1 - back_step
        shifted = padded[:, first_row:first_row + length]
        same_doc = (padded_ids[:, first_row:first_row + length] == doc_ids).astype(values.dtype)
        result = result + shifted * same_doc[:, :, None] * weights[:, kernel_len - 1 - back_step]
    return result

def scan_block(hidden_state, pieces, decay_rates):
    inputs, steps_in, in_gate, out_gate, keep_mask = pieces
    outputs = []
    for position in range(inputs.shape[0]):
        decay_now = jnp.exp(steps_in[position][:, None, :] * decay_rates[None]) * keep_mask[position][:, None, None]
        hidden_state = decay_now * hidden_state + (steps_in[position] * inputs[position])[:, None, :] * in_gate[position][:, :, None]
        outputs.append(lax.optimization_barrier(jnp.sum(hidden_state * out_gate[position][:, :, None], axis=1)))
    return (hidden_state, jnp.stack(outputs))

def time_major(member, blocks, block_len):
    return member.swapaxes(0, 1).reshape((blocks, block_len, member.shape[0]) + member.shape[2:])

def selective_scan(inputs, steps_in, in_gate, out_gate, keep_mask, decay_rates):
    length = inputs.shape[1]
    block_len = math.gcd(length, 16)
    blocks = length // block_len
    pieces = tuple((time_major(member, blocks, block_len) for member in (inputs, steps_in, in_gate, out_gate, keep_mask)))
    initial = jnp.zeros((inputs.shape[0], decay_rates.shape[0], inputs.shape[2]), inputs.dtype)
    runner = jax.checkpoint(partial(scan_block, decay_rates=decay_rates))
    final_state, outputs = lax.scan(runner, initial, pieces)
    return outputs.reshape((length,) + outputs.shape[2:]).swapaxes(0, 1)

def layer(values, group_ids, norm_gain, in_weight, conv_taps, conv_offset, select_weight, step_weight, step_bias, decay_log, skip_gain, out_weight):
    inner_width = step_weight.shape[0]
    rank_width = step_weight.shape[1]
    state_size = decay_log.shape[1]
    mean_square = lax.optimization_barrier(jnp.mean(values * values, axis=-1, keepdims=True))
    normed = low(values * lax.rsqrt(mean_square + epsilon) * norm_gain)
    projected = low_back(jnp.einsum('gtd,de->gte', normed, in_weight, precision=highest))
    conv_in = projected[..., :inner_width]
    gate_in = projected[..., inner_width:]
    selected = low(jax.nn.silu(causal_conv(conv_in, conv_taps, conv_offset, group_ids)))
    selection = low_back(jnp.einsum('gtc,cp->gtp', selected, select_weight, precision=highest))
    rank_in = low(selection[..., :rank_width])
    in_gate = selection[..., rank_width:rank_width + state_size]
    out_gate = selection[..., rank_width + state_size:]
    pre_step = low_back(jnp.einsum('gtr,cr->gtc', rank_in, step_weight, precision=highest))
    steps_in = jax.nn.softplus(pre_step + step_bias)
    same_prev = (group_ids[:, 1:] == group_ids[:, :-1]).astype(jnp.int32)
    keep_mask = jnp.concatenate([jnp.zeros_like(group_ids[:, :1]), same_prev], axis=1).astype(values.dtype)
    scanned = selective_scan(selected, steps_in, in_gate, out_gate, keep_mask, -jnp.exp(decay_log).T) + skip_gain * selected
    gated = low_back(low(scanned * jax.nn.silu(gate_in)))
    return values + jnp.einsum('gtc,cd->gtd', gated, out_weight, precision=highest)

def reference(tokens, doc_ids, norm_gain, in_weight, conv_taps, conv_offset, select_weight, step_weight, step_bias, decay_log, skip_gain, out_weight, cotangent):
    params = tuple((member.astype(jnp.float32) for member in (norm_gain, in_weight, conv_taps, conv_offset, select_weight, step_weight, step_bias, decay_log, skip_gain, out_weight)))
    per_group = math.gcd(SEQS, max(1, 4096 // SEQ_LEN))
    groups = SEQS // per_group
    inputs = tokens.astype(jnp.float32).reshape(groups, per_group, SEQ_LEN, D)
    doc_groups = doc_ids.reshape(groups, per_group, SEQ_LEN)
    cot_groups = cotangent.astype(jnp.float32).reshape(groups, per_group, SEQ_LEN, D)

    def one_group(totals, pieces):
        values, group_ids, group_cot = pieces

        def forward(inner_values, *weights):
            return layer(inner_values, group_ids, *weights)
        result, pullback = jax.vjp(forward, values, *params)
        gradients = pullback(group_cot)
        summed = tuple((total + extra for total, extra in zip(totals, gradients[1:])))
        return (summed, (result.astype(jnp.bfloat16), gradients[0].astype(jnp.bfloat16)))
    zeros = tuple((jnp.zeros_like(member) for member in params))
    totals, (outputs, input_grads) = lax.scan(one_group, zeros, (inputs, doc_groups, cot_groups))
    return (outputs.reshape(TOKENS, D), input_grads.reshape(TOKENS, D), totals[0], totals[1], totals[2], totals[3], totals[4], totals[5], totals[6], totals[7], totals[8], totals[9])
```

```python
import functools

import jax
import jax.numpy as jnp
from jax import lax
from jax.experimental import pallas as pl
from jax.experimental.pallas import tpu as pltpu
from jax.sharding import Mesh
from jax.sharding import PartitionSpec as P

F32 = jnp.float32
BF16 = jnp.bfloat16
epsilon = 1e-05
PLANE = ("x", "y", "c")
BIG = 1e30
STEPS = 32
INNER = 4
LOG2E = 1.4426950408889634


def dot(a, b, dims):
    return lax.dot_general(a, b, (dims, ((), ())), preferred_element_type=F32)


def dot_nn(a, b):
    return dot(a, b, ((1,), (0,)))


def dot_tn(a, b):
    return dot(a, b, ((0,), (0,)))


def dot_nt(a, b):
    return dot(a, b, ((1,), (1,)))


def fwd_kernel(states, dt_ref, dtm_ref, x_ref, bc_ref, rate_ref, y_ref, hist_ref, last_ref, h_ref):
    @pl.when(pl.program_id(0) == 0)
    def _():
        h_ref[...] = jnp.zeros_like(h_ref)

    width = dt_ref.shape[2]
    groups = width // 128

    def body(tb, carry):
        t0 = tb * INNER
        bc = [bc_ref[t0 + i] for i in range(INNER)]
        for g in range(groups):
            lanes = pl.ds(g * 128, 128)
            dtm = [dtm_ref[t0 + i, :, lanes] for i in range(INNER)]
            u = [dt_ref[t0 + i, :, lanes] * x_ref[t0 + i, :, lanes] for i in range(INNER)]
            y = [None] * INNER
            for n in range(states):
                h = h_ref[n, :, lanes]
                rate = rate_ref[n, :, lanes]
                for i in range(INNER):
                    hist_ref[t0 + i, n, :, lanes] = h
                    a = jnp.exp2(dtm[i] * rate)
                    h = a * h + u[i] * bc[i][:, n : n + 1]
                    term = h * bc[i][:, states + n : states + n + 1]
                    y[i] = term if y[i] is None else y[i] + term
                h_ref[n, :, lanes] = h
            for i in range(INNER):
                y_ref[t0 + i, :, lanes] = y[i]
        return carry

    lax.fori_loop(0, dt_ref.shape[0] // INNER, body, 0)
    last_ref[...] = h_ref[...]


def scan_forward(dt, dtm, x, bc, rate):
    length, seqs, width = dt.shape
    states = rate.shape[0]
    block = lambda *tail: pl.BlockSpec((STEPS,) + tail, lambda i: (i,) + (0,) * len(tail))
    whole = lambda *dims: pl.BlockSpec(dims, lambda i: (0,) * len(dims))
    return pl.pallas_call(
        functools.partial(fwd_kernel, states),
        grid=(length // STEPS,),
        in_specs=[
            block(seqs, width),
            block(seqs, width),
            block(seqs, width),
            block(seqs, 2 * states),
            whole(states, seqs, width),
        ],
        out_specs=[block(seqs, width), block(states, seqs, width), whole(states, seqs, width)],
        out_shape=[
            jax.ShapeDtypeStruct(dt.shape, F32),
            jax.ShapeDtypeStruct((length, states, seqs, width), F32),
            jax.ShapeDtypeStruct((states, seqs, width), F32),
        ],
        scratch_shapes=[pltpu.VMEM((states, seqs, width), F32)],
        compiler_params=pltpu.CompilerParams(vmem_limit_bytes=56 << 20),
    )(dt, dtm, x, bc, rate)


def bwd_kernel(
    states,
    dt_ref,
    dtm_ref,
    x_ref,
    ds_ref,
    bc_ref,
    rate_ref,
    hist_ref,
    last_ref,
    ones_ref,
    s1_ref,
    s2_ref,
    gates_ref,
    da_ref,
    ag_ref,
    h_ref,
    pb_ref,
    pc_ref,
):
    @pl.when(pl.program_id(0) == 0)
    def _():
        ag_ref[...] = jnp.zeros_like(ag_ref)
        da_ref[...] = jnp.zeros_like(da_ref)
        h_ref[...] = last_ref[...]

    steps, seqs, width = dt_ref.shape
    groups = width // 128
    blocks = steps // INNER

    def body(back, carry):
        t0 = (blocks - 1 - back) * INNER
        rows = pl.multiple_of(t0 * seqs, INNER * seqs)
        bc = [bc_ref[t0 + i] for i in range(INNER)]
        for g in range(groups):
            lanes = pl.ds(g * 128, 128)
            dt = [dt_ref[t0 + i, :, lanes] for i in range(INNER)]
            dtm = [dtm_ref[t0 + i, :, lanes] for i in range(INNER)]
            ds = [ds_ref[t0 + i, :, lanes] for i in range(INNER)]
            u = [dt[i] * x_ref[t0 + i, :, lanes] for i in range(INNER)]
            s1 = [None] * INNER
            s2 = [None] * INNER
            for n in range(states):
                ag = ag_ref[n, :, lanes]
                h = h_ref[n, :, lanes]
                rate = rate_ref[n, :, lanes]
                da = da_ref[n, :, lanes]
                pb = [None] * INNER
                pc = [None] * INNER
                for i in reversed(range(INNER)):
                    prev = hist_ref[t0 + i, n, :, lanes]
                    a = jnp.exp2(dtm[i] * rate)
                    adj = ds[i] * bc[i][:, states + n : states + n + 1] + ag
                    pc[i] = ds[i] * h
                    pb[i] = adj * u[i]
                    ag = a * adj
                    w = ag * prev
                    rw = rate * w
                    gb = adj * bc[i][:, n : n + 1]
                    s1[i] = rw if s1[i] is None else s1[i] + rw
                    s2[i] = gb if s2[i] is None else s2[i] + gb
                    da = da + dt[i] * w
                    h = prev
                ag_ref[n, :, lanes] = ag
                h_ref[n, :, lanes] = h
                da_ref[n, :, lanes] = da
                cols = pl.ds((g * states + n) * 128, 128)
                pb_ref[pl.ds(rows, INNER * seqs), cols] = jnp.concatenate(pb, axis=0).astype(BF16)
                pc_ref[pl.ds(rows, INNER * seqs), cols] = jnp.concatenate(pc, axis=0).astype(BF16)
            for i in range(INNER):
                s1_ref[t0 + i, :, lanes] = s1[i]
                s2_ref[t0 + i, :, lanes] = s2[i]
        return carry

    lax.fori_loop(0, blocks, body, 0)
    span = states * 128
    total = jnp.zeros((steps * seqs, 128), F32)
    for g in range(groups):
        total = total + dot_nn(pb_ref[:, pl.ds(g * span, span)], ones_ref[0])
        total = total + dot_nn(pc_ref[:, pl.ds(g * span, span)], ones_ref[1])
    gates_ref[...] = total


def scan_backward(dt, dtm, x, ds, bc, rate, hist, last):
    length, seqs, width = dt.shape
    states = rate.shape[0]
    chunks = length // STEPS
    block = lambda *tail: pl.BlockSpec((STEPS,) + tail, lambda i: (chunks - 1 - i,) + (0,) * len(tail))
    whole = lambda *dims: pl.BlockSpec(dims, lambda i: (0,) * len(dims))
    span = states * 128
    entry = jnp.arange(span)[:, None] // 128
    column = jnp.arange(128)[None, :]
    ones = jnp.stack([entry == column, entry + states == column]).astype(BF16)
    return pl.pallas_call(
        functools.partial(bwd_kernel, states),
        grid=(chunks,),
        in_specs=[
            block(seqs, width),
            block(seqs, width),
            block(seqs, width),
            block(seqs, width),
            block(seqs, 2 * states),
            whole(states, seqs, width),
            block(states, seqs, width),
            whole(states, seqs, width),
            whole(2, span, 128),
        ],
        out_specs=[
            block(seqs, width),
            block(seqs, width),
            pl.BlockSpec((STEPS * seqs, 128), lambda i: (chunks - 1 - i, 0)),
            whole(states, seqs, width),
        ],
        out_shape=[
            jax.ShapeDtypeStruct(dt.shape, F32),
            jax.ShapeDtypeStruct(dt.shape, F32),
            jax.ShapeDtypeStruct((length * seqs, 128), F32),
            jax.ShapeDtypeStruct((states, seqs, width), F32),
        ],
        scratch_shapes=[
            pltpu.VMEM((states, seqs, width), F32),
            pltpu.VMEM((states, seqs, width), F32),
            pltpu.VMEM((STEPS * seqs, width // 128 * span), BF16),
            pltpu.VMEM((STEPS * seqs, width // 128 * span), BF16),
        ],
        compiler_params=pltpu.CompilerParams(vmem_limit_bytes=60 << 20),
    )(dt, dtm, x, ds, bc, rate, hist, last, ones)


MESH = pl.DeviceIdType.MESH
RING = 4


def place():
    return {a: lax.axis_index(a) for a in ("x", "z", "y", "c")}


def ring_chip(p):
    y = p // 2
    return (p + y) % 2, y


def ring_at(x, y):
    return 2 * y + (x + y) % 2


def share_at(f):
    return {"z": f // 4, "y": f // 2 % 2, "c": f % 2}


def remote(src, dst, send, recv, device):
    return pltpu.make_async_remote_copy(
        src_ref=src, dst_ref=dst, send_sem=send, recv_sem=recv, device_id=device, device_id_type=MESH
    )


def greet(devices):
    barrier = pltpu.get_barrier_semaphore()
    for device in devices:
        pl.semaphore_signal(barrier, inc=1, device_id=device, device_id_type=MESH)
    pl.semaphore_wait(barrier, len(devices))


def plane_others(me):
    out = []
    for dx in range(2):
        for dy in range(2):
            for dc in range(2):
                if dx + dy + dc:
                    out.append(
                        {"x": (me["x"] + dx) % 2, "y": (me["y"] + dy) % 2, "c": (me["c"] + dc) % 2}
                    )
    return out


def share_others(me, shares):
    f = me["z"] * 4 + me["y"] * 2 + me["c"]
    return [share_at((f + k) % shares) for k in range(1, shares)]


def z_only(me, shares):
    f = me["c"] + 2 * me["y"]
    out = []
    for dz in range(1, shares // 4):
        for k in range(4):
            out.append(
                {
                    "z": (me["z"] + dz) % (shares // 4),
                    "y": (f + k) % 4 // 2,
                    "c": (f + k) % 2,
                }
            )
    return out


def start_kernel(
    z_size,
    tokens_ref,
    gain_ref,
    ids_ref,
    conv_ref,
    gate_ref,
    small_ref,
    normed_all,
    conv_all,
    gate_all,
    small_all,
    ids_all,
    gain_all,
    normed_ref,
    gain_got,
    local_sem,
    gain_send,
    gain_recv,
    ids_send,
    ids_recv,
    conv_send,
    conv_recv,
    gate_send,
    gate_recv,
    ring_send,
    ring_recv,
    sib_send,
    sib_recv,
    up_send,
    up_recv,
    down_send,
    down_recv,
):
    me = place()
    x, y, z, c = me["x"], me["y"], me["z"], me["c"]
    shares = z_size * 4
    share = z * 4 + y * 2 + c
    corner = y * 2 + c
    seq = x * 4 + y * 2 + c
    greet(plane_others(me) + z_only(me, shares))

    swaps = []
    for k in range(1, 4):
        to = (corner + k) % 4
        device = {"y": to // 2, "c": to % 2}
        swaps.append(
            remote(conv_ref.at[to], conv_all.at[z, corner], conv_send.at[k - 1], conv_recv.at[k - 1], device)
        )
    for copy in swaps:
        copy.start()
    gains = [
        remote(gain_ref, gain_got.at[share], gain_send.at[k], gain_recv.at[k], device)
        for k, device in enumerate(share_others(me, shares))
    ]
    for copy in gains:
        copy.start()
    own = [
        pltpu.make_async_copy(conv_ref.at[corner], conv_all.at[z, corner], local_sem.at[0]),
        pltpu.make_async_copy(small_ref, small_all.at[z], local_sem.at[1]),
        pltpu.make_async_copy(gate_ref.at[corner], gate_all.at[corner], local_sem.at[2]),
    ]
    for copy in own:
        copy.start()
    others = plane_others(me)
    ids_copies = [
        remote(ids_ref, ids_all.at[seq], ids_send.at[k], ids_recv.at[k], device)
        for k, device in enumerate(others)
    ]
    for copy in ids_copies:
        copy.start()
    ids_all[seq] = ids_ref[...]
    gain_got[share] = gain_ref[...]

    values = tokens_ref[...].astype(F32)
    rstd = lax.rsqrt(jnp.mean(values * values, axis=-1, keepdims=True) + epsilon)
    for copy in gains:
        copy.wait()
    piece = gain_ref.shape[1]
    for f in range(shares):
        cols = pl.ds(f * piece, piece)
        part = tokens_ref[:, cols].astype(F32) * rstd * gain_got[f, 0:1, :]
        normed_ref[:, cols] = part.astype(BF16)
    gain_all[...] = gain_got[...]

    at = ring_at(x, y)
    step = 1 + 2 * c
    nx, ny = ring_chip((at + step) % RING)
    following = {"x": nx, "y": ny}
    sibling = {"c": 1 - c}

    def slot(k):
        ox, oy = ring_chip((at + (RING - step) * k) % RING)
        return ox * 4 + oy * 2 + c

    def ring(k):
        src = normed_ref if k == 0 else normed_all.at[slot(k)]
        return remote(src, normed_all.at[slot(k)], ring_send.at[k], ring_recv.at[k], following)

    def sib(k):
        src = normed_ref if k == 0 else normed_all.at[slot(k)]
        return remote(src, normed_all.at[slot(k)], sib_send.at[k], sib_recv.at[k], sibling)

    keep = pltpu.make_async_copy(normed_ref, normed_all.at[seq], local_sem.at[3])
    keep.start()
    ring(0).start()
    sib(0).start()

    for copy in swaps:
        copy.wait()
    for copy in own:
        copy.wait()

    def upward(k, j):
        ref = (conv_all, small_all)[j].at[z - k]
        return remote(ref, ref, up_send.at[k, j], up_recv.at[k, j], {"z": z + 1})

    def downward(k, j):
        ref = (conv_all, small_all)[j].at[z + k]
        return remote(ref, ref, down_send.at[k, j], down_recv.at[k, j], {"z": z - 1})

    def send_up(k):
        @pl.when((z < z_size - 1) & (z >= k))
        def _():
            upward(k, 0).start()
            upward(k, 1).start()

    def send_down(k):
        @pl.when((z > 0) & (z + k < z_size))
        def _():
            downward(k, 0).start()
            downward(k, 1).start()

    send_up(0)
    send_down(0)
    gates = []
    for k in range(1, 4):
        to = (corner + k) % 4
        device = {"y": to // 2, "c": to % 2}
        gates.append(
            remote(gate_ref.at[to], gate_all.at[corner], gate_send.at[k - 1], gate_recv.at[k - 1], device)
        )
    for copy in gates:
        copy.start()
    for k in range(max(z_size - 1, RING - 1)):
        if k < z_size - 1:
            @pl.when(z > k)
            def _():
                upward(k, 0).wait_recv()
                upward(k, 1).wait_recv()

            send_up(k + 1)

            @pl.when(z + k < z_size - 1)
            def _():
                downward(k, 0).wait_recv()
                downward(k, 1).wait_recv()

            send_down(k + 1)
        if k < RING - 1:
            ring(k).wait_recv()
            if k + 1 < RING - 1:
                ring(k + 1).start()
            sib(k + 1).start()

    for k in range(z_size - 1):
        @pl.when((z < z_size - 1) & (z >= k))
        def _():
            upward(k, 0).wait_send()
            upward(k, 1).wait_send()

        @pl.when((z > 0) & (z + k < z_size))
        def _():
            downward(k, 0).wait_send()
            downward(k, 1).wait_send()

    for k in range(RING - 1):
        ring(k).wait_send()
    for k in range(RING):
        sib(k).wait()
    for copy in gates + ids_copies + [keep]:
        copy.wait()


def start_gathers(z_size, tokens, gain, ids, conv, gate, small):
    length, width = tokens.shape
    shares = z_size * 4
    any_space = pl.BlockSpec(memory_space=pl.ANY)
    vmem = pl.BlockSpec(memory_space=pltpu.VMEM)
    dma = pltpu.SemaphoreType.DMA
    hops = max(z_size - 1, 1)
    return pl.pallas_call(
        functools.partial(start_kernel, z_size),
        in_specs=[vmem, vmem, vmem, any_space, any_space, any_space],
        out_specs=[any_space, any_space, any_space, any_space, vmem, vmem],
        out_shape=[
            jax.ShapeDtypeStruct((8,) + tokens.shape, BF16),
            jax.ShapeDtypeStruct((z_size,) + conv.shape, BF16),
            jax.ShapeDtypeStruct(gate.shape, BF16),
            jax.ShapeDtypeStruct((z_size,) + small.shape, BF16),
            jax.ShapeDtypeStruct((8,) + ids.shape, ids.dtype),
            jax.ShapeDtypeStruct((shares,) + gain.shape, F32),
        ],
        scratch_shapes=[
            pltpu.VMEM(tokens.shape, BF16),
            pltpu.VMEM((shares,) + gain.shape, F32),
            dma((4,)),
            dma((shares - 1,)),
            dma((shares - 1,)),
            dma((7,)),
            dma((7,)),
            dma((3,)),
            dma((3,)),
            dma((3,)),
            dma((3,)),
            dma((RING - 1,)),
            dma((RING - 1,)),
            dma((RING,)),
            dma((RING,)),
            dma((hops, 2)),
            dma((hops, 2)),
            dma((hops, 2)),
            dma((hops, 2)),
        ],
        compiler_params=pltpu.CompilerParams(
            collective_id=0, has_side_effects=True, vmem_limit_bytes=40 << 20
        ),
    )(tokens, gain, ids, conv, gate, small)


def total_kernel(part_ref, out_ref, first, from_sib, stage, got, sib_s, sib_r, rs_s, rs_r, ag_s, ag_r, fw_s, fw_r):
    me = place()
    x, y, c = me["x"], me["y"], me["c"]
    greet(plane_others(me))
    sibling = {"c": 1 - c}
    first[...] = part_ref[:, 1 - c].astype(BF16)
    swap = remote(first, from_sib, sib_s, sib_r, sibling)
    swap.start()
    swap.wait()
    mine = x * 2 + y
    chips = [((x + d // 2) % 2, (y + d % 2) % 2) for d in (1, 2, 3)]
    sends = []
    for k in (2, 1, 0):
        ox, oy = chips[k]
        j = ox * 2 + oy
        stage[k] = (part_ref[j, c] + from_sib[j].astype(F32)).astype(BF16)
        copy = remote(stage.at[k], got.at[k], rs_s.at[k], rs_r.at[k], {"x": ox, "y": oy})
        copy.start()
        sends.append(copy)
    total = part_ref[mine, c] + from_sib[mine].astype(F32)
    for copy in sends:
        copy.wait()
    for k in range(3):
        total = total + got[k].astype(F32)
    out_ref[mine, c] = total.astype(BF16)
    spreads = []
    for k in (2, 1, 0):
        ox, oy = chips[k]
        here = out_ref.at[mine, c]
        copy = remote(here, here, ag_s.at[k], ag_r.at[k], {"x": ox, "y": oy})
        copy.start()
        spreads.append((k, copy))
    forwards = []
    here = out_ref.at[mine, c]
    forwards.append(remote(here, here, fw_s.at[3], fw_r.at[3], sibling))
    forwards[0].start()
    for k, copy in reversed(spreads):
        copy.wait_recv()
        ox, oy = chips[k]
        block = out_ref.at[ox * 2 + oy, c]
        forwards.append(remote(block, block, fw_s.at[k], fw_r.at[k], sibling))
        forwards[-1].start()
    for _, copy in spreads:
        copy.wait_send()
    for copy in forwards:
        copy.wait()


def plane_total(part, collective_id):
    rows, cols = part.shape
    block = (rows // 8, cols)
    vmem = pl.BlockSpec(memory_space=pltpu.VMEM)
    dma = pltpu.SemaphoreType.DMA
    out = pl.pallas_call(
        total_kernel,
        in_specs=[vmem],
        out_specs=vmem,
        out_shape=jax.ShapeDtypeStruct((4, 2) + block, BF16),
        scratch_shapes=[
            pltpu.VMEM((4,) + block, BF16),
            pltpu.VMEM((4,) + block, BF16),
            pltpu.VMEM((3,) + block, BF16),
            pltpu.VMEM((3,) + block, BF16),
            dma(()),
            dma(()),
            dma((3,)),
            dma((3,)),
            dma((3,)),
            dma((3,)),
            dma((4,)),
            dma((4,)),
        ],
        compiler_params=pltpu.CompilerParams(
            collective_id=collective_id, has_side_effects=True, vmem_limit_bytes=40 << 20
        ),
    )(part.reshape((4, 2) + block))
    return out.reshape(rows, cols)


def add_rows(dst, srcs, rows):
    count = dst.shape[0] // rows

    def body(i, carry):
        at = pl.ds(pl.multiple_of(i * rows, rows), rows)
        total = srcs[0][at].astype(F32)
        for src in srcs[1:]:
            total = total + src[at].astype(F32)
        dst[at] = total.astype(dst.dtype)
        return carry

    lax.fori_loop(0, count, body, 0)


def finish_kernel(
    z_size,
    back_ref,
    small_ref,
    gate_ref,
    conv_ref,
    tokens_ref,
    cot_ref,
    gain_ref,
    tgrad_ref,
    in_ref,
    small_out,
    gain_out,
    own_back,
    sib_back,
    ring_stage,
    ring_got,
    own_small,
    own_gate,
    own_conv,
    up_small,
    up_gate,
    up_conv,
    down_small,
    down_gate,
    down_conv,
    up_stage_small,
    up_stage_gate,
    up_stage_conv,
    down_stage_small,
    down_stage_gate,
    down_stage_conv,
    fin_gate,
    fin_conv,
    both_gate,
    both_conv,
    gain_parts,
    gain_got,
    gain_half,
    gain_pair,
    local_sem,
    back_sem,
    sib_send,
    sib_recv,
    ring_send,
    ring_recv,
    up_send,
    up_recv,
    down_send,
    down_recv,
    swap_send,
    swap_recv,
    x_send,
    x_recv,
    gain_send,
    gain_recv,
):
    me = place()
    x, y, z, c = me["x"], me["y"], me["z"], me["c"]
    shares = z_size * 4
    share = z * 4 + y * 2 + c
    corner = y * 2 + c
    sibling = {"c": 1 - c}
    over_x = {"x": 1 - x}
    greet(plane_others(me) + z_only(me, shares))

    at = ring_at(x, y)
    step = 1 + 2 * c
    sib_step = 3 - 2 * c
    nx, ny = ring_chip((at + step) % RING)
    following = {"x": nx, "y": ny}

    def chip_index(p):
        cx, cy = ring_chip(p % RING)
        return cx * 2 + cy

    owns = (own_small, own_gate, own_conv)
    locals_ = [
        pltpu.make_async_copy(src, dst, local_sem.at[i])
        for i, (src, dst) in enumerate(zip((small_ref, gate_ref, conv_ref), owns))
    ]
    for copy in locals_:
        copy.start()
    backs = []
    sibs = []
    for k in range(RING):
        backs.append(
            pltpu.make_async_copy(
                back_ref.at[chip_index(at + step * (RING - 1 - k)), c], own_back.at[k], back_sem.at[k]
            )
        )
        sibs.append(
            remote(
                back_ref.at[chip_index(at + sib_step * (RING - 1 - k)), 1 - c],
                sib_back.at[k],
                sib_send.at[k],
                sib_recv.at[k],
                sibling,
            )
        )
    for k in range(RING):
        backs[k].start()
        sibs[k].start()

    ups = (up_small, up_gate, up_conv)
    downs = (down_small, down_gate, down_conv)
    up_stages = (up_stage_small, up_stage_gate, up_stage_conv)
    down_stages = (down_stage_small, down_stage_gate, down_stage_conv)
    blocks = (16, 64, 64)

    def up_copy(k, h):
        return remote(
            up_stages[h].at[k], ups[h].at[k], up_send.at[k, h], up_recv.at[k, h], {"z": z + 1}
        )

    def down_copy(k, h):
        return remote(
            down_stages[h].at[k], downs[h].at[k], down_send.at[k, h], down_recv.at[k, h], {"z": z - 1}
        )

    def line(k, h):
        high = z_size - 1 - k

        @pl.when((z < high) & (z > 0))
        def _():
            up_copy(k, h).wait_recv()
            add_rows(up_stages[h].at[k], [owns[h].at[high], ups[h].at[k]], blocks[h])
            up_copy(k, h).start()

        @pl.when((z < high) & (z == 0))
        def _():
            add_rows(up_stages[h].at[k], [owns[h].at[high]], blocks[h])
            up_copy(k, h).start()

        @pl.when((z > k) & (z < z_size - 1))
        def _():
            down_copy(k, h).wait_recv()
            add_rows(down_stages[h].at[k], [owns[h].at[k], downs[h].at[k]], blocks[h])
            down_copy(k, h).start()

        @pl.when((z > k) & (z == z_size - 1))
        def _():
            add_rows(down_stages[h].at[k], [owns[h].at[k]], blocks[h])
            down_copy(k, h).start()

    def settle(h, dst):
        low = z
        high = z_size - 1 - z

        @pl.when(z == 0)
        def _():
            down_copy(low, h).wait_recv()
            add_rows(dst, [owns[h].at[z], downs[h].at[low]], blocks[h])

        @pl.when(z == z_size - 1)
        def _():
            up_copy(high, h).wait_recv()
            add_rows(dst, [owns[h].at[z], ups[h].at[high]], blocks[h])

        @pl.when((z > 0) & (z < z_size - 1))
        def _():
            down_copy(low, h).wait_recv()
            up_copy(high, h).wait_recv()
            add_rows(dst, [owns[h].at[z], downs[h].at[low], ups[h].at[high]], blocks[h])

    def ring(k):
        return remote(ring_stage.at[k], ring_got.at[k], ring_send.at[k], ring_recv.at[k], following)

    def ring_step(k):
        backs[k].wait()
        sibs[k].wait_recv()
        srcs = [own_back.at[k], sib_back.at[k]]
        if k:
            ring(k - 1).wait_recv()
            srcs.append(ring_got.at[k - 1])
        add_rows(ring_stage.at[k], srcs, 16)
        ring(k).start()

    def ring_end():
        last = RING - 1
        backs[last].wait()
        sibs[last].wait_recv()
        ring(last - 1).wait_recv()
        rows = 16
        width = tokens_ref.shape[1]

        def body(i, total):
            r = pl.ds(pl.multiple_of(i * rows, rows), rows)
            back = (
                own_back[last, r].astype(F32)
                + sib_back[last, r].astype(F32)
                + ring_got[last - 1, r].astype(F32)
            )
            values = tokens_ref[r].astype(F32)
            rstd = lax.rsqrt(jnp.mean(values * values, axis=-1, keepdims=True) + epsilon)
            scaled = back * gain_ref[...]
            inner = jnp.mean(scaled * values, axis=-1, keepdims=True)
            grad = cot_ref[r].astype(F32) + rstd * scaled - values * (rstd * rstd * rstd * inner)
            tgrad_ref[r] = grad.astype(BF16)
            terms = back * values * rstd
            return total + terms[:8] + terms[8:]

        total = lax.fori_loop(
            0, tokens_ref.shape[0] // rows, body, jnp.zeros((8, width), F32)
        )
        total = jnp.broadcast_to(jnp.sum(total, axis=0, keepdims=True), (8, width))
        piece = gain_parts.shape[2]
        for f in range(shares):
            gain_parts[f] = total[:, f * piece : (f + 1) * piece]
        gain_got[share] = gain_parts[share]

    gains = []
    for k in range(1, shares):
        f = (share + k) % shares
        gains.append(
            remote(
                gain_parts.at[f], gain_got.at[share], gain_send.at[k - 1], gain_recv.at[k - 1], share_at(f)
            )
        )

    for copy in locals_:
        copy.wait()
    hops = z_size - 1
    for h in range(3):
        line(0, h)
    ring_step(0)
    line(1, 0)
    line(1, 1)
    ring_step(1)
    line(1, 2)
    ring_step(2)
    line(2, 0)
    line(2, 1)
    ring_end()
    for copy in gains:
        copy.start()
    line(2, 2)
    for k in range(3, hops):
        for h in range(3):
            line(k, h)

    settle(0, small_out.at[x])
    small_x = remote(small_out.at[x], small_out.at[x], x_send.at[0], x_recv.at[0], over_x)
    small_x.start()
    fins = (None, fin_gate, fin_conv)
    boths = (None, both_gate, both_conv)
    rows_in = in_ref.shape[0]
    swaps = {}
    for h in (1, 2):
        settle(h, fins[h])
        swaps[h] = []
        for k in range(1, 4):
            to = (corner + k) % 4
            copy = remote(
                fins[h].at[pl.ds(pl.multiple_of(to * rows_in, rows_in), rows_in)],
                boths[h].at[x, corner],
                swap_send.at[h - 1, k - 1],
                swap_recv.at[h - 1, k - 1],
                {"y": to // 2, "c": to % 2},
            )
            copy.start()
            swaps[h].append(copy)
        boths[h][x, corner] = fins[h][pl.ds(pl.multiple_of(corner * rows_in, rows_in), rows_in)]
        if h == 1:
            for copy in gains:
                copy.wait()
            gain_half[...] = jnp.sum(gain_got[...], axis=0)
            gain_x = remote(gain_half, gain_pair, x_send.at[3], x_recv.at[3], over_x)
            gain_x.start()
            for copy in swaps[1]:
                copy.wait()
            gate_x = remote(both_gate.at[x], both_gate.at[x], x_send.at[1], x_recv.at[1], over_x)
            gate_x.start()
    for copy in swaps[2]:
        copy.wait()
    conv_x = remote(both_conv.at[x], both_conv.at[x], x_send.at[2], x_recv.at[2], over_x)
    conv_x.start()

    half = small_ref.shape[1]
    branch = 8 * half * z_size

    def lay(h):
        first = branch if h == 1 else 0
        for zz in range(z_size):
            for j in range(4):
                for xx in range(2):
                    col = first + (zz * 4 + j) * 2 * half + xx * half
                    in_ref[:, col : col + half] = boths[h][xx, j, :, zz * half : (zz + 1) * half].astype(F32)

    gate_x.wait()
    lay(1)
    gain_x.wait()
    gain_out[...] = gain_half[...] + gain_pair[...]
    small_x.wait()
    conv_x.wait()
    lay(2)

    for k in range(hops):
        high = z_size - 1 - k
        for h in range(3):

            @pl.when(z < high)
            def _():
                up_copy(k, h).wait_send()

            @pl.when(z > k)
            def _():
                down_copy(k, h).wait_send()

    for k in range(RING - 1):
        ring(k).wait_send()
    for copy in sibs:
        copy.wait_send()


def last_sums(z_size, back, small, gate, conv, tokens, cot, gain, in_width):
    length, width = tokens.shape
    shares = z_size * 4
    hops = z_size - 1
    rows_in = gate.shape[1] // 4
    any_space = pl.BlockSpec(memory_space=pl.ANY)
    vmem = pl.BlockSpec(memory_space=pltpu.VMEM)
    dma = pltpu.SemaphoreType.DMA
    block = (length, width)
    slabs = [small.shape[1:], gate.shape[1:], conv.shape[1:]]
    bufs = lambda n: [pltpu.VMEM((n,) + s, BF16) for s in slabs]
    both = pltpu.VMEM((2, 4, rows_in, gate.shape[2]), BF16)
    piece = (8, width // shares)
    return pl.pallas_call(
        functools.partial(finish_kernel, z_size),
        in_specs=[any_space] * 4 + [vmem] * 3,
        out_specs=[vmem] * 4,
        out_shape=[
            jax.ShapeDtypeStruct(tokens.shape, BF16),
            jax.ShapeDtypeStruct((rows_in, in_width), F32),
            jax.ShapeDtypeStruct((2,) + slabs[0], BF16),
            jax.ShapeDtypeStruct(piece, F32),
        ],
        scratch_shapes=[
            pltpu.VMEM((RING,) + block, BF16),
            pltpu.VMEM((RING,) + block, BF16),
            pltpu.VMEM((RING - 1,) + block, BF16),
            pltpu.VMEM((RING - 1,) + block, BF16),
        ]
        + bufs(z_size)
        + bufs(hops)
        + bufs(hops)
        + bufs(hops)
        + bufs(hops)
        + [
            pltpu.VMEM(slabs[1], BF16),
            pltpu.VMEM(slabs[2], BF16),
            both,
            both,
            pltpu.VMEM((shares,) + piece, F32),
            pltpu.VMEM((shares,) + piece, F32),
            pltpu.VMEM(piece, F32),
            pltpu.VMEM(piece, F32),
            dma((3,)),
            dma((RING,)),
            dma((RING,)),
            dma((RING,)),
            dma((RING - 1,)),
            dma((RING - 1,)),
            dma((hops, 3)),
            dma((hops, 3)),
            dma((hops, 3)),
            dma((hops, 3)),
            dma((2, 3)),
            dma((2, 3)),
            dma((4,)),
            dma((4,)),
            dma((shares - 1,)),
            dma((shares - 1,)),
        ],
        compiler_params=pltpu.CompilerParams(
            collective_id=3, has_side_effects=True, vmem_limit_bytes=60 << 20
        ),
    )(back, small, gate, conv, tokens, cot, gain)


def silu_and_slope(v):
    s = jax.nn.sigmoid(v)
    return v * s, s * (1.0 + v * (1.0 - s))


def shift_down(v, j):
    return jnp.pad(v, ((j, 0),) + ((0, 0),) * (v.ndim - 1))[: v.shape[0]]


def shift_up(v, j):
    return jnp.pad(v, ((0, j),) + ((0, 0),) * (v.ndim - 1))[j:]


def shards(
    tokens,
    doc_ids,
    norm_gain,
    in_weight,
    conv_taps,
    conv_offset,
    select_weight,
    step_weight,
    step_bias,
    decay_log,
    skip_gain,
    out_weight,
    cotangent,
):
    z_size = lax.axis_size("z")
    rh_size = lax.axis_size("rh")
    seqs = 8
    length = doc_ids.shape[1]
    width = tokens.shape[1]
    in_rows = in_weight.shape[0]
    rows = out_weight.shape[0]
    half = rows // 2
    chans = half * z_size
    taps = conv_taps.shape[1]
    rank = step_weight.shape[1]
    states = decay_log.shape[1]
    x_at = lax.axis_index("x")

    def own_half(w):
        return lax.dynamic_slice_in_dim(w, x_at * half, half, 0)

    cuts = [taps, 1, 1, 1, states, rank + 2 * states, rank]
    ends = [sum(cuts[: i + 1]) for i in range(len(cuts))]
    room = -ends[-1] % 128

    def parts(v):
        return [v[:, e - n : e] for e, n in zip(ends, cuts)]

    small = jnp.concatenate(
        [
            own_half(conv_taps),
            own_half(conv_offset)[:, None],
            own_half(step_bias)[:, None],
            own_half(skip_gain)[:, None],
            own_half(decay_log),
            own_half(select_weight),
            own_half(step_weight),
            jnp.zeros((half, room), BF16),
        ],
        axis=1,
    )
    picked = lax.dynamic_index_in_dim(
        in_weight.reshape(in_rows, 2, z_size, 4, 2, half), x_at, 4, keepdims=False
    )
    packed = picked.transpose(1, 3, 0, 2, 4).reshape(2, 4, in_rows, chans)
    gain_tile = jnp.broadcast_to(norm_gain.astype(F32)[None, :], (8, norm_gain.shape[0]))
    ids_tile = jnp.broadcast_to(doc_ids, (8, length))
    all_normed, w_conv, gate_slab, small_all, ids, gains = start_gathers(
        z_size, tokens, gain_tile, ids_tile, packed[0], packed[1], small
    )
    all_normed = all_normed.reshape(-1, width)
    w_conv = w_conv.reshape(-1, chans)
    w_gate = lax.all_gather(gate_slab, "z", axis=0, tiled=True).reshape(-1, chans)
    w_taps, w_offset, w_bias, w_skip, w_decay, w_select, w_step = parts(
        small_all.reshape(chans, -1)
    )
    w_out = lax.all_gather(own_half(out_weight), "z", axis=0, tiled=True)
    gain = gains[:, 0, :].reshape(1, width)
    ids = ids[:, 0, :].T
    all_cot = lax.all_gather(cotangent, PLANE, axis=0, tiled=True)
    residual = tokens.astype(F32)

    def time_major(v):
        return v.reshape(seqs, length, -1).swapaxes(0, 1)

    def seq_major(v):
        return v.reshape(length, seqs, -1).swapaxes(0, 1).reshape(seqs * length, -1)

    conv_in = time_major(dot_nn(all_normed, w_conv))
    gate_in = time_major(dot_nn(all_normed, w_gate))
    same = [
        (shift_down(ids + 1, j) == ids + 1).astype(F32)[:, :, None] for j in range(taps)
    ]
    tap = [w_taps[:, taps - 1 - j].astype(F32) for j in range(taps)]
    conv_out = w_offset[:, 0].astype(F32) + sum(
        shift_down(conv_in, j) * same[j] * tap[j] for j in range(taps)
    )
    selected_f, conv_slope = silu_and_slope(conv_out)
    selected = selected_f.astype(BF16)
    x = selected.astype(F32)
    flat = lambda v: v.reshape(length * seqs, -1)
    spare = -(rank + 2 * states) % 128
    wide_select = jnp.pad(w_select, ((0, 0), (0, spare)))
    selection = plane_total(dot_nn(flat(selected), wide_select), 1)
    rank_in = selection[:, :rank]
    bc = selection[:, rank : rank + 2 * states].astype(F32).reshape(length, seqs, 2 * states)
    pre = dot_nt(rank_in, w_step).reshape(length, seqs, chans) + w_bias[:, 0].astype(F32)
    dt = jax.nn.softplus(pre)
    dtm = dt + (1.0 - same[1]) * BIG
    rates = -jnp.exp(w_decay.astype(F32)).T
    rate2 = jnp.broadcast_to((rates * LOG2E)[:, None, :], (states, seqs, chans))
    y, hist, last = scan_forward(dt, dtm, x, bc, rate2)
    skip = w_skip[:, 0].astype(F32)
    scanned = y + skip * x
    gate, gate_slope = silu_and_slope(gate_in)
    gated = seq_major((scanned * gate).astype(BF16))
    out_part = dot_nn(gated, w_out).astype(BF16)
    layer_sum = lax.psum_scatter(out_part, PLANE, scatter_dimension=0, tiled=True)
    layer_out = (residual + layer_sum.astype(F32)).astype(BF16)

    grad_out = dot_tn(gated, all_cot).astype(BF16)
    back_gated = time_major(dot_nt(all_cot, w_out).astype(BF16)).astype(F32)
    back_scan = back_gated * gate
    back_gate_in = back_gated * scanned * gate_slope
    s1, s2, back_bc, da = scan_backward(dt, dtm, x, back_scan, bc, rate2, hist, last)
    back_steps = s1 * (1.0 / LOG2E) + x * s2
    back_x = dt * s2 + skip * back_scan
    grad_decay = da.sum(1).T * rates.T
    grad_skip = (back_scan * x).sum((0, 1))
    back_pre = back_steps * jax.nn.sigmoid(pre)
    grad_bias = back_pre.sum((0, 1))
    back_pre = flat(back_pre.astype(BF16))
    grad_step = dot_tn(back_pre, rank_in)
    back_rank = dot_nn(back_pre, w_step)
    back_selection = plane_total(
        jnp.concatenate([back_rank, back_bc[:, : rank + 2 * states + spare - rank]], axis=1), 2
    )[:, : rank + 2 * states]
    grad_select = dot_tn(flat(selected), back_selection)
    back_selected = dot_nt(back_selection, w_select).reshape(length, seqs, chans) + back_x
    back_conv = back_selected * conv_slope
    grad_offset = back_conv.sum((0, 1))
    grad_taps = jnp.stack(
        [
            (back_conv * shift_down(conv_in, j) * same[j]).sum((0, 1))
            for j in reversed(range(taps))
        ],
        axis=1,
    )
    back_conv_in = sum(
        shift_up(back_conv * same[j], j) * tap[j] for j in range(taps)
    )
    back_conv_in = seq_major(back_conv_in.astype(BF16))
    back_gate_in = seq_major(back_gate_in.astype(BF16))
    back_part = (dot_nt(back_conv_in, w_conv) + dot_nt(back_gate_in, w_gate)).astype(BF16)
    grad_conv = dot_tn(all_normed, back_conv_in).astype(BF16)
    grad_gate = dot_tn(all_normed, back_gate_in).astype(BF16)
    small_grad = jnp.concatenate(
        [
            grad_taps,
            grad_offset[:, None],
            grad_bias[:, None],
            grad_skip[:, None],
            grad_decay,
            grad_select,
            grad_step,
            jnp.zeros((chans, room), F32),
        ],
        axis=1,
    ).astype(BF16)
    tokens_grad, g_in, small_own, g_gain = last_sums(
        z_size,
        back_part.reshape(4, 2, length, width),
        small_grad.reshape(z_size, half, -1),
        grad_gate.reshape(z_size, -1, chans),
        grad_conv.reshape(z_size, -1, chans),
        tokens,
        cotangent,
        gain,
        in_weight.shape[1],
    )
    g_gain = g_gain[0]
    own_out = lax.psum_scatter(grad_out, "z", scatter_dimension=0, tiled=True)
    if rh_size > 1:
        small_own, g_in, own_out, g_gain = lax.psum(
            (small_own.astype(F32), g_in, own_out, g_gain), "rh"
        )
    g_out = lax.all_gather(own_out, "x", axis=0, tiled=True).astype(F32)
    g_taps, g_offset, g_bias, g_skip, g_decay, g_select, g_step = [
        v.astype(F32) for v in parts(small_own.reshape(rows, -1))
    ]
    return (
        layer_out,
        tokens_grad,
        g_gain,
        g_in,
        g_taps,
        g_offset[:, 0],
        g_select,
        g_step,
        g_bias[:, 0],
        g_decay,
        g_skip[:, 0],
        g_out,
    )


def solution(mesh):
    replicas = mesh.shape["replica"]
    shares = mesh.shape["fsdp"]
    grid = Mesh(
        mesh.devices.reshape(replicas // 2, 2, shares // 4, 2, 2), ("rh", "x", "z", "y", "c")
    )
    tok = ("rh", "x", "z", "y", "c")
    own = ("z", "y", "c")
    return jax.shard_map(
        shards,
        mesh=grid,
        in_specs=(
            P(tok, None),
            P(tok, None),
            P(own),
            P(own, None),
            P(own, None),
            P(own),
            P(own, None),
            P(own, None),
            P(own),
            P(own, None),
            P(own),
            P(own, None),
            P(tok, None),
        ),
        out_specs=(
            P(tok, None),
            P(tok, None),
            P(own),
            P(own, None),
            P(own, None),
            P(own),
            P(own, None),
            P(own, None),
            P(own),
            P(own, None),
            P(own),
            P(own, None),
        ),
        check_vma=False,
    )
```

```python
import functools

import jax
import jax.numpy as jnp
from jax import lax
from jax.experimental import pallas as pl
from jax.experimental.pallas import tpu as pltpu
from jax.sharding import Mesh
from jax.sharding import PartitionSpec as P

F32 = jnp.float32
BF16 = jnp.bfloat16
epsilon = 1e-05
PLANE = ("x", "y", "c")
BIG = 1e30
STEPS = 32
INNER = 4
LOG2E = 1.4426950408889634


def dot(a, b, dims):
    return lax.dot_general(a, b, (dims, ((), ())), preferred_element_type=F32)


def dot_nn(a, b):
    return dot(a, b, ((1,), (0,)))


def dot_tn(a, b):
    return dot(a, b, ((0,), (0,)))


def dot_nt(a, b):
    return dot(a, b, ((1,), (1,)))


def busy(micros):
    return pl.CostEstimate(flops=micros * 10**9, bytes_accessed=micros * 10**6, transcendentals=0)


def fwd_kernel(states, dt_ref, dtm_ref, x_ref, bc_ref, rate_ref, y_ref, hist_ref, last_ref, h_ref):
    @pl.when(pl.program_id(0) == 0)
    def _():
        h_ref[...] = jnp.zeros_like(h_ref)

    width = dt_ref.shape[2]
    groups = width // 128

    def body(tb, carry):
        t0 = tb * INNER
        bc = [bc_ref[t0 + i] for i in range(INNER)]
        for g in range(groups):
            lanes = pl.ds(g * 128, 128)
            dtm = [dtm_ref[t0 + i, :, lanes] for i in range(INNER)]
            u = [dt_ref[t0 + i, :, lanes] * x_ref[t0 + i, :, lanes] for i in range(INNER)]
            y = [None] * INNER
            for n in range(states):
                h = h_ref[n, :, lanes]
                rate = rate_ref[n, :, lanes]
                for i in range(INNER):
                    hist_ref[t0 + i, n, :, lanes] = h
                    a = jnp.exp2(dtm[i] * rate)
                    h = a * h + u[i] * bc[i][:, n : n + 1]
                    term = h * bc[i][:, states + n : states + n + 1]
                    y[i] = term if y[i] is None else y[i] + term
                h_ref[n, :, lanes] = h
            for i in range(INNER):
                y_ref[t0 + i, :, lanes] = y[i]
        return carry

    lax.fori_loop(0, dt_ref.shape[0] // INNER, body, 0)
    last_ref[...] = h_ref[...]


def scan_forward(dt, dtm, x, bc, rate):
    length, seqs, width = dt.shape
    states = rate.shape[0]
    block = lambda *tail: pl.BlockSpec((STEPS,) + tail, lambda i: (i,) + (0,) * len(tail))
    whole = lambda *dims: pl.BlockSpec(dims, lambda i: (0,) * len(dims))
    return pl.pallas_call(
        functools.partial(fwd_kernel, states),
        grid=(length // STEPS,),
        in_specs=[
            block(seqs, width),
            block(seqs, width),
            block(seqs, width),
            block(seqs, 2 * states),
            whole(states, seqs, width),
        ],
        out_specs=[block(seqs, width), block(states, seqs, width), whole(states, seqs, width)],
        out_shape=[
            jax.ShapeDtypeStruct(dt.shape, F32),
            jax.ShapeDtypeStruct((length, states, seqs, width), F32),
            jax.ShapeDtypeStruct((states, seqs, width), F32),
        ],
        scratch_shapes=[pltpu.VMEM((states, seqs, width), F32)],
        cost_estimate=busy(30),
        compiler_params=pltpu.CompilerParams(vmem_limit_bytes=56 << 20),
    )(dt, dtm, x, bc, rate)


def bwd_kernel(
    states,
    dt_ref,
    dtm_ref,
    x_ref,
    ds_ref,
    bc_ref,
    rate_ref,
    hist_ref,
    last_ref,
    ones_ref,
    s1_ref,
    s2_ref,
    gates_ref,
    da_ref,
    ag_ref,
    h_ref,
    pb_ref,
    pc_ref,
):
    @pl.when(pl.program_id(0) == 0)
    def _():
        ag_ref[...] = jnp.zeros_like(ag_ref)
        da_ref[...] = jnp.zeros_like(da_ref)
        h_ref[...] = last_ref[...]

    steps, seqs, width = dt_ref.shape
    groups = width // 128
    blocks = steps // INNER

    def body(back, carry):
        t0 = (blocks - 1 - back) * INNER
        rows = pl.multiple_of(t0 * seqs, INNER * seqs)
        bc = [bc_ref[t0 + i] for i in range(INNER)]
        for g in range(groups):
            lanes = pl.ds(g * 128, 128)
            dt = [dt_ref[t0 + i, :, lanes] for i in range(INNER)]
            dtm = [dtm_ref[t0 + i, :, lanes] for i in range(INNER)]
            ds = [ds_ref[t0 + i, :, lanes] for i in range(INNER)]
            u = [dt[i] * x_ref[t0 + i, :, lanes] for i in range(INNER)]
            s1 = [None] * INNER
            s2 = [None] * INNER
            for n in range(states):
                ag = ag_ref[n, :, lanes]
                h = h_ref[n, :, lanes]
                rate = rate_ref[n, :, lanes]
                da = da_ref[n, :, lanes]
                pb = [None] * INNER
                pc = [None] * INNER
                for i in reversed(range(INNER)):
                    prev = hist_ref[t0 + i, n, :, lanes]
                    a = jnp.exp2(dtm[i] * rate)
                    adj = ds[i] * bc[i][:, states + n : states + n + 1] + ag
                    pc[i] = ds[i] * h
                    pb[i] = adj * u[i]
                    ag = a * adj
                    w = ag * prev
                    rw = rate * w
                    gb = adj * bc[i][:, n : n + 1]
                    s1[i] = rw if s1[i] is None else s1[i] + rw
                    s2[i] = gb if s2[i] is None else s2[i] + gb
                    da = da + dt[i] * w
                    h = prev
                ag_ref[n, :, lanes] = ag
                h_ref[n, :, lanes] = h
                da_ref[n, :, lanes] = da
                cols = pl.ds((g * states + n) * 128, 128)
                pb_ref[pl.ds(rows, INNER * seqs), cols] = jnp.concatenate(pb, axis=0).astype(BF16)
                pc_ref[pl.ds(rows, INNER * seqs), cols] = jnp.concatenate(pc, axis=0).astype(BF16)
            for i in range(INNER):
                s1_ref[t0 + i, :, lanes] = s1[i]
                s2_ref[t0 + i, :, lanes] = s2[i]
        return carry

    lax.fori_loop(0, blocks, body, 0)
    span = states * 128
    total = jnp.zeros((steps * seqs, 128), F32)
    for g in range(groups):
        total = total + dot_nn(pb_ref[:, pl.ds(g * span, span)], ones_ref[0])
        total = total + dot_nn(pc_ref[:, pl.ds(g * span, span)], ones_ref[1])
    gates_ref[...] = total


def scan_backward(dt, dtm, x, ds, bc, rate, hist, last):
    length, seqs, width = dt.shape
    states = rate.shape[0]
    chunks = length // STEPS
    block = lambda *tail: pl.BlockSpec((STEPS,) + tail, lambda i: (chunks - 1 - i,) + (0,) * len(tail))
    whole = lambda *dims: pl.BlockSpec(dims, lambda i: (0,) * len(dims))
    span = states * 128
    entry = jnp.arange(span)[:, None] // 128
    column = jnp.arange(128)[None, :]
    ones = jnp.stack([entry == column, entry + states == column]).astype(BF16)
    return pl.pallas_call(
        functools.partial(bwd_kernel, states),
        grid=(chunks,),
        in_specs=[
            block(seqs, width),
            block(seqs, width),
            block(seqs, width),
            block(seqs, width),
            block(seqs, 2 * states),
            whole(states, seqs, width),
            block(states, seqs, width),
            whole(states, seqs, width),
            whole(2, span, 128),
        ],
        out_specs=[
            block(seqs, width),
            block(seqs, width),
            pl.BlockSpec((STEPS * seqs, 128), lambda i: (chunks - 1 - i, 0)),
            whole(states, seqs, width),
        ],
        out_shape=[
            jax.ShapeDtypeStruct(dt.shape, F32),
            jax.ShapeDtypeStruct(dt.shape, F32),
            jax.ShapeDtypeStruct((length * seqs, 128), F32),
            jax.ShapeDtypeStruct((states, seqs, width), F32),
        ],
        scratch_shapes=[
            pltpu.VMEM((states, seqs, width), F32),
            pltpu.VMEM((states, seqs, width), F32),
            pltpu.VMEM((STEPS * seqs, width // 128 * span), BF16),
            pltpu.VMEM((STEPS * seqs, width // 128 * span), BF16),
        ],
        cost_estimate=busy(70),
        compiler_params=pltpu.CompilerParams(vmem_limit_bytes=60 << 20),
    )(dt, dtm, x, ds, bc, rate, hist, last, ones)


MESH = pl.DeviceIdType.MESH
RING = 4


def place():
    return {a: lax.axis_index(a) for a in ("x", "z", "y", "c")}


def ring_chip(p):
    y = p // 2
    return (p + y) % 2, y


def ring_at(x, y):
    return 2 * y + (x + y) % 2


def share_at(f):
    return {"z": f // 4, "y": f // 2 % 2, "c": f % 2}


def remote(src, dst, send, recv, device):
    return pltpu.make_async_remote_copy(
        src_ref=src, dst_ref=dst, send_sem=send, recv_sem=recv, device_id=device, device_id_type=MESH
    )


def greet(devices):
    barrier = pltpu.get_barrier_semaphore()
    for device in devices:
        pl.semaphore_signal(barrier, inc=1, device_id=device, device_id_type=MESH)
    pl.semaphore_wait(barrier, len(devices))


def plane_others(me):
    out = []
    for dx in range(2):
        for dy in range(2):
            for dc in range(2):
                if dx + dy + dc:
                    out.append(
                        {"x": (me["x"] + dx) % 2, "y": (me["y"] + dy) % 2, "c": (me["c"] + dc) % 2}
                    )
    return out


def share_others(me, shares):
    f = me["z"] * 4 + me["y"] * 2 + me["c"]
    return [share_at((f + k) % shares) for k in range(1, shares)]


def z_only(me, shares):
    f = me["c"] + 2 * me["y"]
    out = []
    for dz in range(1, shares // 4):
        for k in range(4):
            out.append(
                {
                    "z": (me["z"] + dz) % (shares // 4),
                    "y": (f + k) % 4 // 2,
                    "c": (f + k) % 2,
                }
            )
    return out


def z_line(z, z_size, pieces, sems):
    up_s, up_r, down_s, down_r = sems

    def up(k):
        return [
            remote(p(z - k), p(z - k), up_s.at[k, j], up_r.at[k, j], {"z": z + 1})
            for j, p in enumerate(pieces)
        ]

    def down(k):
        return [
            remote(p(z + k), p(z + k), down_s.at[k, j], down_r.at[k, j], {"z": z - 1})
            for j, p in enumerate(pieces)
        ]

    def start(k):
        @pl.when((z < z_size - 1) & (z >= k))
        def _():
            for copy in up(k):
                copy.start()

        @pl.when((z > 0) & (z + k < z_size))
        def _():
            for copy in down(k):
                copy.start()

    def arrive(k):
        @pl.when(z > k)
        def _():
            for copy in up(k):
                copy.wait_recv()

        @pl.when(z + k < z_size - 1)
        def _():
            for copy in down(k):
                copy.wait_recv()

    def sent(k):
        @pl.when((z < z_size - 1) & (z >= k))
        def _():
            for copy in up(k):
                copy.wait_send()

        @pl.when((z > 0) & (z + k < z_size))
        def _():
            for copy in down(k):
                copy.wait_send()

    return start, arrive, sent


class Ring:
    def __init__(self, me, blocks, own, ring_send, ring_recv, sib_send, sib_recv):
        self.me, self.blocks, self.own = me, blocks, own
        self.sems = ring_send, ring_recv, sib_send, sib_recv
        self.at = ring_at(me["x"], me["y"])
        self.step = 1 + 2 * me["c"]
        nx, ny = ring_chip((self.at + self.step) % RING)
        self.following = {"x": nx, "y": ny}
        self.sibling = {"c": 1 - me["c"]}
        self.half = blocks.shape[1] // 2

    def slot(self, k):
        ox, oy = ring_chip((self.at + (RING - self.step) * k) % RING)
        return ox * 4 + oy * 2 + self.me["c"]

    def hop(self, k):
        out = []
        for p in range(2):
            rows = pl.ds(p * self.half, self.half)
            dst = self.blocks.at[self.slot(k), rows]
            src = self.own.at[rows] if k == 0 and self.own is not None else dst
            out.append(remote(src, dst, self.sems[0].at[k, p], self.sems[1].at[k, p], self.following))
        return out

    def cross(self, k):
        dst = self.blocks.at[self.slot(k)]
        src = self.own if k == 0 and self.own is not None else dst
        return remote(src, dst, self.sems[2].at[k], self.sems[3].at[k], self.sibling)

    def start(self, k):
        if k < RING - 1:
            for copy in self.hop(k):
                copy.start()
        self.cross(k).start()

    def arrive(self, k):
        for copy in self.hop(k):
            copy.wait_recv()

    def sent(self, k):
        if k < RING - 1:
            for copy in self.hop(k):
                copy.wait_send()
        self.cross(k).wait()


def softplus(v):
    e = jnp.exp(-jnp.abs(v))
    small = e * (1.0 - e * (0.5 - e * (1.0 / 3.0)))
    return jnp.maximum(v, 0.0) + jnp.where(e < 1e-3, small, jnp.log(1.0 + e))


def front_kernel(
    z_size,
    taps,
    rank,
    tokens_ref,
    gain_ref,
    ids_ref,
    rows_ref,
    cot_ref,
    conv_ref,
    gate_ref,
    out_ref,
    mats_ref,
    normed_hbm,
    cot_all,
    conv_hbm,
    gate_all,
    out_all,
    mats_hbm,
    keep_hbm,
    cin_hbm,
    x_hbm,
    dt_hbm,
    pre_hbm,
    params,
    gain_all,
    selection,
    normed_all,
    conv_w,
    mats,
    rows_all,
    gain_got,
    ids_all,
    proj,
    cin,
    xs,
    picked,
    part,
    dts,
    pres,
    keep,
    first,
    from_sib,
    stage,
    got,
    local_sem,
    gain_send,
    gain_recv,
    ids_send,
    ids_recv,
    conv_send,
    conv_recv,
    gate_send,
    gate_recv,
    ring_send,
    ring_recv,
    sib_send,
    sib_recv,
    cot_ring_send,
    cot_ring_recv,
    cot_sib_send,
    cot_sib_recv,
    a_us,
    a_ur,
    a_ds,
    a_dr,
    b_us,
    b_ur,
    b_ds,
    b_dr,
    sw_s,
    sw_r,
    rs_s,
    rs_r,
    ag_s,
    ag_r,
    fw_s,
    fw_r,
):
    me = place()
    x, y, z, c = me["x"], me["y"], me["z"], me["c"]
    shares = z_size * 4
    share = z * 4 + y * 2 + c
    corner = y * 2 + c
    seq = x * 4 + y * 2 + c
    sibling = {"c": 1 - c}
    length, width = tokens_ref.shape
    chans = conv_ref.shape[2]
    rows_in = conv_ref.shape[1]
    half = mats_ref.shape[0]
    hops = z_size - 1
    greet(plane_others(me) + z_only(me, shares))

    def rows_at(ref, index, count):
        return ref.at[pl.ds(pl.multiple_of(index * count, count), count)]

    def corner_sends(src, dst, send, recv):
        out = []
        for k in range(1, 4):
            to = (corner + k) % 4
            out.append(
                remote(
                    src.at[to],
                    rows_at(dst, share, rows_in),
                    send.at[k - 1],
                    recv.at[k - 1],
                    {"y": to // 2, "c": to % 2},
                )
            )
        return out

    swaps = corner_sends(conv_ref, conv_w, conv_send, conv_recv)
    gates = corner_sends(gate_ref, gate_all, gate_send, gate_recv)
    for copy in swaps:
        copy.start()
    gains = [
        remote(gain_ref, gain_got.at[share], gain_send.at[k], gain_recv.at[k], device)
        for k, device in enumerate(share_others(me, shares))
    ]
    for copy in gains:
        copy.start()
    locals_ = [
        pltpu.make_async_copy(conv_ref.at[corner], rows_at(conv_w, share, rows_in), local_sem.at[0]),
        pltpu.make_async_copy(mats_ref, rows_at(mats, z, half), local_sem.at[1]),
        pltpu.make_async_copy(gate_ref.at[corner], rows_at(gate_all, share, rows_in), local_sem.at[2]),
        pltpu.make_async_copy(out_ref, rows_at(out_all, z, half), local_sem.at[3]),
        pltpu.make_async_copy(cot_ref, cot_all.at[seq], local_sem.at[4]),
    ]
    for copy in locals_:
        copy.start()
    ids_copies = [
        remote(ids_ref, ids_all.at[seq], ids_send.at[k], ids_recv.at[k], device)
        for k, device in enumerate(plane_others(me))
    ]
    for copy in ids_copies:
        copy.start()
    ids_all[seq] = ids_ref[...]
    gain_got[share] = gain_ref[...]
    rows_all[z] = rows_ref[...]

    values = tokens_ref[...].astype(F32)
    rstd = lax.rsqrt(jnp.mean(values * values, axis=-1, keepdims=True) + epsilon)
    for copy in gains:
        copy.wait()
    piece = gain_ref.shape[1]
    for f in range(shares):
        cols = pl.ds(f * piece, piece)
        normed = tokens_ref[:, cols].astype(F32) * rstd * gain_got[f, 0:1, :]
        normed_all[seq, :, cols] = normed.astype(BF16)
    gain_all[...] = gain_got[...]

    ring = Ring(me, normed_all, None, ring_send, ring_recv, sib_send, sib_recv)
    cot_ring = Ring(me, cot_all, cot_ref, cot_ring_send, cot_ring_recv, cot_sib_send, cot_sib_recv)
    ring.start(0)
    for copy in swaps:
        copy.wait()
    for copy in locals_:
        copy.wait()
    a_start, a_arrive, a_sent = z_line(
        z,
        z_size,
        [
            lambda k: rows_at(conv_w, k, 4 * rows_in),
            lambda k: rows_at(mats, k, half),
            lambda k: rows_all.at[k],
        ],
        (a_us, a_ur, a_ds, a_dr),
    )
    b_start, b_arrive, b_sent = z_line(
        z,
        z_size,
        [lambda k: rows_at(gate_all, k, 4 * rows_in), lambda k: rows_at(out_all, k, half)],
        (b_us, b_ur, b_ds, b_dr),
    )
    a_start(0)
    for copy in gates:
        copy.start()

    for copy in ids_copies:
        copy.wait()
    ids = jnp.concatenate([ids_all[s, 0:1, :] for s in range(8)], axis=0).astype(F32)
    before = pltpu.roll(ids, 1, 1)
    lane = lax.broadcasted_iota(jnp.int32, ids.shape, 1)
    same = jnp.where((ids == before) & (lane > 0), 1.0, 0.0)
    for t in range(length):
        keep[t] = jnp.broadcast_to(same[:, t : t + 1], (8, 128))
    keep_copy = pltpu.make_async_copy(keep, keep_hbm, local_sem.at[5])
    keep_copy.start()

    for k in range(max(hops, RING - 1)):
        if k < hops:
            a_arrive(k)
            if k + 1 < hops:
                a_start(k + 1)
        if k < RING - 1:
            ring.arrive(k)
            ring.start(k + 1)
        if k == RING - 2:
            cot_ring.start(0)
    for copy in gates:
        copy.wait()
    b_start(0)
    for k in range(RING):
        ring.sent(k)
    outs = [
        pltpu.make_async_copy(normed_all, normed_hbm, local_sem.at[6]),
        pltpu.make_async_copy(conv_w, conv_hbm, local_sem.at[7]),
        pltpu.make_async_copy(mats, mats_hbm, local_sem.at[8]),
    ]
    for copy in outs:
        copy.start()
    for zz in range(z_size):
        params[:, zz * half : (zz + 1) * half] = rows_all[zz].astype(F32)

    def project(s, carry):
        proj[s] = dot_nn(normed_all[s], conv_w[...])
        return carry

    lax.fori_loop(0, 8, project, 0)

    cin[0:3] = jnp.zeros((3, 8, chans), F32)
    block = 32
    fine = 4

    def turn(i, carry):
        t0 = pl.multiple_of(i * block, block)
        cin[pl.ds(3 + t0, block)] = jnp.swapaxes(proj[:, pl.ds(t0, block), :], 0, 1)
        return carry

    lax.fori_loop(0, length // block, turn, 0)

    def convolve(i, carry):
        t0 = i * fine
        for g in range(chans // 128):
            lanes = pl.ds(g * 128, 128)
            tap = [jnp.broadcast_to(params[taps - 1 - j : taps - j, lanes], (8, 128)) for j in range(taps)]
            offset = jnp.broadcast_to(params[taps : taps + 1, lanes], (8, 128))
            chosen = []
            for j in range(fine):
                t = t0 + j
                total = tap[3] * cin[t, :, lanes] * keep[jnp.maximum(t - 2, 0)]
                total = (total + tap[2] * cin[t + 1, :, lanes]) * keep[jnp.maximum(t - 1, 0)]
                total = (total + tap[1] * cin[t + 2, :, lanes]) * keep[t]
                v = total + tap[0] * cin[t + 3, :, lanes] + offset
                chosen.append((v / (1.0 + jnp.exp(-v))).astype(BF16))
                xs[t, :, lanes] = chosen[-1].astype(F32)
            rows = pl.ds(pl.multiple_of(t0 * 8, fine * 8), fine * 8)
            picked[rows, lanes] = jnp.concatenate(chosen, axis=0)
        return carry

    lax.fori_loop(0, length // fine, convolve, 0)
    outs += [
        pltpu.make_async_copy(cin.at[pl.ds(3, length)], cin_hbm, local_sem.at[9]),
        pltpu.make_async_copy(xs, x_hbm, local_sem.at[10]),
    ]
    for copy in outs[3:]:
        copy.start()

    wide = part.shape[3]

    def select(b, carry):
        rows = pl.ds(pl.multiple_of(b * length, length), length)
        part[b // 2, b % 2] = dot_nn(picked[rows, :], mats[:, :wide])
        return carry

    lax.fori_loop(0, 8, select, 0)
    first[...] = part[:, 1 - c].astype(BF16)
    swap = remote(first, from_sib, sw_s.at[0], sw_r.at[0], sibling)
    swap.start()
    swap.wait()
    mine = x * 2 + y
    chips = [((x + d // 2) % 2, (y + d % 2) % 2) for d in (1, 2, 3)]
    sends = []
    for k in (2, 1, 0):
        ox, oy = chips[k]
        j = ox * 2 + oy
        stage[k] = (part[j, c] + from_sib[j].astype(F32)).astype(BF16)
        copy = remote(stage.at[k], got.at[k], rs_s.at[k], rs_r.at[k], {"x": ox, "y": oy})
        copy.start()
        sends.append(copy)
    total = part[mine, c] + from_sib[mine].astype(F32)
    for copy in sends:
        copy.wait()
    for k in range(3):
        total = total + got[k].astype(F32)
    selection[mine, c] = total.astype(BF16)
    here = selection.at[mine, c]
    spreads = []
    for k in (2, 1, 0):
        ox, oy = chips[k]
        copy = remote(here, here, ag_s.at[k], ag_r.at[k], {"x": ox, "y": oy})
        copy.start()
        spreads.append((k, copy))
    forwards = [remote(here, here, fw_s.at[3], fw_r.at[3], sibling)]
    forwards[0].start()
    if hops > 1:
        b_arrive(0)
        b_start(1)
    cot_ring.arrive(0)
    cot_ring.start(1)
    for k, copy in reversed(spreads):
        copy.wait_recv()
        ox, oy = chips[k]
        there = selection.at[ox * 2 + oy, c]
        forwards.append(remote(there, there, fw_s.at[k], fw_r.at[k], sibling))
        forwards[-1].start()
    for _, copy in spreads:
        copy.wait_send()
    for copy in forwards:
        copy.wait()

    bias = params[taps + 1 : taps + 2, :]

    def steps(i, carry):
        rows = 64
        per = length // rows
        b = i // per
        at = pl.ds(pl.multiple_of((i % per) * rows, rows), rows)
        v = dot_nt(selection[b // 2, b % 2, at, :rank], mats[:, wide : wide + rank]) + bias
        t = pl.ds(i * (rows // 8), rows // 8)
        pres[t] = v.reshape(rows // 8, 8, chans)
        dts[t] = softplus(v).reshape(rows // 8, 8, chans)
        return carry

    lax.fori_loop(0, length * 8 // 64, steps, 0)
    outs += [
        pltpu.make_async_copy(dts, dt_hbm, local_sem.at[11]),
        pltpu.make_async_copy(pres, pre_hbm, local_sem.at[12]),
    ]
    for copy in outs[5:]:
        copy.start()

    cot_ring.arrive(1)
    cot_ring.start(2)
    for k in range(1 if hops > 1 else 0, hops):
        b_arrive(k)
        if k + 1 < hops:
            b_start(k + 1)
    cot_ring.arrive(2)
    cot_ring.start(3)
    for k in range(RING):
        cot_ring.sent(k)
    for k in range(hops):
        a_sent(k)
        b_sent(k)
    for copy in outs + [keep_copy]:
        copy.wait()


def front(z_size, taps, rank, tokens, gain, ids, rows, cot, conv, gate, out, mats):
    length, width = tokens.shape
    shares = z_size * 4
    chans = conv.shape[2]
    wide = mats.shape[1] - rank
    any_space = pl.BlockSpec(memory_space=pl.ANY)
    vmem = pl.BlockSpec(memory_space=pltpu.VMEM)
    dma = pltpu.SemaphoreType.DMA
    hops = z_size - 1
    shape = jax.ShapeDtypeStruct
    everyone = (8,) + tokens.shape
    per_token = (length, 8, chans)
    block = (length, wide)
    return pl.pallas_call(
        functools.partial(front_kernel, z_size, taps, rank),
        in_specs=[vmem] * 8 + [any_space],
        out_specs=[any_space] * 11 + [vmem] * 3,
        out_shape=[
            shape(everyone, BF16),
            shape(everyone, BF16),
            shape((width, chans), BF16),
            shape((width, chans), BF16),
            shape((chans, width), BF16),
            shape((chans, mats.shape[1]), BF16),
            shape((length, 8, 128), F32),
            shape(per_token, F32),
            shape(per_token, F32),
            shape(per_token, F32),
            shape(per_token, F32),
            shape((rows.shape[0], chans), F32),
            shape((shares,) + gain.shape, F32),
            shape((4, 2) + block, BF16),
        ],
        scratch_shapes=[
            pltpu.VMEM(everyone, BF16),
            pltpu.VMEM((width, chans), BF16),
            pltpu.VMEM((chans, mats.shape[1]), BF16),
            pltpu.VMEM((z_size,) + rows.shape, BF16),
            pltpu.VMEM((shares,) + gain.shape, F32),
            pltpu.VMEM((8,) + ids.shape, ids.dtype),
            pltpu.VMEM((8, length, chans), F32),
            pltpu.VMEM((length + 3, 8, chans), F32),
            pltpu.VMEM(per_token, F32),
            pltpu.VMEM((length * 8, chans), BF16),
            pltpu.VMEM((4, 2) + block, F32),
            pltpu.VMEM(per_token, F32),
            pltpu.VMEM(per_token, F32),
            pltpu.VMEM((length, 8, 128), F32),
            pltpu.VMEM((4,) + block, BF16),
            pltpu.VMEM((4,) + block, BF16),
            pltpu.VMEM((3,) + block, BF16),
            pltpu.VMEM((3,) + block, BF16),
            dma((13,)),
            dma((shares - 1,)),
            dma((shares - 1,)),
            dma((7,)),
            dma((7,)),
        ]
        + [dma((3,))] * 4
        + [dma((RING - 1, 2)), dma((RING - 1, 2)), dma((RING,)), dma((RING,))] * 2
        + [dma((hops, 3))] * 4
        + [dma((hops, 2))] * 4
        + [dma((1,))] * 2
        + [dma((3,))] * 4
        + [dma((4,))] * 2,
        cost_estimate=busy(120),
        compiler_params=pltpu.CompilerParams(
            collective_id=0, has_side_effects=True, vmem_limit_bytes=60 << 20
        ),
    )(tokens, gain, ids, rows, cot, conv, gate, out, mats)


def total_kernel(part_ref, out_ref, first, from_sib, stage, got, sib_s, sib_r, rs_s, rs_r, ag_s, ag_r, fw_s, fw_r):
    me = place()
    x, y, c = me["x"], me["y"], me["c"]
    greet(plane_others(me))
    sibling = {"c": 1 - c}
    first[...] = part_ref[:, 1 - c].astype(BF16)
    swap = remote(first, from_sib, sib_s, sib_r, sibling)
    swap.start()
    swap.wait()
    mine = x * 2 + y
    chips = [((x + d // 2) % 2, (y + d % 2) % 2) for d in (1, 2, 3)]
    sends = []
    for k in (2, 1, 0):
        ox, oy = chips[k]
        j = ox * 2 + oy
        stage[k] = (part_ref[j, c] + from_sib[j].astype(F32)).astype(BF16)
        copy = remote(stage.at[k], got.at[k], rs_s.at[k], rs_r.at[k], {"x": ox, "y": oy})
        copy.start()
        sends.append(copy)
    total = part_ref[mine, c] + from_sib[mine].astype(F32)
    for copy in sends:
        copy.wait()
    for k in range(3):
        total = total + got[k].astype(F32)
    out_ref[mine, c] = total.astype(BF16)
    spreads = []
    for k in (2, 1, 0):
        ox, oy = chips[k]
        here = out_ref.at[mine, c]
        copy = remote(here, here, ag_s.at[k], ag_r.at[k], {"x": ox, "y": oy})
        copy.start()
        spreads.append((k, copy))
    forwards = []
    here = out_ref.at[mine, c]
    forwards.append(remote(here, here, fw_s.at[3], fw_r.at[3], sibling))
    forwards[0].start()
    for k, copy in reversed(spreads):
        copy.wait_recv()
        ox, oy = chips[k]
        block = out_ref.at[ox * 2 + oy, c]
        forwards.append(remote(block, block, fw_s.at[k], fw_r.at[k], sibling))
        forwards[-1].start()
    for _, copy in spreads:
        copy.wait_send()
    for copy in forwards:
        copy.wait()


def plane_total(part, collective_id):
    rows, cols = part.shape
    block = (rows // 8, cols)
    vmem = pl.BlockSpec(memory_space=pltpu.VMEM)
    dma = pltpu.SemaphoreType.DMA
    out = pl.pallas_call(
        total_kernel,
        in_specs=[vmem],
        out_specs=vmem,
        out_shape=jax.ShapeDtypeStruct((4, 2) + block, BF16),
        scratch_shapes=[
            pltpu.VMEM((4,) + block, BF16),
            pltpu.VMEM((4,) + block, BF16),
            pltpu.VMEM((3,) + block, BF16),
            pltpu.VMEM((3,) + block, BF16),
            dma(()),
            dma(()),
            dma((3,)),
            dma((3,)),
            dma((3,)),
            dma((3,)),
            dma((4,)),
            dma((4,)),
        ],
        cost_estimate=busy(20),
        compiler_params=pltpu.CompilerParams(
            collective_id=collective_id, has_side_effects=True, vmem_limit_bytes=40 << 20
        ),
    )(part.reshape((4, 2) + block))
    return out.reshape(rows, cols)


def add_rows(dst, srcs, rows):
    count = dst.shape[0] // rows

    def body(i, carry):
        at = pl.ds(pl.multiple_of(i * rows, rows), rows)
        total = srcs[0][at].astype(F32)
        for src in srcs[1:]:
            total = total + src[at].astype(F32)
        dst[at] = total.astype(dst.dtype)
        return carry

    lax.fori_loop(0, count, body, 0)


def finish_kernel(
    z_size,
    back_ref,
    small_ref,
    gate_ref,
    conv_ref,
    tokens_ref,
    cot_ref,
    gain_ref,
    tgrad_ref,
    in_ref,
    small_out,
    gain_out,
    own_back,
    sib_back,
    ring_stage,
    ring_got,
    own_small,
    own_gate,
    own_conv,
    up_small,
    up_gate,
    up_conv,
    down_small,
    down_gate,
    down_conv,
    up_stage_small,
    up_stage_gate,
    up_stage_conv,
    down_stage_small,
    down_stage_gate,
    down_stage_conv,
    fin_gate,
    fin_conv,
    both_gate,
    both_conv,
    gain_parts,
    gain_got,
    gain_half,
    gain_pair,
    local_sem,
    back_sem,
    sib_send,
    sib_recv,
    ring_send,
    ring_recv,
    up_send,
    up_recv,
    down_send,
    down_recv,
    swap_send,
    swap_recv,
    x_send,
    x_recv,
    gain_send,
    gain_recv,
):
    me = place()
    x, y, z, c = me["x"], me["y"], me["z"], me["c"]
    shares = z_size * 4
    share = z * 4 + y * 2 + c
    corner = y * 2 + c
    sibling = {"c": 1 - c}
    over_x = {"x": 1 - x}
    greet(plane_others(me) + z_only(me, shares))

    at = ring_at(x, y)
    step = 1 + 2 * c
    sib_step = 3 - 2 * c
    nx, ny = ring_chip((at + step) % RING)
    following = {"x": nx, "y": ny}

    def chip_index(p):
        cx, cy = ring_chip(p % RING)
        return cx * 2 + cy

    owns = (own_small, own_gate, own_conv)
    locals_ = [
        pltpu.make_async_copy(src, dst, local_sem.at[i])
        for i, (src, dst) in enumerate(zip((small_ref, gate_ref, conv_ref), owns))
    ]
    for copy in locals_:
        copy.start()
    backs = []
    sibs = []
    for k in range(RING):
        backs.append(
            pltpu.make_async_copy(
                back_ref.at[chip_index(at + step * (RING - 1 - k)), c], own_back.at[k], back_sem.at[k]
            )
        )
        sibs.append(
            remote(
                back_ref.at[chip_index(at + sib_step * (RING - 1 - k)), 1 - c],
                sib_back.at[k],
                sib_send.at[k],
                sib_recv.at[k],
                sibling,
            )
        )
    for k in range(RING):
        backs[k].start()
        sibs[k].start()

    ups = (up_small, up_gate, up_conv)
    downs = (down_small, down_gate, down_conv)
    up_stages = (up_stage_small, up_stage_gate, up_stage_conv)
    down_stages = (down_stage_small, down_stage_gate, down_stage_conv)
    blocks = (16, 64, 64)

    def up_copy(k, h):
        return remote(
            up_stages[h].at[k], ups[h].at[k], up_send.at[k, h], up_recv.at[k, h], {"z": z + 1}
        )

    def down_copy(k, h):
        return remote(
            down_stages[h].at[k], downs[h].at[k], down_send.at[k, h], down_recv.at[k, h], {"z": z - 1}
        )

    def line(tau, h):
        k = tau - z
        high = z_size - 1 - k

        @pl.when((k >= 0) & (z < high) & (z > 0))
        def _():
            up_copy(k, h).wait_recv()
            add_rows(up_stages[h].at[k], [owns[h].at[high], ups[h].at[k]], blocks[h])
            up_copy(k, h).start()

        @pl.when((k >= 0) & (z < high) & (z == 0))
        def _():
            add_rows(up_stages[h].at[k], [owns[h].at[high]], blocks[h])
            up_copy(k, h).start()

        m = tau - (z_size - 1 - z)

        @pl.when((m >= 0) & (z > m) & (z < z_size - 1))
        def _():
            down_copy(m, h).wait_recv()
            add_rows(down_stages[h].at[m], [owns[h].at[m], downs[h].at[m]], blocks[h])
            down_copy(m, h).start()

        @pl.when((m >= 0) & (z > m) & (z == z_size - 1))
        def _():
            add_rows(down_stages[h].at[m], [owns[h].at[m]], blocks[h])
            down_copy(m, h).start()

    def settle(h, dst):
        low = z
        high = z_size - 1 - z

        @pl.when(z == 0)
        def _():
            down_copy(low, h).wait_recv()
            add_rows(dst, [owns[h].at[z], downs[h].at[low]], blocks[h])

        @pl.when(z == z_size - 1)
        def _():
            up_copy(high, h).wait_recv()
            add_rows(dst, [owns[h].at[z], ups[h].at[high]], blocks[h])

        @pl.when((z > 0) & (z < z_size - 1))
        def _():
            down_copy(low, h).wait_recv()
            up_copy(high, h).wait_recv()
            add_rows(dst, [owns[h].at[z], downs[h].at[low], ups[h].at[high]], blocks[h])

    def ring(k):
        return remote(ring_stage.at[k], ring_got.at[k], ring_send.at[k], ring_recv.at[k], following)

    def ring_step(k):
        backs[k].wait()
        sibs[k].wait_recv()
        srcs = [own_back.at[k], sib_back.at[k]]
        if k:
            ring(k - 1).wait_recv()
            srcs.append(ring_got.at[k - 1])
        add_rows(ring_stage.at[k], srcs, 16)
        ring(k).start()

    def ring_end():
        last = RING - 1
        backs[last].wait()
        sibs[last].wait_recv()
        ring(last - 1).wait_recv()
        rows = 16
        width = tokens_ref.shape[1]

        def body(i, total):
            r = pl.ds(pl.multiple_of(i * rows, rows), rows)
            back = (
                own_back[last, r].astype(F32)
                + sib_back[last, r].astype(F32)
                + ring_got[last - 1, r].astype(F32)
            )
            values = tokens_ref[r].astype(F32)
            rstd = lax.rsqrt(jnp.mean(values * values, axis=-1, keepdims=True) + epsilon)
            scaled = back * gain_ref[...]
            inner = jnp.mean(scaled * values, axis=-1, keepdims=True)
            grad = cot_ref[r].astype(F32) + rstd * scaled - values * (rstd * rstd * rstd * inner)
            tgrad_ref[r] = grad.astype(BF16)
            terms = back * values * rstd
            return total + terms[:8] + terms[8:]

        total = lax.fori_loop(
            0, tokens_ref.shape[0] // rows, body, jnp.zeros((8, width), F32)
        )
        total = jnp.broadcast_to(jnp.sum(total, axis=0, keepdims=True), (8, width))
        piece = gain_parts.shape[2]
        for f in range(shares):
            gain_parts[f] = total[:, f * piece : (f + 1) * piece]
        gain_got[share] = gain_parts[share]

    gains = []
    for k in range(1, shares):
        f = (share + k) % shares
        gains.append(
            remote(
                gain_parts.at[f], gain_got.at[share], gain_send.at[k - 1], gain_recv.at[k - 1], share_at(f)
            )
        )

    for copy in locals_:
        copy.wait()
    hops = z_size - 1
    ring_step(0)
    for h in range(3):
        line(0, h)
    ring_step(1)
    ring_step(2)
    for h in range(3):
        line(1, h)
    ring_end()
    for copy in gains:
        copy.start()
    for tau in range(2, hops):
        for h in range(3):
            line(tau, h)

    settle(0, small_out.at[x])
    small_x = remote(small_out.at[x], small_out.at[x], x_send.at[0], x_recv.at[0], over_x)
    small_x.start()
    fins = (None, fin_gate, fin_conv)
    boths = (None, both_gate, both_conv)
    rows_in = in_ref.shape[0]
    swaps = {}
    for h in (1, 2):
        settle(h, fins[h])
        swaps[h] = []
        for k in range(1, 4):
            to = (corner + k) % 4
            copy = remote(
                fins[h].at[pl.ds(pl.multiple_of(to * rows_in, rows_in), rows_in)],
                boths[h].at[x, corner],
                swap_send.at[h - 1, k - 1],
                swap_recv.at[h - 1, k - 1],
                {"y": to // 2, "c": to % 2},
            )
            copy.start()
            swaps[h].append(copy)
        boths[h][x, corner] = fins[h][pl.ds(pl.multiple_of(corner * rows_in, rows_in), rows_in)]
        if h == 1:
            for copy in gains:
                copy.wait()
            gain_half[...] = jnp.sum(gain_got[...], axis=0)
            gain_x = remote(gain_half, gain_pair, x_send.at[3], x_recv.at[3], over_x)
            gain_x.start()
            for copy in swaps[1]:
                copy.wait()
            gate_x = remote(both_gate.at[x], both_gate.at[x], x_send.at[1], x_recv.at[1], over_x)
            gate_x.start()
    for copy in swaps[2]:
        copy.wait()
    conv_x = remote(both_conv.at[x], both_conv.at[x], x_send.at[2], x_recv.at[2], over_x)
    conv_x.start()

    half = small_ref.shape[1]
    branch = 8 * half * z_size

    def lay(h):
        first = branch if h == 1 else 0
        for zz in range(z_size):
            for j in range(4):
                for xx in range(2):
                    col = first + (zz * 4 + j) * 2 * half + xx * half
                    in_ref[:, col : col + half] = boths[h][xx, j, :, zz * half : (zz + 1) * half].astype(F32)

    gate_x.wait()
    lay(1)
    gain_x.wait()
    gain_out[...] = gain_half[...] + gain_pair[...]
    small_x.wait()
    conv_x.wait()
    lay(2)

    for k in range(hops):
        high = z_size - 1 - k
        for h in range(3):

            @pl.when(z < high)
            def _():
                up_copy(k, h).wait_send()

            @pl.when(z > k)
            def _():
                down_copy(k, h).wait_send()

    for k in range(RING - 1):
        ring(k).wait_send()
    for copy in sibs:
        copy.wait_send()


def last_sums(z_size, back, small, gate, conv, tokens, cot, gain, in_width):
    length, width = tokens.shape
    shares = z_size * 4
    hops = z_size - 1
    rows_in = gate.shape[1] // 4
    any_space = pl.BlockSpec(memory_space=pl.ANY)
    vmem = pl.BlockSpec(memory_space=pltpu.VMEM)
    dma = pltpu.SemaphoreType.DMA
    block = (length, width)
    slabs = [small.shape[1:], gate.shape[1:], conv.shape[1:]]
    bufs = lambda n: [pltpu.VMEM((n,) + s, BF16) for s in slabs]
    both = pltpu.VMEM((2, 4, rows_in, gate.shape[2]), BF16)
    piece = (8, width // shares)
    return pl.pallas_call(
        functools.partial(finish_kernel, z_size),
        in_specs=[any_space] * 4 + [vmem] * 3,
        out_specs=[vmem] * 4,
        out_shape=[
            jax.ShapeDtypeStruct(tokens.shape, BF16),
            jax.ShapeDtypeStruct((rows_in, in_width), F32),
            jax.ShapeDtypeStruct((2,) + slabs[0], BF16),
            jax.ShapeDtypeStruct(piece, F32),
        ],
        scratch_shapes=[
            pltpu.VMEM((RING,) + block, BF16),
            pltpu.VMEM((RING,) + block, BF16),
            pltpu.VMEM((RING - 1,) + block, BF16),
            pltpu.VMEM((RING - 1,) + block, BF16),
        ]
        + bufs(z_size)
        + bufs(hops)
        + bufs(hops)
        + bufs(hops)
        + bufs(hops)
        + [
            pltpu.VMEM(slabs[1], BF16),
            pltpu.VMEM(slabs[2], BF16),
            both,
            both,
            pltpu.VMEM((shares,) + piece, F32),
            pltpu.VMEM((shares,) + piece, F32),
            pltpu.VMEM(piece, F32),
            pltpu.VMEM(piece, F32),
            dma((3,)),
            dma((RING,)),
            dma((RING,)),
            dma((RING,)),
            dma((RING - 1,)),
            dma((RING - 1,)),
            dma((hops, 3)),
            dma((hops, 3)),
            dma((hops, 3)),
            dma((hops, 3)),
            dma((2, 3)),
            dma((2, 3)),
            dma((4,)),
            dma((4,)),
            dma((shares - 1,)),
            dma((shares - 1,)),
        ],
        cost_estimate=busy(100),
        compiler_params=pltpu.CompilerParams(
            collective_id=3, has_side_effects=True, vmem_limit_bytes=60 << 20
        ),
    )(back, small, gate, conv, tokens, cot, gain)


def silu_and_slope(v):
    s = jax.nn.sigmoid(v)
    return v * s, s * (1.0 + v * (1.0 - s))


def shift_down(v, j):
    return jnp.pad(v, ((j, 0),) + ((0, 0),) * (v.ndim - 1))[: v.shape[0]]


def shift_up(v, j):
    return jnp.pad(v, ((0, j),) + ((0, 0),) * (v.ndim - 1))[j:]


def shards(
    tokens,
    doc_ids,
    norm_gain,
    in_weight,
    conv_taps,
    conv_offset,
    select_weight,
    step_weight,
    step_bias,
    decay_log,
    skip_gain,
    out_weight,
    cotangent,
):
    z_size = lax.axis_size("z")
    rh_size = lax.axis_size("rh")
    seqs = 8
    length = doc_ids.shape[1]
    width = tokens.shape[1]
    in_rows = in_weight.shape[0]
    rows = out_weight.shape[0]
    half = rows // 2
    chans = half * z_size
    taps = conv_taps.shape[1]
    rank = step_weight.shape[1]
    states = decay_log.shape[1]
    x_at = lax.axis_index("x")

    def own_half(w):
        return lax.dynamic_slice_in_dim(w, x_at * half, half, 0)

    cuts = [taps, 1, 1, 1, states, rank + 2 * states, rank]
    ends = [sum(cuts[: i + 1]) for i in range(len(cuts))]
    room = -ends[-1] % 128

    def parts(v):
        return [v[:, e - n : e] for e, n in zip(ends, cuts)]

    spare = -(rank + 2 * states) % 128
    wide = rank + 2 * states + spare
    vectors = jnp.concatenate(
        [
            own_half(conv_taps),
            own_half(conv_offset)[:, None],
            own_half(step_bias)[:, None],
            own_half(skip_gain)[:, None],
            own_half(decay_log),
        ],
        axis=1,
    ).T
    vectors = jnp.pad(vectors, ((0, -vectors.shape[0] % 32), (0, 0)))
    mats = jnp.concatenate(
        [jnp.pad(own_half(select_weight), ((0, 0), (0, spare))), own_half(step_weight)], axis=1
    )
    picked = lax.dynamic_index_in_dim(
        in_weight.reshape(in_rows, 2, z_size, 4, 2, half), x_at, 4, keepdims=False
    )
    packed = picked.transpose(1, 3, 0, 2, 4).reshape(2, 4, in_rows, chans)
    gain_tile = jnp.broadcast_to(norm_gain.astype(F32)[None, :], (8, norm_gain.shape[0]))
    ids_tile = jnp.broadcast_to(doc_ids, (8, length))
    (
        all_normed,
        all_cot,
        w_conv,
        w_gate,
        w_out,
        w_mats,
        keep,
        conv_in,
        x,
        dt,
        pre,
        vectors,
        gains,
        selection,
    ) = front(
        z_size,
        taps,
        rank,
        tokens,
        gain_tile,
        ids_tile,
        vectors,
        cotangent,
        packed[0],
        packed[1],
        own_half(out_weight),
        mats,
    )
    all_normed = all_normed.reshape(-1, width)
    all_cot = all_cot.reshape(-1, width)
    w_select = w_mats[:, : rank + 2 * states]
    w_step = w_mats[:, wide:]
    tap = [vectors[taps - 1 - j] for j in range(taps)]
    skip = vectors[taps + 2]
    rates = -jnp.exp(vectors[taps + 3 : taps + 3 + states])
    gain = gains[:, 0, :].reshape(1, width)
    residual = tokens.astype(F32)

    def time_major(v):
        return v.reshape(seqs, length, -1).swapaxes(0, 1)

    def seq_major(v):
        return v.reshape(length, seqs, -1).swapaxes(0, 1).reshape(seqs * length, -1)

    gate_in = time_major(dot_nn(all_normed, w_gate))
    keep1 = keep[:, :, :1]
    same = [None, keep1]
    for j in range(2, taps):
        same.append(same[-1] * shift_down(keep1, j - 1))
    conv_out = vectors[taps] + conv_in * tap[0]
    for j in range(1, taps):
        conv_out = conv_out + shift_down(conv_in, j) * same[j] * tap[j]
    conv_slope = silu_and_slope(conv_out)[1]
    selected = x.astype(BF16)
    flat = lambda v: v.reshape(length * seqs, -1)
    selection = selection.reshape(length * seqs, wide)
    rank_in = selection[:, :rank]
    bc = selection[:, rank : rank + 2 * states].astype(F32).reshape(length, seqs, 2 * states)
    dtm = dt + (1.0 - keep1) * BIG
    rate2 = jnp.broadcast_to((rates * LOG2E)[:, None, :], (states, seqs, chans))
    y, hist, last = scan_forward(dt, dtm, x, bc, rate2)
    scanned = y + skip * x
    gate, gate_slope = silu_and_slope(gate_in)
    gated = seq_major((scanned * gate).astype(BF16))
    out_part = dot_nn(gated, w_out).astype(BF16)

    def shifted(v, j):
        return shift_down(v, j) * same[j] if j else v

    grad_out = dot_tn(gated, all_cot).astype(BF16)
    back_gated = time_major(dot_nt(all_cot, w_out).astype(BF16)).astype(F32)
    back_scan = back_gated * gate
    back_gate_in = back_gated * scanned * gate_slope
    back_scan, out_part, grad_out = lax.optimization_barrier((back_scan, out_part, grad_out))
    layer_sum = lax.psum_scatter(out_part, PLANE, scatter_dimension=0, tiled=True)
    layer_out = (residual + layer_sum.astype(F32)).astype(BF16)
    s1, s2, back_bc, da = scan_backward(dt, dtm, x, back_scan, bc, rate2, hist, last)
    s1, grad_out = lax.optimization_barrier((s1, grad_out))
    own_out = lax.psum_scatter(grad_out, "z", scatter_dimension=0, tiled=True)
    back_steps = s1 * (1.0 / LOG2E) + x * s2
    back_x = dt * s2 + skip * back_scan
    grad_decay = da.sum(1).T * rates.T
    grad_skip = (back_scan * x).sum((0, 1))
    back_pre = back_steps * jax.nn.sigmoid(pre)
    grad_bias = back_pre.sum((0, 1))
    back_pre = flat(back_pre.astype(BF16))
    grad_step = dot_tn(back_pre, rank_in)
    back_rank = dot_nn(back_pre, w_step)
    back_selection = plane_total(
        jnp.concatenate([back_rank, back_bc[:, : wide - rank]], axis=1), 2
    )[:, : rank + 2 * states]
    grad_select = dot_tn(flat(selected), back_selection)
    back_selected = dot_nt(back_selection, w_select).reshape(length, seqs, chans) + back_x
    back_conv = back_selected * conv_slope
    grad_offset = back_conv.sum((0, 1))
    grad_taps = jnp.stack(
        [
            (back_conv * shifted(conv_in, j)).sum((0, 1))
            for j in reversed(range(taps))
        ],
        axis=1,
    )
    back_conv_in = back_conv * tap[0]
    for j in range(1, taps):
        back_conv_in = back_conv_in + shift_up(back_conv * same[j], j) * tap[j]
    back_conv_in = seq_major(back_conv_in.astype(BF16))
    back_gate_in = seq_major(back_gate_in.astype(BF16))
    back_part = (dot_nt(back_conv_in, w_conv) + dot_nt(back_gate_in, w_gate)).astype(BF16)
    grad_conv = dot_tn(all_normed, back_conv_in).astype(BF16)
    grad_gate = dot_tn(all_normed, back_gate_in).astype(BF16)
    small_grad = jnp.concatenate(
        [
            grad_taps,
            grad_offset[:, None],
            grad_bias[:, None],
            grad_skip[:, None],
            grad_decay,
            grad_select,
            grad_step,
            jnp.zeros((chans, room), F32),
        ],
        axis=1,
    ).astype(BF16)
    tokens_grad, g_in, small_own, g_gain = last_sums(
        z_size,
        back_part.reshape(4, 2, length, width),
        small_grad.reshape(z_size, half, -1),
        grad_gate.reshape(z_size, -1, chans),
        grad_conv.reshape(z_size, -1, chans),
        tokens,
        cotangent,
        gain,
        in_weight.shape[1],
    )
    g_gain = g_gain[0]
    if rh_size > 1:
        small_own, g_in, own_out, g_gain = lax.psum(
            (small_own.astype(F32), g_in, own_out, g_gain), "rh"
        )
    g_out = lax.all_gather(own_out, "x", axis=0, tiled=True).astype(F32)
    g_taps, g_offset, g_bias, g_skip, g_decay, g_select, g_step = [
        v.astype(F32) for v in parts(small_own.reshape(rows, -1))
    ]
    return (
        layer_out,
        tokens_grad,
        g_gain,
        g_in,
        g_taps,
        g_offset[:, 0],
        g_select,
        g_step,
        g_bias[:, 0],
        g_decay,
        g_skip[:, 0],
        g_out,
    )


def solution(mesh):
    replicas = mesh.shape["replica"]
    shares = mesh.shape["fsdp"]
    grid = Mesh(
        mesh.devices.reshape(replicas // 2, 2, shares // 4, 2, 2), ("rh", "x", "z", "y", "c")
    )
    tok = ("rh", "x", "z", "y", "c")
    own = ("z", "y", "c")
    return jax.shard_map(
        shards,
        mesh=grid,
        in_specs=(
            P(tok, None),
            P(tok, None),
            P(own),
            P(own, None),
            P(own, None),
            P(own),
            P(own, None),
            P(own, None),
            P(own),
            P(own, None),
            P(own),
            P(own, None),
            P(tok, None),
        ),
        out_specs=(
            P(tok, None),
            P(tok, None),
            P(own),
            P(own, None),
            P(own, None),
            P(own),
            P(own, None),
            P(own, None),
            P(own),
            P(own, None),
            P(own),
            P(own, None),
        ),
        check_vma=False,
    )
```

```python
import functools

import jax
import jax.numpy as jnp
from jax import lax
from jax.experimental import pallas as pl
from jax.experimental.pallas import tpu as pltpu
from jax.sharding import Mesh
from jax.sharding import PartitionSpec as P

F32 = jnp.float32
BF16 = jnp.bfloat16
epsilon = 1e-05
PLANE = ("x", "y", "c")
BIG = 1e30
STEPS = 32
INNER = 4
LOG2E = 1.4426950408889634


def dot(a, b, dims):
    return lax.dot_general(a, b, (dims, ((), ())), preferred_element_type=F32)


def dot_nn(a, b):
    return dot(a, b, ((1,), (0,)))


def dot_tn(a, b):
    return dot(a, b, ((0,), (0,)))


def dot_nt(a, b):
    return dot(a, b, ((1,), (1,)))


def busy(micros):
    return pl.CostEstimate(flops=micros * 10**9, bytes_accessed=micros * 10**6, transcendentals=0)


MESH = pl.DeviceIdType.MESH
RING = 4


def place():
    return {a: lax.axis_index(a) for a in ("x", "z", "y", "c")}


def ring_chip(p):
    y = p // 2
    return (p + y) % 2, y


def ring_at(x, y):
    return 2 * y + (x + y) % 2


def share_at(f):
    return {"z": f // 4, "y": f // 2 % 2, "c": f % 2}


def remote(src, dst, send, recv, device):
    return pltpu.make_async_remote_copy(
        src_ref=src, dst_ref=dst, send_sem=send, recv_sem=recv, device_id=device, device_id_type=MESH
    )


def greet(devices):
    barrier = pltpu.get_barrier_semaphore()
    for device in devices:
        pl.semaphore_signal(barrier, inc=1, device_id=device, device_id_type=MESH)
    pl.semaphore_wait(barrier, len(devices))


def plane_others(me):
    out = []
    for dx in range(2):
        for dy in range(2):
            for dc in range(2):
                if dx + dy + dc:
                    out.append(
                        {"x": (me["x"] + dx) % 2, "y": (me["y"] + dy) % 2, "c": (me["c"] + dc) % 2}
                    )
    return out


def share_others(me, shares):
    f = me["z"] * 4 + me["y"] * 2 + me["c"]
    return [share_at((f + k) % shares) for k in range(1, shares)]


def z_only(me, shares):
    f = me["c"] + 2 * me["y"]
    out = []
    for dz in range(1, shares // 4):
        for k in range(4):
            out.append(
                {
                    "z": (me["z"] + dz) % (shares // 4),
                    "y": (f + k) % 4 // 2,
                    "c": (f + k) % 2,
                }
            )
    return out


def z_line(z, z_size, pieces, sems):
    up_s, up_r, down_s, down_r = sems

    def up(k):
        return [
            remote(p(z - k), p(z - k), up_s.at[k, j], up_r.at[k, j], {"z": z + 1})
            for j, p in enumerate(pieces)
        ]

    def down(k):
        return [
            remote(p(z + k), p(z + k), down_s.at[k, j], down_r.at[k, j], {"z": z - 1})
            for j, p in enumerate(pieces)
        ]

    def start(k):
        @pl.when((z < z_size - 1) & (z >= k))
        def _():
            for copy in up(k):
                copy.start()

        @pl.when((z > 0) & (z + k < z_size))
        def _():
            for copy in down(k):
                copy.start()

    def arrive(k):
        @pl.when(z > k)
        def _():
            for copy in up(k):
                copy.wait_recv()

        @pl.when(z + k < z_size - 1)
        def _():
            for copy in down(k):
                copy.wait_recv()

    def sent(k):
        @pl.when((z < z_size - 1) & (z >= k))
        def _():
            for copy in up(k):
                copy.wait_send()

        @pl.when((z > 0) & (z + k < z_size))
        def _():
            for copy in down(k):
                copy.wait_send()

    return start, arrive, sent


class Ring:
    def __init__(self, me, blocks, own, ring_send, ring_recv, sib_send, sib_recv):
        self.me, self.blocks, self.own = me, blocks, own
        self.sems = ring_send, ring_recv, sib_send, sib_recv
        self.at = ring_at(me["x"], me["y"])
        self.step = 1 + 2 * me["c"]
        nx, ny = ring_chip((self.at + self.step) % RING)
        self.following = {"x": nx, "y": ny}
        self.sibling = {"c": 1 - me["c"]}
        self.half = blocks.shape[1] // 2

    def slot(self, k):
        ox, oy = ring_chip((self.at + (RING - self.step) * k) % RING)
        return ox * 4 + oy * 2 + self.me["c"]

    def hop(self, k):
        out = []
        for p in range(2):
            rows = pl.ds(p * self.half, self.half)
            dst = self.blocks.at[self.slot(k), rows]
            src = self.own.at[rows] if k == 0 and self.own is not None else dst
            out.append(remote(src, dst, self.sems[0].at[k, p], self.sems[1].at[k, p], self.following))
        return out

    def cross(self, k):
        dst = self.blocks.at[self.slot(k)]
        src = self.own if k == 0 and self.own is not None else dst
        return remote(src, dst, self.sems[2].at[k], self.sems[3].at[k], self.sibling)

    def start(self, k):
        if k < RING - 1:
            for copy in self.hop(k):
                copy.start()
        self.cross(k).start()

    def arrive(self, k):
        for copy in self.hop(k):
            copy.wait_recv()

    def sent(self, k):
        if k < RING - 1:
            for copy in self.hop(k):
                copy.wait_send()
        self.cross(k).wait()


def softplus(v):
    e = jnp.exp(-jnp.abs(v))
    small = e * (1.0 - e * (0.5 - e * (1.0 / 3.0)))
    return jnp.maximum(v, 0.0) + jnp.where(e < 1e-3, small, jnp.log(1.0 + e))


def front_kernel(
    z_size,
    taps,
    rank,
    tokens_ref,
    gain_ref,
    ids_ref,
    rows_ref,
    cot_ref,
    conv_ref,
    gate_ref,
    out_ref,
    mats_ref,
    normed_hbm,
    cot_all,
    conv_hbm,
    gate_all,
    out_all,
    mats_hbm,
    keep_hbm,
    cin_hbm,
    x_hbm,
    dt_hbm,
    pre_hbm,
    picked_hbm,
    params,
    gain_all,
    selection,
    normed_all,
    conv_w,
    mats,
    rows_all,
    gain_got,
    ids_all,
    proj,
    cin,
    xs,
    picked,
    part,
    dts,
    pres,
    keep,
    first,
    from_sib,
    stage,
    got,
    local_sem,
    gain_send,
    gain_recv,
    ids_send,
    ids_recv,
    conv_send,
    conv_recv,
    gate_send,
    gate_recv,
    ring_send,
    ring_recv,
    sib_send,
    sib_recv,
    cot_ring_send,
    cot_ring_recv,
    cot_sib_send,
    cot_sib_recv,
    a_us,
    a_ur,
    a_ds,
    a_dr,
    b_us,
    b_ur,
    b_ds,
    b_dr,
    sw_s,
    sw_r,
    rs_s,
    rs_r,
    ag_s,
    ag_r,
    fw_s,
    fw_r,
):
    me = place()
    x, y, z, c = me["x"], me["y"], me["z"], me["c"]
    shares = z_size * 4
    share = z * 4 + y * 2 + c
    corner = y * 2 + c
    seq = x * 4 + y * 2 + c
    sibling = {"c": 1 - c}
    length, width = tokens_ref.shape
    chans = conv_ref.shape[2]
    rows_in = conv_ref.shape[1]
    half = mats_ref.shape[0]
    hops = z_size - 1
    greet(plane_others(me) + z_only(me, shares))

    def rows_at(ref, index, count):
        return ref.at[pl.ds(pl.multiple_of(index * count, count), count)]

    def corner_sends(src, dst, send, recv):
        out = []
        for k in range(1, 4):
            to = (corner + k) % 4
            out.append(
                remote(
                    src.at[to],
                    rows_at(dst, share, rows_in),
                    send.at[k - 1],
                    recv.at[k - 1],
                    {"y": to // 2, "c": to % 2},
                )
            )
        return out

    swaps = corner_sends(conv_ref, conv_w, conv_send, conv_recv)
    gates = corner_sends(gate_ref, gate_all, gate_send, gate_recv)
    for copy in swaps:
        copy.start()
    gains = [
        remote(gain_ref, gain_got.at[share], gain_send.at[k], gain_recv.at[k], device)
        for k, device in enumerate(share_others(me, shares))
    ]
    for copy in gains:
        copy.start()
    locals_ = [
        pltpu.make_async_copy(conv_ref.at[corner], rows_at(conv_w, share, rows_in), local_sem.at[0]),
        pltpu.make_async_copy(mats_ref, rows_at(mats, z, half), local_sem.at[1]),
        pltpu.make_async_copy(gate_ref.at[corner], rows_at(gate_all, share, rows_in), local_sem.at[2]),
        pltpu.make_async_copy(out_ref, rows_at(out_all, z, half), local_sem.at[3]),
        pltpu.make_async_copy(cot_ref, cot_all.at[seq], local_sem.at[4]),
    ]
    for copy in locals_:
        copy.start()
    ids_copies = [
        remote(ids_ref, ids_all.at[seq], ids_send.at[k], ids_recv.at[k], device)
        for k, device in enumerate(plane_others(me))
    ]
    for copy in ids_copies:
        copy.start()
    ids_all[seq] = ids_ref[...]
    gain_got[share] = gain_ref[...]
    rows_all[z] = rows_ref[...]

    values = tokens_ref[...].astype(F32)
    rstd = lax.rsqrt(jnp.mean(values * values, axis=-1, keepdims=True) + epsilon)
    for copy in gains:
        copy.wait()
    piece = gain_ref.shape[1]
    for f in range(shares):
        cols = pl.ds(f * piece, piece)
        normed = tokens_ref[:, cols].astype(F32) * rstd * gain_got[f, 0:1, :]
        normed_all[seq, :, cols] = normed.astype(BF16)
    gain_all[...] = gain_got[...]

    ring = Ring(me, normed_all, None, ring_send, ring_recv, sib_send, sib_recv)
    cot_ring = Ring(me, cot_all, cot_ref, cot_ring_send, cot_ring_recv, cot_sib_send, cot_sib_recv)
    ring.start(0)
    for copy in swaps:
        copy.wait()
    for copy in locals_:
        copy.wait()
    a_start, a_arrive, a_sent = z_line(
        z,
        z_size,
        [
            lambda k: rows_at(conv_w, k, 4 * rows_in),
            lambda k: rows_at(mats, k, half),
            lambda k: rows_all.at[k],
        ],
        (a_us, a_ur, a_ds, a_dr),
    )
    b_start, b_arrive, b_sent = z_line(
        z,
        z_size,
        [lambda k: rows_at(gate_all, k, 4 * rows_in), lambda k: rows_at(out_all, k, half)],
        (b_us, b_ur, b_ds, b_dr),
    )
    a_start(0)
    for copy in gates:
        copy.start()

    for copy in ids_copies:
        copy.wait()
    ids = jnp.concatenate([ids_all[s, 0:1, :] for s in range(8)], axis=0).astype(F32)
    before = pltpu.roll(ids, 1, 1)
    lane = lax.broadcasted_iota(jnp.int32, ids.shape, 1)
    same = jnp.where((ids == before) & (lane > 0), 1.0, 0.0)
    for t in range(length):
        keep[t] = jnp.broadcast_to(same[:, t : t + 1], (8, 128))
    keep_copy = pltpu.make_async_copy(keep, keep_hbm, local_sem.at[5])
    keep_copy.start()

    for k in range(max(hops, RING - 1)):
        if k < hops:
            a_arrive(k)
            if k + 1 < hops:
                a_start(k + 1)
        if k < RING - 1:
            ring.arrive(k)
            ring.start(k + 1)
        if k == RING - 2:
            cot_ring.start(0)
    for copy in gates:
        copy.wait()
    b_start(0)
    for k in range(RING):
        ring.sent(k)
    outs = [
        pltpu.make_async_copy(normed_all, normed_hbm, local_sem.at[6]),
        pltpu.make_async_copy(conv_w, conv_hbm, local_sem.at[7]),
        pltpu.make_async_copy(mats, mats_hbm, local_sem.at[8]),
    ]
    for copy in outs:
        copy.start()
    for zz in range(z_size):
        params[:, zz * half : (zz + 1) * half] = rows_all[zz].astype(F32)

    def project(s, carry):
        proj[s] = dot_nn(normed_all[s], conv_w[...])
        return carry

    lax.fori_loop(0, 8, project, 0)

    cin[0:3] = jnp.zeros((3, 8, chans), F32)
    block = 32
    fine = 4

    def turn(i, carry):
        t0 = pl.multiple_of(i * block, block)
        cin[pl.ds(3 + t0, block)] = jnp.swapaxes(proj[:, pl.ds(t0, block), :], 0, 1)
        return carry

    lax.fori_loop(0, length // block, turn, 0)

    def convolve(i, carry):
        t0 = i * fine
        for g in range(chans // 128):
            lanes = pl.ds(g * 128, 128)
            tap = [jnp.broadcast_to(params[taps - 1 - j : taps - j, lanes], (8, 128)) for j in range(taps)]
            offset = jnp.broadcast_to(params[taps : taps + 1, lanes], (8, 128))
            chosen = []
            for j in range(fine):
                t = t0 + j
                total = tap[3] * cin[t, :, lanes] * keep[jnp.maximum(t - 2, 0)]
                total = (total + tap[2] * cin[t + 1, :, lanes]) * keep[jnp.maximum(t - 1, 0)]
                total = (total + tap[1] * cin[t + 2, :, lanes]) * keep[t]
                v = total + tap[0] * cin[t + 3, :, lanes] + offset
                chosen.append((v / (1.0 + jnp.exp(-v))).astype(BF16))
                xs[t, :, lanes] = chosen[-1].astype(F32)
            rows = pl.ds(pl.multiple_of(t0 * 8, fine * 8), fine * 8)
            picked[rows, lanes] = jnp.concatenate(chosen, axis=0)
        return carry

    lax.fori_loop(0, length // fine, convolve, 0)
    outs += [
        pltpu.make_async_copy(cin.at[pl.ds(3, length)], cin_hbm, local_sem.at[9]),
        pltpu.make_async_copy(xs, x_hbm, local_sem.at[10]),
        pltpu.make_async_copy(picked, picked_hbm, local_sem.at[13]),
    ]
    for copy in outs[3:]:
        copy.start()

    wide = part.shape[3]

    def select(b, carry):
        rows = pl.ds(pl.multiple_of(b * length, length), length)
        part[b // 2, b % 2] = dot_nn(picked[rows, :], mats[:, :wide])
        return carry

    lax.fori_loop(0, 8, select, 0)
    first[...] = part[:, 1 - c].astype(BF16)
    swap = remote(first, from_sib, sw_s.at[0], sw_r.at[0], sibling)
    swap.start()
    swap.wait()
    mine = x * 2 + y
    chips = [((x + d // 2) % 2, (y + d % 2) % 2) for d in (1, 2, 3)]
    sends = []
    for k in (2, 1, 0):
        ox, oy = chips[k]
        j = ox * 2 + oy
        stage[k] = (part[j, c] + from_sib[j].astype(F32)).astype(BF16)
        copy = remote(stage.at[k], got.at[k], rs_s.at[k], rs_r.at[k], {"x": ox, "y": oy})
        copy.start()
        sends.append(copy)
    total = part[mine, c] + from_sib[mine].astype(F32)
    for copy in sends:
        copy.wait()
    for k in range(3):
        total = total + got[k].astype(F32)
    selection[mine, c] = total.astype(BF16)
    here = selection.at[mine, c]
    spreads = []
    for k in (2, 1, 0):
        ox, oy = chips[k]
        copy = remote(here, here, ag_s.at[k], ag_r.at[k], {"x": ox, "y": oy})
        copy.start()
        spreads.append((k, copy))
    forwards = [remote(here, here, fw_s.at[3], fw_r.at[3], sibling)]
    forwards[0].start()
    if hops > 1:
        b_arrive(0)
        b_start(1)
    cot_ring.arrive(0)
    cot_ring.start(1)
    for k, copy in reversed(spreads):
        copy.wait_recv()
        ox, oy = chips[k]
        there = selection.at[ox * 2 + oy, c]
        forwards.append(remote(there, there, fw_s.at[k], fw_r.at[k], sibling))
        forwards[-1].start()
    for _, copy in spreads:
        copy.wait_send()
    for copy in forwards:
        copy.wait()

    bias = params[taps + 1 : taps + 2, :]

    def steps(i, carry):
        rows = 64
        per = length // rows
        b = i // per
        at = pl.ds(pl.multiple_of((i % per) * rows, rows), rows)
        v = dot_nt(selection[b // 2, b % 2, at, :rank], mats[:, wide : wide + rank]) + bias
        t = pl.ds(i * (rows // 8), rows // 8)
        pres[t] = v.reshape(rows // 8, 8, chans)
        dts[t] = softplus(v).reshape(rows // 8, 8, chans)
        return carry

    lax.fori_loop(0, length * 8 // 64, steps, 0)
    outs += [
        pltpu.make_async_copy(dts, dt_hbm, local_sem.at[11]),
        pltpu.make_async_copy(pres, pre_hbm, local_sem.at[12]),
    ]
    for copy in outs[6:]:
        copy.start()

    cot_ring.arrive(1)
    cot_ring.start(2)
    for k in range(1 if hops > 1 else 0, hops):
        b_arrive(k)
        if k + 1 < hops:
            b_start(k + 1)
    cot_ring.arrive(2)
    cot_ring.start(3)
    for k in range(RING):
        cot_ring.sent(k)
    for k in range(hops):
        a_sent(k)
        b_sent(k)
    for copy in outs + [keep_copy]:
        copy.wait()


def front(z_size, taps, rank, tokens, gain, ids, rows, cot, conv, gate, out, mats):
    length, width = tokens.shape
    shares = z_size * 4
    chans = conv.shape[2]
    wide = mats.shape[1] - rank
    any_space = pl.BlockSpec(memory_space=pl.ANY)
    vmem = pl.BlockSpec(memory_space=pltpu.VMEM)
    dma = pltpu.SemaphoreType.DMA
    hops = z_size - 1
    shape = jax.ShapeDtypeStruct
    everyone = (8,) + tokens.shape
    per_token = (length, 8, chans)
    block = (length, wide)
    return pl.pallas_call(
        functools.partial(front_kernel, z_size, taps, rank),
        in_specs=[vmem] * 8 + [any_space],
        out_specs=[any_space] * 12 + [vmem] * 3,
        out_shape=[
            shape(everyone, BF16),
            shape(everyone, BF16),
            shape((width, chans), BF16),
            shape((width, chans), BF16),
            shape((chans, width), BF16),
            shape((chans, mats.shape[1]), BF16),
            shape((length, 8, 128), F32),
            shape(per_token, F32),
            shape(per_token, F32),
            shape(per_token, F32),
            shape(per_token, F32),
            shape((length * 8, chans), BF16),
            shape((rows.shape[0], chans), F32),
            shape((shares,) + gain.shape, F32),
            shape((4, 2) + block, BF16),
        ],
        scratch_shapes=[
            pltpu.VMEM(everyone, BF16),
            pltpu.VMEM((width, chans), BF16),
            pltpu.VMEM((chans, mats.shape[1]), BF16),
            pltpu.VMEM((z_size,) + rows.shape, BF16),
            pltpu.VMEM((shares,) + gain.shape, F32),
            pltpu.VMEM((8,) + ids.shape, ids.dtype),
            pltpu.VMEM((8, length, chans), F32),
            pltpu.VMEM((length + 3, 8, chans), F32),
            pltpu.VMEM(per_token, F32),
            pltpu.VMEM((length * 8, chans), BF16),
            pltpu.VMEM((4, 2) + block, F32),
            pltpu.VMEM(per_token, F32),
            pltpu.VMEM(per_token, F32),
            pltpu.VMEM((length, 8, 128), F32),
            pltpu.VMEM((4,) + block, BF16),
            pltpu.VMEM((4,) + block, BF16),
            pltpu.VMEM((3,) + block, BF16),
            pltpu.VMEM((3,) + block, BF16),
            dma((14,)),
            dma((shares - 1,)),
            dma((shares - 1,)),
            dma((7,)),
            dma((7,)),
        ]
        + [dma((3,))] * 4
        + [dma((RING - 1, 2)), dma((RING - 1, 2)), dma((RING,)), dma((RING,))] * 2
        + [dma((hops, 3))] * 4
        + [dma((hops, 2))] * 4
        + [dma((1,))] * 2
        + [dma((3,))] * 4
        + [dma((4,))] * 2,
        cost_estimate=busy(120),
        compiler_params=pltpu.CompilerParams(
            collective_id=0, has_side_effects=True, vmem_limit_bytes=60 << 20
        ),
    )(tokens, gain, ids, rows, cot, conv, gate, out, mats)


def add_rows(dst, srcs, rows):
    count = dst.shape[0] // rows

    def body(i, carry):
        at = pl.ds(pl.multiple_of(i * rows, rows), rows)
        total = srcs[0][at].astype(F32)
        for src in srcs[1:]:
            total = total + src[at].astype(F32)
        dst[at] = total.astype(dst.dtype)
        return carry

    lax.fori_loop(0, count, body, 0)


def forward_kernel(
    states,
    rank,
    skip_row,
    dt_ref,
    x_ref,
    sel_ref,
    keep_ref,
    rate_ref,
    normed_ref,
    cot_ref,
    gate_w_ref,
    out_w_ref,
    params_ref,
    hist_ref,
    last_ref,
    ds_ref,
    bgi_ref,
    part_ref,
    gout_ref,
    ggate_ref,
    h_ref,
    bc_ref,
    y_ref,
    ys_ref,
    gate_ref,
    bg_ref,
    gated_ref,
    gout_acc,
    ggate_acc,
):
    chunk = pl.program_id(0)

    @pl.when(chunk == 0)
    def _():
        h_ref[...] = jnp.zeros_like(h_ref)
        gout_acc[...] = jnp.zeros_like(gout_acc)
        ggate_acc[...] = jnp.zeros_like(ggate_acc)

    steps, seqs, width = dt_ref.shape
    groups = width // 128
    rows = steps * seqs
    bc_ref[...] = sel_ref[:, rank:].astype(F32).reshape(bc_ref.shape)

    def body(tb, carry):
        t0 = tb * INNER
        bc = [bc_ref[t0 + i] for i in range(INNER)]
        off = [(1.0 - keep_ref[t0 + i]) * BIG for i in range(INNER)]
        for g in range(groups):
            lanes = pl.ds(g * 128, 128)
            dt = [dt_ref[t0 + i, :, lanes] for i in range(INNER)]
            dtm = [dt[i] + off[i] for i in range(INNER)]
            u = [dt[i] * x_ref[t0 + i, :, lanes] for i in range(INNER)]
            y = [None] * INNER
            for n in range(states):
                h = h_ref[n, :, lanes]
                rate = rate_ref[n, :, lanes]
                for i in range(INNER):
                    hist_ref[t0 + i, n, :, lanes] = h
                    a = jnp.exp2(dtm[i] * rate)
                    h = a * h + u[i] * bc[i][:, n : n + 1]
                    term = h * bc[i][:, states + n : states + n + 1]
                    y[i] = term if y[i] is None else y[i] + term
                h_ref[n, :, lanes] = h
            skip = params_ref[skip_row : skip_row + 1, lanes]
            for i in range(INNER):
                y_ref[t0 + i, :, lanes] = y[i] + skip * x_ref[t0 + i, :, lanes]
        return carry

    lax.fori_loop(0, steps // INNER, body, 0)
    last_ref[...] = h_ref[...]

    normed = normed_ref[...].reshape(rows, normed_ref.shape[2])
    cot = cot_ref[...].reshape(rows, cot_ref.shape[2])
    gate_ref[...] = dot_nn(normed, gate_w_ref[...])
    bg_ref[...] = dot_nt(cot, out_w_ref[...]).astype(BF16).astype(F32)
    ys_ref[...] = jnp.swapaxes(y_ref[...], 0, 1).reshape(rows, width)
    fine = 16

    def gating(i, carry):
        r = pl.ds(pl.multiple_of(i * fine, fine), fine)
        v = gate_ref[r, :]
        bg = bg_ref[r, :]
        y = ys_ref[r, :]
        s = 1.0 / (1.0 + jnp.exp(-v))
        gate = v * s
        gated_ref[r, :] = (y * gate).astype(BF16)
        bg_ref[r, :] = bg * gate
        gate_ref[r, :] = bg * y * (s * (1.0 + v * (1.0 - s)))
        return carry

    lax.fori_loop(0, rows // fine, gating, 0)
    ds_ref[...] = jnp.swapaxes(bg_ref[...].reshape(seqs, steps, width), 0, 1)
    bgi = gate_ref[...].astype(BF16)
    bgi_ref[...] = bgi.reshape(bgi_ref.shape)
    gated = gated_ref[...]
    part_ref[...] = dot_nn(gated, out_w_ref[...]).astype(BF16).reshape(part_ref.shape)
    gout_acc[...] += dot_tn(gated, cot)
    ggate_acc[...] += dot_tn(normed, bgi)

    @pl.when(chunk == pl.num_programs(0) - 1)
    def _():
        gout_ref[...] = gout_acc[...].astype(BF16)
        ggate_ref[...] = ggate_acc[...].astype(BF16)


def scan_forward(rank, skip_row, dt, x, selection, keep, rate, normed, cot, gate_w, out_w, params):
    length, seqs, width = dt.shape
    model = normed.shape[2]
    states = rate.shape[0]
    wide = selection.shape[1]
    block = lambda *tail: pl.BlockSpec((STEPS,) + tail, lambda i: (i,) + (0,) * len(tail))
    across = lambda n: pl.BlockSpec((seqs, STEPS, n), lambda i: (0, i, 0))
    whole = lambda *dims: pl.BlockSpec(dims, lambda i: (0,) * len(dims))
    rows = STEPS * seqs
    shape = jax.ShapeDtypeStruct
    return pl.pallas_call(
        functools.partial(forward_kernel, states, rank, skip_row),
        grid=(length // STEPS,),
        in_specs=[
            block(seqs, width),
            block(seqs, width),
            pl.BlockSpec((rows, wide), lambda i: (i, 0)),
            block(seqs, 128),
            whole(states, seqs, width),
            across(model),
            across(model),
            whole(model, width),
            whole(width, model),
            whole(*params.shape),
        ],
        out_specs=[
            block(states, seqs, width),
            whole(states, seqs, width),
            block(seqs, width),
            across(width),
            across(model),
            whole(width, model),
            whole(model, width),
        ],
        out_shape=[
            shape((length, states, seqs, width), F32),
            shape((states, seqs, width), F32),
            shape(dt.shape, F32),
            shape((seqs, length, width), BF16),
            shape((seqs, length, model), BF16),
            shape((width, model), BF16),
            shape((model, width), BF16),
        ],
        scratch_shapes=[
            pltpu.VMEM((states, seqs, width), F32),
            pltpu.VMEM((STEPS, seqs, wide - rank), F32),
            pltpu.VMEM((STEPS, seqs, width), F32),
            pltpu.VMEM((rows, width), F32),
            pltpu.VMEM((rows, width), F32),
            pltpu.VMEM((rows, width), F32),
            pltpu.VMEM((rows, width), BF16),
            pltpu.VMEM((width, model), F32),
            pltpu.VMEM((model, width), F32),
        ],
        cost_estimate=busy(60),
        compiler_params=pltpu.CompilerParams(vmem_limit_bytes=60 << 20),
    )(dt, x, selection, keep, rate, normed, cot, gate_w, out_w, params)


def z_sums(z, z_size, owns, ups, downs, sems, blocks):
    up_s, up_r, down_s, down_r = sems

    def up_copy(k, j, own):
        src = owns[j].at[z_size - 1 - k] if own else ups[j].at[k]
        return remote(src, ups[j].at[k], up_s.at[k, j], up_r.at[k, j], {"z": z + 1})

    def down_copy(k, j, own):
        src = owns[j].at[k] if own else downs[j].at[k]
        return remote(src, downs[j].at[k], down_s.at[k, j], down_r.at[k, j], {"z": z - 1})

    def line(tau, j):
        k = tau - z
        high = z_size - 1 - k

        @pl.when((k >= 0) & (z < high) & (z > 0))
        def _():
            up_copy(k, j, False).wait_recv()
            add_rows(ups[j].at[k], [owns[j].at[high], ups[j].at[k]], blocks[j])
            up_copy(k, j, False).start()

        @pl.when((k >= 0) & (z < high) & (z == 0))
        def _():
            up_copy(k, j, True).start()

        m = tau - (z_size - 1 - z)

        @pl.when((m >= 0) & (z > m) & (z < z_size - 1))
        def _():
            down_copy(m, j, False).wait_recv()
            add_rows(downs[j].at[m], [owns[j].at[m], downs[j].at[m]], blocks[j])
            down_copy(m, j, False).start()

        @pl.when((m >= 0) & (z > m) & (z == z_size - 1))
        def _():
            down_copy(m, j, True).start()

    def settle(j, dst):
        low = z
        high = z_size - 1 - z

        @pl.when(z == 0)
        def _():
            down_copy(low, j, False).wait_recv()
            add_rows(dst, [owns[j].at[z], downs[j].at[low]], blocks[j])

        @pl.when(z == z_size - 1)
        def _():
            up_copy(high, j, False).wait_recv()
            add_rows(dst, [owns[j].at[z], ups[j].at[high]], blocks[j])

        @pl.when((z > 0) & (z < z_size - 1))
        def _():
            down_copy(low, j, False).wait_recv()
            up_copy(high, j, False).wait_recv()
            add_rows(dst, [owns[j].at[z], downs[j].at[low], ups[j].at[high]], blocks[j])

    def sent(j):
        for k in range(z_size - 1):

            @pl.when(z < z_size - 1 - k)
            def _():
                up_copy(k, j, False).wait_send()

            @pl.when(z > k)
            def _():
                down_copy(k, j, False).wait_send()

    return line, settle, sent


def backward_kernel(
    chunks_all,
    z_size,
    states,
    rank,
    skip_row,
    dt_ref,
    x_ref,
    ds_ref,
    pre_ref,
    sel_ref,
    keep_ref,
    rate_ref,
    hist_ref,
    last_ref,
    ones_ref,
    params_ref,
    step_w_ref,
    gate_hbm,
    out_hbm,
    bx_ref,
    part_ref,
    da_ref,
    gstep_ref,
    bias_ref,
    skip_ref,
    gate_fin,
    out_fin,
    ag_ref,
    h_ref,
    pb_ref,
    pc_ref,
    bc_ref,
    bp_ref,
    gate_own,
    out_own,
    gate_up,
    out_up,
    gate_down,
    out_down,
    local_sem,
    up_s,
    up_r,
    down_s,
    down_r,
):
    chunk = pl.program_id(0)
    chunks = pl.num_programs(0)
    me = place()
    z = me["z"]
    hops = z_size - 1
    line, settle, sent = z_sums(
        z,
        z_size,
        (gate_own, out_own),
        (gate_up, out_up),
        (gate_down, out_down),
        (up_s, up_r, down_s, down_r),
        (64, 16),
    )

    @pl.when(chunk == 0)
    def _():
        greet([{"z": (z + 1) % z_size}, {"z": (z + z_size - 1) % z_size}])
        loads = [
            pltpu.make_async_copy(gate_hbm, gate_own, local_sem.at[0]),
            pltpu.make_async_copy(out_hbm, out_own, local_sem.at[1]),
        ]
        for copy in loads:
            copy.start()
        ag_ref[...] = jnp.zeros_like(ag_ref)
        da_ref[...] = jnp.zeros_like(da_ref)
        gstep_ref[...] = jnp.zeros_like(gstep_ref)
        bias_ref[...] = jnp.zeros_like(bias_ref)
        skip_ref[...] = jnp.zeros_like(skip_ref)
        h_ref[...] = last_ref[...]
        for copy in loads:
            copy.wait()

    for tau in range(hops):

        @pl.when(chunk == -(-tau * chunks_all // hops))
        def _():
            line(tau, 0)
            line(tau, 1)

    steps, seqs, width = dt_ref.shape
    groups = width // 128
    blocks = steps // INNER
    bc_ref[...] = sel_ref[:, rank:].astype(F32).reshape(bc_ref.shape)

    def body(back, carry):
        t0 = (blocks - 1 - back) * INNER
        rows = pl.ds(pl.multiple_of(t0 * seqs, INNER * seqs), INNER * seqs)
        bc = [bc_ref[t0 + i] for i in range(INNER)]
        off = [(1.0 - keep_ref[t0 + i]) * BIG for i in range(INNER)]
        for g in range(groups):
            lanes = pl.ds(g * 128, 128)
            dt = [dt_ref[t0 + i, :, lanes] for i in range(INNER)]
            dtm = [dt[i] + off[i] for i in range(INNER)]
            ds = [ds_ref[t0 + i, :, lanes] for i in range(INNER)]
            u = [dt[i] * x_ref[t0 + i, :, lanes] for i in range(INNER)]
            s1 = [None] * INNER
            s2 = [None] * INNER
            for n in range(states):
                ag = ag_ref[n, :, lanes]
                h = h_ref[n, :, lanes]
                rate = rate_ref[n, :, lanes]
                da = da_ref[n, :, lanes]
                pb = [None] * INNER
                pc = [None] * INNER
                for i in reversed(range(INNER)):
                    prev = hist_ref[t0 + i, n, :, lanes]
                    a = jnp.exp2(dtm[i] * rate)
                    adj = ds[i] * bc[i][:, states + n : states + n + 1] + ag
                    pc[i] = ds[i] * h
                    pb[i] = adj * u[i]
                    ag = a * adj
                    w = ag * prev
                    rw = rate * w
                    gb = adj * bc[i][:, n : n + 1]
                    s1[i] = rw if s1[i] is None else s1[i] + rw
                    s2[i] = gb if s2[i] is None else s2[i] + gb
                    da = da + dt[i] * w
                    h = prev
                ag_ref[n, :, lanes] = ag
                h_ref[n, :, lanes] = h
                da_ref[n, :, lanes] = da
                cols = pl.ds((g * states + n) * 128, 128)
                pb_ref[rows, cols] = jnp.concatenate(pb, axis=0).astype(BF16)
                pc_ref[rows, cols] = jnp.concatenate(pc, axis=0).astype(BF16)
            skip = params_ref[skip_row : skip_row + 1, lanes]
            bias = bias_ref[:, lanes]
            direct = skip_ref[:, lanes]
            low = []
            for i in range(INNER):
                x = x_ref[t0 + i, :, lanes]
                bx_ref[t0 + i, :, lanes] = dt[i] * s2[i] + skip * ds[i]
                back = (s1[i] * (1.0 / LOG2E) + x * s2[i]) / (1.0 + jnp.exp(-pre_ref[t0 + i, :, lanes]))
                low.append(back)
                bias = bias + back
                direct = direct + ds[i] * x
            bias_ref[:, lanes] = bias
            skip_ref[:, lanes] = direct
            bp_ref[rows, lanes] = jnp.concatenate(low, axis=0).astype(BF16)
        return carry

    lax.fori_loop(0, blocks, body, 0)
    span = states * 128
    total = jnp.zeros((steps * seqs, 128), F32)
    for g in range(groups):
        total = total + dot_nn(pb_ref[:, pl.ds(g * span, span)], ones_ref[0])
        total = total + dot_nn(pc_ref[:, pl.ds(g * span, span)], ones_ref[1])
    part_ref[:, rank:] = total
    part_ref[:, :rank] = dot_nn(bp_ref[...], step_w_ref[...])
    gstep_ref[...] += dot_tn(bp_ref[...], sel_ref[:, :rank])

    @pl.when(chunk == chunks - 1)
    def _():
        settle(0, gate_fin)
        settle(1, out_fin)
        sent(0)
        sent(1)


def scan_backward(
    z_size, rank, skip_row, dt, x, ds, pre, selection, keep, rate, hist, last, params, step_w, gate, out
):
    length, seqs, width = dt.shape
    states = rate.shape[0]
    chunks = length // STEPS
    wide = selection.shape[1]
    rows = STEPS * seqs
    block = lambda *tail: pl.BlockSpec((STEPS,) + tail, lambda i: (chunks - 1 - i,) + (0,) * len(tail))
    flat = lambda n: pl.BlockSpec((rows, n), lambda i: (chunks - 1 - i, 0))
    whole = lambda *dims: pl.BlockSpec(dims, lambda i: (0,) * len(dims))
    any_space = pl.BlockSpec(memory_space=pl.ANY)
    span = states * 128
    entry = jnp.arange(span)[:, None] // 128
    column = jnp.arange(128)[None, :]
    ones = jnp.stack([entry == column, entry + states == column]).astype(BF16)
    hops = z_size - 1
    gate_shape, out_shape = gate.shape[1:], out.shape[1:]
    shape = jax.ShapeDtypeStruct
    dma = pltpu.SemaphoreType.DMA
    return pl.pallas_call(
        functools.partial(backward_kernel, chunks, z_size, states, rank, skip_row),
        grid=(chunks,),
        in_specs=[
            block(seqs, width),
            block(seqs, width),
            block(seqs, width),
            block(seqs, width),
            flat(wide),
            block(seqs, 128),
            whole(states, seqs, width),
            block(states, seqs, width),
            whole(states, seqs, width),
            whole(2, span, 128),
            whole(*params.shape),
            whole(width, rank),
            any_space,
            any_space,
        ],
        out_specs=[
            block(seqs, width),
            flat(wide),
            whole(states, seqs, width),
            whole(width, rank),
            whole(seqs, width),
            whole(seqs, width),
            whole(*gate_shape),
            whole(*out_shape),
        ],
        out_shape=[
            shape(dt.shape, F32),
            shape((length * seqs, wide), F32),
            shape((states, seqs, width), F32),
            shape((width, rank), F32),
            shape((seqs, width), F32),
            shape((seqs, width), F32),
            shape(gate_shape, BF16),
            shape(out_shape, BF16),
        ],
        scratch_shapes=[
            pltpu.VMEM((states, seqs, width), F32),
            pltpu.VMEM((states, seqs, width), F32),
            pltpu.VMEM((rows, width // 128 * span), BF16),
            pltpu.VMEM((rows, width // 128 * span), BF16),
            pltpu.VMEM((STEPS, seqs, wide - rank), F32),
            pltpu.VMEM((rows, width), BF16),
            pltpu.VMEM(gate.shape, BF16),
            pltpu.VMEM(out.shape, BF16),
            pltpu.VMEM((hops,) + gate_shape, BF16),
            pltpu.VMEM((hops,) + out_shape, BF16),
            pltpu.VMEM((hops,) + gate_shape, BF16),
            pltpu.VMEM((hops,) + out_shape, BF16),
            dma((2,)),
            dma((hops, 2)),
            dma((hops, 2)),
            dma((hops, 2)),
            dma((hops, 2)),
        ],
        cost_estimate=busy(80),
        compiler_params=pltpu.CompilerParams(
            collective_id=4, has_side_effects=True, vmem_limit_bytes=62 << 20
        ),
    )(dt, x, ds, pre, selection, keep, rate, hist, last, ones, params, step_w, gate, out)


def last_kernel(
    z_size,
    taps,
    part_ref,
    keep_ref,
    mats_ref,
    params_ref,
    gate_fin,
    out_fin,
    da_ref,
    gstep_ref,
    bias_ref,
    skip_ref,
    tokens_ref,
    cot_ref,
    gain_ref,
    bx_hbm,
    cin_hbm,
    picked_hbm,
    normed_hbm,
    conv_hbm,
    gate_hbm,
    bgi_hbm,
    tgrad_ref,
    in_ref,
    out_ref,
    small_out,
    vec_out,
    gain_out,
    chosen,
    first,
    from_sib,
    stage,
    got,
    bx,
    cin,
    picked,
    conv_w,
    gate_w,
    bgi,
    turned,
    bci,
    gsel,
    sums,
    columns,
    own_back,
    sib_stage,
    sib_back,
    ring_got,
    own_small,
    own_vec,
    own_conv,
    up_small,
    up_vec,
    up_conv,
    down_small,
    down_vec,
    down_conv,
    fin_conv,
    both_gate,
    both_conv,
    gain_parts,
    gain_got,
    gain_half,
    gain_pair,
    local_sem,
    column_sem,
    sw_s,
    sw_r,
    rs_s,
    rs_r,
    ag_s,
    ag_r,
    fw_s,
    fw_r,
    sib_send,
    sib_recv,
    ring_send,
    ring_recv,
    up_send,
    up_recv,
    down_send,
    down_recv,
    swap_send,
    swap_recv,
    x_send,
    x_recv,
    gain_send,
    gain_recv,
):
    me = place()
    x, y, z, c = me["x"], me["y"], me["z"], me["c"]
    shares = z_size * 4
    share = z * 4 + y * 2 + c
    corner = y * 2 + c
    sibling = {"c": 1 - c}
    over_x = {"x": 1 - x}
    length, width = tokens_ref.shape
    chans = bx.shape[2]
    rows_in = in_ref.shape[0]
    half = out_fin.shape[0]
    hops = z_size - 1
    wide = part_ref.shape[3]
    greet(plane_others(me) + z_only(me, shares))

    loads = [
        pltpu.make_async_copy(src, dst, local_sem.at[i])
        for i, (src, dst) in enumerate(
            [
                (cin_hbm, cin.at[pl.ds(3, length)]),
                (bx_hbm, bx.at[pl.ds(0, length)]),
                (picked_hbm, picked),
                (bgi_hbm, bgi),
                (conv_hbm, conv_w),
                (gate_hbm, gate_w),
            ]
        )
    ]
    for copy in loads:
        copy.start()

    first[...] = part_ref[:, 1 - c].astype(BF16)
    swap = remote(first, from_sib, sw_s.at[0], sw_r.at[0], sibling)
    swap.start()
    cin[0:3] = jnp.zeros((3, 8, chans), F32)
    bx[length : length + 3] = jnp.zeros((3, 8, chans), F32)
    sums[...] = jnp.zeros_like(sums)
    gsel[...] = jnp.zeros_like(gsel)
    swap.wait()
    mine = x * 2 + y
    chips = [((x + d // 2) % 2, (y + d % 2) % 2) for d in (1, 2, 3)]
    sends = []
    for k in (2, 1, 0):
        ox, oy = chips[k]
        j = ox * 2 + oy
        stage[k] = (part_ref[j, c] + from_sib[j].astype(F32)).astype(BF16)
        copy = remote(stage.at[k], got.at[k], rs_s.at[k], rs_r.at[k], {"x": ox, "y": oy})
        copy.start()
        sends.append(copy)
    total = part_ref[mine, c] + from_sib[mine].astype(F32)
    for copy in sends:
        copy.wait()
    for k in range(3):
        total = total + got[k].astype(F32)
    chosen[mine, c] = total.astype(BF16)
    here = chosen.at[mine, c]
    spreads = []
    for k in (2, 1, 0):
        ox, oy = chips[k]
        copy = remote(here, here, ag_s.at[k], ag_r.at[k], {"x": ox, "y": oy})
        copy.start()
        spreads.append((k, copy))
    forwards = [remote(here, here, fw_s.at[3], fw_r.at[3], sibling)]
    forwards[0].start()

    def corner_sends(src, dst, index):
        out = []
        for k in range(1, 4):
            to = (corner + k) % 4
            out.append(
                remote(
                    src.at[pl.ds(pl.multiple_of(to * rows_in, rows_in), rows_in)],
                    dst.at[x, corner],
                    swap_send.at[index, k - 1],
                    swap_recv.at[index, k - 1],
                    {"y": to // 2, "c": to % 2},
                )
            )
        return out

    gate_swaps = corner_sends(gate_fin, both_gate, 0)
    conv_swaps = corner_sends(fin_conv, both_conv, 1)
    for copy in gate_swaps:
        copy.start()
    both_gate[x, corner] = gate_fin[pl.ds(pl.multiple_of(corner * rows_in, rows_in), rows_in)]
    out_ref[x] = out_fin[...]
    out_x = remote(out_ref.at[x], out_ref.at[x], x_send.at[0], x_recv.at[0], over_x)
    for k, copy in reversed(spreads):
        copy.wait_recv()
        ox, oy = chips[k]
        there = chosen.at[ox * 2 + oy, c]
        forwards.append(remote(there, there, fw_s.at[k], fw_r.at[k], sibling))
        forwards[-1].start()
    out_x.start()
    for copy in loads:
        copy.wait()
    for _, copy in spreads:
        copy.wait_send()
    for copy in forwards:
        copy.wait()

    fine = 4
    block = length // 8

    def taps_of(lanes):
        return [
            jnp.broadcast_to(params_ref[taps - 1 - j : taps - j, lanes], (8, 128)) for j in range(taps)
        ]

    def select(b, carry):
        rows = pl.ds(pl.multiple_of(b * length, length), length)
        back = chosen[b // 2, b % 2]
        t0 = b * block
        bx[pl.ds(t0, block)] += dot_nt(back, mats_ref[:, :wide]).reshape(block, 8, chans)
        gsel[...] += dot_tn(picked[rows, :], back)

        def convolve(i, carry):
            for g in range(chans // 128):
                lanes = pl.ds(g * 128, 128)
                tap = taps_of(lanes)
                offset = jnp.broadcast_to(params_ref[taps : taps + 1, lanes], (8, 128))
                acc = [sums[r, :, lanes] for r in range(taps + 1)]
                for j in range(fine):
                    t = t0 + i * fine + j
                    k0 = keep_ref[t]
                    k1 = k0 * keep_ref[jnp.maximum(t - 1, 0)]
                    k2 = k1 * keep_ref[jnp.maximum(t - 2, 0)]
                    v0 = cin[t + 3, :, lanes]
                    v1 = cin[t + 2, :, lanes] * k0
                    v2 = cin[t + 1, :, lanes] * k1
                    v3 = cin[t, :, lanes] * k2
                    v = offset + tap[0] * v0 + tap[1] * v1 + tap[2] * v2 + tap[3] * v3
                    s = 1.0 / (1.0 + jnp.exp(-v))
                    back = bx[t, :, lanes] * (s * (1.0 + v * (1.0 - s)))
                    bx[t, :, lanes] = back
                    acc[0] = acc[0] + back * v0
                    acc[1] = acc[1] + back * v1
                    acc[2] = acc[2] + back * v2
                    acc[3] = acc[3] + back * v3
                    acc[4] = acc[4] + back
                for r in range(taps + 1):
                    sums[r, :, lanes] = acc[r]
            return carry

        lax.fori_loop(0, block // fine, convolve, 0)
        return carry

    lax.fori_loop(0, 8, select, 0)
    for copy in gate_swaps:
        copy.wait()
    gate_x = remote(both_gate.at[x], both_gate.at[x], x_send.at[1], x_recv.at[1], over_x)
    gate_x.start()

    def unfold(b, carry):
        t0 = b * block

        def convolve(i, carry):
            for g in range(chans // 128):
                lanes = pl.ds(g * 128, 128)
                tap = taps_of(lanes)
                for j in range(fine):
                    t = t0 + i * fine + j
                    total = tap[3] * bx[t + 3, :, lanes] * keep_ref[jnp.minimum(t + 3, length - 1)]
                    total = (total + tap[2] * bx[t + 2, :, lanes]) * keep_ref[
                        jnp.minimum(t + 2, length - 1)
                    ]
                    total = (total + tap[1] * bx[t + 1, :, lanes]) * keep_ref[
                        jnp.minimum(t + 1, length - 1)
                    ]
                    turned[i * fine + j, :, lanes] = total + tap[0] * bx[t, :, lanes]
            return carry

        lax.fori_loop(0, block // fine, convolve, 0)
        bci[:, pl.ds(pl.multiple_of(t0, block), block), :] = jnp.swapaxes(turned[...], 0, 1).astype(BF16)
        return carry

    def column(i, slot):
        zz = jnp.where(z * 2 < z_size, z_size - 1 - i, i)
        cols = pl.ds(pl.multiple_of(zz * 4 * rows_in, 4 * rows_in), 4 * rows_in)
        return zz, pltpu.make_async_copy(normed_hbm.at[:, :, cols], columns.at[slot], column_sem.at[slot])

    column(0, 0)[1].start()
    lax.fori_loop(0, 8, unfold, 0)

    owns = (own_small, own_vec, own_conv)
    line, settle, sent = z_sums(
        z,
        z_size,
        owns,
        (up_small, up_vec, up_conv),
        (down_small, down_vec, down_conv),
        (up_send, up_recv, down_send, down_recv),
        (16, 16, 64),
    )

    rates = -jnp.exp(params_ref[taps + 3 : taps + 3 + da_ref.shape[0], :])
    vectors = (
        [jnp.sum(sums[taps - 1 - r], axis=0, keepdims=True) for r in range(taps)]
        + [
            jnp.sum(sums[taps], axis=0, keepdims=True),
            jnp.sum(bias_ref[...], axis=0, keepdims=True),
            jnp.sum(skip_ref[...], axis=0, keepdims=True),
        ]
        + [jnp.sum(da_ref[...], axis=1) * rates]
    )
    used = taps + 3 + da_ref.shape[0]
    vectors = jnp.concatenate(
        vectors + [jnp.zeros((own_vec.shape[1] - used, chans), F32)], axis=0
    ).astype(BF16)
    for zz in range(z_size):
        own_vec[zz] = vectors[:, zz * half : (zz + 1) * half]
        own_small[zz, :, :wide] = gsel[zz * half : (zz + 1) * half, :].astype(BF16)
        own_small[zz, :, wide:] = gstep_ref[zz * half : (zz + 1) * half, :].astype(BF16)

    at = ring_at(x, y)
    step = 1 + 2 * c
    sib_step = 3 - 2 * c
    nx, ny = ring_chip((at + step) % RING)
    following = {"x": nx, "y": ny}

    def grad_column(i):
        slot = i % 2
        zz, copy = column(i, slot)
        copy.wait()
        if i + 1 < z_size:
            column(i + 1, 1 - slot)[1].start()
        tall = columns[slot].reshape(8 * length, 4 * rows_in)
        own_conv[zz] = dot_tn(tall, bci[...].reshape(8 * length, chans)).astype(BF16)

    def back_block(dst, p, core):
        cx, cy = ring_chip(p % RING)
        s = cx * 4 + cy * 2 + core

        def cols(i, carry):
            n = pl.ds(pl.multiple_of(i * 512, 512), 512)
            total = dot_nt(bci[s], conv_w[n, :]) + dot_nt(bgi[s], gate_w[n, :])
            dst[:, n] = total.astype(BF16)
            return carry

        lax.fori_loop(0, width // 512, cols, 0)

    def cross(k):
        slot = k % 2
        return remote(sib_stage.at[slot], sib_back.at[k], sib_send.at[k], sib_recv.at[k], sibling)

    def ring(k, p):
        r = pl.ds(p * (length // 2), length // 2)
        return remote(
            own_back.at[k, r], ring_got.at[k, r], ring_send.at[k, p], ring_recv.at[k, p], following
        )

    def blocks_for(k):
        if k >= 2:
            cross(k - 2).wait_send()
        back_block(sib_stage.at[k % 2], at + sib_step * (RING - 1 - k), 1 - c)
        cross(k).start()
        back_block(own_back.at[k], at + step * (RING - 1 - k), c)

    def ring_step(k):
        cross(k).wait_recv()
        srcs = [own_back.at[k], sib_back.at[k]]
        if k:
            for p in range(2):
                ring(k - 1, p).wait_recv()
            srcs.append(ring_got.at[k - 1])
        add_rows(own_back.at[k], srcs, 16)
        for p in range(2):
            ring(k, p).start()

    def ring_end():
        last = RING - 1
        cross(last).wait_recv()
        for p in range(2):
            ring(last - 1, p).wait_recv()
        rows = 16

        def body(i, total):
            r = pl.ds(pl.multiple_of(i * rows, rows), rows)
            back = (
                own_back[last, r].astype(F32)
                + sib_back[last, r].astype(F32)
                + ring_got[last - 1, r].astype(F32)
            )
            values = tokens_ref[r].astype(F32)
            rstd = lax.rsqrt(jnp.mean(values * values, axis=-1, keepdims=True) + epsilon)
            scaled = back * gain_ref[...]
            inner = jnp.mean(scaled * values, axis=-1, keepdims=True)
            grad = cot_ref[r].astype(F32) + rstd * scaled - values * (rstd * rstd * rstd * inner)
            tgrad_ref[r] = grad.astype(BF16)
            terms = back * values * rstd
            return total + terms[:8] + terms[8:]

        total = lax.fori_loop(0, length // rows, body, jnp.zeros((8, width), F32))
        total = jnp.broadcast_to(jnp.sum(total, axis=0, keepdims=True), (8, width))
        piece = gain_parts.shape[2]
        for f in range(shares):
            gain_parts[f] = total[:, f * piece : (f + 1) * piece]
        gain_got[share] = gain_parts[share]

    gains = []
    for k in range(1, shares):
        f = (share + k) % shares
        gains.append(
            remote(
                gain_parts.at[f], gain_got.at[share], gain_send.at[k - 1], gain_recv.at[k - 1], share_at(f)
            )
        )

    def lines(tau):
        for j in (2, 0, 1):
            line(tau, j)

    blocks_for(0)
    ring_step(0)
    grad_column(0)
    lines(0)
    for i in range(1, z_size):
        grad_column(i)
    blocks_for(1)
    ring_step(1)
    blocks_for(2)
    lines(1)
    blocks_for(3)
    ring_step(2)
    for tau in range(2, hops):
        lines(tau)
    ring_end()
    for copy in gains:
        copy.start()

    settle(2, fin_conv)
    for copy in conv_swaps:
        copy.start()
    both_conv[x, corner] = fin_conv[pl.ds(pl.multiple_of(corner * rows_in, rows_in), rows_in)]
    settle(0, small_out.at[x])
    settle(1, vec_out.at[x])
    small_x = remote(small_out.at[x], small_out.at[x], x_send.at[2], x_recv.at[2], over_x)
    vec_x = remote(vec_out.at[x], vec_out.at[x], x_send.at[3], x_recv.at[3], over_x)
    for copy in conv_swaps:
        copy.wait()
    conv_x = remote(both_conv.at[x], both_conv.at[x], x_send.at[4], x_recv.at[4], over_x)
    conv_x.start()
    small_x.start()
    vec_x.start()

    branch = 8 * half * z_size

    def lay(first, both):
        for zz in range(z_size):
            for j in range(4):
                for xx in range(2):
                    col = first + (zz * 4 + j) * 2 * half + xx * half
                    in_ref[:, col : col + half] = both[xx, j, :, zz * half : (zz + 1) * half].astype(F32)

    for copy in gains:
        copy.wait()
    gain_half[...] = jnp.sum(gain_got[...], axis=0)
    gain_x = remote(gain_half, gain_pair, x_send.at[5], x_recv.at[5], over_x)
    gain_x.start()
    gate_x.wait()
    lay(branch, both_gate)
    gain_x.wait()
    gain_out[...] = gain_half[...] + gain_pair[...]
    conv_x.wait()
    lay(0, both_conv)
    for copy in (out_x, small_x, vec_x):
        copy.wait()
    for j in range(3):
        sent(j)
    for k in range(RING - 1):
        for p in range(2):
            ring(k, p).wait_send()
    for k in range(2, RING):
        cross(k).wait_send()


def last_part(
    z_size,
    taps,
    part,
    keep,
    mats,
    params,
    gate_fin,
    out_fin,
    da,
    gstep,
    bias,
    skip,
    tokens,
    cot,
    gain,
    bx,
    cin,
    picked,
    normed,
    conv,
    gate,
    bgi,
    in_width,
):
    length, width = tokens.shape
    chans = bx.shape[2]
    shares = z_size * 4
    hops = z_size - 1
    rows_in = gate_fin.shape[0] // 4
    half = out_fin.shape[0]
    wide = part.shape[3]
    any_space = pl.BlockSpec(memory_space=pl.ANY)
    vmem = pl.BlockSpec(memory_space=pltpu.VMEM)
    dma = pltpu.SemaphoreType.DMA
    shape = jax.ShapeDtypeStruct
    block = (length, width)
    slabs = [(half, mats.shape[1]), (params.shape[0], half), (4 * rows_in, chans)]
    bufs = lambda n: [pltpu.VMEM((n,) + s, BF16) for s in slabs]
    both = pltpu.VMEM((2, 4, rows_in, chans), BF16)
    piece = (8, width // shares)
    few = (length, wide)
    return pl.pallas_call(
        functools.partial(last_kernel, z_size, taps),
        in_specs=[vmem] * 13 + [any_space] * 7,
        out_specs=[vmem] * 6,
        out_shape=[
            shape(tokens.shape, BF16),
            shape((rows_in, in_width), F32),
            shape((2,) + out_fin.shape, BF16),
            shape((2,) + slabs[0], BF16),
            shape((2,) + slabs[1], BF16),
            shape(piece, F32),
        ],
        scratch_shapes=[
            pltpu.VMEM((4, 2) + few, BF16),
            pltpu.VMEM((4,) + few, BF16),
            pltpu.VMEM((4,) + few, BF16),
            pltpu.VMEM((3,) + few, BF16),
            pltpu.VMEM((3,) + few, BF16),
            pltpu.VMEM((length + 3, 8, chans), F32),
            pltpu.VMEM((length + 3, 8, chans), F32),
            pltpu.VMEM(picked.shape, BF16),
            pltpu.VMEM(conv.shape, BF16),
            pltpu.VMEM(gate.shape, BF16),
            pltpu.VMEM(bgi.shape, BF16),
            pltpu.VMEM((length // 8, 8, chans), F32),
            pltpu.VMEM(bgi.shape, BF16),
            pltpu.VMEM((chans, wide), F32),
            pltpu.VMEM((taps + 1, 8, chans), F32),
            pltpu.VMEM((2, 8, length, 4 * rows_in), BF16),
            pltpu.VMEM((RING,) + block, BF16),
            pltpu.VMEM((2,) + block, BF16),
            pltpu.VMEM((RING,) + block, BF16),
            pltpu.VMEM((RING - 1,) + block, BF16),
        ]
        + bufs(z_size)
        + bufs(hops)
        + bufs(hops)
        + [
            pltpu.VMEM(slabs[2], BF16),
            both,
            both,
            pltpu.VMEM((shares,) + piece, F32),
            pltpu.VMEM((shares,) + piece, F32),
            pltpu.VMEM(piece, F32),
            pltpu.VMEM(piece, F32),
            dma((6,)),
            dma((2,)),
            dma((1,)),
            dma((1,)),
        ]
        + [dma((3,))] * 4
        + [dma((4,))] * 2
        + [dma((RING,))] * 2
        + [dma((RING - 1, 2))] * 2
        + [dma((hops, 3))] * 4
        + [dma((2, 3))] * 2
        + [dma((6,))] * 2
        + [dma((shares - 1,))] * 2,
        cost_estimate=busy(120),
        compiler_params=pltpu.CompilerParams(
            collective_id=3, has_side_effects=True, vmem_limit_bytes=63 << 20
        ),
    )(
        part,
        keep,
        mats,
        params,
        gate_fin,
        out_fin,
        da,
        gstep,
        bias,
        skip,
        tokens,
        cot,
        gain,
        bx,
        cin,
        picked,
        normed,
        conv,
        gate,
        bgi,
    )


def shards(
    tokens,
    doc_ids,
    norm_gain,
    in_weight,
    conv_taps,
    conv_offset,
    select_weight,
    step_weight,
    step_bias,
    decay_log,
    skip_gain,
    out_weight,
    cotangent,
):
    z_size = lax.axis_size("z")
    rh_size = lax.axis_size("rh")
    seqs = 8
    length = doc_ids.shape[1]
    width = tokens.shape[1]
    in_rows = in_weight.shape[0]
    rows = out_weight.shape[0]
    half = rows // 2
    chans = half * z_size
    taps = conv_taps.shape[1]
    rank = step_weight.shape[1]
    states = decay_log.shape[1]
    x_at = lax.axis_index("x")

    def own_half(w):
        return lax.dynamic_slice_in_dim(w, x_at * half, half, 0)

    spare = -(rank + 2 * states) % 128
    wide = rank + 2 * states + spare
    vectors = jnp.concatenate(
        [
            own_half(conv_taps),
            own_half(conv_offset)[:, None],
            own_half(step_bias)[:, None],
            own_half(skip_gain)[:, None],
            own_half(decay_log),
        ],
        axis=1,
    ).T
    vectors = jnp.pad(vectors, ((0, -vectors.shape[0] % 32), (0, 0)))
    mats = jnp.concatenate(
        [jnp.pad(own_half(select_weight), ((0, 0), (0, spare))), own_half(step_weight)], axis=1
    )
    columns = lax.dynamic_index_in_dim(
        in_weight.reshape(in_rows, 2, z_size, 4, 2, half), x_at, 4, keepdims=False
    )
    packed = columns.transpose(1, 3, 0, 2, 4).reshape(2, 4, in_rows, chans)
    gain_tile = jnp.broadcast_to(norm_gain.astype(F32)[None, :], (8, norm_gain.shape[0]))
    ids_tile = jnp.broadcast_to(doc_ids, (8, length))
    (
        all_normed,
        all_cot,
        w_conv,
        w_gate,
        w_out,
        w_mats,
        keep,
        conv_in,
        x,
        dt,
        pre,
        picked,
        vectors,
        gains,
        selection,
    ) = front(
        z_size,
        taps,
        rank,
        tokens,
        gain_tile,
        ids_tile,
        vectors,
        cotangent,
        packed[0],
        packed[1],
        own_half(out_weight),
        mats,
    )
    gain = gains[:, 0, :].reshape(1, width)
    selection = selection.reshape(length * seqs, wide)
    rates = -jnp.exp(vectors[taps + 3 : taps + 3 + states])
    rate2 = jnp.broadcast_to((rates * LOG2E)[:, None, :], (states, seqs, chans))

    hist, last, back_scan, back_gate_in, out_part, grad_out, grad_gate = scan_forward(
        rank, taps + 2, dt, x, selection, keep, rate2, all_normed, all_cot, w_gate, w_out, vectors
    )
    layer_sum = lax.psum_scatter(
        out_part.reshape(-1, width), PLANE, scatter_dimension=0, tiled=True
    )
    layer_out = (tokens.astype(F32) + layer_sum.astype(F32)).astype(BF16)
    back_x, part, da, g_step, g_bias, g_skip, gate_fin, out_fin = scan_backward(
        z_size,
        rank,
        taps + 2,
        dt,
        x,
        back_scan,
        pre,
        selection,
        keep,
        rate2,
        hist,
        last,
        vectors,
        w_mats[:, wide:],
        grad_gate.reshape(z_size, -1, chans),
        grad_out.reshape(z_size, half, width),
    )
    tokens_grad, g_in, g_out, g_mats, g_vectors, g_gain = last_part(
        z_size,
        taps,
        part.reshape(4, 2, length, wide),
        keep,
        w_mats,
        vectors,
        gate_fin,
        out_fin,
        da,
        g_step,
        g_bias,
        g_skip,
        tokens,
        cotangent,
        gain,
        back_x,
        conv_in,
        picked,
        all_normed,
        w_conv,
        w_gate,
        back_gate_in,
        in_weight.shape[1],
    )
    g_gain = g_gain[0]
    g_out = g_out.reshape(rows, width).astype(F32)
    g_mats = g_mats.reshape(rows, -1).astype(F32)
    g_vectors = g_vectors.transpose(0, 2, 1).reshape(rows, -1).astype(F32)
    if rh_size > 1:
        g_mats, g_vectors, g_in, g_out, g_gain = lax.psum(
            (g_mats, g_vectors, g_in, g_out, g_gain), "rh"
        )
    return (
        layer_out,
        tokens_grad,
        g_gain,
        g_in,
        g_vectors[:, :taps],
        g_vectors[:, taps],
        g_mats[:, : rank + 2 * states],
        g_mats[:, wide:],
        g_vectors[:, taps + 1],
        g_vectors[:, taps + 3 : taps + 3 + states],
        g_vectors[:, taps + 2],
        g_out,
    )


def solution(mesh):
    replicas = mesh.shape["replica"]
    shares = mesh.shape["fsdp"]
    grid = Mesh(
        mesh.devices.reshape(replicas // 2, 2, shares // 4, 2, 2), ("rh", "x", "z", "y", "c")
    )
    tok = ("rh", "x", "z", "y", "c")
    own = ("z", "y", "c")
    return jax.shard_map(
        shards,
        mesh=grid,
        in_specs=(
            P(tok, None),
            P(tok, None),
            P(own),
            P(own, None),
            P(own, None),
            P(own),
            P(own, None),
            P(own, None),
            P(own),
            P(own, None),
            P(own),
            P(own, None),
            P(tok, None),
        ),
        out_specs=(
            P(tok, None),
            P(tok, None),
            P(own),
            P(own, None),
            P(own, None),
            P(own),
            P(own, None),
            P(own, None),
            P(own),
            P(own, None),
            P(own),
            P(own, None),
        ),
        check_vma=False,
    )
```

```python
import functools

import jax
import jax.numpy as jnp
import numpy as np
from jax import lax
from jax.experimental import pallas as pl
from jax.experimental.pallas import tpu as pltpu
from jax.sharding import Mesh
from jax.sharding import PartitionSpec as P

F32 = jnp.float32
BF16 = jnp.bfloat16
epsilon = 1e-05
PLANE = ("x", "y", "c")
BIG = 1e30
STEPS = 32
COLUMNS = 512
INNER = 4
BACK_INNER = 8
TOGETHER = 4
LOG2E = 1.4426950408889634


def dot(a, b, dims):
    return lax.dot_general(a, b, (dims, ((), ())), preferred_element_type=F32)


def dot_nn(a, b):
    return dot(a, b, ((1,), (0,)))


def dot_tn(a, b):
    return dot(a, b, ((0,), (0,)))


def dot_nt(a, b):
    return dot(a, b, ((1,), (1,)))


def busy(micros):
    return pl.CostEstimate(flops=micros * 10**9, bytes_accessed=micros * 10**6, transcendentals=0)


MESH = pl.DeviceIdType.MESH
RING = 4


def place():
    return {a: lax.axis_index(a) for a in ("x", "z", "y", "c")}


def ring_chip(p):
    y = p // 2
    return (p + y) % 2, y


def ring_at(x, y):
    return 2 * y + (x + y) % 2


def share_at(f):
    return {"z": f // 4, "y": f // 2 % 2, "c": f % 2}


def remote(src, dst, send, recv, device):
    return pltpu.make_async_remote_copy(
        src_ref=src, dst_ref=dst, send_sem=send, recv_sem=recv, device_id=device, device_id_type=MESH
    )


def greet(devices):
    barrier = pltpu.get_barrier_semaphore()
    for device in devices:
        pl.semaphore_signal(barrier, inc=1, device_id=device, device_id_type=MESH)
    pl.semaphore_wait(barrier, len(devices))


def plane_others(me):
    out = []
    for dx in range(2):
        for dy in range(2):
            for dc in range(2):
                if dx + dy + dc:
                    out.append(
                        {"x": (me["x"] + dx) % 2, "y": (me["y"] + dy) % 2, "c": (me["c"] + dc) % 2}
                    )
    return out


def share_others(me, shares):
    f = me["z"] * 4 + me["y"] * 2 + me["c"]
    return [share_at((f + k) % shares) for k in range(1, shares)]


def z_only(me, shares):
    f = me["c"] + 2 * me["y"]
    out = []
    for dz in range(1, shares // 4):
        for k in range(4):
            out.append(
                {
                    "z": (me["z"] + dz) % (shares // 4),
                    "y": (f + k) % 4 // 2,
                    "c": (f + k) % 2,
                }
            )
    return out


def z_line(z, z_size, pieces, sems):
    up_s, up_r, down_s, down_r = sems

    def up(k):
        return [
            remote(p(z - k), p(z - k), up_s.at[k, j], up_r.at[k, j], {"z": z + 1})
            for j, p in enumerate(pieces)
        ]

    def down(k):
        return [
            remote(p(z + k), p(z + k), down_s.at[k, j], down_r.at[k, j], {"z": z - 1})
            for j, p in enumerate(pieces)
        ]

    def start(k):
        @pl.when((z < z_size - 1) & (z >= k))
        def _():
            for copy in up(k):
                copy.start()

        @pl.when((z > 0) & (z + k < z_size))
        def _():
            for copy in down(k):
                copy.start()

    def arrive(k):
        @pl.when(z > k)
        def _():
            for copy in up(k):
                copy.wait_recv()

        @pl.when(z + k < z_size - 1)
        def _():
            for copy in down(k):
                copy.wait_recv()

    def sent(k):
        @pl.when((z < z_size - 1) & (z >= k))
        def _():
            for copy in up(k):
                copy.wait_send()

        @pl.when((z > 0) & (z + k < z_size))
        def _():
            for copy in down(k):
                copy.wait_send()

    return start, arrive, sent


class Ring:
    def __init__(self, me, blocks, own, ring_send, ring_recv, sib_send, sib_recv):
        self.me, self.blocks, self.own = me, blocks, own
        self.sems = ring_send, ring_recv, sib_send, sib_recv
        self.at = ring_at(me["x"], me["y"])
        self.step = 1 + 2 * me["c"]
        nx, ny = ring_chip((self.at + self.step) % RING)
        self.following = {"x": nx, "y": ny}
        self.sibling = {"c": 1 - me["c"]}
        self.half = blocks.shape[1] // 2

    def slot(self, k):
        ox, oy = ring_chip((self.at + (RING - self.step) * k) % RING)
        return ox * 4 + oy * 2 + self.me["c"]

    def hop(self, k):
        out = []
        for p in range(2):
            rows = pl.ds(p * self.half, self.half)
            dst = self.blocks.at[self.slot(k), rows]
            src = self.own.at[rows] if k == 0 and self.own is not None else dst
            out.append(remote(src, dst, self.sems[0].at[k, p], self.sems[1].at[k, p], self.following))
        return out

    def cross(self, k):
        dst = self.blocks.at[self.slot(k)]
        src = self.own if k == 0 and self.own is not None else dst
        return remote(src, dst, self.sems[2].at[k], self.sems[3].at[k], self.sibling)

    def start(self, k):
        if k < RING - 1:
            for copy in self.hop(k):
                copy.start()
        self.cross(k).start()

    def arrive(self, k):
        for copy in self.hop(k):
            copy.wait_recv()

    def sent(self, k):
        if k < RING - 1:
            for copy in self.hop(k):
                copy.wait_send()
        self.cross(k).wait()


def sigmoid(v):
    return 0.5 + 0.5 * jnp.tanh(0.5 * v)


def softplus(v):
    e = jnp.exp(-jnp.abs(v))
    small = e * (1.0 - e * (0.5 - e * (1.0 / 3.0)))
    return jnp.maximum(v, 0.0) + jnp.where(e < 1e-3, small, jnp.log(1.0 + e))


def front_kernel(
    z_size,
    taps,
    rank,
    tokens_ref,
    gain_ref,
    ids_ref,
    rows_ref,
    cot_ref,
    in_ref,
    out_ref,
    select_ref,
    step_ref,
    normed_hbm,
    cot_all,
    conv_hbm,
    gate_all,
    out_all,
    mats_hbm,
    keep_hbm,
    cin_hbm,
    x_hbm,
    dt_hbm,
    pre_hbm,
    params,
    gain_all,
    selection,
    normed_all,
    conv_w,
    mats,
    rows_all,
    gain_got,
    ids_all,
    proj,
    cin,
    xs,
    picked,
    part,
    dts,
    pres,
    keep,
    first,
    from_sib,
    stage,
    got,
    local_sem,
    own_sem,
    gain_send,
    gain_recv,
    ids_send,
    ids_recv,
    conv_send,
    conv_recv,
    gate_send,
    gate_recv,
    ring_send,
    ring_recv,
    sib_send,
    sib_recv,
    cot_ring_send,
    cot_ring_recv,
    cot_sib_send,
    cot_sib_recv,
    a_us,
    a_ur,
    a_ds,
    a_dr,
    m_us,
    m_ur,
    m_ds,
    m_dr,
    b_us,
    b_ur,
    b_ds,
    b_dr,
    sw_s,
    sw_r,
    rs_s,
    rs_r,
    ag_s,
    ag_r,
    fw_s,
    fw_r,
):
    me = place()
    x, y, z, c = me["x"], me["y"], me["z"], me["c"]
    shares = z_size * 4
    share = z * 4 + y * 2 + c
    corner = y * 2 + c
    seq = x * 4 + y * 2 + c
    sibling = {"c": 1 - c}
    length, width = tokens_ref.shape
    chans = conv_w.shape[1]
    rows_in = width // shares
    half = chans // z_size
    hops = z_size - 1
    branch = 8 * chans
    greet(plane_others(me) + z_only(me, shares))

    def rows_at(ref, index, count):
        return ref.at[pl.ds(pl.multiple_of(index * count, count), count)]

    def pieces(first, dst, to):
        rows = rows_at(dst, share, rows_in)
        if len(in_ref.shape) == 4:
            return [(in_ref.at[1 if first else 0, to], rows)]
        out = []
        for zz in range(z_size):
            col = first + (zz * 4 + to) * 2 * half + x * half
            src = in_ref.at[:, pl.ds(pl.multiple_of(col, half), half)]
            out.append((src, rows.at[:, pl.ds(zz * half, half)]))
        return out

    def corner_sends(first, dst, send, recv):
        out = []
        for k in range(1, 4):
            to = (corner + k) % 4
            for i, (src, there) in enumerate(pieces(first, dst, to)):
                out.append(
                    remote(
                        src, there, send.at[k - 1, i], recv.at[k - 1, i], {"y": to // 2, "c": to % 2}
                    )
                )
        return out

    swaps = corner_sends(0, conv_w, conv_send, conv_recv)
    gates = corner_sends(branch, gate_all, gate_send, gate_recv)
    for copy in swaps:
        copy.start()
    gains = [
        remote(gain_ref, gain_got.at[share], gain_send.at[k], gain_recv.at[k], device)
        for k, device in enumerate(share_others(me, shares))
    ]
    for copy in gains:
        copy.start()
    locals_ = [
        pltpu.make_async_copy(
            out_ref.at[pl.ds(pl.multiple_of(x * half, half), half)], rows_at(out_all, z, half), local_sem.at[3]
        ),
        pltpu.make_async_copy(cot_ref, cot_all.at[seq], local_sem.at[4]),
    ]
    for i, (src, there) in enumerate(pieces(0, conv_w, corner)):
        locals_.append(pltpu.make_async_copy(src, there, own_sem.at[0, i]))
    for i, (src, there) in enumerate(pieces(branch, gate_all, corner)):
        locals_.append(pltpu.make_async_copy(src, there, own_sem.at[1, i]))
    for copy in locals_:
        copy.start()
    ids_copies = [
        remote(ids_ref, ids_all.at[seq], ids_send.at[k], ids_recv.at[k], device)
        for k, device in enumerate(plane_others(me))
    ]
    for copy in ids_copies:
        copy.start()
    ids_all[seq] = ids_ref[...]
    gain_got[share] = gain_ref[...]
    rows_all[z] = rows_ref[...]
    mine_rows = pl.ds(pl.multiple_of(x * half, half), half)
    at_rows = pl.ds(pl.multiple_of(z * half, half), half)
    wide = mats.shape[1] - rank
    mats[at_rows, :wide] = jnp.concatenate(
        [
            select_ref[mine_rows, :],
            jnp.zeros((half, wide - select_ref.shape[1]), BF16),
        ],
        axis=1,
    )
    mats[at_rows, wide:] = step_ref[mine_rows, :]

    values = tokens_ref[...].astype(F32)
    rstd = lax.rsqrt(jnp.mean(values * values, axis=-1, keepdims=True) + epsilon)
    for copy in gains:
        copy.wait()
    piece = gain_ref.shape[1]
    for f in range(shares):
        cols = pl.ds(f * piece, piece)
        normed = tokens_ref[:, cols].astype(F32) * rstd * gain_got[f, 0:1, :]
        normed_all[seq, :, cols] = normed.astype(BF16)
    for f in range(shares):
        gain_all[:, f * piece : (f + 1) * piece] = gain_got[f]

    ring = Ring(me, normed_all, None, ring_send, ring_recv, sib_send, sib_recv)
    cot_ring = Ring(me, cot_all, cot_ref, cot_ring_send, cot_ring_recv, cot_sib_send, cot_sib_recv)
    ring.start(0)
    for copy in swaps:
        copy.wait()
    for copy in locals_:
        copy.wait()
    a_start, a_arrive, a_sent = z_line(
        z,
        z_size,
        [
            lambda k: rows_at(conv_w, k, 4 * rows_in),
            lambda k: rows_all.at[k],
        ],
        (a_us, a_ur, a_ds, a_dr),
    )
    m_start, m_arrive, m_sent = z_line(
        z, z_size, [lambda k: rows_at(mats, k, half)], (m_us, m_ur, m_ds, m_dr)
    )
    b_start, b_arrive, b_sent = z_line(
        z,
        z_size,
        [lambda k: rows_at(gate_all, k, 4 * rows_in), lambda k: rows_at(out_all, k, half)],
        (b_us, b_ur, b_ds, b_dr),
    )
    a_start(0)
    for copy in gates:
        copy.start()

    for copy in ids_copies:
        copy.wait()
    ids = jnp.concatenate([ids_all[s, 0:1, :] for s in range(8)], axis=0).astype(F32)
    before = pltpu.roll(ids, 1, 1)
    lane = lax.broadcasted_iota(jnp.int32, ids.shape, 1)
    same = jnp.where((ids == before) & (lane > 0), 1.0, 0.0)
    for t in range(length):
        keep[t] = jnp.broadcast_to(same[:, t : t + 1], (8, 128))
    keep_copy = pltpu.make_async_copy(keep, keep_hbm, local_sem.at[5])
    keep_copy.start()

    for k in range(max(hops, RING - 1)):
        if k < hops:
            a_arrive(k)
            if k + 1 < hops:
                a_start(k + 1)
            if k + 1 == hops - 1:
                m_start(0)
        if k < RING - 1:
            ring.arrive(k)
            ring.start(k + 1)
        if k == RING - 2:
            cot_ring.start(0)
    m_arrive(0)
    m_start(1)
    for copy in gates:
        copy.wait()
    b_start(0)
    for k in range(RING):
        ring.sent(k)
    outs = [
        pltpu.make_async_copy(normed_all, normed_hbm, local_sem.at[6]),
        pltpu.make_async_copy(conv_w, conv_hbm, local_sem.at[7]),
    ]
    for copy in outs:
        copy.start()
    for zz in range(z_size):
        params[:, zz * half : (zz + 1) * half] = rows_all[zz].astype(F32)

    def project(s, carry):
        proj[s] = dot_nn(normed_all[s], conv_w[...])
        return carry

    lax.fori_loop(0, 8, project, 0)
    for k in range(1, hops):
        m_arrive(k)
        if k + 1 < hops:
            m_start(k + 1)
    cot_ring.arrive(0)
    cot_ring.start(1)

    cin[0:3] = jnp.zeros((3, 8, chans), F32)
    block = 32
    fine = 4

    def turn(i, carry):
        t0 = pl.multiple_of(i * block, block)
        cin[pl.ds(3 + t0, block)] = jnp.swapaxes(proj[:, pl.ds(t0, block), :], 0, 1)
        return carry

    lax.fori_loop(0, length // block, turn, 0)

    def convolve(i, carry):
        t0 = i * fine
        for g in range(chans // 128):
            lanes = pl.ds(g * 128, 128)
            tap = [jnp.broadcast_to(params[taps - 1 - j : taps - j, lanes], (8, 128)) for j in range(taps)]
            offset = jnp.broadcast_to(params[taps : taps + 1, lanes], (8, 128))
            chosen = []
            for j in range(fine):
                t = t0 + j
                total = tap[3] * cin[t, :, lanes] * keep[jnp.maximum(t - 2, 0)]
                total = (total + tap[2] * cin[t + 1, :, lanes]) * keep[jnp.maximum(t - 1, 0)]
                total = (total + tap[1] * cin[t + 2, :, lanes]) * keep[t]
                v = total + tap[0] * cin[t + 3, :, lanes] + offset
                chosen.append((v * sigmoid(v)).astype(BF16))
                xs[t, :, lanes] = chosen[-1].astype(F32)
            rows = pl.ds(pl.multiple_of(t0 * 8, fine * 8), fine * 8)
            picked[rows, lanes] = jnp.concatenate(chosen, axis=0)
        return carry

    lax.fori_loop(0, length // fine, convolve, 0)
    outs += [
        pltpu.make_async_copy(mats, mats_hbm, local_sem.at[8]),
        pltpu.make_async_copy(cin.at[pl.ds(3, length)], cin_hbm, local_sem.at[9]),
        pltpu.make_async_copy(xs, x_hbm, local_sem.at[10]),
    ]
    for copy in outs[2:]:
        copy.start()

    wide = part.shape[3]

    def select(b, carry):
        rows = pl.ds(pl.multiple_of(b * length, length), length)
        part[b // 2, b % 2] = dot_nn(picked[rows, :], mats[:, :wide])
        return carry

    lax.fori_loop(0, 8, select, 0)
    first[...] = part[:, 1 - c].astype(BF16)
    swap = remote(first, from_sib, sw_s.at[0], sw_r.at[0], sibling)
    swap.start()
    swap.wait()
    mine = x * 2 + y
    chips = [((x + d // 2) % 2, (y + d % 2) % 2) for d in (1, 2, 3)]
    sends = []
    for k in (2, 1, 0):
        ox, oy = chips[k]
        j = ox * 2 + oy
        stage[k] = (part[j, c] + from_sib[j].astype(F32)).astype(BF16)
        copy = remote(stage.at[k], got.at[k], rs_s.at[k], rs_r.at[k], {"x": ox, "y": oy})
        copy.start()
        sends.append(copy)
    total = part[mine, c] + from_sib[mine].astype(F32)
    for copy in sends:
        copy.wait()
    for k in range(3):
        total = total + got[k].astype(F32)
    selection[mine, c] = total.astype(BF16)
    here = selection.at[mine, c]
    spreads = []
    for k in (2, 1, 0):
        ox, oy = chips[k]
        copy = remote(here, here, ag_s.at[k], ag_r.at[k], {"x": ox, "y": oy})
        copy.start()
        spreads.append((k, copy))
    forwards = [remote(here, here, fw_s.at[3], fw_r.at[3], sibling)]
    forwards[0].start()
    b_arrive(0)
    if hops > 2:
        b_start(1)
    cot_ring.arrive(1)
    for k, copy in reversed(spreads):
        copy.wait_recv()
        ox, oy = chips[k]
        there = selection.at[ox * 2 + oy, c]
        forwards.append(remote(there, there, fw_s.at[k], fw_r.at[k], sibling))
        forwards[-1].start()
    for _, copy in spreads:
        copy.wait_send()
    for copy in forwards:
        copy.wait()
    cot_ring.start(2)

    bias = params[taps + 1 : taps + 2, :]

    def steps(i, carry):
        rows = 64
        per = length // rows
        b = i // per
        at = pl.ds(pl.multiple_of((i % per) * rows, rows), rows)
        v = dot_nt(selection[b // 2, b % 2, at, :rank], mats[:, wide : wide + rank]) + bias
        t = pl.ds(i * (rows // 8), rows // 8)
        pres[t] = v.reshape(rows // 8, 8, chans)
        dts[t] = softplus(v).reshape(rows // 8, 8, chans)
        return carry

    lax.fori_loop(0, length * 8 // 64, steps, 0)
    outs += [
        pltpu.make_async_copy(dts, dt_hbm, local_sem.at[11]),
        pltpu.make_async_copy(pres, pre_hbm, local_sem.at[12]),
    ]
    for copy in outs[5:]:
        copy.start()

    for k in range(1, hops - 1):
        b_arrive(k)
        if k + 1 < hops - 1:
            b_start(k + 1)
    cot_ring.arrive(2)
    cot_ring.start(3)
    for k in range(RING):
        cot_ring.sent(k)
    for k in range(hops):
        a_sent(k)
        m_sent(k)
    for k in range(hops - 1):
        b_sent(k)
    for copy in outs + [keep_copy]:
        copy.wait()


def front(z_size, taps, rank, tokens, gain, ids, rows, cot, weight_in, out, select, step):
    length, width = tokens.shape
    shares = z_size * 4
    half = rows.shape[1]
    chans = half * z_size
    wide = select.shape[1] + -select.shape[1] % 128
    cuts = 1 if weight_in.ndim == 4 else z_size
    any_space = pl.BlockSpec(memory_space=pl.ANY)
    vmem = pl.BlockSpec(memory_space=pltpu.VMEM)
    dma = pltpu.SemaphoreType.DMA
    hops = z_size - 1
    shape = jax.ShapeDtypeStruct
    everyone = (8,) + tokens.shape
    per_token = (length, 8, chans)
    block = (length, wide)
    return pl.pallas_call(
        functools.partial(front_kernel, z_size, taps, rank),
        in_specs=[vmem] * 5 + [any_space] + [vmem] * 3,
        out_specs=[any_space] * 11 + [vmem] * 3,
        out_shape=[
            shape(everyone, BF16),
            shape(everyone, BF16),
            shape((width, chans), BF16),
            shape((width, chans), BF16),
            shape((chans, width), BF16),
            shape((chans, wide + rank), BF16),
            shape((length, 8, 128), F32),
            shape(per_token, F32),
            shape(per_token, F32),
            shape(per_token, F32),
            shape(per_token, F32),
            shape((rows.shape[0], chans), F32),
            shape((gain.shape[0], width), F32),
            shape((4, 2) + block, BF16),
        ],
        scratch_shapes=[
            pltpu.VMEM(everyone, BF16),
            pltpu.VMEM((width, chans), BF16),
            pltpu.VMEM((chans, wide + rank), BF16),
            pltpu.VMEM((z_size,) + rows.shape, BF16),
            pltpu.VMEM((shares,) + gain.shape, F32),
            pltpu.VMEM((8,) + ids.shape, ids.dtype),
            pltpu.VMEM((8, length, chans), F32),
            pltpu.VMEM((length + 3, 8, chans), F32),
            pltpu.VMEM(per_token, F32),
            pltpu.VMEM((length * 8, chans), BF16),
            pltpu.VMEM((4, 2) + block, F32),
            pltpu.VMEM(per_token, F32),
            pltpu.VMEM(per_token, F32),
            pltpu.VMEM((length, 8, 128), F32),
            pltpu.VMEM((4,) + block, BF16),
            pltpu.VMEM((4,) + block, BF16),
            pltpu.VMEM((3,) + block, BF16),
            pltpu.VMEM((3,) + block, BF16),
            dma((13,)),
            dma((2, cuts)),
            dma((shares - 1,)),
            dma((shares - 1,)),
            dma((7,)),
            dma((7,)),
        ]
        + [dma((3, cuts))] * 4
        + [dma((RING - 1, 2)), dma((RING - 1, 2)), dma((RING,)), dma((RING,))] * 2
        + [dma((hops, 2))] * 4
        + [dma((hops, 1))] * 4
        + [dma((hops, 2))] * 4
        + [dma((1,))] * 2
        + [dma((3,))] * 4
        + [dma((4,))] * 2,
        cost_estimate=busy(120),
        compiler_params=pltpu.CompilerParams(
            collective_id=0, has_side_effects=True, vmem_limit_bytes=60 << 20
        ),
    )(tokens, gain, ids, rows, cot, weight_in, out, select, step)


def add_rows(dst, srcs, rows):
    count = dst.shape[0] // rows

    def body(i, carry):
        at = pl.ds(pl.multiple_of(i * rows, rows), rows)
        total = srcs[0][at].astype(F32)
        for src in srcs[1:]:
            total = total + src[at].astype(F32)
        dst[at] = total.astype(dst.dtype)
        return carry

    lax.fori_loop(0, count, body, 0)


def forward_kernel(
    z_size,
    chunks,
    states,
    rank,
    skip_row,
    dt_ref,
    x_ref,
    sel_ref,
    keep_ref,
    rate_ref,
    normed_ref,
    cot_ref,
    normed_col,
    cot_col,
    params_ref,
    gate_given,
    out_given,
    hist_ref,
    last_ref,
    ds_ref,
    bgi_ref,
    part_ref,
    gout_ref,
    ggate_ref,
    gate_all,
    out_all,
    h_ref,
    bc_ref,
    y_ref,
    ys_ref,
    gate_ref,
    bg_ref,
    gated_ref,
    gated_all,
    bgi_all,
    gate_w_ref,
    out_w_ref,
    load_sem,
    up_s,
    up_r,
    down_s,
    down_r,
):
    step = pl.program_id(0)
    me = place()
    z = me["z"]
    hops = z_size - 1
    slab_rows = gate_all.shape[0] // z_size
    half = out_all.shape[0] // z_size
    line_start, line_arrive, line_sent = z_line(
        z,
        z_size,
        [
            lambda k: gate_all.at[pl.ds(pl.multiple_of(k * slab_rows, slab_rows), slab_rows)],
            lambda k: out_all.at[pl.ds(pl.multiple_of(k * half, half), half)],
        ],
        (up_s, up_r, down_s, down_r),
    )

    @pl.when(step == 0)
    def _():
        greet([{"z": (z + 1) % z_size}, {"z": (z + z_size - 1) % z_size}])
        line_start(hops - 1)
        h_ref[...] = jnp.zeros_like(h_ref)

    steps, seqs, width = dt_ref.shape
    groups = width // 128
    rows = steps * seqs
    @pl.when(step < chunks)
    def _():
        bc_ref[...] = sel_ref[:, rank:].astype(F32).reshape(bc_ref.shape)

        def body(tb, carry):
            t0 = tb * INNER
            bc = [bc_ref[t0 + i] for i in range(INNER)]
            off = [(1.0 - keep_ref[t0 + i]) * BIG for i in range(INNER)]
            for g in range(groups):
                lanes = pl.ds(g * 128, 128)
                dt = [dt_ref[t0 + i, :, lanes] for i in range(INNER)]
                dtm = [dt[i] + off[i] for i in range(INNER)]
                u = [dt[i] * x_ref[t0 + i, :, lanes] for i in range(INNER)]
                y = [None] * INNER
                for n in range(states):
                    h = h_ref[n, :, lanes]
                    rate = rate_ref[n, :, lanes]
                    before = []
                    for i in range(INNER):
                        before.append(h)
                        a = jnp.exp2(dtm[i] * rate)
                        h = a * h + u[i] * bc[i][:, n : n + 1]
                        term = h * bc[i][:, states + n : states + n + 1]
                        y[i] = term if y[i] is None else y[i] + term
                    for i in range(0, INNER, 2):
                        pair = jnp.concatenate(before[i : i + 2], axis=0).astype(BF16)
                        hist_ref[t0 // 2 + i // 2, n, :, lanes] = pair
                    h_ref[n, :, lanes] = h
                skip = params_ref[skip_row : skip_row + 1, lanes]
                for i in range(INNER):
                    y_ref[step * steps + t0 + i, :, lanes] = y[i] + skip * x_ref[t0 + i, :, lanes]
            return carry

        lax.fori_loop(0, steps // INNER, body, 0)
        last_ref[...] = h_ref[...]

    @pl.when(step == chunks)
    def _():
        line_arrive(hops - 1)
        line_sent(hops - 1)
        loads = [
            pltpu.make_async_copy(gate_all, gate_w_ref, load_sem.at[0]),
            pltpu.make_async_copy(out_all, out_w_ref, load_sem.at[1]),
        ]
        for copy in loads:
            copy.start()
        for copy in loads:
            copy.wait()

    @pl.when((step >= chunks) & (step < 2 * chunks))
    def _():
        normed = normed_ref[...].reshape(rows, normed_ref.shape[2])
        cot = cot_ref[...].reshape(rows, cot_ref.shape[2])
        gate_ref[...] = dot_nn(normed, gate_w_ref[...])
        bg_ref[...] = dot_nt(cot, out_w_ref[...]).astype(BF16).astype(F32)
        y = y_ref[pl.ds((step - chunks) * steps, steps)]
        ys_ref[...] = jnp.swapaxes(y, 0, 1).reshape(rows, width)
        fine = 16

        def gating(i, carry):
            r = pl.ds(pl.multiple_of(i * fine, fine), fine)
            v = gate_ref[r, :]
            bg = bg_ref[r, :]
            y = ys_ref[r, :]
            s = sigmoid(v)
            gate = v * s
            gated_ref[r, :] = (y * gate).astype(BF16)
            bg_ref[r, :] = bg * gate
            gate_ref[r, :] = bg * y * (s + gate * (1.0 - s))
            return carry

        lax.fori_loop(0, rows // fine, gating, 0)
        ds_ref[...] = jnp.swapaxes(bg_ref[...].reshape(seqs, steps, width), 0, 1)
        bgi = gate_ref[...].astype(BF16).reshape(bgi_ref.shape)
        bgi_ref[...] = bgi
        gated = gated_ref[...]
        part_ref[...] = dot_nn(gated, out_w_ref[...]).astype(BF16).reshape(part_ref.shape)
        at = pl.ds(pl.multiple_of((step - chunks) * steps, steps), steps)
        gated_all[:, at, :] = gated.reshape(bgi_ref.shape)
        bgi_all[:, at, :] = bgi

    @pl.when(step >= 2 * chunks)
    def _():
        tall = (gated_all.shape[0] * gated_all.shape[1], width)
        cols = (tall[0], normed_col.shape[2])
        gout_ref[...] = dot_tn(gated_all[...].reshape(tall), cot_col[...].reshape(cols)).astype(BF16)
        ggate_ref[...] = dot_tn(normed_col[...].reshape(cols), bgi_all[...].reshape(tall)).astype(BF16)


def scan_forward(z_size, rank, skip_row, dt, x, selection, keep, rate, normed, cot, gate_w, out_w, params):
    length, seqs, width = dt.shape
    model = normed.shape[2]
    states = rate.shape[0]
    wide = selection.shape[1]
    chunks = length // STEPS
    early = lambda i: jnp.minimum(i, chunks - 1)
    late = lambda i: jnp.clip(i - chunks, 0, chunks - 1)
    pieces = model // COLUMNS
    last_of = lambda i: jnp.maximum(i - 2 * chunks, 0)
    column = pl.BlockSpec((seqs, length, COLUMNS), lambda i: (0, 0, last_of(i)))
    block = lambda *tail: pl.BlockSpec((STEPS,) + tail, lambda i: (early(i),) + (0,) * len(tail))
    across = lambda n: pl.BlockSpec((seqs, STEPS, n), lambda i: (0, late(i), 0))
    any_space = pl.BlockSpec(memory_space=pl.ANY)
    dma = pltpu.SemaphoreType.DMA
    hops = z_size - 1
    whole = lambda *dims: pl.BlockSpec(dims, lambda i: (0,) * len(dims))
    rows = STEPS * seqs
    shape = jax.ShapeDtypeStruct
    return pl.pallas_call(
        functools.partial(forward_kernel, z_size, chunks, states, rank, skip_row),
        grid=(2 * chunks + pieces,),
        in_specs=[
            block(seqs, width),
            block(seqs, width),
            pl.BlockSpec((rows, wide), lambda i: (early(i), 0)),
            block(seqs, 128),
            whole(states, seqs, width),
            across(model),
            across(model),
            column,
            column,
            whole(*params.shape),
            any_space,
            any_space,
        ],
        out_specs=[
            pl.BlockSpec((STEPS // 2, states, 2 * seqs, width), lambda i: (early(i), 0, 0, 0)),
            whole(states, seqs, width),
            pl.BlockSpec((STEPS, seqs, width), lambda i: (late(i), 0, 0)),
            across(width),
            across(model),
            pl.BlockSpec((width, COLUMNS), lambda i: (0, last_of(i))),
            pl.BlockSpec((COLUMNS, width), lambda i: (last_of(i), 0)),
            any_space,
            any_space,
        ],
        out_shape=[
            shape((length // 2, states, 2 * seqs, width), BF16),
            shape((states, seqs, width), F32),
            shape(dt.shape, F32),
            shape((seqs, length, width), BF16),
            shape((seqs, length, model), BF16),
            shape((width, model), BF16),
            shape((model, width), BF16),
            shape(gate_w.shape, BF16),
            shape(out_w.shape, BF16),
        ],
        input_output_aliases={10: 7, 11: 8},
        scratch_shapes=[
            pltpu.VMEM((states, seqs, width), F32),
            pltpu.VMEM((STEPS, seqs, wide - rank), F32),
            pltpu.VMEM((length, seqs, width), F32),
            pltpu.VMEM((rows, width), F32),
            pltpu.VMEM((rows, width), F32),
            pltpu.VMEM((rows, width), F32),
            pltpu.VMEM((rows, width), BF16),
            pltpu.VMEM((seqs, length, width), BF16),
            pltpu.VMEM((seqs, length, width), BF16),
            pltpu.VMEM(gate_w.shape, BF16),
            pltpu.VMEM(out_w.shape, BF16),
            dma((2,)),
        ]
        + [dma((hops, 2))] * 4,
        cost_estimate=busy(60),
        compiler_params=pltpu.CompilerParams(
            collective_id=5, has_side_effects=True, vmem_limit_bytes=60 << 20
        ),
    )(dt, x, selection, keep, rate, normed, cot, normed, cot, params, gate_w, out_w)


def z_sums(z, z_size, owns, ups, downs, sems, blocks):
    up_s, up_r, down_s, down_r = sems

    def up_copy(k, j, own):
        src = owns[j].at[z_size - 1 - k] if own else ups[j].at[k]
        return remote(src, ups[j].at[k], up_s.at[k, j], up_r.at[k, j], {"z": z + 1})

    def down_copy(k, j, own):
        src = owns[j].at[k] if own else downs[j].at[k]
        return remote(src, downs[j].at[k], down_s.at[k, j], down_r.at[k, j], {"z": z - 1})

    def line(tau, j):
        k = tau - z
        high = z_size - 1 - k

        @pl.when((k >= 0) & (z < high) & (z > 0))
        def _():
            up_copy(k, j, False).wait_recv()
            add_rows(ups[j].at[k], [owns[j].at[high], ups[j].at[k]], blocks[j])
            up_copy(k, j, False).start()

        @pl.when((k >= 0) & (z < high) & (z == 0))
        def _():
            up_copy(k, j, True).start()

        m = tau - (z_size - 1 - z)

        @pl.when((m >= 0) & (z > m) & (z < z_size - 1))
        def _():
            down_copy(m, j, False).wait_recv()
            add_rows(downs[j].at[m], [owns[j].at[m], downs[j].at[m]], blocks[j])
            down_copy(m, j, False).start()

        @pl.when((m >= 0) & (z > m) & (z == z_size - 1))
        def _():
            down_copy(m, j, True).start()

    def settle(j, dst):
        low = z
        high = z_size - 1 - z

        @pl.when(z == 0)
        def _():
            down_copy(low, j, False).wait_recv()
            add_rows(dst, [owns[j].at[z], downs[j].at[low]], blocks[j])

        @pl.when(z == z_size - 1)
        def _():
            up_copy(high, j, False).wait_recv()
            add_rows(dst, [owns[j].at[z], ups[j].at[high]], blocks[j])

        @pl.when((z > 0) & (z < z_size - 1))
        def _():
            down_copy(low, j, False).wait_recv()
            up_copy(high, j, False).wait_recv()
            add_rows(dst, [owns[j].at[z], downs[j].at[low], ups[j].at[high]], blocks[j])

    def sent(j):
        for k in range(z_size - 1):

            @pl.when(z < z_size - 1 - k)
            def _():
                up_copy(k, j, False).wait_send()

            @pl.when(z > k)
            def _():
                down_copy(k, j, False).wait_send()

    return line, settle, sent


def backward_kernel(
    chunks_all,
    z_size,
    states,
    rank,
    skip_row,
    dt_ref,
    x_ref,
    ds_ref,
    pre_ref,
    sel_ref,
    keep_ref,
    rate_ref,
    hist_ref,
    last_ref,
    ones_ref,
    params_ref,
    step_w_ref,
    gate_hbm,
    out_hbm,
    bx_ref,
    part_ref,
    da_ref,
    gstep_ref,
    bias_ref,
    skip_ref,
    gate_fin,
    out_fin,
    ag_ref,
    h_ref,
    p_ref,
    bc_ref,
    bp_ref,
    gate_own,
    out_own,
    gate_up,
    out_up,
    gate_down,
    out_down,
    local_sem,
    up_s,
    up_r,
    down_s,
    down_r,
):
    chunk = pl.program_id(0)
    chunks = pl.num_programs(0)
    me = place()
    z = me["z"]
    hops = z_size - 1
    line, settle, sent = z_sums(
        z,
        z_size,
        (gate_own, out_own),
        (gate_up, out_up),
        (gate_down, out_down),
        (up_s, up_r, down_s, down_r),
        (64, 16),
    )

    @pl.when(chunk == 0)
    def _():
        greet([{"z": (z + 1) % z_size}, {"z": (z + z_size - 1) % z_size}])
        early = pl.ds(0, out_own.shape[2])
        loads = [
            pltpu.make_async_copy(gate_hbm, gate_own, local_sem.at[0]),
            pltpu.make_async_copy(out_hbm.at[:, :, early], out_own, local_sem.at[1]),
        ]
        for copy in loads:
            copy.start()
        ag_ref[...] = jnp.zeros_like(ag_ref)
        da_ref[...] = jnp.zeros_like(da_ref)
        gstep_ref[...] = jnp.zeros_like(gstep_ref)
        bias_ref[...] = jnp.zeros_like(bias_ref)
        skip_ref[...] = jnp.zeros_like(skip_ref)
        h_ref[...] = last_ref[...]
        for copy in loads:
            copy.wait()

    for tau in range(hops):

        @pl.when(chunk == -(-tau * (chunks_all - 1) // hops))
        def _():
            line(tau, 0)
            line(tau, 1)

    steps, seqs, width = dt_ref.shape
    groups = width // 128
    blocks = steps // BACK_INNER
    bc_ref[...] = sel_ref[:, rank:].astype(F32).reshape(bc_ref.shape)

    inner = BACK_INNER

    def body(back, carry):
        t0 = (blocks - 1 - back) * inner
        rows = pl.ds(pl.multiple_of(t0 * seqs, inner * seqs), inner * seqs)
        bc = [bc_ref[t0 + i] for i in range(inner)]
        off = [(1.0 - keep_ref[t0 + i]) * BIG for i in range(inner)]
        for g0 in range(0, groups, TOGETHER):
            lanes = [pl.ds((g0 + q) * 128, 128) for q in range(TOGETHER)]
            each = [(q, i) for q in range(TOGETHER) for i in range(inner)]
            dt = {(q, i): dt_ref[t0 + i, :, lanes[q]] for q, i in each}
            dtm = {(q, i): dt[q, i] + off[i] for q, i in each}
            ds = {(q, i): ds_ref[t0 + i, :, lanes[q]] for q, i in each}
            u = {(q, i): dt[q, i] * x_ref[t0 + i, :, lanes[q]] for q, i in each}
            s1 = {}
            s2 = {}
            for n in range(states):
                pb = [None] * inner
                pc = [None] * inner
                for q in range(TOGETHER):
                    ag = ag_ref[n, :, lanes[q]]
                    h = h_ref[n, :, lanes[q]]
                    rate = rate_ref[n, :, lanes[q]]
                    da = da_ref[n, :, lanes[q]]
                    before = []
                    for i in range(0, inner, 2):
                        pair = hist_ref[t0 // 2 + i // 2, n, :, lanes[q]].astype(F32)
                        before += [pair[:seqs], pair[seqs:]]
                    for i in reversed(range(inner)):
                        prev = before[i]
                        a = jnp.exp2(dtm[q, i] * rate)
                        adj = ds[q, i] * bc[i][:, states + n : states + n + 1] + ag
                        c_term = ds[q, i] * h
                        b_term = adj * u[q, i]
                        pc[i] = c_term if q == 0 else pc[i] + c_term
                        pb[i] = b_term if q == 0 else pb[i] + b_term
                        ag = a * adj
                        w = ag * prev
                        rw = rate * w
                        gb = adj * bc[i][:, n : n + 1]
                        s1[q, i] = rw if n == 0 else s1[q, i] + rw
                        s2[q, i] = gb if n == 0 else s2[q, i] + gb
                        da = da + dt[q, i] * w
                        h = prev
                    ag_ref[n, :, lanes[q]] = ag
                    h_ref[n, :, lanes[q]] = h
                    da_ref[n, :, lanes[q]] = da
                cols = pl.ds(n * 128, 128)
                p_ref[0, g0 // TOGETHER, rows, cols] = jnp.concatenate(pb, axis=0).astype(BF16)
                p_ref[1, g0 // TOGETHER, rows, cols] = jnp.concatenate(pc, axis=0).astype(BF16)
            for q in range(TOGETHER):
                skip = params_ref[skip_row : skip_row + 1, lanes[q]]
                bias = bias_ref[:, lanes[q]]
                direct = skip_ref[:, lanes[q]]
                low = []
                for i in range(inner):
                    x = x_ref[t0 + i, :, lanes[q]]
                    bx_ref[t0 + i, :, lanes[q]] = dt[q, i] * s2[q, i] + skip * ds[q, i]
                    back_step = s1[q, i] * (1.0 / LOG2E) + x * s2[q, i]
                    back_pre = back_step / (1.0 + jnp.exp(-pre_ref[t0 + i, :, lanes[q]]))
                    low.append(back_pre)
                    bias = bias + back_pre
                    direct = direct + ds[q, i] * x
                bias_ref[:, lanes[q]] = bias
                skip_ref[:, lanes[q]] = direct
                bp_ref[rows, lanes[q]] = jnp.concatenate(low, axis=0).astype(BF16)
        return carry

    lax.fori_loop(0, blocks, body, 0)
    span = states * 128
    sets = groups // TOGETHER
    folded = dot_nn(p_ref[...].reshape(2 * sets * steps * seqs, span), ones_ref[...])
    folded = folded.reshape(2, sets, steps * seqs, 128)
    in_sum = folded[0, 0]
    out_sum = folded[1, 0]
    for g in range(1, sets):
        in_sum = in_sum + folded[0, g]
        out_sum = out_sum + folded[1, g]
    part_ref[:, rank:] = (in_sum + pltpu.roll(out_sum, states, 1)).astype(BF16)
    part_ref[:, :rank] = dot_nn(bp_ref[...], step_w_ref[...]).astype(BF16)
    gstep_ref[...] += dot_tn(bp_ref[...], sel_ref[:, :rank])

    @pl.when(chunk == chunks - 1)
    def _():
        settle(0, gate_fin)
        settle(1, out_fin)
        sent(0)
        sent(1)


def scan_backward(
    z_size, rank, skip_row, dt, x, ds, pre, selection, keep, rate, hist, last, params, step_w, gate, out
):
    length, seqs, width = dt.shape
    states = rate.shape[0]
    chunks = length // STEPS
    wide = selection.shape[1]
    rows = STEPS * seqs
    block = lambda *tail: pl.BlockSpec((STEPS,) + tail, lambda i: (chunks - 1 - i,) + (0,) * len(tail))
    flat = lambda n: pl.BlockSpec((rows, n), lambda i: (chunks - 1 - i, 0))
    whole = lambda *dims: pl.BlockSpec(dims, lambda i: (0,) * len(dims))
    any_space = pl.BlockSpec(memory_space=pl.ANY)
    span = states * 128
    ones = jnp.asarray((np.arange(span)[:, None] // 128 == np.arange(128)[None, :]).astype(np.float32), BF16)
    hops = z_size - 1
    gate_shape = gate.shape[1:]
    out_shape = (out.shape[1], out.shape[2] // 2)
    shape = jax.ShapeDtypeStruct
    dma = pltpu.SemaphoreType.DMA
    return pl.pallas_call(
        functools.partial(backward_kernel, chunks, z_size, states, rank, skip_row),
        grid=(chunks,),
        in_specs=[
            block(seqs, width),
            block(seqs, width),
            block(seqs, width),
            block(seqs, width),
            flat(wide),
            block(seqs, 128),
            whole(states, seqs, width),
            pl.BlockSpec((STEPS // 2, states, 2 * seqs, width), lambda i: (chunks - 1 - i, 0, 0, 0)),
            whole(states, seqs, width),
            whole(span, 128),
            whole(*params.shape),
            pl.BlockSpec((width, rank), lambda i: (0, wide // rank)),
            any_space,
            any_space,
        ],
        out_specs=[
            block(seqs, width),
            flat(wide),
            whole(states, seqs, width),
            whole(width, rank),
            whole(seqs, width),
            whole(seqs, width),
            whole(*gate_shape),
            whole(*out_shape),
        ],
        out_shape=[
            shape(dt.shape, F32),
            shape((length * seqs, wide), BF16),
            shape((states, seqs, width), F32),
            shape((width, rank), F32),
            shape((seqs, width), F32),
            shape((seqs, width), F32),
            shape(gate_shape, BF16),
            shape(out_shape, BF16),
        ],
        scratch_shapes=[
            pltpu.VMEM((states, seqs, width), F32),
            pltpu.VMEM((states, seqs, width), F32),
            pltpu.VMEM((2, width // 128 // TOGETHER, rows, span), BF16),
            pltpu.VMEM((STEPS, seqs, wide - rank), F32),
            pltpu.VMEM((rows, width), BF16),
            pltpu.VMEM(gate.shape, BF16),
            pltpu.VMEM(out.shape[:1] + out_shape, BF16),
            pltpu.VMEM((hops,) + gate_shape, BF16),
            pltpu.VMEM((hops,) + out_shape, BF16),
            pltpu.VMEM((hops,) + gate_shape, BF16),
            pltpu.VMEM((hops,) + out_shape, BF16),
            dma((2,)),
            dma((hops, 2)),
            dma((hops, 2)),
            dma((hops, 2)),
            dma((hops, 2)),
        ],
        cost_estimate=busy(80),
        compiler_params=pltpu.CompilerParams(
            collective_id=4, has_side_effects=True, vmem_limit_bytes=62 << 20
        ),
    )(dt, x, ds, pre, selection, keep, rate, hist, last, ones, params, step_w, gate, out)


def last_kernel(
    z_size,
    taps,
    part_ref,
    keep_ref,
    mats_ref,
    params_ref,
    gate_fin,
    out_fin,
    da_ref,
    gstep_ref,
    bias_ref,
    skip_ref,
    tokens_ref,
    cot_ref,
    gain_ref,
    bx_hbm,
    cin_hbm,
    normed_hbm,
    conv_hbm,
    gate_hbm,
    bgi_hbm,
    gout_hbm,
    tgrad_ref,
    in_ref,
    out_ref,
    small_out,
    vec_out,
    gain_out,
    chosen,
    from_sib,
    stage,
    got,
    bx,
    cin,
    picked,
    conv_w,
    gate_w,
    bgi,
    turned,
    bci,
    gsel,
    sums,
    columns,
    own_back,
    sib_stage,
    sib_back,
    ring_got,
    own_small,
    own_vec,
    own_conv,
    up_small,
    up_vec,
    up_conv,
    down_small,
    down_vec,
    down_conv,
    own_out,
    up_out,
    down_out,
    fin_conv,
    both_gate,
    both_conv,
    gain_parts,
    gain_got,
    gain_half,
    gain_pair,
    local_sem,
    column_sem,
    sw_s,
    sw_r,
    rs_s,
    rs_r,
    ag_s,
    ag_r,
    fw_s,
    fw_r,
    sib_send,
    sib_recv,
    ring_send,
    ring_recv,
    up_send,
    up_recv,
    down_send,
    down_recv,
    out_us,
    out_ur,
    out_ds,
    out_dr,
    swap_send,
    swap_recv,
    x_send,
    x_recv,
    gain_send,
    gain_recv,
):
    me = place()
    x, y, z, c = me["x"], me["y"], me["z"], me["c"]
    shares = z_size * 4
    share = z * 4 + y * 2 + c
    corner = y * 2 + c
    sibling = {"c": 1 - c}
    over_x = {"x": 1 - x}
    length, width = tokens_ref.shape
    chans = bx.shape[2]
    rows_in = in_ref.shape[0]
    half = own_out.shape[1]
    hops = z_size - 1
    wide = part_ref.shape[3]
    out_line, out_settle, out_sent = z_sums(
        z, z_size, (own_out,), (up_out,), (down_out,), (out_us, out_ur, out_ds, out_dr), (16,)
    )
    greet(plane_others(me) + z_only(me, shares))

    loads = [
        pltpu.make_async_copy(src, dst, local_sem.at[i])
        for i, (src, dst) in enumerate(
            [
                (cin_hbm, cin.at[pl.ds(3, length)]),
                (bx_hbm, bx.at[pl.ds(0, length)]),
                (bgi_hbm, bgi),
                (conv_hbm, conv_w),
                (gate_hbm, gate_w),
            ]
        )
    ]
    later = pl.ds(own_out.shape[2], own_out.shape[2])
    out_load = pltpu.make_async_copy(gout_hbm.at[:, :, later], own_out, local_sem.at[6])
    out_load.start()

    swap = remote(part_ref.at[:, 1 - c], from_sib, sw_s.at[0], sw_r.at[0], sibling)
    swap.start()
    for copy in loads:
        copy.start()
    out_load.wait()
    out_line(0, 0)
    cin[0:3] = jnp.zeros((3, 8, chans), F32)
    bx[length : length + 3] = jnp.zeros((3, 8, chans), F32)
    sums[...] = jnp.zeros_like(sums)
    gsel[...] = jnp.zeros_like(gsel)
    swap.wait()
    mine = x * 2 + y
    chips = [((x + d // 2) % 2, (y + d % 2) % 2) for d in (1, 2, 3)]
    sends = []
    for k in (2, 1, 0):
        ox, oy = chips[k]
        j = ox * 2 + oy
        stage[k] = (part_ref[j, c].astype(F32) + from_sib[j].astype(F32)).astype(BF16)
        copy = remote(stage.at[k], got.at[k], rs_s.at[k], rs_r.at[k], {"x": ox, "y": oy})
        copy.start()
        sends.append(copy)
    total = part_ref[mine, c].astype(F32) + from_sib[mine].astype(F32)
    if hops > 1:
        out_line(1, 0)
    for copy in sends:
        copy.wait()
    for k in range(3):
        total = total + got[k].astype(F32)
    chosen[mine, c] = total.astype(BF16)
    here = chosen.at[mine, c]
    spreads = []
    for k in (2, 1, 0):
        ox, oy = chips[k]
        copy = remote(here, here, ag_s.at[k], ag_r.at[k], {"x": ox, "y": oy})
        copy.start()
        spreads.append((k, copy))
    forwards = [remote(here, here, fw_s.at[3], fw_r.at[3], sibling)]
    forwards[0].start()

    def corner_sends(src, dst, index):
        out = []
        for e in range(1, 8):
            to = (corner + e % 4) % 4
            out.append(
                remote(
                    src.at[pl.ds(pl.multiple_of(to * rows_in, rows_in), rows_in)],
                    dst.at[x, corner],
                    swap_send.at[index, e - 1],
                    swap_recv.at[index, e - 1],
                    {"x": (x + e // 4) % 2, "y": to // 2, "c": to % 2},
                )
            )
        return out

    gate_swaps = corner_sends(gate_fin, both_gate, 0)
    conv_swaps = corner_sends(fin_conv, both_conv, 1)
    both_gate[x, corner] = gate_fin[pl.ds(pl.multiple_of(corner * rows_in, rows_in), rows_in)]
    out_ref[x, :, : own_out.shape[2]] = out_fin[...]
    out_x = remote(out_ref.at[x], out_ref.at[x], x_send.at[0], x_recv.at[0], over_x)
    for k, copy in reversed(spreads):
        copy.wait_recv()
        ox, oy = chips[k]
        there = chosen.at[ox * 2 + oy, c]
        forwards.append(remote(there, there, fw_s.at[k], fw_r.at[k], sibling))
        forwards[-1].start()
    for copy in loads:
        copy.wait()
    for _, copy in spreads:
        copy.wait_send()
    for copy in forwards:
        copy.wait()
    for copy in gate_swaps:
        copy.start()
    for tau in range(2, hops):
        out_line(tau, 0)

    fine = 4
    block = length // 8

    def taps_of(lanes):
        return [
            jnp.broadcast_to(params_ref[taps - 1 - j : taps - j, lanes], (8, 128)) for j in range(taps)
        ]

    def select(b, carry):
        back = chosen[b // 2, b % 2]
        t0 = b * block
        bx[pl.ds(t0, block)] += dot_nt(back, mats_ref[:, :wide]).reshape(block, 8, chans)
        def convolve(i, carry):
            for g in range(chans // 128):
                lanes = pl.ds(g * 128, 128)
                tap = taps_of(lanes)
                offset = jnp.broadcast_to(params_ref[taps : taps + 1, lanes], (8, 128))
                acc = [sums[r, :, lanes] for r in range(taps + 1)]
                taken = []
                for j in range(fine):
                    t = t0 + i * fine + j
                    k0 = keep_ref[t]
                    k1 = k0 * keep_ref[jnp.maximum(t - 1, 0)]
                    k2 = k1 * keep_ref[jnp.maximum(t - 2, 0)]
                    v0 = cin[t + 3, :, lanes]
                    v1 = cin[t + 2, :, lanes] * k0
                    v2 = cin[t + 1, :, lanes] * k1
                    v3 = cin[t, :, lanes] * k2
                    v = offset + tap[0] * v0 + tap[1] * v1 + tap[2] * v2 + tap[3] * v3
                    s = sigmoid(v)
                    silu = v * s
                    taken.append(silu)
                    back = bx[t, :, lanes] * (s + silu * (1.0 - s))
                    bx[t, :, lanes] = back
                    acc[0] = acc[0] + back * v0
                    acc[1] = acc[1] + back * v1
                    acc[2] = acc[2] + back * v2
                    acc[3] = acc[3] + back * v3
                    acc[4] = acc[4] + back
                for r in range(taps + 1):
                    sums[r, :, lanes] = acc[r]
                rows = pl.ds(pl.multiple_of(i * fine * 8, fine * 8), fine * 8)
                picked[rows, lanes] = jnp.concatenate(taken, axis=0).astype(BF16)
            return carry

        lax.fori_loop(0, block // fine, convolve, 0)
        gsel[...] += dot_tn(picked[...], back)
        return carry

    lax.fori_loop(0, 8, select, 0)

    def unfold(b, carry):
        t0 = b * block

        def convolve(i, carry):
            for g in range(chans // 128):
                lanes = pl.ds(g * 128, 128)
                tap = taps_of(lanes)
                for j in range(fine):
                    t = t0 + i * fine + j
                    total = tap[3] * bx[t + 3, :, lanes] * keep_ref[jnp.minimum(t + 3, length - 1)]
                    total = (total + tap[2] * bx[t + 2, :, lanes]) * keep_ref[
                        jnp.minimum(t + 2, length - 1)
                    ]
                    total = (total + tap[1] * bx[t + 1, :, lanes]) * keep_ref[
                        jnp.minimum(t + 1, length - 1)
                    ]
                    turned[i * fine + j, :, lanes] = total + tap[0] * bx[t, :, lanes]
            return carry

        lax.fori_loop(0, block // fine, convolve, 0)
        bci[:, pl.ds(pl.multiple_of(t0, block), block), :] = jnp.swapaxes(turned[...], 0, 1).astype(BF16)
        return carry

    def column(i, slot):
        zz = jnp.where(z * 2 < z_size, z_size - 1 - i, i)
        cols = pl.ds(pl.multiple_of(zz * 4 * rows_in, 4 * rows_in), 4 * rows_in)
        return zz, pltpu.make_async_copy(normed_hbm.at[:, :, cols], columns.at[slot], column_sem.at[slot])

    column(0, 0)[1].start()
    out_settle(0, out_ref.at[x, :, later])
    out_x.start()
    lax.fori_loop(0, 8, unfold, 0)

    owns = (own_small, own_vec, own_conv)
    line, settle, sent = z_sums(
        z,
        z_size,
        owns,
        (up_small, up_vec, up_conv),
        (down_small, down_vec, down_conv),
        (up_send, up_recv, down_send, down_recv),
        (16, 16, 64),
    )

    rates = -jnp.exp(params_ref[taps + 3 : taps + 3 + da_ref.shape[0], :])
    vectors = (
        [jnp.sum(sums[taps - 1 - r], axis=0, keepdims=True) for r in range(taps)]
        + [
            jnp.sum(sums[taps], axis=0, keepdims=True),
            jnp.sum(bias_ref[...], axis=0, keepdims=True),
            jnp.sum(skip_ref[...], axis=0, keepdims=True),
        ]
        + [jnp.sum(da_ref[...], axis=1) * rates]
    )
    used = taps + 3 + da_ref.shape[0]
    vectors = jnp.concatenate(
        vectors + [jnp.zeros((own_vec.shape[1] - used, chans), F32)], axis=0
    ).astype(BF16)
    for zz in range(z_size):
        own_vec[zz] = vectors[:, zz * half : (zz + 1) * half]
        own_small[zz, :, :wide] = gsel[zz * half : (zz + 1) * half, :].astype(BF16)
        own_small[zz, :, wide:] = gstep_ref[zz * half : (zz + 1) * half, :].astype(BF16)

    at = ring_at(x, y)
    step = 1 + 2 * c
    sib_step = 3 - 2 * c
    nx, ny = ring_chip((at + step) % RING)
    following = {"x": nx, "y": ny}

    def grad_column(i):
        slot = i % 2
        zz, copy = column(i, slot)
        copy.wait()
        if i + 1 < z_size:
            column(i + 1, 1 - slot)[1].start()
        tall = columns[slot].reshape(8 * length, 4 * rows_in)
        own_conv[zz] = dot_tn(tall, bci[...].reshape(8 * length, chans)).astype(BF16)

    def back_block(dst, p, core):
        cx, cy = ring_chip(p % RING)
        s = cx * 4 + cy * 2 + core

        def cols(i, carry):
            n = pl.ds(pl.multiple_of(i * 512, 512), 512)
            total = dot_nt(bci[s], conv_w[n, :]) + dot_nt(bgi[s], gate_w[n, :])
            dst[:, n] = total.astype(BF16)
            return carry

        lax.fori_loop(0, width // 512, cols, 0)

    def cross(k):
        slot = k % 2
        return remote(sib_stage.at[slot], sib_back.at[k], sib_send.at[k], sib_recv.at[k], sibling)

    def ring(k, p):
        r = pl.ds(p * (length // 2), length // 2)
        return remote(
            own_back.at[k, r], ring_got.at[k, r], ring_send.at[k, p], ring_recv.at[k, p], following
        )

    def blocks_for(k):
        if k >= 2:
            cross(k - 2).wait_send()
        back_block(sib_stage.at[k % 2], at + sib_step * (RING - 1 - k), 1 - c)
        cross(k).start()
        back_block(own_back.at[k], at + step * (RING - 1 - k), c)

    def ring_step(k):
        cross(k).wait_recv()
        srcs = [own_back.at[k], sib_back.at[k]]
        if k:
            for p in range(2):
                ring(k - 1, p).wait_recv()
            srcs.append(ring_got.at[k - 1])
        add_rows(own_back.at[k], srcs, 16)
        for p in range(2):
            ring(k, p).start()

    def ring_end():
        last = RING - 1
        cross(last).wait_recv()
        for p in range(2):
            ring(last - 1, p).wait_recv()
        rows = 16

        def body(i, total):
            r = pl.ds(pl.multiple_of(i * rows, rows), rows)
            back = (
                own_back[last, r].astype(F32)
                + sib_back[last, r].astype(F32)
                + ring_got[last - 1, r].astype(F32)
            )
            values = tokens_ref[r].astype(F32)
            rstd = lax.rsqrt(jnp.mean(values * values, axis=-1, keepdims=True) + epsilon)
            scaled = back * gain_ref[0:1, :]
            inner = jnp.mean(scaled * values, axis=-1, keepdims=True)
            grad = cot_ref[r].astype(F32) + rstd * scaled - values * (rstd * rstd * rstd * inner)
            tgrad_ref[r] = grad.astype(BF16)
            terms = back * values * rstd
            return total + terms[:8] + terms[8:]

        total = lax.fori_loop(0, length // rows, body, jnp.zeros((8, width), F32))
        total = jnp.broadcast_to(jnp.sum(total, axis=0, keepdims=True), (8, width))
        piece = gain_parts.shape[2]
        for f in range(shares):
            gain_parts[f] = total[:, f * piece : (f + 1) * piece]
        gain_got[share] = gain_parts[share]

    gains = []
    for k in range(1, shares):
        f = (share + k) % shares
        gains.append(
            remote(
                gain_parts.at[f], gain_got.at[share], gain_send.at[k - 1], gain_recv.at[k - 1], share_at(f)
            )
        )

    def lines(tau):
        for j in (2, 0, 1):
            line(tau, j)

    blocks_for(0)
    ring_step(0)
    grad_column(0)
    lines(0)
    for i in range(1, z_size):
        grad_column(i)
    blocks_for(1)
    ring_step(1)
    blocks_for(2)
    lines(1)
    blocks_for(3)
    ring_step(2)
    for tau in range(2, hops):
        lines(tau)

    settle(2, fin_conv)
    for copy in conv_swaps:
        copy.start()
    ring_end()
    for copy in gains:
        copy.start()
    both_conv[x, corner] = fin_conv[pl.ds(pl.multiple_of(corner * rows_in, rows_in), rows_in)]
    settle(0, small_out.at[x])
    settle(1, vec_out.at[x])
    small_x = remote(small_out.at[x], small_out.at[x], x_send.at[2], x_recv.at[2], over_x)
    vec_x = remote(vec_out.at[x], vec_out.at[x], x_send.at[3], x_recv.at[3], over_x)
    small_x.start()
    vec_x.start()

    branch = 8 * half * z_size

    def lay(first, both):
        for zz in range(z_size):
            for j in range(4):
                for xx in range(2):
                    col = first + (zz * 4 + j) * 2 * half + xx * half
                    in_ref[:, col : col + half] = both[xx, j, :, zz * half : (zz + 1) * half].astype(F32)

    for copy in gains:
        copy.wait()
    gain_half[...] = jnp.sum(gain_got[...], axis=0)
    gain_x = remote(gain_half, gain_pair, x_send.at[5], x_recv.at[5], over_x)
    gain_x.start()
    for copy in gate_swaps:
        copy.wait()
    lay(branch, both_gate)
    gain_x.wait()
    gain_out[...] = gain_half[...] + gain_pair[...]
    for copy in conv_swaps:
        copy.wait()
    lay(0, both_conv)
    for copy in (out_x, small_x, vec_x):
        copy.wait()
    for j in range(3):
        sent(j)
    out_sent(0)
    for k in range(RING - 1):
        for p in range(2):
            ring(k, p).wait_send()
    for k in range(2, RING):
        cross(k).wait_send()


def last_part(
    z_size,
    taps,
    part,
    keep,
    mats,
    params,
    gate_fin,
    out_fin,
    gout,
    da,
    gstep,
    bias,
    skip,
    tokens,
    cot,
    gain,
    bx,
    cin,
    normed,
    conv,
    gate,
    bgi,
    in_width,
):
    length, width = tokens.shape
    chans = bx.shape[2]
    shares = z_size * 4
    hops = z_size - 1
    rows_in = gate_fin.shape[0] // 4
    half = gout.shape[1]
    wide = part.shape[3]
    any_space = pl.BlockSpec(memory_space=pl.ANY)
    vmem = pl.BlockSpec(memory_space=pltpu.VMEM)
    dma = pltpu.SemaphoreType.DMA
    shape = jax.ShapeDtypeStruct
    block = (length, width)
    slabs = [(half, mats.shape[1]), (params.shape[0], half), (4 * rows_in, chans)]
    bufs = lambda n: [pltpu.VMEM((n,) + s, BF16) for s in slabs]
    both = pltpu.VMEM((2, 4, rows_in, chans), BF16)
    piece = (8, width // shares)
    few = (length, wide)
    late_out = (half, width // 2)
    return pl.pallas_call(
        functools.partial(last_kernel, z_size, taps),
        in_specs=[vmem] * 13 + [any_space] * 7,
        out_specs=[vmem] * 6,
        out_shape=[
            shape(tokens.shape, BF16),
            shape((rows_in, in_width), F32),
            shape((2,) + gout.shape[1:], BF16),
            shape((2,) + slabs[0], BF16),
            shape((2,) + slabs[1], BF16),
            shape(piece, F32),
        ],
        scratch_shapes=[
            pltpu.VMEM((4, 2) + few, BF16),
            pltpu.VMEM((4,) + few, BF16),
            pltpu.VMEM((3,) + few, BF16),
            pltpu.VMEM((3,) + few, BF16),
            pltpu.VMEM((length + 3, 8, chans), F32),
            pltpu.VMEM((length + 3, 8, chans), F32),
            pltpu.VMEM((length, chans), BF16),
            pltpu.VMEM(conv.shape, BF16),
            pltpu.VMEM(gate.shape, BF16),
            pltpu.VMEM(bgi.shape, BF16),
            pltpu.VMEM((length // 8, 8, chans), F32),
            pltpu.VMEM(bgi.shape, BF16),
            pltpu.VMEM((chans, wide), F32),
            pltpu.VMEM((taps + 1, 8, chans), F32),
            pltpu.VMEM((2, 8, length, 4 * rows_in), BF16),
            pltpu.VMEM((RING,) + block, BF16),
            pltpu.VMEM((2,) + block, BF16),
            pltpu.VMEM((RING,) + block, BF16),
            pltpu.VMEM((RING - 1,) + block, BF16),
        ]
        + bufs(z_size)
        + bufs(hops)
        + bufs(hops)
        + [
            pltpu.VMEM((z_size,) + late_out, BF16),
            pltpu.VMEM((hops,) + late_out, BF16),
            pltpu.VMEM((hops,) + late_out, BF16),
            pltpu.VMEM(slabs[2], BF16),
            both,
            both,
            pltpu.VMEM((shares,) + piece, F32),
            pltpu.VMEM((shares,) + piece, F32),
            pltpu.VMEM(piece, F32),
            pltpu.VMEM(piece, F32),
            dma((7,)),
            dma((2,)),
            dma((1,)),
            dma((1,)),
        ]
        + [dma((3,))] * 4
        + [dma((4,))] * 2
        + [dma((RING,))] * 2
        + [dma((RING - 1, 2))] * 2
        + [dma((hops, 3))] * 4
        + [dma((hops, 1))] * 4
        + [dma((2, 7))] * 2
        + [dma((6,))] * 2
        + [dma((shares - 1,))] * 2,
        cost_estimate=busy(120),
        compiler_params=pltpu.CompilerParams(
            collective_id=3, has_side_effects=True, vmem_limit_bytes=63 << 20
        ),
    )(
        part,
        keep,
        mats,
        params,
        gate_fin,
        out_fin,
        da,
        gstep,
        bias,
        skip,
        tokens,
        cot,
        gain,
        bx,
        cin,
        normed,
        conv,
        gate,
        bgi,
        gout,
    )


def shards(
    tokens,
    doc_ids,
    norm_gain,
    in_weight,
    conv_taps,
    conv_offset,
    select_weight,
    step_weight,
    step_bias,
    decay_log,
    skip_gain,
    out_weight,
    cotangent,
):
    z_size = lax.axis_size("z")
    rh_size = lax.axis_size("rh")
    seqs = 8
    length = doc_ids.shape[1]
    width = tokens.shape[1]
    in_rows = in_weight.shape[0]
    rows = out_weight.shape[0]
    half = rows // 2
    chans = half * z_size
    taps = conv_taps.shape[1]
    rank = step_weight.shape[1]
    states = decay_log.shape[1]
    x_at = lax.axis_index("x")

    def own_half(w):
        return lax.dynamic_slice_in_dim(w, x_at * half, half, 0)

    spare = -(rank + 2 * states) % 128
    wide = rank + 2 * states + spare
    vectors = jnp.concatenate(
        [
            own_half(conv_taps),
            own_half(conv_offset)[:, None],
            own_half(step_bias)[:, None],
            own_half(skip_gain)[:, None],
            own_half(decay_log),
        ],
        axis=1,
    ).T
    vectors = jnp.pad(vectors, ((0, -vectors.shape[0] % 32), (0, 0)))
    weight_in = in_weight
    if half % 128:
        columns = lax.dynamic_index_in_dim(
            in_weight.reshape(in_rows, 2, z_size, 4, 2, half), x_at, 4, keepdims=False
        )
        weight_in = columns.transpose(1, 3, 0, 2, 4).reshape(2, 4, in_rows, chans)
    gain_tile = jnp.broadcast_to(norm_gain.astype(F32)[None, :], (8, norm_gain.shape[0]))
    ids_tile = jnp.broadcast_to(doc_ids, (8, length))
    (
        all_normed,
        all_cot,
        w_conv,
        w_gate,
        w_out,
        w_mats,
        keep,
        conv_in,
        x,
        dt,
        pre,
        vectors,
        gains,
        selection,
    ) = front(
        z_size,
        taps,
        rank,
        tokens,
        gain_tile,
        ids_tile,
        vectors,
        cotangent,
        weight_in,
        out_weight,
        select_weight,
        step_weight,
    )
    selection = selection.reshape(length * seqs, wide)
    rates = -jnp.exp(vectors[taps + 3 : taps + 3 + states])
    rate2 = jnp.broadcast_to((rates * LOG2E)[:, None, :], (states, seqs, chans))

    hist, last, back_scan, back_gate_in, out_part, grad_out, grad_gate, w_gate, _ = scan_forward(
        z_size, rank, taps + 2, dt, x, selection, keep, rate2, all_normed, all_cot, w_gate, w_out, vectors
    )
    layer_sum = lax.psum_scatter(
        out_part.reshape(-1, width), PLANE, scatter_dimension=0, tiled=True
    )
    layer_out = (tokens.astype(F32) + layer_sum.astype(F32)).astype(BF16)
    back_x, part, da, g_step, g_bias, g_skip, gate_fin, out_fin = scan_backward(
        z_size,
        rank,
        taps + 2,
        dt,
        x,
        back_scan,
        pre,
        selection,
        keep,
        rate2,
        hist,
        last,
        vectors,
        w_mats,
        grad_gate.reshape(z_size, -1, chans),
        grad_out.reshape(z_size, half, width),
    )
    tokens_grad, g_in, g_out, g_mats, g_vectors, g_gain = last_part(
        z_size,
        taps,
        part.reshape(4, 2, length, wide),
        keep,
        w_mats,
        vectors,
        gate_fin,
        out_fin,
        grad_out.reshape(z_size, half, width),
        da,
        g_step,
        g_bias,
        g_skip,
        tokens,
        cotangent,
        gains,
        back_x,
        conv_in,
        all_normed,
        w_conv,
        w_gate,
        back_gate_in,
        in_weight.shape[1],
    )
    g_gain = g_gain[0]
    g_out = g_out.reshape(rows, width).astype(F32)
    g_mats = g_mats.reshape(rows, -1).astype(F32)
    g_vectors = g_vectors.transpose(0, 2, 1).reshape(rows, -1).astype(F32)
    if rh_size > 1:
        g_mats, g_vectors, g_in, g_out, g_gain = lax.psum(
            (g_mats, g_vectors, g_in, g_out, g_gain), "rh"
        )
    return (
        layer_out,
        tokens_grad,
        g_gain,
        g_in,
        g_vectors[:, :taps],
        g_vectors[:, taps],
        g_mats[:, : rank + 2 * states],
        g_mats[:, wide:],
        g_vectors[:, taps + 1],
        g_vectors[:, taps + 3 : taps + 3 + states],
        g_vectors[:, taps + 2],
        g_out,
    )


def solution(mesh):
    replicas = mesh.shape["replica"]
    shares = mesh.shape["fsdp"]
    grid = Mesh(
        mesh.devices.reshape(replicas // 2, 2, shares // 4, 2, 2), ("rh", "x", "z", "y", "c")
    )
    tok = ("rh", "x", "z", "y", "c")
    own = ("z", "y", "c")
    return jax.shard_map(
        shards,
        mesh=grid,
        in_specs=(
            P(tok, None),
            P(tok, None),
            P(own),
            P(own, None),
            P(own, None),
            P(own),
            P(own, None),
            P(own, None),
            P(own),
            P(own, None),
            P(own),
            P(own, None),
            P(tok, None),
        ),
        out_specs=(
            P(tok, None),
            P(tok, None),
            P(own),
            P(own, None),
            P(own, None),
            P(own),
            P(own, None),
            P(own, None),
            P(own),
            P(own, None),
            P(own),
            P(own, None),
        ),
        check_vma=False,
    )
```

```python
import functools

import jax
import jax.numpy as jnp
import numpy as np
from jax import lax
from jax.experimental import pallas as pl
from jax.experimental.pallas import tpu as pltpu
from jax.sharding import Mesh
from jax.sharding import PartitionSpec as P

F32 = jnp.float32
BF16 = jnp.bfloat16
epsilon = 1e-05
PLANE = ("x", "y", "c")
BIG = 1e30
STEPS = 32
COLUMNS = 512
INNER = 4
BACK_INNER = 8
TOGETHER = 4
LOG2E = 1.4426950408889634


def dot(a, b, dims):
    return lax.dot_general(a, b, (dims, ((), ())), preferred_element_type=F32)


def dot_nn(a, b):
    return dot(a, b, ((1,), (0,)))


def dot_tn(a, b):
    return dot(a, b, ((0,), (0,)))


def dot_nt(a, b):
    return dot(a, b, ((1,), (1,)))


def busy(micros):
    return pl.CostEstimate(flops=micros * 10**9, bytes_accessed=micros * 10**6, transcendentals=0)


MESH = pl.DeviceIdType.MESH
RING = 4


def place():
    return {a: lax.axis_index(a) for a in ("x", "z", "y", "c")}


def ring_chip(p):
    y = p // 2
    return (p + y) % 2, y


def ring_at(x, y):
    return 2 * y + (x + y) % 2


def share_at(f):
    return {"z": f // 4, "y": f // 2 % 2, "c": f % 2}


def remote(src, dst, send, recv, device):
    return pltpu.make_async_remote_copy(
        src_ref=src, dst_ref=dst, send_sem=send, recv_sem=recv, device_id=device, device_id_type=MESH
    )


def greet(devices):
    barrier = pltpu.get_barrier_semaphore()
    for device in devices:
        pl.semaphore_signal(barrier, inc=1, device_id=device, device_id_type=MESH)
    pl.semaphore_wait(barrier, len(devices))


def plane_others(me):
    out = []
    for dx in range(2):
        for dy in range(2):
            for dc in range(2):
                if dx + dy + dc:
                    out.append(
                        {"x": (me["x"] + dx) % 2, "y": (me["y"] + dy) % 2, "c": (me["c"] + dc) % 2}
                    )
    return out


def share_others(me, shares):
    f = me["z"] * 4 + me["y"] * 2 + me["c"]
    return [share_at((f + k) % shares) for k in range(1, shares)]


def z_only(me, shares):
    f = me["c"] + 2 * me["y"]
    out = []
    for dz in range(1, shares // 4):
        for k in range(4):
            out.append(
                {
                    "z": (me["z"] + dz) % (shares // 4),
                    "y": (f + k) % 4 // 2,
                    "c": (f + k) % 2,
                }
            )
    return out


def z_line(z, z_size, pieces, sems):
    up_s, up_r, down_s, down_r = sems

    def up(k):
        return [
            remote(p(z - k), p(z - k), up_s.at[k, j], up_r.at[k, j], {"z": z + 1})
            for j, p in enumerate(pieces)
        ]

    def down(k):
        return [
            remote(p(z + k), p(z + k), down_s.at[k, j], down_r.at[k, j], {"z": z - 1})
            for j, p in enumerate(pieces)
        ]

    def start(k):
        @pl.when((z < z_size - 1) & (z >= k))
        def _():
            for copy in up(k):
                copy.start()

        @pl.when((z > 0) & (z + k < z_size))
        def _():
            for copy in down(k):
                copy.start()

    def arrive(k):
        @pl.when(z > k)
        def _():
            for copy in up(k):
                copy.wait_recv()

        @pl.when(z + k < z_size - 1)
        def _():
            for copy in down(k):
                copy.wait_recv()

    def sent(k):
        @pl.when((z < z_size - 1) & (z >= k))
        def _():
            for copy in up(k):
                copy.wait_send()

        @pl.when((z > 0) & (z + k < z_size))
        def _():
            for copy in down(k):
                copy.wait_send()

    return start, arrive, sent


class Ring:
    def __init__(self, me, blocks, own, ring_send, ring_recv, sib_send, sib_recv):
        self.me, self.blocks, self.own = me, blocks, own
        self.sems = ring_send, ring_recv, sib_send, sib_recv
        self.at = ring_at(me["x"], me["y"])
        self.step = 1 + 2 * me["c"]
        nx, ny = ring_chip((self.at + self.step) % RING)
        self.following = {"x": nx, "y": ny}
        self.sibling = {"c": 1 - me["c"]}
        self.half = blocks.shape[1] // 2

    def slot(self, k):
        ox, oy = ring_chip((self.at + (RING - self.step) * k) % RING)
        return ox * 4 + oy * 2 + self.me["c"]

    def hop(self, k):
        out = []
        for p in range(2):
            rows = pl.ds(p * self.half, self.half)
            dst = self.blocks.at[self.slot(k), rows]
            src = self.own.at[rows] if k == 0 and self.own is not None else dst
            out.append(remote(src, dst, self.sems[0].at[k, p], self.sems[1].at[k, p], self.following))
        return out

    def cross(self, k):
        dst = self.blocks.at[self.slot(k)]
        src = self.own if k == 0 and self.own is not None else dst
        return remote(src, dst, self.sems[2].at[k], self.sems[3].at[k], self.sibling)

    def start(self, k):
        if k < RING - 1:
            for copy in self.hop(k):
                copy.start()
        self.cross(k).start()

    def arrive(self, k):
        for copy in self.hop(k):
            copy.wait_recv()

    def sent(self, k):
        if k < RING - 1:
            for copy in self.hop(k):
                copy.wait_send()
        self.cross(k).wait()


def sigmoid(v):
    return 0.5 + 0.5 * jnp.tanh(0.5 * v)


def softplus(v):
    e = jnp.exp(-jnp.abs(v))
    small = e * (1.0 - e * (0.5 - e * (1.0 / 3.0)))
    return jnp.maximum(v, 0.0) + jnp.where(e < 1e-3, small, jnp.log(1.0 + e))


def front_kernel(
    z_size,
    taps,
    rank,
    tokens_ref,
    gain_ref,
    ids_ref,
    rows_ref,
    cot_ref,
    in_ref,
    out_ref,
    select_ref,
    step_ref,
    normed_hbm,
    cot_all,
    conv_hbm,
    gate_all,
    out_all,
    mats_hbm,
    keep_hbm,
    cin_hbm,
    x_hbm,
    dt_hbm,
    pre_hbm,
    params,
    gain_all,
    selection,
    normed_all,
    conv_w,
    mats,
    rows_all,
    gain_got,
    ids_all,
    proj,
    cin,
    xs,
    picked,
    part,
    dts,
    pres,
    keep,
    first,
    from_sib,
    stage,
    got,
    local_sem,
    own_sem,
    gain_send,
    gain_recv,
    ids_send,
    ids_recv,
    conv_send,
    conv_recv,
    gate_send,
    gate_recv,
    ring_send,
    ring_recv,
    sib_send,
    sib_recv,
    cot_ring_send,
    cot_ring_recv,
    cot_sib_send,
    cot_sib_recv,
    a_us,
    a_ur,
    a_ds,
    a_dr,
    m_us,
    m_ur,
    m_ds,
    m_dr,
    b_us,
    b_ur,
    b_ds,
    b_dr,
    sw_s,
    sw_r,
    rs_s,
    rs_r,
    ag_s,
    ag_r,
    fw_s,
    fw_r,
):
    me = place()
    x, y, z, c = me["x"], me["y"], me["z"], me["c"]
    shares = z_size * 4
    share = z * 4 + y * 2 + c
    corner = y * 2 + c
    seq = x * 4 + y * 2 + c
    sibling = {"c": 1 - c}
    length, width = tokens_ref.shape
    chans = conv_w.shape[1]
    rows_in = width // shares
    half = chans // z_size
    hops = z_size - 1
    branch = 8 * chans
    greet(plane_others(me) + z_only(me, shares))

    def rows_at(ref, index, count):
        return ref.at[pl.ds(pl.multiple_of(index * count, count), count)]

    def pieces(first, dst, to):
        rows = rows_at(dst, share, rows_in)
        if len(in_ref.shape) == 4:
            return [(in_ref.at[1 if first else 0, to], rows)]
        out = []
        for zz in range(z_size):
            col = first + (zz * 4 + to) * 2 * half + x * half
            src = in_ref.at[:, pl.ds(pl.multiple_of(col, half), half)]
            out.append((src, rows.at[:, pl.ds(zz * half, half)]))
        return out

    def corner_sends(first, dst, send, recv):
        out = []
        for k in range(1, 4):
            to = (corner + k) % 4
            for i, (src, there) in enumerate(pieces(first, dst, to)):
                out.append(
                    remote(
                        src, there, send.at[k - 1, i], recv.at[k - 1, i], {"y": to // 2, "c": to % 2}
                    )
                )
        return out

    gain_got[share] = jnp.broadcast_to(gain_ref[...].astype(F32), gain_got.shape[1:])
    ids_all[seq] = jnp.broadcast_to(ids_ref[...], ids_all.shape[1:])
    swaps = corner_sends(0, conv_w, conv_send, conv_recv)
    gates = corner_sends(branch, gate_all, gate_send, gate_recv)
    for copy in swaps:
        copy.start()
    gains = [
        remote(gain_got.at[share], gain_got.at[share], gain_send.at[k], gain_recv.at[k], device)
        for k, device in enumerate(share_others(me, shares))
    ]
    for copy in gains:
        copy.start()
    locals_ = [
        pltpu.make_async_copy(
            out_ref.at[pl.ds(pl.multiple_of(x * half, half), half)], rows_at(out_all, z, half), local_sem.at[3]
        ),
        pltpu.make_async_copy(cot_ref, cot_all.at[seq], local_sem.at[4]),
    ]
    for i, (src, there) in enumerate(pieces(0, conv_w, corner)):
        locals_.append(pltpu.make_async_copy(src, there, own_sem.at[0, i]))
    for i, (src, there) in enumerate(pieces(branch, gate_all, corner)):
        locals_.append(pltpu.make_async_copy(src, there, own_sem.at[1, i]))
    for copy in locals_:
        copy.start()
    ids_copies = [
        remote(ids_all.at[seq], ids_all.at[seq], ids_send.at[k], ids_recv.at[k], device)
        for k, device in enumerate(plane_others(me))
    ]
    for copy in ids_copies:
        copy.start()
    rows_all[z] = rows_ref[...]
    mine_rows = pl.ds(pl.multiple_of(x * half, half), half)
    at_rows = pl.ds(pl.multiple_of(z * half, half), half)
    wide = mats.shape[1] - rank
    mats[at_rows, :wide] = jnp.concatenate(
        [
            select_ref[mine_rows, :],
            jnp.zeros((half, wide - select_ref.shape[1]), BF16),
        ],
        axis=1,
    )
    mats[at_rows, wide:] = step_ref[mine_rows, :]

    values = tokens_ref[...].astype(F32)
    rstd = lax.rsqrt(jnp.mean(values * values, axis=-1, keepdims=True) + epsilon)
    for copy in gains:
        copy.wait()
    piece = gain_ref.shape[1]
    for f in range(shares):
        cols = pl.ds(f * piece, piece)
        normed = tokens_ref[:, cols].astype(F32) * rstd * gain_got[f, 0:1, :]
        normed_all[seq, :, cols] = normed.astype(BF16)
    for f in range(shares):
        gain_all[:, f * piece : (f + 1) * piece] = gain_got[f]

    ring = Ring(me, normed_all, None, ring_send, ring_recv, sib_send, sib_recv)
    cot_ring = Ring(me, cot_all, cot_ref, cot_ring_send, cot_ring_recv, cot_sib_send, cot_sib_recv)
    ring.start(0)
    for copy in swaps:
        copy.wait()
    for copy in locals_:
        copy.wait()
    a_start, a_arrive, a_sent = z_line(
        z,
        z_size,
        [
            lambda k: rows_at(conv_w, k, 4 * rows_in),
            lambda k: rows_all.at[k],
        ],
        (a_us, a_ur, a_ds, a_dr),
    )
    m_start, m_arrive, m_sent = z_line(
        z, z_size, [lambda k: rows_at(mats, k, half)], (m_us, m_ur, m_ds, m_dr)
    )
    b_start, b_arrive, b_sent = z_line(
        z,
        z_size,
        [lambda k: rows_at(gate_all, k, 4 * rows_in), lambda k: rows_at(out_all, k, half)],
        (b_us, b_ur, b_ds, b_dr),
    )
    a_start(0)
    for copy in gates:
        copy.start()

    for copy in ids_copies:
        copy.wait()
    ids = jnp.concatenate([ids_all[s, 0:1, :] for s in range(8)], axis=0).astype(F32)
    before = pltpu.roll(ids, 1, 1)
    lane = lax.broadcasted_iota(jnp.int32, ids.shape, 1)
    same = jnp.where((ids == before) & (lane > 0), 1.0, 0.0)
    for t in range(length):
        keep[t] = jnp.broadcast_to(same[:, t : t + 1], (8, 128))
    keep_copy = pltpu.make_async_copy(keep, keep_hbm, local_sem.at[5])
    keep_copy.start()

    for k in range(max(hops, RING - 1)):
        if k < hops:
            a_arrive(k)
            if k + 1 < hops:
                a_start(k + 1)
            if k + 1 == hops - 1:
                m_start(0)
        if k < RING - 1:
            ring.arrive(k)
            ring.start(k + 1)
        if k == RING - 2:
            cot_ring.start(0)
    m_arrive(0)
    m_start(1)
    for copy in gates:
        copy.wait()
    b_start(0)
    for k in range(RING):
        ring.sent(k)
    outs = [
        pltpu.make_async_copy(normed_all, normed_hbm, local_sem.at[6]),
        pltpu.make_async_copy(conv_w, conv_hbm, local_sem.at[7]),
    ]
    for copy in outs:
        copy.start()
    for zz in range(z_size):
        params[:, zz * half : (zz + 1) * half] = rows_all[zz].astype(F32)

    def project(s, carry):
        proj[s] = dot_nn(normed_all[s], conv_w[...])
        return carry

    lax.fori_loop(0, 8, project, 0)
    for k in range(1, hops):
        m_arrive(k)
        if k + 1 < hops:
            m_start(k + 1)
    cot_ring.arrive(0)
    cot_ring.start(1)

    cin[0:3] = jnp.zeros((3, 8, chans), F32)
    block = 32
    fine = 4

    def turn(i, carry):
        t0 = pl.multiple_of(i * block, block)
        cin[pl.ds(3 + t0, block)] = jnp.swapaxes(proj[:, pl.ds(t0, block), :], 0, 1)
        return carry

    lax.fori_loop(0, length // block, turn, 0)

    def convolve(i, carry):
        t0 = i * fine
        for g in range(chans // 128):
            lanes = pl.ds(g * 128, 128)
            tap = [jnp.broadcast_to(params[taps - 1 - j : taps - j, lanes], (8, 128)) for j in range(taps)]
            offset = jnp.broadcast_to(params[taps : taps + 1, lanes], (8, 128))
            chosen = []
            for j in range(fine):
                t = t0 + j
                total = tap[3] * cin[t, :, lanes] * keep[jnp.maximum(t - 2, 0)]
                total = (total + tap[2] * cin[t + 1, :, lanes]) * keep[jnp.maximum(t - 1, 0)]
                total = (total + tap[1] * cin[t + 2, :, lanes]) * keep[t]
                v = total + tap[0] * cin[t + 3, :, lanes] + offset
                chosen.append((v * sigmoid(v)).astype(BF16))
                xs[t, :, lanes] = chosen[-1].astype(F32)
            rows = pl.ds(pl.multiple_of(t0 * 8, fine * 8), fine * 8)
            picked[rows, lanes] = jnp.concatenate(chosen, axis=0)
        return carry

    lax.fori_loop(0, length // fine, convolve, 0)
    outs += [
        pltpu.make_async_copy(mats, mats_hbm, local_sem.at[8]),
        pltpu.make_async_copy(cin.at[pl.ds(3, length)], cin_hbm, local_sem.at[9]),
        pltpu.make_async_copy(xs, x_hbm, local_sem.at[10]),
    ]
    for copy in outs[2:]:
        copy.start()

    wide = part.shape[3]

    def select(b, carry):
        rows = pl.ds(pl.multiple_of(b * length, length), length)
        part[b // 2, b % 2] = dot_nn(picked[rows, :], mats[:, :wide])
        return carry

    lax.fori_loop(0, 8, select, 0)
    first[...] = part[:, 1 - c].astype(BF16)
    swap = remote(first, from_sib, sw_s.at[0], sw_r.at[0], sibling)
    swap.start()
    swap.wait()
    mine = x * 2 + y
    chips = [((x + d // 2) % 2, (y + d % 2) % 2) for d in (1, 2, 3)]
    sends = []
    for k in (2, 1, 0):
        ox, oy = chips[k]
        j = ox * 2 + oy
        stage[k] = (part[j, c] + from_sib[j].astype(F32)).astype(BF16)
        copy = remote(stage.at[k], got.at[k], rs_s.at[k], rs_r.at[k], {"x": ox, "y": oy})
        copy.start()
        sends.append(copy)
    total = part[mine, c] + from_sib[mine].astype(F32)
    for copy in sends:
        copy.wait()
    for k in range(3):
        total = total + got[k].astype(F32)
    selection[mine, c] = total.astype(BF16)
    here = selection.at[mine, c]
    spreads = []
    for k in (2, 1, 0):
        ox, oy = chips[k]
        copy = remote(here, here, ag_s.at[k], ag_r.at[k], {"x": ox, "y": oy})
        copy.start()
        spreads.append((k, copy))
    forwards = [remote(here, here, fw_s.at[3], fw_r.at[3], sibling)]
    forwards[0].start()
    b_arrive(0)
    if hops > 2:
        b_start(1)
    cot_ring.arrive(1)
    for k, copy in reversed(spreads):
        copy.wait_recv()
        ox, oy = chips[k]
        there = selection.at[ox * 2 + oy, c]
        forwards.append(remote(there, there, fw_s.at[k], fw_r.at[k], sibling))
        forwards[-1].start()
    for _, copy in spreads:
        copy.wait_send()
    for copy in forwards:
        copy.wait()
    cot_ring.start(2)

    bias = params[taps + 1 : taps + 2, :]

    def steps(i, carry):
        rows = 64
        per = length // rows
        b = i // per
        at = pl.ds(pl.multiple_of((i % per) * rows, rows), rows)
        v = dot_nt(selection[b // 2, b % 2, at, :rank], mats[:, wide : wide + rank]) + bias
        t = pl.ds(i * (rows // 8), rows // 8)
        pres[t] = v.reshape(rows // 8, 8, chans)
        dts[t] = softplus(v).reshape(rows // 8, 8, chans)
        return carry

    lax.fori_loop(0, length * 8 // 64, steps, 0)
    outs += [
        pltpu.make_async_copy(dts, dt_hbm, local_sem.at[11]),
        pltpu.make_async_copy(pres, pre_hbm, local_sem.at[12]),
    ]
    for copy in outs[5:]:
        copy.start()

    for k in range(1, hops - 1):
        b_arrive(k)
        if k + 1 < hops - 1:
            b_start(k + 1)
    cot_ring.arrive(2)
    cot_ring.start(3)
    for k in range(RING):
        cot_ring.sent(k)
    for k in range(hops):
        a_sent(k)
        m_sent(k)
    for k in range(hops - 1):
        b_sent(k)
    for copy in outs + [keep_copy]:
        copy.wait()


def front(z_size, taps, rank, tokens, gain, ids, rows, cot, weight_in, out, select, step):
    length, width = tokens.shape
    shares = z_size * 4
    half = rows.shape[1]
    chans = half * z_size
    wide = select.shape[1] + -select.shape[1] % 128
    cuts = 1 if weight_in.ndim == 4 else z_size
    any_space = pl.BlockSpec(memory_space=pl.ANY)
    vmem = pl.BlockSpec(memory_space=pltpu.VMEM)
    dma = pltpu.SemaphoreType.DMA
    hops = z_size - 1
    shape = jax.ShapeDtypeStruct
    everyone = (8,) + tokens.shape
    per_token = (length, 8, chans)
    block = (length, wide)
    return pl.pallas_call(
        functools.partial(front_kernel, z_size, taps, rank),
        in_specs=[vmem] * 5 + [any_space] + [vmem] * 3,
        out_specs=[any_space] * 11 + [vmem] * 3,
        out_shape=[
            shape(everyone, BF16),
            shape(everyone, BF16),
            shape((width, chans), BF16),
            shape((width, chans), BF16),
            shape((chans, width), BF16),
            shape((chans, wide + rank), BF16),
            shape((length, 8, 128), F32),
            shape(per_token, F32),
            shape(per_token, F32),
            shape(per_token, F32),
            shape(per_token, F32),
            shape((rows.shape[0], chans), F32),
            shape((8, width), F32),
            shape((4, 2) + block, BF16),
        ],
        scratch_shapes=[
            pltpu.VMEM(everyone, BF16),
            pltpu.VMEM((width, chans), BF16),
            pltpu.VMEM((chans, wide + rank), BF16),
            pltpu.VMEM((z_size,) + rows.shape, BF16),
            pltpu.VMEM((shares, 8, gain.shape[1]), F32),
            pltpu.VMEM((8, 8, length), ids.dtype),
            pltpu.VMEM((8, length, chans), F32),
            pltpu.VMEM((length + 3, 8, chans), F32),
            pltpu.VMEM(per_token, F32),
            pltpu.VMEM((length * 8, chans), BF16),
            pltpu.VMEM((4, 2) + block, F32),
            pltpu.VMEM(per_token, F32),
            pltpu.VMEM(per_token, F32),
            pltpu.VMEM((length, 8, 128), F32),
            pltpu.VMEM((4,) + block, BF16),
            pltpu.VMEM((4,) + block, BF16),
            pltpu.VMEM((3,) + block, BF16),
            pltpu.VMEM((3,) + block, BF16),
            dma((13,)),
            dma((2, cuts)),
            dma((shares - 1,)),
            dma((shares - 1,)),
            dma((7,)),
            dma((7,)),
        ]
        + [dma((3, cuts))] * 4
        + [dma((RING - 1, 2)), dma((RING - 1, 2)), dma((RING,)), dma((RING,))] * 2
        + [dma((hops, 2))] * 4
        + [dma((hops, 1))] * 4
        + [dma((hops, 2))] * 4
        + [dma((1,))] * 2
        + [dma((3,))] * 4
        + [dma((4,))] * 2,
        cost_estimate=busy(120),
        compiler_params=pltpu.CompilerParams(
            collective_id=0, has_side_effects=True, vmem_limit_bytes=60 << 20
        ),
    )(tokens, gain, ids, rows, cot, weight_in, out, select, step)


def add_rows(dst, srcs, rows):
    count = dst.shape[0] // rows

    def body(i, carry):
        at = pl.ds(pl.multiple_of(i * rows, rows), rows)
        total = srcs[0][at].astype(F32)
        for src in srcs[1:]:
            total = total + src[at].astype(F32)
        dst[at] = total.astype(dst.dtype)
        return carry

    lax.fori_loop(0, count, body, 0)


def fill_rates(rate_ref, params_ref, first):
    states = rate_ref.shape[0]
    rows = -LOG2E * jnp.exp(params_ref[first : first + states, :])
    for n in range(states):
        rate_ref[n] = jnp.broadcast_to(rows[n : n + 1, :], rate_ref.shape[1:])


def forward_kernel(
    z_size,
    chunks,
    states,
    rank,
    skip_row,
    dt_ref,
    x_ref,
    sel_ref,
    keep_ref,
    normed_ref,
    cot_ref,
    normed_col,
    cot_col,
    params_ref,
    gate_given,
    out_given,
    hist_ref,
    last_ref,
    ds_ref,
    bgi_ref,
    part_ref,
    gout_ref,
    ggate_ref,
    gate_all,
    out_all,
    rate_ref,
    h_ref,
    bc_ref,
    y_ref,
    ys_ref,
    gate_ref,
    bg_ref,
    gated_ref,
    gated_all,
    bgi_all,
    gate_w_ref,
    out_w_ref,
    load_sem,
    up_s,
    up_r,
    down_s,
    down_r,
):
    step = pl.program_id(0)
    me = place()
    z = me["z"]
    hops = z_size - 1
    slab_rows = gate_all.shape[0] // z_size
    half = out_all.shape[0] // z_size
    line_start, line_arrive, line_sent = z_line(
        z,
        z_size,
        [
            lambda k: gate_all.at[pl.ds(pl.multiple_of(k * slab_rows, slab_rows), slab_rows)],
            lambda k: out_all.at[pl.ds(pl.multiple_of(k * half, half), half)],
        ],
        (up_s, up_r, down_s, down_r),
    )

    @pl.when(step == 0)
    def _():
        greet([{"z": (z + 1) % z_size}, {"z": (z + z_size - 1) % z_size}])
        line_start(hops - 1)
        fill_rates(rate_ref, params_ref, skip_row + 1)
        h_ref[...] = jnp.zeros_like(h_ref)

    steps, seqs, width = dt_ref.shape
    groups = width // 128
    rows = steps * seqs
    @pl.when(step < chunks)
    def _():
        bc_ref[...] = sel_ref[:, rank:].astype(F32).reshape(bc_ref.shape)

        def body(tb, carry):
            t0 = tb * INNER
            bc = [bc_ref[t0 + i] for i in range(INNER)]
            off = [(1.0 - keep_ref[t0 + i]) * BIG for i in range(INNER)]
            for g in range(groups):
                lanes = pl.ds(g * 128, 128)
                dt = [dt_ref[t0 + i, :, lanes] for i in range(INNER)]
                dtm = [dt[i] + off[i] for i in range(INNER)]
                u = [dt[i] * x_ref[t0 + i, :, lanes] for i in range(INNER)]
                y = [None] * INNER
                for n in range(states):
                    h = h_ref[n, :, lanes]
                    rate = rate_ref[n, :, lanes]
                    before = []
                    for i in range(INNER):
                        before.append(h)
                        a = jnp.exp2(dtm[i] * rate)
                        h = a * h + u[i] * bc[i][:, n : n + 1]
                        term = h * bc[i][:, states + n : states + n + 1]
                        y[i] = term if y[i] is None else y[i] + term
                    for i in range(0, INNER, 2):
                        pair = jnp.concatenate(before[i : i + 2], axis=0).astype(BF16)
                        hist_ref[t0 // 2 + i // 2, n, :, lanes] = pair
                    h_ref[n, :, lanes] = h
                skip = params_ref[skip_row : skip_row + 1, lanes]
                for i in range(INNER):
                    y_ref[step * steps + t0 + i, :, lanes] = y[i] + skip * x_ref[t0 + i, :, lanes]
            return carry

        lax.fori_loop(0, steps // INNER, body, 0)
        last_ref[...] = h_ref[...]

    @pl.when(step == chunks)
    def _():
        line_arrive(hops - 1)
        line_sent(hops - 1)
        loads = [
            pltpu.make_async_copy(gate_all, gate_w_ref, load_sem.at[0]),
            pltpu.make_async_copy(out_all, out_w_ref, load_sem.at[1]),
        ]
        for copy in loads:
            copy.start()
        for copy in loads:
            copy.wait()

    @pl.when((step >= chunks) & (step < 2 * chunks))
    def _():
        normed = normed_ref[...].reshape(rows, normed_ref.shape[2])
        cot = cot_ref[...].reshape(rows, cot_ref.shape[2])
        gate_ref[...] = dot_nn(normed, gate_w_ref[...])
        bg_ref[...] = dot_nt(cot, out_w_ref[...]).astype(BF16).astype(F32)
        y = y_ref[pl.ds((step - chunks) * steps, steps)]
        ys_ref[...] = jnp.swapaxes(y, 0, 1).reshape(rows, width)
        fine = 16

        def gating(i, carry):
            r = pl.ds(pl.multiple_of(i * fine, fine), fine)
            v = gate_ref[r, :]
            bg = bg_ref[r, :]
            y = ys_ref[r, :]
            s = sigmoid(v)
            gate = v * s
            gated_ref[r, :] = (y * gate).astype(BF16)
            bg_ref[r, :] = bg * gate
            gate_ref[r, :] = bg * y * (s + gate * (1.0 - s))
            return carry

        lax.fori_loop(0, rows // fine, gating, 0)
        ds_ref[...] = jnp.swapaxes(bg_ref[...].reshape(seqs, steps, width), 0, 1)
        bgi = gate_ref[...].astype(BF16).reshape(bgi_ref.shape)
        bgi_ref[...] = bgi
        gated = gated_ref[...]
        part_ref[...] = dot_nn(gated, out_w_ref[...]).astype(BF16).reshape(part_ref.shape)
        at = pl.ds(pl.multiple_of((step - chunks) * steps, steps), steps)
        gated_all[:, at, :] = gated.reshape(bgi_ref.shape)
        bgi_all[:, at, :] = bgi

    @pl.when(step >= 2 * chunks)
    def _():
        tall = (gated_all.shape[0] * gated_all.shape[1], width)
        cols = (tall[0], normed_col.shape[2])
        gout_ref[...] = dot_tn(gated_all[...].reshape(tall), cot_col[...].reshape(cols)).astype(BF16)
        ggate_ref[...] = dot_tn(normed_col[...].reshape(cols), bgi_all[...].reshape(tall)).astype(BF16)


def scan_forward(
    z_size, rank, states, skip_row, dt, x, selection, keep, normed, cot, gate_w, out_w, params
):
    length, seqs, width = dt.shape
    model = normed.shape[2]
    wide = selection.shape[1]
    chunks = length // STEPS
    early = lambda i: jnp.minimum(i, chunks - 1)
    late = lambda i: jnp.clip(i - chunks, 0, chunks - 1)
    pieces = model // COLUMNS
    last_of = lambda i: jnp.maximum(i - 2 * chunks, 0)
    column = pl.BlockSpec((seqs, length, COLUMNS), lambda i: (0, 0, last_of(i)))
    block = lambda *tail: pl.BlockSpec((STEPS,) + tail, lambda i: (early(i),) + (0,) * len(tail))
    across = lambda n: pl.BlockSpec((seqs, STEPS, n), lambda i: (0, late(i), 0))
    any_space = pl.BlockSpec(memory_space=pl.ANY)
    dma = pltpu.SemaphoreType.DMA
    hops = z_size - 1
    whole = lambda *dims: pl.BlockSpec(dims, lambda i: (0,) * len(dims))
    rows = STEPS * seqs
    shape = jax.ShapeDtypeStruct
    return pl.pallas_call(
        functools.partial(forward_kernel, z_size, chunks, states, rank, skip_row),
        grid=(2 * chunks + pieces,),
        in_specs=[
            block(seqs, width),
            block(seqs, width),
            pl.BlockSpec((rows, wide), lambda i: (early(i), 0)),
            block(seqs, 128),
            across(model),
            across(model),
            column,
            column,
            whole(*params.shape),
            any_space,
            any_space,
        ],
        out_specs=[
            pl.BlockSpec((STEPS // 2, states, 2 * seqs, width), lambda i: (early(i), 0, 0, 0)),
            whole(states, seqs, width),
            pl.BlockSpec((STEPS, seqs, width), lambda i: (late(i), 0, 0)),
            across(width),
            across(model),
            pl.BlockSpec((width, COLUMNS), lambda i: (0, last_of(i))),
            pl.BlockSpec((COLUMNS, width), lambda i: (last_of(i), 0)),
            any_space,
            any_space,
        ],
        out_shape=[
            shape((length // 2, states, 2 * seqs, width), BF16),
            shape((states, seqs, width), F32),
            shape(dt.shape, F32),
            shape((seqs, length, width), BF16),
            shape((seqs, length, model), BF16),
            shape((width, model), BF16),
            shape((model, width), BF16),
            shape(gate_w.shape, BF16),
            shape(out_w.shape, BF16),
        ],
        input_output_aliases={9: 7, 10: 8},
        scratch_shapes=[
            pltpu.VMEM((states, seqs, width), F32),
            pltpu.VMEM((states, seqs, width), F32),
            pltpu.VMEM((STEPS, seqs, wide - rank), F32),
            pltpu.VMEM((length, seqs, width), F32),
            pltpu.VMEM((rows, width), F32),
            pltpu.VMEM((rows, width), F32),
            pltpu.VMEM((rows, width), F32),
            pltpu.VMEM((rows, width), BF16),
            pltpu.VMEM((seqs, length, width), BF16),
            pltpu.VMEM((seqs, length, width), BF16),
            pltpu.VMEM(gate_w.shape, BF16),
            pltpu.VMEM(out_w.shape, BF16),
            dma((2,)),
        ]
        + [dma((hops, 2))] * 4,
        cost_estimate=busy(60),
        compiler_params=pltpu.CompilerParams(
            collective_id=5, has_side_effects=True, vmem_limit_bytes=60 << 20
        ),
    )(dt, x, selection, keep, normed, cot, normed, cot, params, gate_w, out_w)


def z_sums(z, z_size, owns, ups, downs, sems, blocks):
    up_s, up_r, down_s, down_r = sems

    def up_copy(k, j, own):
        src = owns[j].at[z_size - 1 - k] if own else ups[j].at[k]
        return remote(src, ups[j].at[k], up_s.at[k, j], up_r.at[k, j], {"z": z + 1})

    def down_copy(k, j, own):
        src = owns[j].at[k] if own else downs[j].at[k]
        return remote(src, downs[j].at[k], down_s.at[k, j], down_r.at[k, j], {"z": z - 1})

    def line(tau, j):
        k = tau - z
        high = z_size - 1 - k

        @pl.when((k >= 0) & (z < high) & (z > 0))
        def _():
            up_copy(k, j, False).wait_recv()
            add_rows(ups[j].at[k], [owns[j].at[high], ups[j].at[k]], blocks[j])
            up_copy(k, j, False).start()

        @pl.when((k >= 0) & (z < high) & (z == 0))
        def _():
            up_copy(k, j, True).start()

        m = tau - (z_size - 1 - z)

        @pl.when((m >= 0) & (z > m) & (z < z_size - 1))
        def _():
            down_copy(m, j, False).wait_recv()
            add_rows(downs[j].at[m], [owns[j].at[m], downs[j].at[m]], blocks[j])
            down_copy(m, j, False).start()

        @pl.when((m >= 0) & (z > m) & (z == z_size - 1))
        def _():
            down_copy(m, j, True).start()

    def settle(j, dst):
        low = z
        high = z_size - 1 - z

        @pl.when(z == 0)
        def _():
            down_copy(low, j, False).wait_recv()
            add_rows(dst, [owns[j].at[z], downs[j].at[low]], blocks[j])

        @pl.when(z == z_size - 1)
        def _():
            up_copy(high, j, False).wait_recv()
            add_rows(dst, [owns[j].at[z], ups[j].at[high]], blocks[j])

        @pl.when((z > 0) & (z < z_size - 1))
        def _():
            down_copy(low, j, False).wait_recv()
            up_copy(high, j, False).wait_recv()
            add_rows(dst, [owns[j].at[z], downs[j].at[low], ups[j].at[high]], blocks[j])

    def sent(j):
        for k in range(z_size - 1):

            @pl.when(z < z_size - 1 - k)
            def _():
                up_copy(k, j, False).wait_send()

            @pl.when(z > k)
            def _():
                down_copy(k, j, False).wait_send()

    return line, settle, sent


def backward_kernel(
    chunks_all,
    z_size,
    states,
    rank,
    skip_row,
    dt_ref,
    x_ref,
    ds_ref,
    pre_ref,
    sel_ref,
    keep_ref,
    hist_ref,
    last_ref,
    ones_ref,
    params_ref,
    step_w_ref,
    gate_hbm,
    out_hbm,
    bx_ref,
    part_ref,
    da_ref,
    gstep_ref,
    bias_ref,
    skip_ref,
    gate_fin,
    out_fin,
    rate_ref,
    ag_ref,
    h_ref,
    p_ref,
    bc_ref,
    bp_ref,
    gate_own,
    out_own,
    gate_up,
    out_up,
    gate_down,
    out_down,
    local_sem,
    up_s,
    up_r,
    down_s,
    down_r,
):
    chunk = pl.program_id(0)
    chunks = pl.num_programs(0)
    me = place()
    z = me["z"]
    hops = z_size - 1
    line, settle, sent = z_sums(
        z,
        z_size,
        (gate_own, out_own),
        (gate_up, out_up),
        (gate_down, out_down),
        (up_s, up_r, down_s, down_r),
        (64, 16),
    )

    @pl.when(chunk == 0)
    def _():
        greet([{"z": (z + 1) % z_size}, {"z": (z + z_size - 1) % z_size}])
        early = pl.ds(0, out_own.shape[2])
        loads = [
            pltpu.make_async_copy(gate_hbm, gate_own, local_sem.at[0]),
            pltpu.make_async_copy(out_hbm.at[:, :, early], out_own, local_sem.at[1]),
        ]
        for copy in loads:
            copy.start()
        fill_rates(rate_ref, params_ref, skip_row + 1)
        ag_ref[...] = jnp.zeros_like(ag_ref)
        da_ref[...] = jnp.zeros_like(da_ref)
        gstep_ref[...] = jnp.zeros_like(gstep_ref)
        bias_ref[...] = jnp.zeros_like(bias_ref)
        skip_ref[...] = jnp.zeros_like(skip_ref)
        h_ref[...] = last_ref[...]
        for copy in loads:
            copy.wait()

    for tau in range(hops):

        @pl.when(chunk == -(-tau * (chunks_all - 1) // hops))
        def _():
            line(tau, 0)
            line(tau, 1)

    steps, seqs, width = dt_ref.shape
    groups = width // 128
    blocks = steps // BACK_INNER
    bc_ref[...] = sel_ref[:, rank:].astype(F32).reshape(bc_ref.shape)

    inner = BACK_INNER

    def body(back, carry):
        t0 = (blocks - 1 - back) * inner
        rows = pl.ds(pl.multiple_of(t0 * seqs, inner * seqs), inner * seqs)
        bc = [bc_ref[t0 + i] for i in range(inner)]
        off = [(1.0 - keep_ref[t0 + i]) * BIG for i in range(inner)]
        for g0 in range(0, groups, TOGETHER):
            lanes = [pl.ds((g0 + q) * 128, 128) for q in range(TOGETHER)]
            each = [(q, i) for q in range(TOGETHER) for i in range(inner)]
            dt = {(q, i): dt_ref[t0 + i, :, lanes[q]] for q, i in each}
            dtm = {(q, i): dt[q, i] + off[i] for q, i in each}
            ds = {(q, i): ds_ref[t0 + i, :, lanes[q]] for q, i in each}
            u = {(q, i): dt[q, i] * x_ref[t0 + i, :, lanes[q]] for q, i in each}
            s1 = {}
            s2 = {}
            for n in range(states):
                pb = [None] * inner
                pc = [None] * inner
                for q in range(TOGETHER):
                    ag = ag_ref[n, :, lanes[q]]
                    h = h_ref[n, :, lanes[q]]
                    rate = rate_ref[n, :, lanes[q]]
                    da = da_ref[n, :, lanes[q]]
                    before = []
                    for i in range(0, inner, 2):
                        pair = hist_ref[t0 // 2 + i // 2, n, :, lanes[q]].astype(F32)
                        before += [pair[:seqs], pair[seqs:]]
                    for i in reversed(range(inner)):
                        prev = before[i]
                        a = jnp.exp2(dtm[q, i] * rate)
                        adj = ds[q, i] * bc[i][:, states + n : states + n + 1] + ag
                        c_term = ds[q, i] * h
                        b_term = adj * u[q, i]
                        pc[i] = c_term if q == 0 else pc[i] + c_term
                        pb[i] = b_term if q == 0 else pb[i] + b_term
                        ag = a * adj
                        w = ag * prev
                        rw = rate * w
                        gb = adj * bc[i][:, n : n + 1]
                        s1[q, i] = rw if n == 0 else s1[q, i] + rw
                        s2[q, i] = gb if n == 0 else s2[q, i] + gb
                        da = da + dt[q, i] * w
                        h = prev
                    ag_ref[n, :, lanes[q]] = ag
                    h_ref[n, :, lanes[q]] = h
                    da_ref[n, :, lanes[q]] = da
                cols = pl.ds(n * 128, 128)
                p_ref[0, g0 // TOGETHER, rows, cols] = jnp.concatenate(pb, axis=0).astype(BF16)
                p_ref[1, g0 // TOGETHER, rows, cols] = jnp.concatenate(pc, axis=0).astype(BF16)
            for q in range(TOGETHER):
                skip = params_ref[skip_row : skip_row + 1, lanes[q]]
                bias = bias_ref[:, lanes[q]]
                direct = skip_ref[:, lanes[q]]
                low = []
                for i in range(inner):
                    x = x_ref[t0 + i, :, lanes[q]]
                    bx_ref[t0 + i, :, lanes[q]] = dt[q, i] * s2[q, i] + skip * ds[q, i]
                    back_step = s1[q, i] * (1.0 / LOG2E) + x * s2[q, i]
                    back_pre = back_step / (1.0 + jnp.exp(-pre_ref[t0 + i, :, lanes[q]]))
                    low.append(back_pre)
                    bias = bias + back_pre
                    direct = direct + ds[q, i] * x
                bias_ref[:, lanes[q]] = bias
                skip_ref[:, lanes[q]] = direct
                bp_ref[rows, lanes[q]] = jnp.concatenate(low, axis=0).astype(BF16)
        return carry

    lax.fori_loop(0, blocks, body, 0)
    span = states * 128
    sets = groups // TOGETHER
    folded = dot_nn(p_ref[...].reshape(2 * sets * steps * seqs, span), ones_ref[...])
    folded = folded.reshape(2, sets, steps * seqs, 128)
    in_sum = folded[0, 0]
    out_sum = folded[1, 0]
    for g in range(1, sets):
        in_sum = in_sum + folded[0, g]
        out_sum = out_sum + folded[1, g]
    part_ref[:, rank:] = (in_sum + pltpu.roll(out_sum, states, 1)).astype(BF16)
    part_ref[:, :rank] = dot_nn(bp_ref[...], step_w_ref[...]).astype(BF16)
    gstep_ref[...] += dot_tn(bp_ref[...], sel_ref[:, :rank])

    @pl.when(chunk == chunks - 1)
    def _():
        settle(0, gate_fin)
        settle(1, out_fin)
        sent(0)
        sent(1)


def scan_backward(
    z_size, rank, skip_row, dt, x, ds, pre, selection, keep, hist, last, params, step_w, gate, out
):
    length, seqs, width = dt.shape
    states = last.shape[0]
    chunks = length // STEPS
    wide = selection.shape[1]
    rows = STEPS * seqs
    block = lambda *tail: pl.BlockSpec((STEPS,) + tail, lambda i: (chunks - 1 - i,) + (0,) * len(tail))
    flat = lambda n: pl.BlockSpec((rows, n), lambda i: (chunks - 1 - i, 0))
    whole = lambda *dims: pl.BlockSpec(dims, lambda i: (0,) * len(dims))
    any_space = pl.BlockSpec(memory_space=pl.ANY)
    span = states * 128
    ones = jnp.asarray((np.arange(span)[:, None] // 128 == np.arange(128)[None, :]).astype(np.float32), BF16)
    hops = z_size - 1
    gate_shape = gate.shape[1:]
    out_shape = (out.shape[1], out.shape[2] // 2)
    shape = jax.ShapeDtypeStruct
    dma = pltpu.SemaphoreType.DMA
    return pl.pallas_call(
        functools.partial(backward_kernel, chunks, z_size, states, rank, skip_row),
        grid=(chunks,),
        in_specs=[
            block(seqs, width),
            block(seqs, width),
            block(seqs, width),
            block(seqs, width),
            flat(wide),
            block(seqs, 128),
            pl.BlockSpec((STEPS // 2, states, 2 * seqs, width), lambda i: (chunks - 1 - i, 0, 0, 0)),
            whole(states, seqs, width),
            whole(span, 128),
            whole(*params.shape),
            pl.BlockSpec((width, rank), lambda i: (0, wide // rank)),
            any_space,
            any_space,
        ],
        out_specs=[
            block(seqs, width),
            flat(wide),
            whole(states, seqs, width),
            whole(width, rank),
            whole(seqs, width),
            whole(seqs, width),
            whole(*gate_shape),
            whole(*out_shape),
        ],
        out_shape=[
            shape(dt.shape, F32),
            shape((length * seqs, wide), BF16),
            shape((states, seqs, width), F32),
            shape((width, rank), F32),
            shape((seqs, width), F32),
            shape((seqs, width), F32),
            shape(gate_shape, BF16),
            shape(out_shape, BF16),
        ],
        scratch_shapes=[
            pltpu.VMEM((states, seqs, width), F32),
            pltpu.VMEM((states, seqs, width), F32),
            pltpu.VMEM((states, seqs, width), F32),
            pltpu.VMEM((2, width // 128 // TOGETHER, rows, span), BF16),
            pltpu.VMEM((STEPS, seqs, wide - rank), F32),
            pltpu.VMEM((rows, width), BF16),
            pltpu.VMEM(gate.shape, BF16),
            pltpu.VMEM(out.shape[:1] + out_shape, BF16),
            pltpu.VMEM((hops,) + gate_shape, BF16),
            pltpu.VMEM((hops,) + out_shape, BF16),
            pltpu.VMEM((hops,) + gate_shape, BF16),
            pltpu.VMEM((hops,) + out_shape, BF16),
            dma((2,)),
            dma((hops, 2)),
            dma((hops, 2)),
            dma((hops, 2)),
            dma((hops, 2)),
        ],
        cost_estimate=busy(80),
        compiler_params=pltpu.CompilerParams(
            collective_id=4, has_side_effects=True, vmem_limit_bytes=62 << 20
        ),
    )(dt, x, ds, pre, selection, keep, hist, last, ones, params, step_w, gate, out)


def last_kernel(
    z_size,
    taps,
    part_ref,
    keep_ref,
    mats_ref,
    params_ref,
    gate_fin,
    out_fin,
    da_ref,
    gstep_ref,
    bias_ref,
    skip_ref,
    tokens_ref,
    cot_ref,
    gain_ref,
    bx_hbm,
    cin_hbm,
    normed_hbm,
    conv_hbm,
    gate_hbm,
    bgi_hbm,
    gout_hbm,
    tgrad_ref,
    both_gate,
    both_conv,
    out_ref,
    small_out,
    vec_out,
    gain_out,
    chosen,
    from_sib,
    stage,
    got,
    bx,
    cin,
    picked,
    conv_w,
    gate_w,
    bgi,
    turned,
    bci,
    gsel,
    sums,
    columns,
    own_back,
    sib_stage,
    sib_back,
    ring_got,
    own_small,
    own_vec,
    own_conv,
    up_small,
    up_vec,
    up_conv,
    down_small,
    down_vec,
    down_conv,
    own_out,
    up_out,
    down_out,
    fin_conv,
    gain_parts,
    gain_got,
    gain_half,
    gain_pair,
    local_sem,
    column_sem,
    sw_s,
    sw_r,
    rs_s,
    rs_r,
    ag_s,
    ag_r,
    fw_s,
    fw_r,
    sib_send,
    sib_recv,
    ring_send,
    ring_recv,
    up_send,
    up_recv,
    down_send,
    down_recv,
    out_us,
    out_ur,
    out_ds,
    out_dr,
    swap_send,
    swap_recv,
    x_send,
    x_recv,
    gain_send,
    gain_recv,
):
    me = place()
    x, y, z, c = me["x"], me["y"], me["z"], me["c"]
    shares = z_size * 4
    share = z * 4 + y * 2 + c
    corner = y * 2 + c
    sibling = {"c": 1 - c}
    over_x = {"x": 1 - x}
    length, width = tokens_ref.shape
    chans = bx.shape[2]
    rows_in = both_gate.shape[2]
    half = own_out.shape[1]
    hops = z_size - 1
    wide = part_ref.shape[3]
    out_line, out_settle, out_sent = z_sums(
        z, z_size, (own_out,), (up_out,), (down_out,), (out_us, out_ur, out_ds, out_dr), (16,)
    )
    greet(plane_others(me) + z_only(me, shares))

    loads = [
        pltpu.make_async_copy(src, dst, local_sem.at[i])
        for i, (src, dst) in enumerate(
            [
                (cin_hbm, cin.at[pl.ds(3, length)]),
                (bx_hbm, bx.at[pl.ds(0, length)]),
                (bgi_hbm, bgi),
                (conv_hbm, conv_w),
                (gate_hbm, gate_w),
            ]
        )
    ]
    later = pl.ds(own_out.shape[2], own_out.shape[2])
    out_load = pltpu.make_async_copy(gout_hbm.at[:, :, later], own_out, local_sem.at[6])
    out_load.start()

    fine = 4
    block = length // 8

    def taps_of(lanes):
        return [
            jnp.broadcast_to(params_ref[taps - 1 - j : taps - j, lanes], (8, 128)) for j in range(taps)
        ]

    def activate(b, carry):
        t0 = b * block

        def convolve(i, carry):
            for g in range(chans // 128):
                lanes = pl.ds(g * 128, 128)
                tap = taps_of(lanes)
                offset = jnp.broadcast_to(params_ref[taps : taps + 1, lanes], (8, 128))
                taken = []
                slopes = []
                for j in range(fine):
                    t = t0 + i * fine + j
                    total = tap[3] * cin[t, :, lanes] * keep_ref[jnp.maximum(t - 2, 0)]
                    total = (total + tap[2] * cin[t + 1, :, lanes]) * keep_ref[jnp.maximum(t - 1, 0)]
                    total = (total + tap[1] * cin[t + 2, :, lanes]) * keep_ref[t]
                    v = total + tap[0] * cin[t + 3, :, lanes] + offset
                    s = sigmoid(v)
                    silu = v * s
                    taken.append(silu)
                    slopes.append(s + silu * (1.0 - s))
                rows = pl.ds(pl.multiple_of(i * fine * 8, fine * 8), fine * 8)
                picked[b, rows, lanes] = jnp.concatenate(taken, axis=0).astype(BF16)
                bci[b, rows, lanes] = jnp.concatenate(slopes, axis=0).astype(BF16)
            return carry

        lax.fori_loop(0, block // fine, convolve, 0)
        return carry

    swap = remote(part_ref.at[:, 1 - c], from_sib, sw_s.at[0], sw_r.at[0], sibling)
    swap.start()
    for copy in loads:
        copy.start()
    out_load.wait()
    out_line(0, 0)
    cin[0:3] = jnp.zeros((3, 8, chans), F32)
    bx[length : length + 3] = jnp.zeros((3, 8, chans), F32)
    sums[...] = jnp.zeros_like(sums)
    gsel[...] = jnp.zeros_like(gsel)
    swap.wait()
    mine = x * 2 + y
    chips = [((x + d // 2) % 2, (y + d % 2) % 2) for d in (1, 2, 3)]
    sends = []
    for k in (2, 1, 0):
        ox, oy = chips[k]
        j = ox * 2 + oy
        stage[k] = (part_ref[j, c].astype(F32) + from_sib[j].astype(F32)).astype(BF16)
        copy = remote(stage.at[k], got.at[k], rs_s.at[k], rs_r.at[k], {"x": ox, "y": oy})
        copy.start()
        sends.append(copy)
    loads[0].wait()
    lax.fori_loop(0, 8, activate, 0)
    total = part_ref[mine, c].astype(F32) + from_sib[mine].astype(F32)
    if hops > 1:
        out_line(1, 0)
    for copy in sends:
        copy.wait()
    for k in range(3):
        total = total + got[k].astype(F32)
    chosen[mine, c] = total.astype(BF16)
    here = chosen.at[mine, c]
    spreads = []
    for k in (2, 1, 0):
        ox, oy = chips[k]
        copy = remote(here, here, ag_s.at[k], ag_r.at[k], {"x": ox, "y": oy})
        copy.start()
        spreads.append((k, copy))
    forwards = [remote(here, here, fw_s.at[3], fw_r.at[3], sibling)]
    forwards[0].start()

    def corner_sends(src, dst, index):
        out = []
        for e in range(1, 8):
            to = (corner + e % 4) % 4
            out.append(
                remote(
                    src.at[pl.ds(pl.multiple_of(to * rows_in, rows_in), rows_in)],
                    dst.at[x, corner],
                    swap_send.at[index, e - 1],
                    swap_recv.at[index, e - 1],
                    {"x": (x + e // 4) % 2, "y": to // 2, "c": to % 2},
                )
            )
        return out

    gate_swaps = corner_sends(gate_fin, both_gate, 0)
    conv_swaps = corner_sends(fin_conv, both_conv, 1)
    both_gate[x, corner] = gate_fin[pl.ds(pl.multiple_of(corner * rows_in, rows_in), rows_in)]
    out_ref[x, :, : own_out.shape[2]] = out_fin[...]
    out_x = remote(out_ref.at[x], out_ref.at[x], x_send.at[0], x_recv.at[0], over_x)
    for k, copy in reversed(spreads):
        copy.wait_recv()
        ox, oy = chips[k]
        there = chosen.at[ox * 2 + oy, c]
        forwards.append(remote(there, there, fw_s.at[k], fw_r.at[k], sibling))
        forwards[-1].start()
    for copy in loads[1:]:
        copy.wait()
    for _, copy in spreads:
        copy.wait_send()
    for copy in forwards:
        copy.wait()
    for copy in gate_swaps:
        copy.start()
    for tau in range(2, hops):
        out_line(tau, 0)

    def select(b, carry):
        back = chosen[b // 2, b % 2]
        t0 = b * block
        bx[pl.ds(t0, block)] += dot_nt(back, mats_ref[:, :wide]).reshape(block, 8, chans)

        def convolve(i, carry):
            for g in range(chans // 128):
                lanes = pl.ds(g * 128, 128)
                acc = [sums[r, :, lanes] for r in range(taps + 1)]
                slopes = bci[b, pl.ds(pl.multiple_of(i * fine * 8, fine * 8), fine * 8), lanes].astype(F32)
                for j in range(fine):
                    t = t0 + i * fine + j
                    k0 = keep_ref[t]
                    k1 = k0 * keep_ref[jnp.maximum(t - 1, 0)]
                    k2 = k1 * keep_ref[jnp.maximum(t - 2, 0)]
                    back = bx[t, :, lanes] * slopes[j * 8 : (j + 1) * 8]
                    bx[t, :, lanes] = back
                    acc[0] = acc[0] + back * cin[t + 3, :, lanes]
                    acc[1] = acc[1] + back * (cin[t + 2, :, lanes] * k0)
                    acc[2] = acc[2] + back * (cin[t + 1, :, lanes] * k1)
                    acc[3] = acc[3] + back * (cin[t, :, lanes] * k2)
                    acc[4] = acc[4] + back
                for r in range(taps + 1):
                    sums[r, :, lanes] = acc[r]
            return carry

        lax.fori_loop(0, block // fine, convolve, 0)
        gsel[...] += dot_tn(picked[b], back)
        return carry

    lax.fori_loop(0, 8, select, 0)

    def unfold(b, carry):
        t0 = b * block

        def convolve(i, carry):
            for g in range(chans // 128):
                lanes = pl.ds(g * 128, 128)
                tap = taps_of(lanes)
                for j in range(fine):
                    t = t0 + i * fine + j
                    total = tap[3] * bx[t + 3, :, lanes] * keep_ref[jnp.minimum(t + 3, length - 1)]
                    total = (total + tap[2] * bx[t + 2, :, lanes]) * keep_ref[
                        jnp.minimum(t + 2, length - 1)
                    ]
                    total = (total + tap[1] * bx[t + 1, :, lanes]) * keep_ref[
                        jnp.minimum(t + 1, length - 1)
                    ]
                    turned[i * fine + j, :, lanes] = total + tap[0] * bx[t, :, lanes]
            return carry

        lax.fori_loop(0, block // fine, convolve, 0)
        bci[:, pl.ds(pl.multiple_of(t0, block), block), :] = jnp.swapaxes(turned[...], 0, 1).astype(BF16)
        return carry

    def column(i, slot):
        zz = jnp.where(z * 2 < z_size, z_size - 1 - i, i)
        cols = pl.ds(pl.multiple_of(zz * 4 * rows_in, 4 * rows_in), 4 * rows_in)
        return zz, pltpu.make_async_copy(normed_hbm.at[:, :, cols], columns.at[slot], column_sem.at[slot])

    column(0, 0)[1].start()
    out_settle(0, out_ref.at[x, :, later])
    out_x.start()
    lax.fori_loop(0, 8, unfold, 0)

    owns = (own_small, own_vec, own_conv)
    line, settle, sent = z_sums(
        z,
        z_size,
        owns,
        (up_small, up_vec, up_conv),
        (down_small, down_vec, down_conv),
        (up_send, up_recv, down_send, down_recv),
        (16, 16, 64),
    )

    rates = -jnp.exp(params_ref[taps + 3 : taps + 3 + da_ref.shape[0], :])
    vectors = (
        [jnp.sum(sums[taps - 1 - r], axis=0, keepdims=True) for r in range(taps)]
        + [
            jnp.sum(sums[taps], axis=0, keepdims=True),
            jnp.sum(bias_ref[...], axis=0, keepdims=True),
            jnp.sum(skip_ref[...], axis=0, keepdims=True),
        ]
        + [jnp.sum(da_ref[...], axis=1) * rates]
    )
    used = taps + 3 + da_ref.shape[0]
    vectors = jnp.concatenate(
        vectors + [jnp.zeros((own_vec.shape[1] - used, chans), F32)], axis=0
    ).astype(BF16)
    for zz in range(z_size):
        own_vec[zz] = vectors[:, zz * half : (zz + 1) * half]
        own_small[zz, :, :wide] = gsel[zz * half : (zz + 1) * half, :].astype(BF16)
        own_small[zz, :, wide:] = gstep_ref[zz * half : (zz + 1) * half, :].astype(BF16)

    at = ring_at(x, y)
    step = 1 + 2 * c
    sib_step = 3 - 2 * c
    nx, ny = ring_chip((at + step) % RING)
    following = {"x": nx, "y": ny}

    def grad_column(i):
        slot = i % 2
        zz, copy = column(i, slot)
        copy.wait()
        if i + 1 < z_size:
            column(i + 1, 1 - slot)[1].start()
        tall = columns[slot].reshape(8 * length, 4 * rows_in)
        own_conv[zz] = dot_tn(tall, bci[...].reshape(8 * length, chans)).astype(BF16)

    def back_block(dst, p, core):
        cx, cy = ring_chip(p % RING)
        s = cx * 4 + cy * 2 + core

        def cols(i, carry):
            n = pl.ds(pl.multiple_of(i * 512, 512), 512)
            total = dot_nt(bci[s], conv_w[n, :]) + dot_nt(bgi[s], gate_w[n, :])
            dst[:, n] = total.astype(BF16)
            return carry

        lax.fori_loop(0, width // 512, cols, 0)

    def cross(k):
        slot = k % 2
        return remote(sib_stage.at[slot], sib_back.at[k], sib_send.at[k], sib_recv.at[k], sibling)

    def ring(k, p):
        r = pl.ds(p * (length // 2), length // 2)
        return remote(
            own_back.at[k, r], ring_got.at[k, r], ring_send.at[k, p], ring_recv.at[k, p], following
        )

    def blocks_for(k):
        if k >= 2:
            cross(k - 2).wait_send()
        back_block(sib_stage.at[k % 2], at + sib_step * (RING - 1 - k), 1 - c)
        cross(k).start()
        back_block(own_back.at[k], at + step * (RING - 1 - k), c)

    def ring_step(k):
        cross(k).wait_recv()
        srcs = [own_back.at[k], sib_back.at[k]]
        if k:
            for p in range(2):
                ring(k - 1, p).wait_recv()
            srcs.append(ring_got.at[k - 1])
        add_rows(own_back.at[k], srcs, 16)
        for p in range(2):
            ring(k, p).start()

    def ring_end():
        last = RING - 1
        cross(last).wait_recv()
        for p in range(2):
            ring(last - 1, p).wait_recv()
        rows = 16

        def body(i, total):
            r = pl.ds(pl.multiple_of(i * rows, rows), rows)
            back = (
                own_back[last, r].astype(F32)
                + sib_back[last, r].astype(F32)
                + ring_got[last - 1, r].astype(F32)
            )
            values = tokens_ref[r].astype(F32)
            rstd = lax.rsqrt(jnp.mean(values * values, axis=-1, keepdims=True) + epsilon)
            scaled = back * gain_ref[0:1, :]
            inner = jnp.mean(scaled * values, axis=-1, keepdims=True)
            grad = cot_ref[r].astype(F32) + rstd * scaled - values * (rstd * rstd * rstd * inner)
            tgrad_ref[r] = grad.astype(BF16)
            terms = back * values * rstd
            return total + terms[:8] + terms[8:]

        total = lax.fori_loop(0, length // rows, body, jnp.zeros((8, width), F32))
        total = jnp.broadcast_to(jnp.sum(total, axis=0, keepdims=True), (8, width))
        piece = gain_parts.shape[2]
        for f in range(shares):
            gain_parts[f] = total[:, f * piece : (f + 1) * piece]
        gain_got[share] = gain_parts[share]

    gains = []
    for k in range(1, shares):
        f = (share + k) % shares
        gains.append(
            remote(
                gain_parts.at[f], gain_got.at[share], gain_send.at[k - 1], gain_recv.at[k - 1], share_at(f)
            )
        )

    def lines(tau):
        for j in (2, 0, 1):
            line(tau, j)

    blocks_for(0)
    ring_step(0)
    grad_column(0)
    lines(0)
    for i in range(1, z_size):
        grad_column(i)
    blocks_for(1)
    ring_step(1)
    blocks_for(2)
    lines(1)
    blocks_for(3)
    ring_step(2)
    for tau in range(2, hops):
        lines(tau)

    settle(2, fin_conv)
    for copy in conv_swaps:
        copy.start()
    ring_end()
    for copy in gains:
        copy.start()
    both_conv[x, corner] = fin_conv[pl.ds(pl.multiple_of(corner * rows_in, rows_in), rows_in)]
    settle(0, small_out.at[x])
    settle(1, vec_out.at[x])
    small_x = remote(small_out.at[x], small_out.at[x], x_send.at[2], x_recv.at[2], over_x)
    vec_x = remote(vec_out.at[x], vec_out.at[x], x_send.at[3], x_recv.at[3], over_x)
    small_x.start()
    vec_x.start()

    for copy in gains:
        copy.wait()
    gain_half[...] = jnp.sum(gain_got[...], axis=0)
    gain_x = remote(gain_half, gain_pair, x_send.at[5], x_recv.at[5], over_x)
    gain_x.start()
    for copy in gate_swaps:
        copy.wait()
    gain_x.wait()
    gain_out[...] = gain_half[...] + gain_pair[...]
    for copy in conv_swaps:
        copy.wait()
    for copy in (out_x, small_x, vec_x):
        copy.wait()
    for j in range(3):
        sent(j)
    out_sent(0)
    for k in range(RING - 1):
        for p in range(2):
            ring(k, p).wait_send()
    for k in range(2, RING):
        cross(k).wait_send()


def last_part(
    z_size,
    taps,
    part,
    keep,
    mats,
    params,
    gate_fin,
    out_fin,
    gout,
    da,
    gstep,
    bias,
    skip,
    tokens,
    cot,
    gain,
    bx,
    cin,
    normed,
    conv,
    gate,
    bgi,
):
    length, width = tokens.shape
    chans = bx.shape[2]
    shares = z_size * 4
    hops = z_size - 1
    rows_in = gate_fin.shape[0] // 4
    half = gout.shape[1]
    wide = part.shape[3]
    any_space = pl.BlockSpec(memory_space=pl.ANY)
    vmem = pl.BlockSpec(memory_space=pltpu.VMEM)
    dma = pltpu.SemaphoreType.DMA
    shape = jax.ShapeDtypeStruct
    block = (length, width)
    slabs = [(half, mats.shape[1]), (params.shape[0], half), (4 * rows_in, chans)]
    bufs = lambda n: [pltpu.VMEM((n,) + s, BF16) for s in slabs]
    both = shape((2, 4, rows_in, chans), BF16)
    piece = (8, width // shares)
    few = (length, wide)
    late_out = (half, width // 2)
    return pl.pallas_call(
        functools.partial(last_kernel, z_size, taps),
        in_specs=[vmem] * 13 + [any_space] * 7,
        out_specs=[vmem] * 7,
        out_shape=[
            shape(tokens.shape, BF16),
            both,
            both,
            shape((2,) + gout.shape[1:], BF16),
            shape((2,) + slabs[0], BF16),
            shape((2,) + slabs[1], BF16),
            shape(piece, F32),
        ],
        scratch_shapes=[
            pltpu.VMEM((4, 2) + few, BF16),
            pltpu.VMEM((4,) + few, BF16),
            pltpu.VMEM((3,) + few, BF16),
            pltpu.VMEM((3,) + few, BF16),
            pltpu.VMEM((length + 3, 8, chans), F32),
            pltpu.VMEM((length + 3, 8, chans), F32),
            pltpu.VMEM((8, length, chans), BF16),
            pltpu.VMEM(conv.shape, BF16),
            pltpu.VMEM(gate.shape, BF16),
            pltpu.VMEM(bgi.shape, BF16),
            pltpu.VMEM((length // 8, 8, chans), F32),
            pltpu.VMEM(bgi.shape, BF16),
            pltpu.VMEM((chans, wide), F32),
            pltpu.VMEM((taps + 1, 8, chans), F32),
            pltpu.VMEM((2, 8, length, 4 * rows_in), BF16),
            pltpu.VMEM((RING,) + block, BF16),
            pltpu.VMEM((2,) + block, BF16),
            pltpu.VMEM((RING,) + block, BF16),
            pltpu.VMEM((RING - 1,) + block, BF16),
        ]
        + bufs(z_size)
        + bufs(hops)
        + bufs(hops)
        + [
            pltpu.VMEM((z_size,) + late_out, BF16),
            pltpu.VMEM((hops,) + late_out, BF16),
            pltpu.VMEM((hops,) + late_out, BF16),
            pltpu.VMEM(slabs[2], BF16),
            pltpu.VMEM((shares,) + piece, F32),
            pltpu.VMEM((shares,) + piece, F32),
            pltpu.VMEM(piece, F32),
            pltpu.VMEM(piece, F32),
            dma((7,)),
            dma((2,)),
            dma((1,)),
            dma((1,)),
        ]
        + [dma((3,))] * 4
        + [dma((4,))] * 2
        + [dma((RING,))] * 2
        + [dma((RING - 1, 2))] * 2
        + [dma((hops, 3))] * 4
        + [dma((hops, 1))] * 4
        + [dma((2, 7))] * 2
        + [dma((6,))] * 2
        + [dma((shares - 1,))] * 2,
        cost_estimate=busy(120),
        compiler_params=pltpu.CompilerParams(
            collective_id=3, has_side_effects=True, vmem_limit_bytes=63 << 20
        ),
    )(
        part,
        keep,
        mats,
        params,
        gate_fin,
        out_fin,
        da,
        gstep,
        bias,
        skip,
        tokens,
        cot,
        gain,
        bx,
        cin,
        normed,
        conv,
        gate,
        bgi,
        gout,
    )


def close_kernel(
    taps,
    wide,
    tokens_ref,
    sum_ref,
    mats_ref,
    vec_ref,
    weight_ref,
    gate_ref,
    conv_ref,
    layer_ref,
    in_ref,
    taps_ref,
    offset_ref,
    select_ref,
    step_ref,
    bias_ref,
    decay_ref,
    skip_ref,
    out_ref,
):
    layer_ref[...] = (tokens_ref[...].astype(F32) + sum_ref[...].astype(F32)).astype(BF16)
    half = mats_ref.shape[1]
    for xx in range(2):
        rows = pl.ds(xx * half, half)
        select_ref[rows, :] = mats_ref[xx, :, : select_ref.shape[1]].astype(F32)
        step_ref[rows, :] = mats_ref[xx, :, wide:].astype(F32)
        out_ref[rows, :] = weight_ref[xx].astype(F32)
    z_size = conv_ref.shape[3] // half
    for first, both in ((0, conv_ref), (in_ref.shape[1] // 2, gate_ref)):
        for zz in range(z_size):
            for j in range(4):
                for xx in range(2):
                    col = first + (zz * 4 + j) * 2 * half + xx * half
                    in_ref[:, col : col + half] = both[xx, j, :, zz * half : (zz + 1) * half].astype(F32)
    vectors = jnp.concatenate([vec_ref[0].astype(F32), vec_ref[1].astype(F32)], axis=1)
    offset_ref[...] = vectors[taps : taps + 1, :]
    bias_ref[...] = vectors[taps + 1 : taps + 2, :]
    skip_ref[...] = vectors[taps + 2 : taps + 3, :]
    tall = vectors.T
    taps_ref[...] = tall[:, :taps]
    decay_ref[...] = tall[:, taps + 3 : taps + 3 + decay_ref.shape[1]]


def close(taps, states, select_width, tokens, layer_sum, mats, vectors, weight, gate, conv):
    rows = 2 * mats.shape[1]
    wide = select_width + -select_width % 128
    rank = mats.shape[2] - wide
    vmem = pl.BlockSpec(memory_space=pltpu.VMEM)
    shape = jax.ShapeDtypeStruct
    return pl.pallas_call(
        functools.partial(close_kernel, taps, wide),
        in_specs=[vmem] * 7,
        out_specs=[vmem] * 10,
        out_shape=[
            shape(tokens.shape, BF16),
            shape((gate.shape[2], 16 * gate.shape[3]), F32),
            shape((rows, taps), F32),
            shape((1, rows), F32),
            shape((rows, select_width), F32),
            shape((rows, rank), F32),
            shape((1, rows), F32),
            shape((rows, states), F32),
            shape((1, rows), F32),
            shape((rows, weight.shape[2]), F32),
        ],
        compiler_params=pltpu.CompilerParams(vmem_limit_bytes=60 << 20),
    )(tokens, layer_sum, mats, vectors, weight, gate, conv)


def shards(
    tokens,
    doc_ids,
    norm_gain,
    in_weight,
    conv_taps,
    conv_offset,
    select_weight,
    step_weight,
    step_bias,
    decay_log,
    skip_gain,
    out_weight,
    cotangent,
):
    z_size = lax.axis_size("z")
    rh_size = lax.axis_size("rh")
    seqs = 8
    length = doc_ids.shape[1]
    width = tokens.shape[1]
    in_rows = in_weight.shape[0]
    rows = out_weight.shape[0]
    half = rows // 2
    chans = half * z_size
    taps = conv_taps.shape[1]
    rank = step_weight.shape[1]
    states = decay_log.shape[1]
    x_at = lax.axis_index("x")

    def own_half(w):
        return lax.dynamic_slice_in_dim(w, x_at * half, half, 0)

    spare = -(rank + 2 * states) % 128
    wide = rank + 2 * states + spare
    vectors = jnp.concatenate(
        [
            own_half(conv_taps),
            own_half(conv_offset)[:, None],
            own_half(step_bias)[:, None],
            own_half(skip_gain)[:, None],
            own_half(decay_log),
        ],
        axis=1,
    ).T
    vectors = jnp.pad(vectors, ((0, -vectors.shape[0] % 32), (0, 0)))
    weight_in = in_weight
    if half % 128:
        columns = lax.dynamic_index_in_dim(
            in_weight.reshape(in_rows, 2, z_size, 4, 2, half), x_at, 4, keepdims=False
        )
        weight_in = columns.transpose(1, 3, 0, 2, 4).reshape(2, 4, in_rows, chans)
    (
        all_normed,
        all_cot,
        w_conv,
        w_gate,
        w_out,
        w_mats,
        keep,
        conv_in,
        x,
        dt,
        pre,
        vectors,
        gains,
        selection,
    ) = front(
        z_size,
        taps,
        rank,
        tokens,
        norm_gain.reshape(1, -1),
        doc_ids,
        vectors,
        cotangent,
        weight_in,
        out_weight,
        select_weight,
        step_weight,
    )
    selection = selection.reshape(length * seqs, wide)

    hist, last, back_scan, back_gate_in, out_part, grad_out, grad_gate, w_gate, _ = scan_forward(
        z_size, rank, states, taps + 2, dt, x, selection, keep, all_normed, all_cot, w_gate, w_out, vectors
    )
    layer_sum = lax.psum_scatter(
        out_part.reshape(-1, width), PLANE, scatter_dimension=0, tiled=True
    )
    back_x, part, da, g_step, g_bias, g_skip, gate_fin, out_fin = scan_backward(
        z_size,
        rank,
        taps + 2,
        dt,
        x,
        back_scan,
        pre,
        selection,
        keep,
        hist,
        last,
        vectors,
        w_mats,
        grad_gate.reshape(z_size, -1, chans),
        grad_out.reshape(z_size, half, width),
    )
    tokens_grad, g_in_gate, g_in_conv, g_out, g_mats, g_vectors, g_gain = last_part(
        z_size,
        taps,
        part.reshape(4, 2, length, wide),
        keep,
        w_mats,
        vectors,
        gate_fin,
        out_fin,
        grad_out.reshape(z_size, half, width),
        da,
        g_step,
        g_bias,
        g_skip,
        tokens,
        cotangent,
        gains,
        back_x,
        conv_in,
        all_normed,
        w_conv,
        w_gate,
        back_gate_in,
    )
    if rh_size > 1:
        g_mats, g_vectors, g_in_gate, g_in_conv, g_out, g_gain = lax.psum(
            tuple(
                v.astype(F32) for v in (g_mats, g_vectors, g_in_gate, g_in_conv, g_out, g_gain)
            ),
            "rh",
        )
    layer_out, g_in, g_taps, g_offset, g_select, g_step, g_bias, g_decay, g_skip, g_out = close(
        taps, states, rank + 2 * states, tokens, layer_sum, g_mats, g_vectors, g_out, g_in_gate, g_in_conv
    )
    return (
        layer_out,
        tokens_grad,
        g_gain[0],
        g_in,
        g_taps,
        g_offset[0],
        g_select,
        g_step,
        g_bias[0],
        g_decay,
        g_skip[0],
        g_out,
    )


def solution(mesh):
    replicas = mesh.shape["replica"]
    shares = mesh.shape["fsdp"]
    grid = Mesh(
        mesh.devices.reshape(replicas // 2, 2, shares // 4, 2, 2), ("rh", "x", "z", "y", "c")
    )
    tok = ("rh", "x", "z", "y", "c")
    own = ("z", "y", "c")
    return jax.shard_map(
        shards,
        mesh=grid,
        in_specs=(
            P(tok, None),
            P(tok, None),
            P(own),
            P(own, None),
            P(own, None),
            P(own),
            P(own, None),
            P(own, None),
            P(own),
            P(own, None),
            P(own),
            P(own, None),
            P(tok, None),
        ),
        out_specs=(
            P(tok, None),
            P(tok, None),
            P(own),
            P(own, None),
            P(own, None),
            P(own),
            P(own, None),
            P(own, None),
            P(own),
            P(own, None),
            P(own),
            P(own, None),
        ),
        check_vma=False,
    )
```

```python
import functools

import jax
import jax.numpy as jnp
import numpy as np
from jax import lax
from jax.experimental import pallas as pl
from jax.experimental.pallas import tpu as pltpu
from jax.sharding import Mesh
from jax.sharding import PartitionSpec as P

F32 = jnp.float32
BF16 = jnp.bfloat16
epsilon = 1e-05
PLANE = ("x", "y", "c")
BIG = 1e30
STEPS = 32
COLUMNS = 512
INNER = 4
BACK_INNER = 8
TOGETHER = 4
LOG2E = 1.4426950408889634


def dot(a, b, dims):
    return lax.dot_general(a, b, (dims, ((), ())), preferred_element_type=F32)


def dot_nn(a, b):
    return dot(a, b, ((1,), (0,)))


def dot_tn(a, b):
    return dot(a, b, ((0,), (0,)))


def dot_nt(a, b):
    return dot(a, b, ((1,), (1,)))


def busy(micros):
    return pl.CostEstimate(flops=micros * 10**9, bytes_accessed=micros * 10**6, transcendentals=0)


MESH = pl.DeviceIdType.MESH
RING = 4


def place():
    return {a: lax.axis_index(a) for a in ("x", "z", "y", "c")}


def ring_chip(p):
    y = p // 2
    return (p + y) % 2, y


def ring_at(x, y):
    return 2 * y + (x + y) % 2


def share_at(f):
    return {"z": f // 4, "y": f // 2 % 2, "c": f % 2}


def remote(src, dst, send, recv, device):
    return pltpu.make_async_remote_copy(
        src_ref=src, dst_ref=dst, send_sem=send, recv_sem=recv, device_id=device, device_id_type=MESH
    )


def greet(devices):
    barrier = pltpu.get_barrier_semaphore()
    for device in devices:
        pl.semaphore_signal(barrier, inc=1, device_id=device, device_id_type=MESH)
    pl.semaphore_wait(barrier, len(devices))


def plane_others(me):
    out = []
    for dx in range(2):
        for dy in range(2):
            for dc in range(2):
                if dx + dy + dc:
                    out.append(
                        {"x": (me["x"] + dx) % 2, "y": (me["y"] + dy) % 2, "c": (me["c"] + dc) % 2}
                    )
    return out


def share_others(me, shares):
    f = me["z"] * 4 + me["y"] * 2 + me["c"]
    return [share_at((f + k) % shares) for k in range(1, shares)]


def z_only(me, shares):
    f = me["c"] + 2 * me["y"]
    out = []
    for dz in range(1, shares // 4):
        for k in range(4):
            out.append(
                {
                    "z": (me["z"] + dz) % (shares // 4),
                    "y": (f + k) % 4 // 2,
                    "c": (f + k) % 2,
                }
            )
    return out


def z_line(z, z_size, pieces, sems):
    up_s, up_r, down_s, down_r = sems

    def up(k):
        return [
            remote(p(z - k), p(z - k), up_s.at[k, j], up_r.at[k, j], {"z": z + 1})
            for j, p in enumerate(pieces)
        ]

    def down(k):
        return [
            remote(p(z + k), p(z + k), down_s.at[k, j], down_r.at[k, j], {"z": z - 1})
            for j, p in enumerate(pieces)
        ]

    def start(k):
        @pl.when((z < z_size - 1) & (z >= k))
        def _():
            for copy in up(k):
                copy.start()

        @pl.when((z > 0) & (z + k < z_size))
        def _():
            for copy in down(k):
                copy.start()

    def arrive(k):
        @pl.when(z > k)
        def _():
            for copy in up(k):
                copy.wait_recv()

        @pl.when(z + k < z_size - 1)
        def _():
            for copy in down(k):
                copy.wait_recv()

    def sent(k):
        @pl.when((z < z_size - 1) & (z >= k))
        def _():
            for copy in up(k):
                copy.wait_send()

        @pl.when((z > 0) & (z + k < z_size))
        def _():
            for copy in down(k):
                copy.wait_send()

    return start, arrive, sent


class Ring:
    def __init__(self, me, blocks, own, ring_send, ring_recv, sib_send, sib_recv):
        self.me, self.blocks, self.own = me, blocks, own
        self.sems = ring_send, ring_recv, sib_send, sib_recv
        self.at = ring_at(me["x"], me["y"])
        self.step = 1 + 2 * me["c"]
        nx, ny = ring_chip((self.at + self.step) % RING)
        self.following = {"x": nx, "y": ny}
        self.sibling = {"c": 1 - me["c"]}
        self.half = blocks.shape[1] // 2

    def slot(self, k):
        ox, oy = ring_chip((self.at + (RING - self.step) * k) % RING)
        return ox * 4 + oy * 2 + self.me["c"]

    def hop(self, k):
        out = []
        for p in range(2):
            rows = pl.ds(p * self.half, self.half)
            dst = self.blocks.at[self.slot(k), rows]
            src = self.own.at[rows] if k == 0 and self.own is not None else dst
            out.append(remote(src, dst, self.sems[0].at[k, p], self.sems[1].at[k, p], self.following))
        return out

    def cross(self, k):
        dst = self.blocks.at[self.slot(k)]
        src = self.own if k == 0 and self.own is not None else dst
        return remote(src, dst, self.sems[2].at[k], self.sems[3].at[k], self.sibling)

    def start(self, k):
        if k < RING - 1:
            for copy in self.hop(k):
                copy.start()
        self.cross(k).start()

    def arrive(self, k):
        for copy in self.hop(k):
            copy.wait_recv()

    def sent(self, k):
        if k < RING - 1:
            for copy in self.hop(k):
                copy.wait_send()
        self.cross(k).wait()


def sigmoid(v):
    return 0.5 + 0.5 * jnp.tanh(0.5 * v)


def softplus(v):
    e = jnp.exp(-jnp.abs(v))
    small = e * (1.0 - e * (0.5 - e * (1.0 / 3.0)))
    return jnp.maximum(v, 0.0) + jnp.where(e < 1e-3, small, jnp.log(1.0 + e))


def front_kernel(
    z_size,
    taps,
    rank,
    tokens_ref,
    gain_ref,
    ids_ref,
    rows_ref,
    cot_ref,
    in_ref,
    out_ref,
    select_ref,
    step_ref,
    normed_hbm,
    cot_all,
    conv_hbm,
    gate_all,
    out_all,
    mats_hbm,
    keep_hbm,
    cin_hbm,
    x_hbm,
    dt_hbm,
    pre_hbm,
    params,
    gain_all,
    selection,
    normed_all,
    conv_w,
    mats,
    rows_all,
    gain_got,
    ids_all,
    proj,
    cin,
    xs,
    picked,
    part,
    dts,
    pres,
    keep,
    first,
    from_sib,
    stage,
    got,
    local_sem,
    own_sem,
    gain_send,
    gain_recv,
    ids_send,
    ids_recv,
    conv_send,
    conv_recv,
    gate_send,
    gate_recv,
    ring_send,
    ring_recv,
    sib_send,
    sib_recv,
    cot_ring_send,
    cot_ring_recv,
    cot_sib_send,
    cot_sib_recv,
    a_us,
    a_ur,
    a_ds,
    a_dr,
    m_us,
    m_ur,
    m_ds,
    m_dr,
    b_us,
    b_ur,
    b_ds,
    b_dr,
    sw_s,
    sw_r,
    rs_s,
    rs_r,
    ag_s,
    ag_r,
    fw_s,
    fw_r,
):
    me = place()
    x, y, z, c = me["x"], me["y"], me["z"], me["c"]
    shares = z_size * 4
    share = z * 4 + y * 2 + c
    corner = y * 2 + c
    seq = x * 4 + y * 2 + c
    sibling = {"c": 1 - c}
    length, width = tokens_ref.shape
    chans = conv_w.shape[1]
    rows_in = width // shares
    half = chans // z_size
    hops = z_size - 1
    branch = 8 * chans
    greet(plane_others(me) + z_only(me, shares))

    def rows_at(ref, index, count):
        return ref.at[pl.ds(pl.multiple_of(index * count, count), count)]

    def pieces(first, dst, to):
        rows = rows_at(dst, share, rows_in)
        if len(in_ref.shape) == 4:
            return [(in_ref.at[1 if first else 0, to], rows)]
        out = []
        for zz in range(z_size):
            col = first + (zz * 4 + to) * 2 * half + x * half
            src = in_ref.at[:, pl.ds(pl.multiple_of(col, half), half)]
            out.append((src, rows.at[:, pl.ds(zz * half, half)]))
        return out

    def corner_sends(first, dst, send, recv):
        out = []
        for k in range(1, 4):
            to = (corner + k) % 4
            for i, (src, there) in enumerate(pieces(first, dst, to)):
                out.append(
                    remote(
                        src, there, send.at[k - 1, i], recv.at[k - 1, i], {"y": to // 2, "c": to % 2}
                    )
                )
        return out

    gain_got[share] = jnp.broadcast_to(gain_ref[...].astype(F32), gain_got.shape[1:])
    ids_all[seq] = jnp.broadcast_to(ids_ref[...], ids_all.shape[1:])
    swaps = corner_sends(0, conv_w, conv_send, conv_recv)
    gates = corner_sends(branch, gate_all, gate_send, gate_recv)
    for copy in swaps:
        copy.start()
    gains = [
        remote(gain_got.at[share], gain_got.at[share], gain_send.at[k], gain_recv.at[k], device)
        for k, device in enumerate(share_others(me, shares))
    ]
    for copy in gains:
        copy.start()
    locals_ = [
        pltpu.make_async_copy(
            out_ref.at[pl.ds(pl.multiple_of(x * half, half), half)], rows_at(out_all, z, half), local_sem.at[3]
        ),
        pltpu.make_async_copy(cot_ref, cot_all.at[seq], local_sem.at[4]),
    ]
    conv_own = [
        pltpu.make_async_copy(src, there, own_sem.at[0, i])
        for i, (src, there) in enumerate(pieces(0, conv_w, corner))
    ]
    for i, (src, there) in enumerate(pieces(branch, gate_all, corner)):
        locals_.append(pltpu.make_async_copy(src, there, own_sem.at[1, i]))
    for copy in conv_own + locals_:
        copy.start()
    ids_copies = [
        remote(ids_all.at[seq], ids_all.at[seq], ids_send.at[k], ids_recv.at[k], device)
        for k, device in enumerate(plane_others(me))
    ]
    for copy in ids_copies:
        copy.start()
    rows_all[z] = rows_ref[...]
    mine_rows = pl.ds(pl.multiple_of(x * half, half), half)
    at_rows = pl.ds(pl.multiple_of(z * half, half), half)
    wide = mats.shape[1] - rank
    mats[at_rows, :wide] = jnp.concatenate(
        [
            select_ref[mine_rows, :],
            jnp.zeros((half, wide - select_ref.shape[1]), BF16),
        ],
        axis=1,
    )
    mats[at_rows, wide:] = step_ref[mine_rows, :]

    values = tokens_ref[...].astype(F32)
    rstd = lax.rsqrt(jnp.mean(values * values, axis=-1, keepdims=True) + epsilon)
    for copy in gains:
        copy.wait()
    piece = gain_ref.shape[1]
    for f in range(shares):
        cols = pl.ds(f * piece, piece)
        normed = tokens_ref[:, cols].astype(F32) * rstd * gain_got[f, 0:1, :]
        normed_all[seq, :, cols] = normed.astype(BF16)
    for f in range(shares):
        gain_all[:, f * piece : (f + 1) * piece] = gain_got[f]

    ring = Ring(me, normed_all, None, ring_send, ring_recv, sib_send, sib_recv)
    cot_ring = Ring(me, cot_all, cot_ref, cot_ring_send, cot_ring_recv, cot_sib_send, cot_sib_recv)
    ring.start(0)
    for copy in swaps:
        copy.wait()
    for copy in conv_own:
        copy.wait()
    a_start, a_arrive, a_sent = z_line(
        z,
        z_size,
        [
            lambda k: rows_at(conv_w, k, 4 * rows_in),
            lambda k: rows_all.at[k],
        ],
        (a_us, a_ur, a_ds, a_dr),
    )
    m_start, m_arrive, m_sent = z_line(
        z, z_size, [lambda k: rows_at(mats, k, half)], (m_us, m_ur, m_ds, m_dr)
    )
    b_start, b_arrive, b_sent = z_line(
        z,
        z_size,
        [lambda k: rows_at(gate_all, k, 4 * rows_in), lambda k: rows_at(out_all, k, half)],
        (b_us, b_ur, b_ds, b_dr),
    )
    a_start(0)
    for copy in gates:
        copy.start()

    for copy in ids_copies:
        copy.wait()
    ids = jnp.concatenate([ids_all[s, 0:1, :] for s in range(8)], axis=0).astype(F32)
    before = pltpu.roll(ids, 1, 1)
    lane = lax.broadcasted_iota(jnp.int32, ids.shape, 1)
    same = jnp.where((ids == before) & (lane > 0), 1.0, 0.0)
    for t in range(length):
        keep[t] = jnp.broadcast_to(same[:, t : t + 1], (8, 128))
    keep_copy = pltpu.make_async_copy(keep, keep_hbm, local_sem.at[5])
    keep_copy.start()

    for k in range(max(hops, RING - 1)):
        if k < hops:
            a_arrive(k)
            if k + 1 < hops:
                a_start(k + 1)
            if k:
                m_arrive(k - 1)
            m_start(k)
        if k < RING - 1:
            ring.arrive(k)
            ring.start(k + 1)
        if k == RING - 2:
            cot_ring.start(0)
    for copy in gates + locals_:
        copy.wait()
    b_start(0)
    for k in range(RING):
        ring.sent(k)
    outs = [
        pltpu.make_async_copy(normed_all, normed_hbm, local_sem.at[6]),
        pltpu.make_async_copy(conv_w, conv_hbm, local_sem.at[7]),
    ]
    for copy in outs:
        copy.start()
    for zz in range(z_size):
        params[:, zz * half : (zz + 1) * half] = rows_all[zz].astype(F32)

    def project(s, carry):
        proj[s] = dot_nn(normed_all[s], conv_w[...])
        return carry

    lax.fori_loop(0, 8, project, 0)
    m_arrive(hops - 1)
    cot_ring.arrive(0)
    cot_ring.start(1)

    cin[0:3] = jnp.zeros((3, 8, chans), F32)
    block = 32
    fine = 4

    def turn(i, carry):
        t0 = pl.multiple_of(i * block, block)
        cin[pl.ds(3 + t0, block)] = jnp.swapaxes(proj[:, pl.ds(t0, block), :], 0, 1)
        return carry

    lax.fori_loop(0, length // block, turn, 0)

    def convolve(i, carry):
        t0 = i * fine
        for g in range(chans // 128):
            lanes = pl.ds(g * 128, 128)
            tap = [jnp.broadcast_to(params[taps - 1 - j : taps - j, lanes], (8, 128)) for j in range(taps)]
            offset = jnp.broadcast_to(params[taps : taps + 1, lanes], (8, 128))
            chosen = []
            for j in range(fine):
                t = t0 + j
                total = tap[3] * cin[t, :, lanes] * keep[jnp.maximum(t - 2, 0)]
                total = (total + tap[2] * cin[t + 1, :, lanes]) * keep[jnp.maximum(t - 1, 0)]
                total = (total + tap[1] * cin[t + 2, :, lanes]) * keep[t]
                v = total + tap[0] * cin[t + 3, :, lanes] + offset
                chosen.append((v * sigmoid(v)).astype(BF16))
                xs[t, :, lanes] = chosen[-1].astype(F32)
            rows = pl.ds(pl.multiple_of(t0 * 8, fine * 8), fine * 8)
            picked[rows, lanes] = jnp.concatenate(chosen, axis=0)
        return carry

    lax.fori_loop(0, length // fine, convolve, 0)
    outs += [
        pltpu.make_async_copy(mats, mats_hbm, local_sem.at[8]),
        pltpu.make_async_copy(cin.at[pl.ds(3, length)], cin_hbm, local_sem.at[9]),
        pltpu.make_async_copy(xs, x_hbm, local_sem.at[10]),
    ]
    for copy in outs[2:]:
        copy.start()

    wide = part.shape[3]

    def select(b, carry):
        rows = pl.ds(pl.multiple_of(b * length, length), length)
        part[b // 2, b % 2] = dot_nn(picked[rows, :], mats[:, :wide])
        return carry

    lax.fori_loop(0, 8, select, 0)
    first[...] = part[:, 1 - c].astype(BF16)
    swap = remote(first, from_sib, sw_s.at[0], sw_r.at[0], sibling)
    swap.start()
    swap.wait()
    mine = x * 2 + y
    chips = [((x + d // 2) % 2, (y + d % 2) % 2) for d in (1, 2, 3)]
    sends = []
    for k in (2, 1, 0):
        ox, oy = chips[k]
        j = ox * 2 + oy
        stage[k] = (part[j, c] + from_sib[j].astype(F32)).astype(BF16)
        copy = remote(stage.at[k], got.at[k], rs_s.at[k], rs_r.at[k], {"x": ox, "y": oy})
        copy.start()
        sends.append(copy)
    total = part[mine, c] + from_sib[mine].astype(F32)
    for copy in sends:
        copy.wait()
    for k in range(3):
        total = total + got[k].astype(F32)
    selection[mine, c] = total.astype(BF16)
    here = selection.at[mine, c]
    spreads = []
    for k in (2, 1, 0):
        ox, oy = chips[k]
        copy = remote(here, here, ag_s.at[k], ag_r.at[k], {"x": ox, "y": oy})
        copy.start()
        spreads.append((k, copy))
    forwards = [remote(here, here, fw_s.at[3], fw_r.at[3], sibling)]
    forwards[0].start()
    b_arrive(0)
    if hops > 2:
        b_start(1)
    cot_ring.arrive(1)
    for k, copy in reversed(spreads):
        copy.wait_recv()
        ox, oy = chips[k]
        there = selection.at[ox * 2 + oy, c]
        forwards.append(remote(there, there, fw_s.at[k], fw_r.at[k], sibling))
        forwards[-1].start()
    for _, copy in spreads:
        copy.wait_send()
    for copy in forwards:
        copy.wait()
    cot_ring.start(2)

    bias = params[taps + 1 : taps + 2, :]

    def steps(i, carry):
        rows = 64
        per = length // rows
        b = i // per
        at = pl.ds(pl.multiple_of((i % per) * rows, rows), rows)
        v = dot_nt(selection[b // 2, b % 2, at, :rank], mats[:, wide : wide + rank]) + bias
        t = pl.ds(i * (rows // 8), rows // 8)
        pres[t] = v.reshape(rows // 8, 8, chans)
        dts[t] = softplus(v).reshape(rows // 8, 8, chans)
        return carry

    lax.fori_loop(0, length * 8 // 64, steps, 0)
    outs += [
        pltpu.make_async_copy(dts, dt_hbm, local_sem.at[11]),
        pltpu.make_async_copy(pres, pre_hbm, local_sem.at[12]),
    ]
    for copy in outs[5:]:
        copy.start()

    for k in range(1, hops - 1):
        b_arrive(k)
        if k + 1 < hops - 1:
            b_start(k + 1)
    cot_ring.arrive(2)
    cot_ring.start(3)
    for k in range(RING):
        cot_ring.sent(k)
    for k in range(hops):
        a_sent(k)
        m_sent(k)
    for k in range(hops - 1):
        b_sent(k)
    for copy in outs + [keep_copy]:
        copy.wait()


def front(z_size, taps, rank, tokens, gain, ids, rows, cot, weight_in, out, select, step):
    length, width = tokens.shape
    shares = z_size * 4
    half = rows.shape[1]
    chans = half * z_size
    wide = select.shape[1] + -select.shape[1] % 128
    cuts = 1 if weight_in.ndim == 4 else z_size
    any_space = pl.BlockSpec(memory_space=pl.ANY)
    vmem = pl.BlockSpec(memory_space=pltpu.VMEM)
    dma = pltpu.SemaphoreType.DMA
    hops = z_size - 1
    shape = jax.ShapeDtypeStruct
    everyone = (8,) + tokens.shape
    per_token = (length, 8, chans)
    block = (length, wide)
    return pl.pallas_call(
        functools.partial(front_kernel, z_size, taps, rank),
        in_specs=[vmem] * 5 + [any_space] + [vmem] * 3,
        out_specs=[any_space] * 11 + [vmem] * 3,
        out_shape=[
            shape(everyone, BF16),
            shape(everyone, BF16),
            shape((width, chans), BF16),
            shape((width, chans), BF16),
            shape((chans, width), BF16),
            shape((chans, wide + rank), BF16),
            shape((length, 8, 128), F32),
            shape(per_token, F32),
            shape(per_token, F32),
            shape(per_token, F32),
            shape(per_token, F32),
            shape((rows.shape[0], chans), F32),
            shape((8, width), F32),
            shape((4, 2) + block, BF16),
        ],
        scratch_shapes=[
            pltpu.VMEM(everyone, BF16),
            pltpu.VMEM((width, chans), BF16),
            pltpu.VMEM((chans, wide + rank), BF16),
            pltpu.VMEM((z_size,) + rows.shape, BF16),
            pltpu.VMEM((shares, 8, gain.shape[1]), F32),
            pltpu.VMEM((8, 8, length), ids.dtype),
            pltpu.VMEM((8, length, chans), F32),
            pltpu.VMEM((length + 3, 8, chans), F32),
            pltpu.VMEM(per_token, F32),
            pltpu.VMEM((length * 8, chans), BF16),
            pltpu.VMEM((4, 2) + block, F32),
            pltpu.VMEM(per_token, F32),
            pltpu.VMEM(per_token, F32),
            pltpu.VMEM((length, 8, 128), F32),
            pltpu.VMEM((4,) + block, BF16),
            pltpu.VMEM((4,) + block, BF16),
            pltpu.VMEM((3,) + block, BF16),
            pltpu.VMEM((3,) + block, BF16),
            dma((13,)),
            dma((2, cuts)),
            dma((shares - 1,)),
            dma((shares - 1,)),
            dma((7,)),
            dma((7,)),
        ]
        + [dma((3, cuts))] * 4
        + [dma((RING - 1, 2)), dma((RING - 1, 2)), dma((RING,)), dma((RING,))] * 2
        + [dma((hops, 2))] * 4
        + [dma((hops, 1))] * 4
        + [dma((hops, 2))] * 4
        + [dma((1,))] * 2
        + [dma((3,))] * 4
        + [dma((4,))] * 2,
        cost_estimate=busy(120),
        compiler_params=pltpu.CompilerParams(
            collective_id=0, has_side_effects=True, vmem_limit_bytes=60 << 20
        ),
    )(tokens, gain, ids, rows, cot, weight_in, out, select, step)


def add_rows(dst, srcs, rows):
    count = dst.shape[0] // rows

    def body(i, carry):
        at = pl.ds(pl.multiple_of(i * rows, rows), rows)
        total = srcs[0][at].astype(F32)
        for src in srcs[1:]:
            total = total + src[at].astype(F32)
        dst[at] = total.astype(dst.dtype)
        return carry

    lax.fori_loop(0, count, body, 0)


def fill_rates(rate_ref, params_ref, first):
    states = rate_ref.shape[0]
    rows = -LOG2E * jnp.exp(params_ref[first : first + states, :])
    for n in range(states):
        rate_ref[n] = jnp.broadcast_to(rows[n : n + 1, :], rate_ref.shape[1:])


def forward_kernel(
    z_size,
    chunks,
    states,
    rank,
    skip_row,
    dt_ref,
    x_ref,
    sel_ref,
    keep_ref,
    normed_ref,
    cot_ref,
    normed_col,
    cot_col,
    params_ref,
    gate_given,
    out_given,
    hist_ref,
    last_ref,
    ds_ref,
    bgi_ref,
    part_ref,
    gout_ref,
    ggate_ref,
    gate_all,
    out_all,
    rate_ref,
    h_ref,
    bc_ref,
    y_ref,
    ys_ref,
    gate_ref,
    bg_ref,
    gated_ref,
    gated_all,
    bgi_all,
    gate_w_ref,
    out_w_ref,
    load_sem,
    up_s,
    up_r,
    down_s,
    down_r,
):
    step = pl.program_id(0)
    me = place()
    z = me["z"]
    hops = z_size - 1
    slab_rows = gate_all.shape[0] // z_size
    half = out_all.shape[0] // z_size
    line_start, line_arrive, line_sent = z_line(
        z,
        z_size,
        [
            lambda k: gate_all.at[pl.ds(pl.multiple_of(k * slab_rows, slab_rows), slab_rows)],
            lambda k: out_all.at[pl.ds(pl.multiple_of(k * half, half), half)],
        ],
        (up_s, up_r, down_s, down_r),
    )

    @pl.when(step == 0)
    def _():
        greet([{"z": (z + 1) % z_size}, {"z": (z + z_size - 1) % z_size}])
        line_start(hops - 1)
        fill_rates(rate_ref, params_ref, skip_row + 1)
        h_ref[...] = jnp.zeros_like(h_ref)

    steps, seqs, width = dt_ref.shape
    groups = width // 128
    rows = steps * seqs
    @pl.when(step < chunks)
    def _():
        bc_ref[...] = sel_ref[:, rank:].astype(F32).reshape(bc_ref.shape)

        def body(tb, carry):
            t0 = tb * INNER
            bc = [bc_ref[t0 + i] for i in range(INNER)]
            off = [(1.0 - keep_ref[t0 + i]) * BIG for i in range(INNER)]
            for g in range(groups):
                lanes = pl.ds(g * 128, 128)
                dt = [dt_ref[t0 + i, :, lanes] for i in range(INNER)]
                dtm = [dt[i] + off[i] for i in range(INNER)]
                u = [dt[i] * x_ref[t0 + i, :, lanes] for i in range(INNER)]
                y = [None] * INNER
                for n in range(states):
                    h = h_ref[n, :, lanes]
                    rate = rate_ref[n, :, lanes]
                    before = []
                    for i in range(INNER):
                        before.append(h)
                        a = jnp.exp2(dtm[i] * rate)
                        h = a * h + u[i] * bc[i][:, n : n + 1]
                        term = h * bc[i][:, states + n : states + n + 1]
                        y[i] = term if y[i] is None else y[i] + term
                    for i in range(0, INNER, 2):
                        pair = jnp.concatenate(before[i : i + 2], axis=0).astype(BF16)
                        hist_ref[t0 // 2 + i // 2, n, :, lanes] = pair
                    h_ref[n, :, lanes] = h
                skip = params_ref[skip_row : skip_row + 1, lanes]
                for i in range(INNER):
                    y_ref[step * steps + t0 + i, :, lanes] = y[i] + skip * x_ref[t0 + i, :, lanes]
            return carry

        lax.fori_loop(0, steps // INNER, body, 0)
        last_ref[...] = h_ref[...]

    @pl.when(step == chunks)
    def _():
        line_arrive(hops - 1)
        line_sent(hops - 1)
        loads = [
            pltpu.make_async_copy(gate_all, gate_w_ref, load_sem.at[0]),
            pltpu.make_async_copy(out_all, out_w_ref, load_sem.at[1]),
        ]
        for copy in loads:
            copy.start()
        for copy in loads:
            copy.wait()

    @pl.when((step >= chunks) & (step < 2 * chunks))
    def _():
        normed = normed_ref[...].reshape(rows, normed_ref.shape[2])
        cot = cot_ref[...].reshape(rows, cot_ref.shape[2])
        gate_ref[...] = dot_nn(normed, gate_w_ref[...])
        bg_ref[...] = dot_nt(cot, out_w_ref[...]).astype(BF16).astype(F32)
        y = y_ref[pl.ds((step - chunks) * steps, steps)]
        ys_ref[...] = jnp.swapaxes(y, 0, 1).reshape(rows, width)
        fine = 16

        def gating(i, carry):
            r = pl.ds(pl.multiple_of(i * fine, fine), fine)
            v = gate_ref[r, :]
            bg = bg_ref[r, :]
            y = ys_ref[r, :]
            s = sigmoid(v)
            gate = v * s
            gated_ref[r, :] = (y * gate).astype(BF16)
            bg_ref[r, :] = bg * gate
            gate_ref[r, :] = bg * y * (s + gate * (1.0 - s))
            return carry

        lax.fori_loop(0, rows // fine, gating, 0)
        ds_ref[...] = jnp.swapaxes(bg_ref[...].reshape(seqs, steps, width), 0, 1)
        bgi = gate_ref[...].astype(BF16).reshape(bgi_ref.shape)
        bgi_ref[...] = bgi
        gated = gated_ref[...]
        part_ref[...] = dot_nn(gated, out_w_ref[...]).astype(BF16).reshape(part_ref.shape)
        at = pl.ds(pl.multiple_of((step - chunks) * steps, steps), steps)
        gated_all[:, at, :] = gated.reshape(bgi_ref.shape)
        bgi_all[:, at, :] = bgi

    @pl.when(step >= 2 * chunks)
    def _():
        tall = (gated_all.shape[0] * gated_all.shape[1], width)
        cols = (tall[0], normed_col.shape[2])
        gout_ref[...] = dot_tn(gated_all[...].reshape(tall), cot_col[...].reshape(cols)).astype(BF16)
        ggate_ref[...] = dot_tn(normed_col[...].reshape(cols), bgi_all[...].reshape(tall)).astype(BF16)


def scan_forward(
    z_size, rank, states, skip_row, dt, x, selection, keep, normed, cot, gate_w, out_w, params
):
    length, seqs, width = dt.shape
    model = normed.shape[2]
    wide = selection.shape[1]
    chunks = length // STEPS
    early = lambda i: jnp.minimum(i, chunks - 1)
    late = lambda i: jnp.clip(i - chunks, 0, chunks - 1)
    pieces = model // COLUMNS
    last_of = lambda i: jnp.maximum(i - 2 * chunks, 0)
    column = pl.BlockSpec((seqs, length, COLUMNS), lambda i: (0, 0, last_of(i)))
    block = lambda *tail: pl.BlockSpec((STEPS,) + tail, lambda i: (early(i),) + (0,) * len(tail))
    across = lambda n: pl.BlockSpec((seqs, STEPS, n), lambda i: (0, late(i), 0))
    any_space = pl.BlockSpec(memory_space=pl.ANY)
    dma = pltpu.SemaphoreType.DMA
    hops = z_size - 1
    whole = lambda *dims: pl.BlockSpec(dims, lambda i: (0,) * len(dims))
    rows = STEPS * seqs
    shape = jax.ShapeDtypeStruct
    return pl.pallas_call(
        functools.partial(forward_kernel, z_size, chunks, states, rank, skip_row),
        grid=(2 * chunks + pieces,),
        in_specs=[
            block(seqs, width),
            block(seqs, width),
            pl.BlockSpec((rows, wide), lambda i: (early(i), 0)),
            block(seqs, 128),
            across(model),
            across(model),
            column,
            column,
            whole(*params.shape),
            any_space,
            any_space,
        ],
        out_specs=[
            pl.BlockSpec((STEPS // 2, states, 2 * seqs, width), lambda i: (early(i), 0, 0, 0)),
            whole(states, seqs, width),
            pl.BlockSpec((STEPS, seqs, width), lambda i: (late(i), 0, 0)),
            across(width),
            across(model),
            pl.BlockSpec((width, COLUMNS), lambda i: (0, last_of(i))),
            pl.BlockSpec((COLUMNS, width), lambda i: (last_of(i), 0)),
            any_space,
            any_space,
        ],
        out_shape=[
            shape((length // 2, states, 2 * seqs, width), BF16),
            shape((states, seqs, width), F32),
            shape(dt.shape, F32),
            shape((seqs, length, width), BF16),
            shape((seqs, length, model), BF16),
            shape((width, model), BF16),
            shape((model, width), BF16),
            shape(gate_w.shape, BF16),
            shape(out_w.shape, BF16),
        ],
        input_output_aliases={9: 7, 10: 8},
        scratch_shapes=[
            pltpu.VMEM((states, seqs, width), F32),
            pltpu.VMEM((states, seqs, width), F32),
            pltpu.VMEM((STEPS, seqs, wide - rank), F32),
            pltpu.VMEM((length, seqs, width), F32),
            pltpu.VMEM((rows, width), F32),
            pltpu.VMEM((rows, width), F32),
            pltpu.VMEM((rows, width), F32),
            pltpu.VMEM((rows, width), BF16),
            pltpu.VMEM((seqs, length, width), BF16),
            pltpu.VMEM((seqs, length, width), BF16),
            pltpu.VMEM(gate_w.shape, BF16),
            pltpu.VMEM(out_w.shape, BF16),
            dma((2,)),
        ]
        + [dma((hops, 2))] * 4,
        cost_estimate=busy(60),
        compiler_params=pltpu.CompilerParams(
            collective_id=5, has_side_effects=True, vmem_limit_bytes=60 << 20
        ),
    )(dt, x, selection, keep, normed, cot, normed, cot, params, gate_w, out_w)


def z_sums(z, z_size, owns, ups, downs, sems, blocks):
    up_s, up_r, down_s, down_r = sems

    def up_copy(k, j, own):
        src = owns[j].at[z_size - 1 - k] if own else ups[j].at[k]
        return remote(src, ups[j].at[k], up_s.at[k, j], up_r.at[k, j], {"z": z + 1})

    def down_copy(k, j, own):
        src = owns[j].at[k] if own else downs[j].at[k]
        return remote(src, downs[j].at[k], down_s.at[k, j], down_r.at[k, j], {"z": z - 1})

    def line(tau, j):
        k = tau - z
        high = z_size - 1 - k

        @pl.when((k >= 0) & (z < high) & (z > 0))
        def _():
            up_copy(k, j, False).wait_recv()
            add_rows(ups[j].at[k], [owns[j].at[high], ups[j].at[k]], blocks[j])
            up_copy(k, j, False).start()

        @pl.when((k >= 0) & (z < high) & (z == 0))
        def _():
            up_copy(k, j, True).start()

        m = tau - (z_size - 1 - z)

        @pl.when((m >= 0) & (z > m) & (z < z_size - 1))
        def _():
            down_copy(m, j, False).wait_recv()
            add_rows(downs[j].at[m], [owns[j].at[m], downs[j].at[m]], blocks[j])
            down_copy(m, j, False).start()

        @pl.when((m >= 0) & (z > m) & (z == z_size - 1))
        def _():
            down_copy(m, j, True).start()

    def settle(j, dst):
        low = z
        high = z_size - 1 - z

        @pl.when(z == 0)
        def _():
            down_copy(low, j, False).wait_recv()
            add_rows(dst, [owns[j].at[z], downs[j].at[low]], blocks[j])

        @pl.when(z == z_size - 1)
        def _():
            up_copy(high, j, False).wait_recv()
            add_rows(dst, [owns[j].at[z], ups[j].at[high]], blocks[j])

        @pl.when((z > 0) & (z < z_size - 1))
        def _():
            down_copy(low, j, False).wait_recv()
            up_copy(high, j, False).wait_recv()
            add_rows(dst, [owns[j].at[z], downs[j].at[low], ups[j].at[high]], blocks[j])

    def sent(j):
        for k in range(z_size - 1):

            @pl.when(z < z_size - 1 - k)
            def _():
                up_copy(k, j, False).wait_send()

            @pl.when(z > k)
            def _():
                down_copy(k, j, False).wait_send()

    return line, settle, sent


def backward_kernel(
    chunks_all,
    z_size,
    states,
    rank,
    skip_row,
    dt_ref,
    x_ref,
    ds_ref,
    pre_ref,
    sel_ref,
    keep_ref,
    hist_ref,
    last_ref,
    ones_ref,
    params_ref,
    step_w_ref,
    gate_hbm,
    out_hbm,
    bx_ref,
    part_ref,
    da_ref,
    gstep_ref,
    bias_ref,
    skip_ref,
    gate_fin,
    out_fin,
    rate_ref,
    ag_ref,
    h_ref,
    p_ref,
    bc_ref,
    bp_ref,
    gate_own,
    out_own,
    gate_up,
    out_up,
    gate_down,
    out_down,
    local_sem,
    up_s,
    up_r,
    down_s,
    down_r,
):
    chunk = pl.program_id(0)
    chunks = pl.num_programs(0)
    me = place()
    z = me["z"]
    hops = z_size - 1
    line, settle, sent = z_sums(
        z,
        z_size,
        (gate_own, out_own),
        (gate_up, out_up),
        (gate_down, out_down),
        (up_s, up_r, down_s, down_r),
        (64, 16),
    )

    @pl.when(chunk == 0)
    def _():
        greet([{"z": (z + 1) % z_size}, {"z": (z + z_size - 1) % z_size}])
        early = pl.ds(0, out_own.shape[2])
        loads = [
            pltpu.make_async_copy(gate_hbm, gate_own, local_sem.at[0]),
            pltpu.make_async_copy(out_hbm.at[:, :, early], out_own, local_sem.at[1]),
        ]
        for copy in loads:
            copy.start()
        fill_rates(rate_ref, params_ref, skip_row + 1)
        ag_ref[...] = jnp.zeros_like(ag_ref)
        da_ref[...] = jnp.zeros_like(da_ref)
        gstep_ref[...] = jnp.zeros_like(gstep_ref)
        bias_ref[...] = jnp.zeros_like(bias_ref)
        skip_ref[...] = jnp.zeros_like(skip_ref)
        h_ref[...] = last_ref[...]
        for copy in loads:
            copy.wait()

    for tau in range(hops):

        @pl.when(chunk == -(-tau * (chunks_all - 1) // hops))
        def _():
            line(tau, 0)
            line(tau, 1)

    steps, seqs, width = dt_ref.shape
    groups = width // 128
    blocks = steps // BACK_INNER
    bc_ref[...] = sel_ref[:, rank:].astype(F32).reshape(bc_ref.shape)

    inner = BACK_INNER

    def body(back, carry):
        t0 = (blocks - 1 - back) * inner
        rows = pl.ds(pl.multiple_of(t0 * seqs, inner * seqs), inner * seqs)
        bc = [bc_ref[t0 + i] for i in range(inner)]
        off = [(1.0 - keep_ref[t0 + i]) * BIG for i in range(inner)]
        for g0 in range(0, groups, TOGETHER):
            lanes = [pl.ds((g0 + q) * 128, 128) for q in range(TOGETHER)]
            each = [(q, i) for q in range(TOGETHER) for i in range(inner)]
            dt = {(q, i): dt_ref[t0 + i, :, lanes[q]] for q, i in each}
            dtm = {(q, i): dt[q, i] + off[i] for q, i in each}
            ds = {(q, i): ds_ref[t0 + i, :, lanes[q]] for q, i in each}
            u = {(q, i): dt[q, i] * x_ref[t0 + i, :, lanes[q]] for q, i in each}
            s1 = {}
            s2 = {}
            for n in range(states):
                pb = [None] * inner
                pc = [None] * inner
                for q in range(TOGETHER):
                    ag = ag_ref[n, :, lanes[q]]
                    h = h_ref[n, :, lanes[q]]
                    rate = rate_ref[n, :, lanes[q]]
                    da = da_ref[n, :, lanes[q]]
                    before = []
                    for i in range(0, inner, 2):
                        pair = hist_ref[t0 // 2 + i // 2, n, :, lanes[q]].astype(F32)
                        before += [pair[:seqs], pair[seqs:]]
                    for i in reversed(range(inner)):
                        prev = before[i]
                        a = jnp.exp2(dtm[q, i] * rate)
                        adj = ds[q, i] * bc[i][:, states + n : states + n + 1] + ag
                        c_term = ds[q, i] * h
                        b_term = adj * u[q, i]
                        pc[i] = c_term if q == 0 else pc[i] + c_term
                        pb[i] = b_term if q == 0 else pb[i] + b_term
                        ag = a * adj
                        w = ag * prev
                        rw = rate * w
                        gb = adj * bc[i][:, n : n + 1]
                        s1[q, i] = rw if n == 0 else s1[q, i] + rw
                        s2[q, i] = gb if n == 0 else s2[q, i] + gb
                        da = da + dt[q, i] * w
                        h = prev
                    ag_ref[n, :, lanes[q]] = ag
                    h_ref[n, :, lanes[q]] = h
                    da_ref[n, :, lanes[q]] = da
                cols = pl.ds(n * 128, 128)
                p_ref[0, g0 // TOGETHER, rows, cols] = jnp.concatenate(pb, axis=0).astype(BF16)
                p_ref[1, g0 // TOGETHER, rows, cols] = jnp.concatenate(pc, axis=0).astype(BF16)
            for q in range(TOGETHER):
                skip = params_ref[skip_row : skip_row + 1, lanes[q]]
                bias = bias_ref[:, lanes[q]]
                direct = skip_ref[:, lanes[q]]
                low = []
                for i in range(inner):
                    x = x_ref[t0 + i, :, lanes[q]]
                    bx_ref[t0 + i, :, lanes[q]] = dt[q, i] * s2[q, i] + skip * ds[q, i]
                    back_step = s1[q, i] * (1.0 / LOG2E) + x * s2[q, i]
                    back_pre = back_step / (1.0 + jnp.exp(-pre_ref[t0 + i, :, lanes[q]]))
                    low.append(back_pre)
                    bias = bias + back_pre
                    direct = direct + ds[q, i] * x
                bias_ref[:, lanes[q]] = bias
                skip_ref[:, lanes[q]] = direct
                bp_ref[rows, lanes[q]] = jnp.concatenate(low, axis=0).astype(BF16)
        return carry

    lax.fori_loop(0, blocks, body, 0)
    span = states * 128
    sets = groups // TOGETHER
    folded = dot_nn(p_ref[...].reshape(2 * sets * steps * seqs, span), ones_ref[...])
    folded = folded.reshape(2, sets, steps * seqs, 128)
    in_sum = folded[0, 0]
    out_sum = folded[1, 0]
    for g in range(1, sets):
        in_sum = in_sum + folded[0, g]
        out_sum = out_sum + folded[1, g]
    part_ref[:, rank:] = (in_sum + pltpu.roll(out_sum, states, 1)).astype(BF16)
    part_ref[:, :rank] = dot_nn(bp_ref[...], step_w_ref[...]).astype(BF16)
    gstep_ref[...] += dot_tn(bp_ref[...], sel_ref[:, :rank])

    @pl.when(chunk == chunks - 1)
    def _():
        settle(0, gate_fin)
        settle(1, out_fin)
        sent(0)
        sent(1)


def scan_backward(
    z_size, rank, skip_row, dt, x, ds, pre, selection, keep, hist, last, params, step_w, gate, out
):
    length, seqs, width = dt.shape
    states = last.shape[0]
    chunks = length // STEPS
    wide = selection.shape[1]
    rows = STEPS * seqs
    block = lambda *tail: pl.BlockSpec((STEPS,) + tail, lambda i: (chunks - 1 - i,) + (0,) * len(tail))
    flat = lambda n: pl.BlockSpec((rows, n), lambda i: (chunks - 1 - i, 0))
    whole = lambda *dims: pl.BlockSpec(dims, lambda i: (0,) * len(dims))
    any_space = pl.BlockSpec(memory_space=pl.ANY)
    span = states * 128
    ones = jnp.asarray((np.arange(span)[:, None] // 128 == np.arange(128)[None, :]).astype(np.float32), BF16)
    hops = z_size - 1
    gate_shape = gate.shape[1:]
    out_shape = (out.shape[1], out.shape[2] // 2)
    shape = jax.ShapeDtypeStruct
    dma = pltpu.SemaphoreType.DMA
    return pl.pallas_call(
        functools.partial(backward_kernel, chunks, z_size, states, rank, skip_row),
        grid=(chunks,),
        in_specs=[
            block(seqs, width),
            block(seqs, width),
            block(seqs, width),
            block(seqs, width),
            flat(wide),
            block(seqs, 128),
            pl.BlockSpec((STEPS // 2, states, 2 * seqs, width), lambda i: (chunks - 1 - i, 0, 0, 0)),
            whole(states, seqs, width),
            whole(span, 128),
            whole(*params.shape),
            pl.BlockSpec((width, rank), lambda i: (0, wide // rank)),
            any_space,
            any_space,
        ],
        out_specs=[
            block(seqs, width),
            flat(wide),
            whole(states, seqs, width),
            whole(width, rank),
            whole(seqs, width),
            whole(seqs, width),
            whole(*gate_shape),
            whole(*out_shape),
        ],
        out_shape=[
            shape(dt.shape, F32),
            shape((length * seqs, wide), BF16),
            shape((states, seqs, width), F32),
            shape((width, rank), F32),
            shape((seqs, width), F32),
            shape((seqs, width), F32),
            shape(gate_shape, BF16),
            shape(out_shape, BF16),
        ],
        scratch_shapes=[
            pltpu.VMEM((states, seqs, width), F32),
            pltpu.VMEM((states, seqs, width), F32),
            pltpu.VMEM((states, seqs, width), F32),
            pltpu.VMEM((2, width // 128 // TOGETHER, rows, span), BF16),
            pltpu.VMEM((STEPS, seqs, wide - rank), F32),
            pltpu.VMEM((rows, width), BF16),
            pltpu.VMEM(gate.shape, BF16),
            pltpu.VMEM(out.shape[:1] + out_shape, BF16),
            pltpu.VMEM((hops,) + gate_shape, BF16),
            pltpu.VMEM((hops,) + out_shape, BF16),
            pltpu.VMEM((hops,) + gate_shape, BF16),
            pltpu.VMEM((hops,) + out_shape, BF16),
            dma((2,)),
            dma((hops, 2)),
            dma((hops, 2)),
            dma((hops, 2)),
            dma((hops, 2)),
        ],
        cost_estimate=busy(80),
        compiler_params=pltpu.CompilerParams(
            collective_id=4, has_side_effects=True, vmem_limit_bytes=62 << 20
        ),
    )(dt, x, ds, pre, selection, keep, hist, last, ones, params, step_w, gate, out)


def last_kernel(
    z_size,
    taps,
    part_ref,
    keep_ref,
    mats_ref,
    params_ref,
    gate_fin,
    out_fin,
    da_ref,
    gstep_ref,
    bias_ref,
    skip_ref,
    tokens_ref,
    cot_ref,
    gain_ref,
    bx_hbm,
    cin_hbm,
    normed_hbm,
    conv_hbm,
    gate_hbm,
    bgi_hbm,
    gout_hbm,
    tgrad_ref,
    both_gate,
    both_conv,
    out_ref,
    small_out,
    vec_out,
    gain_out,
    chosen,
    from_sib,
    stage,
    got,
    bx,
    cin,
    picked,
    conv_w,
    gate_w,
    bgi,
    turned,
    bci,
    gsel,
    sums,
    columns,
    own_back,
    sib_stage,
    sib_back,
    ring_got,
    own_small,
    own_vec,
    own_conv,
    up_small,
    up_vec,
    up_conv,
    down_small,
    down_vec,
    down_conv,
    own_out,
    up_out,
    down_out,
    fin_conv,
    gain_parts,
    gain_got,
    gain_half,
    gain_pair,
    local_sem,
    column_sem,
    sw_s,
    sw_r,
    rs_s,
    rs_r,
    ag_s,
    ag_r,
    fw_s,
    fw_r,
    sib_send,
    sib_recv,
    ring_send,
    ring_recv,
    up_send,
    up_recv,
    down_send,
    down_recv,
    out_us,
    out_ur,
    out_ds,
    out_dr,
    swap_send,
    swap_recv,
    x_send,
    x_recv,
    gain_send,
    gain_recv,
):
    me = place()
    x, y, z, c = me["x"], me["y"], me["z"], me["c"]
    shares = z_size * 4
    share = z * 4 + y * 2 + c
    corner = y * 2 + c
    sibling = {"c": 1 - c}
    over_x = {"x": 1 - x}
    length, width = tokens_ref.shape
    chans = bx.shape[2]
    rows_in = both_gate.shape[2]
    half = own_out.shape[1]
    hops = z_size - 1
    wide = part_ref.shape[3]
    out_line, out_settle, out_sent = z_sums(
        z, z_size, (own_out,), (up_out,), (down_out,), (out_us, out_ur, out_ds, out_dr), (16,)
    )
    greet(plane_others(me) + z_only(me, shares))

    loads = [
        pltpu.make_async_copy(src, dst, local_sem.at[i])
        for i, (src, dst) in enumerate(
            [
                (cin_hbm, cin.at[pl.ds(3, length)]),
                (bx_hbm, bx.at[pl.ds(0, length)]),
                (bgi_hbm, bgi),
                (conv_hbm, conv_w),
                (gate_hbm, gate_w),
            ]
        )
    ]
    later = pl.ds(own_out.shape[2], own_out.shape[2])
    out_load = pltpu.make_async_copy(gout_hbm.at[:, :, later], own_out, local_sem.at[6])
    out_load.start()

    fine = 4
    block = length // 8

    def taps_of(lanes):
        return [
            jnp.broadcast_to(params_ref[taps - 1 - j : taps - j, lanes], (8, 128)) for j in range(taps)
        ]

    def activate(b, carry):
        t0 = b * block

        def convolve(i, carry):
            for g in range(chans // 128):
                lanes = pl.ds(g * 128, 128)
                tap = taps_of(lanes)
                offset = jnp.broadcast_to(params_ref[taps : taps + 1, lanes], (8, 128))
                taken = []
                slopes = []
                for j in range(fine):
                    t = t0 + i * fine + j
                    total = tap[3] * cin[t, :, lanes] * keep_ref[jnp.maximum(t - 2, 0)]
                    total = (total + tap[2] * cin[t + 1, :, lanes]) * keep_ref[jnp.maximum(t - 1, 0)]
                    total = (total + tap[1] * cin[t + 2, :, lanes]) * keep_ref[t]
                    v = total + tap[0] * cin[t + 3, :, lanes] + offset
                    s = sigmoid(v)
                    silu = v * s
                    taken.append(silu)
                    slopes.append(s + silu * (1.0 - s))
                rows = pl.ds(pl.multiple_of(i * fine * 8, fine * 8), fine * 8)
                picked[b, rows, lanes] = jnp.concatenate(taken, axis=0).astype(BF16)
                bci[b, rows, lanes] = jnp.concatenate(slopes, axis=0).astype(BF16)
            return carry

        lax.fori_loop(0, block // fine, convolve, 0)
        return carry

    swap = remote(part_ref.at[:, 1 - c], from_sib, sw_s.at[0], sw_r.at[0], sibling)
    swap.start()
    for copy in loads:
        copy.start()
    out_load.wait()
    out_line(0, 0)
    cin[0:3] = jnp.zeros((3, 8, chans), F32)
    bx[length : length + 3] = jnp.zeros((3, 8, chans), F32)
    sums[...] = jnp.zeros_like(sums)
    gsel[...] = jnp.zeros_like(gsel)
    swap.wait()
    mine = x * 2 + y
    chips = [((x + d // 2) % 2, (y + d % 2) % 2) for d in (1, 2, 3)]
    sends = []
    for k in (2, 1, 0):
        ox, oy = chips[k]
        j = ox * 2 + oy
        stage[k] = (part_ref[j, c].astype(F32) + from_sib[j].astype(F32)).astype(BF16)
        copy = remote(stage.at[k], got.at[k], rs_s.at[k], rs_r.at[k], {"x": ox, "y": oy})
        copy.start()
        sends.append(copy)
    loads[0].wait()
    lax.fori_loop(0, 8, activate, 0)
    total = part_ref[mine, c].astype(F32) + from_sib[mine].astype(F32)
    if hops > 1:
        out_line(1, 0)
    for copy in sends:
        copy.wait()
    for k in range(3):
        total = total + got[k].astype(F32)
    chosen[mine, c] = total.astype(BF16)
    here = chosen.at[mine, c]
    spreads = []
    for k in (2, 1, 0):
        ox, oy = chips[k]
        copy = remote(here, here, ag_s.at[k], ag_r.at[k], {"x": ox, "y": oy})
        copy.start()
        spreads.append((k, copy))
    forwards = [remote(here, here, fw_s.at[3], fw_r.at[3], sibling)]
    forwards[0].start()

    def corner_sends(src, dst, index):
        out = []
        for e in range(1, 8):
            to = (corner + e % 4) % 4
            out.append(
                remote(
                    src.at[pl.ds(pl.multiple_of(to * rows_in, rows_in), rows_in)],
                    dst.at[x, corner],
                    swap_send.at[index, e - 1],
                    swap_recv.at[index, e - 1],
                    {"x": (x + e // 4) % 2, "y": to // 2, "c": to % 2},
                )
            )
        return out

    gate_swaps = corner_sends(gate_fin, both_gate, 0)
    conv_swaps = corner_sends(fin_conv, both_conv, 1)
    both_gate[x, corner] = gate_fin[pl.ds(pl.multiple_of(corner * rows_in, rows_in), rows_in)]
    out_ref[x, :, : own_out.shape[2]] = out_fin[...]
    out_x = remote(out_ref.at[x], out_ref.at[x], x_send.at[0], x_recv.at[0], over_x)
    for k, copy in reversed(spreads):
        copy.wait_recv()
        ox, oy = chips[k]
        there = chosen.at[ox * 2 + oy, c]
        forwards.append(remote(there, there, fw_s.at[k], fw_r.at[k], sibling))
        forwards[-1].start()
    for copy in loads[1:]:
        copy.wait()
    for _, copy in spreads:
        copy.wait_send()
    for copy in forwards:
        copy.wait()
    for copy in gate_swaps:
        copy.start()
    for tau in range(2, hops):
        out_line(tau, 0)

    def select(b, carry):
        back = chosen[b // 2, b % 2]
        t0 = b * block
        bx[pl.ds(t0, block)] += dot_nt(back, mats_ref[:, :wide]).reshape(block, 8, chans)

        def convolve(i, carry):
            for g in range(chans // 128):
                lanes = pl.ds(g * 128, 128)
                acc = [sums[r, :, lanes] for r in range(taps + 1)]
                slopes = bci[b, pl.ds(pl.multiple_of(i * fine * 8, fine * 8), fine * 8), lanes].astype(F32)
                for j in range(fine):
                    t = t0 + i * fine + j
                    k0 = keep_ref[t]
                    k1 = k0 * keep_ref[jnp.maximum(t - 1, 0)]
                    k2 = k1 * keep_ref[jnp.maximum(t - 2, 0)]
                    back = bx[t, :, lanes] * slopes[j * 8 : (j + 1) * 8]
                    bx[t, :, lanes] = back
                    acc[0] = acc[0] + back * cin[t + 3, :, lanes]
                    acc[1] = acc[1] + back * (cin[t + 2, :, lanes] * k0)
                    acc[2] = acc[2] + back * (cin[t + 1, :, lanes] * k1)
                    acc[3] = acc[3] + back * (cin[t, :, lanes] * k2)
                    acc[4] = acc[4] + back
                for r in range(taps + 1):
                    sums[r, :, lanes] = acc[r]
            return carry

        lax.fori_loop(0, block // fine, convolve, 0)
        gsel[...] += dot_tn(picked[b], back)
        return carry

    lax.fori_loop(0, 8, select, 0)

    def unfold(b, carry):
        t0 = b * block

        def convolve(i, carry):
            for g in range(chans // 128):
                lanes = pl.ds(g * 128, 128)
                tap = taps_of(lanes)
                for j in range(fine):
                    t = t0 + i * fine + j
                    total = tap[3] * bx[t + 3, :, lanes] * keep_ref[jnp.minimum(t + 3, length - 1)]
                    total = (total + tap[2] * bx[t + 2, :, lanes]) * keep_ref[
                        jnp.minimum(t + 2, length - 1)
                    ]
                    total = (total + tap[1] * bx[t + 1, :, lanes]) * keep_ref[
                        jnp.minimum(t + 1, length - 1)
                    ]
                    turned[i * fine + j, :, lanes] = total + tap[0] * bx[t, :, lanes]
            return carry

        lax.fori_loop(0, block // fine, convolve, 0)
        bci[:, pl.ds(pl.multiple_of(t0, block), block), :] = jnp.swapaxes(turned[...], 0, 1).astype(BF16)
        return carry

    def column(i, slot):
        zz = jnp.where(z * 2 < z_size, z_size - 1 - i, i)
        cols = pl.ds(pl.multiple_of(zz * 4 * rows_in, 4 * rows_in), 4 * rows_in)
        return zz, pltpu.make_async_copy(normed_hbm.at[:, :, cols], columns.at[slot], column_sem.at[slot])

    column(0, 0)[1].start()
    out_settle(0, out_ref.at[x, :, later])
    out_x.start()
    lax.fori_loop(0, 8, unfold, 0)

    owns = (own_small, own_vec, own_conv)
    line, settle, sent = z_sums(
        z,
        z_size,
        owns,
        (up_small, up_vec, up_conv),
        (down_small, down_vec, down_conv),
        (up_send, up_recv, down_send, down_recv),
        (16, 16, 64),
    )

    rates = -jnp.exp(params_ref[taps + 3 : taps + 3 + da_ref.shape[0], :])
    vectors = (
        [jnp.sum(sums[taps - 1 - r], axis=0, keepdims=True) for r in range(taps)]
        + [
            jnp.sum(sums[taps], axis=0, keepdims=True),
            jnp.sum(bias_ref[...], axis=0, keepdims=True),
            jnp.sum(skip_ref[...], axis=0, keepdims=True),
        ]
        + [jnp.sum(da_ref[...], axis=1) * rates]
    )
    used = taps + 3 + da_ref.shape[0]
    vectors = jnp.concatenate(
        vectors + [jnp.zeros((own_vec.shape[1] - used, chans), F32)], axis=0
    ).astype(BF16)
    for zz in range(z_size):
        own_vec[zz] = vectors[:, zz * half : (zz + 1) * half]
        own_small[zz, :, :wide] = gsel[zz * half : (zz + 1) * half, :].astype(BF16)
        own_small[zz, :, wide:] = gstep_ref[zz * half : (zz + 1) * half, :].astype(BF16)

    at = ring_at(x, y)
    step = 1 + 2 * c
    sib_step = 3 - 2 * c
    nx, ny = ring_chip((at + step) % RING)
    following = {"x": nx, "y": ny}

    def grad_column(i):
        slot = i % 2
        zz, copy = column(i, slot)
        copy.wait()
        if i + 1 < z_size:
            column(i + 1, 1 - slot)[1].start()
        tall = columns[slot].reshape(8 * length, 4 * rows_in)
        own_conv[zz] = dot_tn(tall, bci[...].reshape(8 * length, chans)).astype(BF16)

    def back_block(dst, p, core):
        cx, cy = ring_chip(p % RING)
        s = cx * 4 + cy * 2 + core

        def cols(i, carry):
            n = pl.ds(pl.multiple_of(i * 512, 512), 512)
            total = dot_nt(bci[s], conv_w[n, :]) + dot_nt(bgi[s], gate_w[n, :])
            dst[:, n] = total.astype(BF16)
            return carry

        lax.fori_loop(0, width // 512, cols, 0)

    def cross(k):
        slot = k % 2
        return remote(sib_stage.at[slot], sib_back.at[k], sib_send.at[k], sib_recv.at[k], sibling)

    def ring(k, p):
        r = pl.ds(p * (length // 2), length // 2)
        return remote(
            own_back.at[k, r], ring_got.at[k, r], ring_send.at[k, p], ring_recv.at[k, p], following
        )

    def blocks_for(k):
        if k >= 2:
            cross(k - 2).wait_send()
        back_block(sib_stage.at[k % 2], at + sib_step * (RING - 1 - k), 1 - c)
        cross(k).start()
        back_block(own_back.at[k], at + step * (RING - 1 - k), c)

    def ring_step(k):
        cross(k).wait_recv()
        srcs = [own_back.at[k], sib_back.at[k]]
        if k:
            for p in range(2):
                ring(k - 1, p).wait_recv()
            srcs.append(ring_got.at[k - 1])
        add_rows(own_back.at[k], srcs, 16)
        for p in range(2):
            ring(k, p).start()

    def ring_end():
        last = RING - 1
        cross(last).wait_recv()
        for p in range(2):
            ring(last - 1, p).wait_recv()
        rows = 16

        def body(i, total):
            r = pl.ds(pl.multiple_of(i * rows, rows), rows)
            back = (
                own_back[last, r].astype(F32)
                + sib_back[last, r].astype(F32)
                + ring_got[last - 1, r].astype(F32)
            )
            values = tokens_ref[r].astype(F32)
            rstd = lax.rsqrt(jnp.mean(values * values, axis=-1, keepdims=True) + epsilon)
            scaled = back * gain_ref[0:1, :]
            inner = jnp.mean(scaled * values, axis=-1, keepdims=True)
            grad = cot_ref[r].astype(F32) + rstd * scaled - values * (rstd * rstd * rstd * inner)
            tgrad_ref[r] = grad.astype(BF16)
            terms = back * values * rstd
            return total + terms[:8] + terms[8:]

        total = lax.fori_loop(0, length // rows, body, jnp.zeros((8, width), F32))
        total = jnp.broadcast_to(jnp.sum(total, axis=0, keepdims=True), (8, width))
        piece = gain_parts.shape[2]
        for f in range(shares):
            gain_parts[f] = total[:, f * piece : (f + 1) * piece]
        gain_got[share] = gain_parts[share]

    gains = []
    for k in range(1, shares):
        f = (share + k) % shares
        gains.append(
            remote(
                gain_parts.at[f], gain_got.at[share], gain_send.at[k - 1], gain_recv.at[k - 1], share_at(f)
            )
        )

    def lines(tau):
        for j in (2, 0, 1):
            line(tau, j)

    blocks_for(0)
    ring_step(0)
    grad_column(0)
    lines(0)
    for i in range(1, z_size):
        grad_column(i)
    blocks_for(1)
    ring_step(1)
    blocks_for(2)
    lines(1)
    blocks_for(3)
    ring_step(2)
    for tau in range(2, hops):
        lines(tau)

    settle(2, fin_conv)
    for copy in conv_swaps:
        copy.start()
    ring_end()
    for copy in gains:
        copy.start()
    both_conv[x, corner] = fin_conv[pl.ds(pl.multiple_of(corner * rows_in, rows_in), rows_in)]
    settle(0, small_out.at[x])
    settle(1, vec_out.at[x])
    small_x = remote(small_out.at[x], small_out.at[x], x_send.at[2], x_recv.at[2], over_x)
    vec_x = remote(vec_out.at[x], vec_out.at[x], x_send.at[3], x_recv.at[3], over_x)
    small_x.start()
    vec_x.start()

    for copy in gains:
        copy.wait()
    gain_half[...] = jnp.sum(gain_got[...], axis=0)
    gain_x = remote(gain_half, gain_pair, x_send.at[5], x_recv.at[5], over_x)
    gain_x.start()
    for copy in gate_swaps:
        copy.wait()
    gain_x.wait()
    gain_out[...] = gain_half[...] + gain_pair[...]
    for copy in conv_swaps:
        copy.wait()
    for copy in (out_x, small_x, vec_x):
        copy.wait()
    for j in range(3):
        sent(j)
    out_sent(0)
    for k in range(RING - 1):
        for p in range(2):
            ring(k, p).wait_send()
    for k in range(2, RING):
        cross(k).wait_send()


def last_part(
    z_size,
    taps,
    part,
    keep,
    mats,
    params,
    gate_fin,
    out_fin,
    gout,
    da,
    gstep,
    bias,
    skip,
    tokens,
    cot,
    gain,
    bx,
    cin,
    normed,
    conv,
    gate,
    bgi,
):
    length, width = tokens.shape
    chans = bx.shape[2]
    shares = z_size * 4
    hops = z_size - 1
    rows_in = gate_fin.shape[0] // 4
    half = gout.shape[1]
    wide = part.shape[3]
    any_space = pl.BlockSpec(memory_space=pl.ANY)
    vmem = pl.BlockSpec(memory_space=pltpu.VMEM)
    dma = pltpu.SemaphoreType.DMA
    shape = jax.ShapeDtypeStruct
    block = (length, width)
    slabs = [(half, mats.shape[1]), (params.shape[0], half), (4 * rows_in, chans)]
    bufs = lambda n: [pltpu.VMEM((n,) + s, BF16) for s in slabs]
    both = shape((2, 4, rows_in, chans), BF16)
    piece = (8, width // shares)
    few = (length, wide)
    late_out = (half, width // 2)
    return pl.pallas_call(
        functools.partial(last_kernel, z_size, taps),
        in_specs=[vmem] * 13 + [any_space] * 7,
        out_specs=[vmem] * 7,
        out_shape=[
            shape(tokens.shape, BF16),
            both,
            both,
            shape((2,) + gout.shape[1:], BF16),
            shape((2,) + slabs[0], BF16),
            shape((2,) + slabs[1], BF16),
            shape(piece, F32),
        ],
        scratch_shapes=[
            pltpu.VMEM((4, 2) + few, BF16),
            pltpu.VMEM((4,) + few, BF16),
            pltpu.VMEM((3,) + few, BF16),
            pltpu.VMEM((3,) + few, BF16),
            pltpu.VMEM((length + 3, 8, chans), F32),
            pltpu.VMEM((length + 3, 8, chans), F32),
            pltpu.VMEM((8, length, chans), BF16),
            pltpu.VMEM(conv.shape, BF16),
            pltpu.VMEM(gate.shape, BF16),
            pltpu.VMEM(bgi.shape, BF16),
            pltpu.VMEM((length // 8, 8, chans), F32),
            pltpu.VMEM(bgi.shape, BF16),
            pltpu.VMEM((chans, wide), F32),
            pltpu.VMEM((taps + 1, 8, chans), F32),
            pltpu.VMEM((2, 8, length, 4 * rows_in), BF16),
            pltpu.VMEM((RING,) + block, BF16),
            pltpu.VMEM((2,) + block, BF16),
            pltpu.VMEM((RING,) + block, BF16),
            pltpu.VMEM((RING - 1,) + block, BF16),
        ]
        + bufs(z_size)
        + bufs(hops)
        + bufs(hops)
        + [
            pltpu.VMEM((z_size,) + late_out, BF16),
            pltpu.VMEM((hops,) + late_out, BF16),
            pltpu.VMEM((hops,) + late_out, BF16),
            pltpu.VMEM(slabs[2], BF16),
            pltpu.VMEM((shares,) + piece, F32),
            pltpu.VMEM((shares,) + piece, F32),
            pltpu.VMEM(piece, F32),
            pltpu.VMEM(piece, F32),
            dma((7,)),
            dma((2,)),
            dma((1,)),
            dma((1,)),
        ]
        + [dma((3,))] * 4
        + [dma((4,))] * 2
        + [dma((RING,))] * 2
        + [dma((RING - 1, 2))] * 2
        + [dma((hops, 3))] * 4
        + [dma((hops, 1))] * 4
        + [dma((2, 7))] * 2
        + [dma((6,))] * 2
        + [dma((shares - 1,))] * 2,
        cost_estimate=busy(120),
        compiler_params=pltpu.CompilerParams(
            collective_id=3, has_side_effects=True, vmem_limit_bytes=63 << 20
        ),
    )(
        part,
        keep,
        mats,
        params,
        gate_fin,
        out_fin,
        da,
        gstep,
        bias,
        skip,
        tokens,
        cot,
        gain,
        bx,
        cin,
        normed,
        conv,
        gate,
        bgi,
        gout,
    )


def close_kernel(
    taps,
    wide,
    tokens_ref,
    sum_ref,
    mats_ref,
    vec_ref,
    weight_ref,
    gate_ref,
    conv_ref,
    layer_ref,
    in_ref,
    taps_ref,
    offset_ref,
    select_ref,
    step_ref,
    bias_ref,
    decay_ref,
    skip_ref,
    out_ref,
):
    layer_ref[...] = (tokens_ref[...].astype(F32) + sum_ref[...].astype(F32)).astype(BF16)
    half = mats_ref.shape[1]
    for xx in range(2):
        rows = pl.ds(xx * half, half)
        select_ref[rows, :] = mats_ref[xx, :, : select_ref.shape[1]].astype(F32)
        step_ref[rows, :] = mats_ref[xx, :, wide:].astype(F32)
        out_ref[rows, :] = weight_ref[xx].astype(F32)
    z_size = conv_ref.shape[3] // half
    for first, both in ((0, conv_ref), (in_ref.shape[1] // 2, gate_ref)):
        for zz in range(z_size):
            for j in range(4):
                for xx in range(2):
                    col = first + (zz * 4 + j) * 2 * half + xx * half
                    in_ref[:, col : col + half] = both[xx, j, :, zz * half : (zz + 1) * half].astype(F32)
    vectors = jnp.concatenate([vec_ref[0].astype(F32), vec_ref[1].astype(F32)], axis=1)
    offset_ref[...] = vectors[taps : taps + 1, :]
    bias_ref[...] = vectors[taps + 1 : taps + 2, :]
    skip_ref[...] = vectors[taps + 2 : taps + 3, :]
    tall = vectors.T
    taps_ref[...] = tall[:, :taps]
    decay_ref[...] = tall[:, taps + 3 : taps + 3 + decay_ref.shape[1]]


def close(taps, states, select_width, tokens, layer_sum, mats, vectors, weight, gate, conv):
    rows = 2 * mats.shape[1]
    wide = select_width + -select_width % 128
    rank = mats.shape[2] - wide
    vmem = pl.BlockSpec(memory_space=pltpu.VMEM)
    shape = jax.ShapeDtypeStruct
    return pl.pallas_call(
        functools.partial(close_kernel, taps, wide),
        in_specs=[vmem] * 7,
        out_specs=[vmem] * 10,
        out_shape=[
            shape(tokens.shape, BF16),
            shape((gate.shape[2], 16 * gate.shape[3]), F32),
            shape((rows, taps), F32),
            shape((1, rows), F32),
            shape((rows, select_width), F32),
            shape((rows, rank), F32),
            shape((1, rows), F32),
            shape((rows, states), F32),
            shape((1, rows), F32),
            shape((rows, weight.shape[2]), F32),
        ],
        compiler_params=pltpu.CompilerParams(vmem_limit_bytes=60 << 20),
    )(tokens, layer_sum, mats, vectors, weight, gate, conv)


def shards(
    tokens,
    doc_ids,
    norm_gain,
    in_weight,
    conv_taps,
    conv_offset,
    select_weight,
    step_weight,
    step_bias,
    decay_log,
    skip_gain,
    out_weight,
    cotangent,
):
    z_size = lax.axis_size("z")
    rh_size = lax.axis_size("rh")
    seqs = 8
    length = doc_ids.shape[1]
    width = tokens.shape[1]
    in_rows = in_weight.shape[0]
    rows = out_weight.shape[0]
    half = rows // 2
    chans = half * z_size
    taps = conv_taps.shape[1]
    rank = step_weight.shape[1]
    states = decay_log.shape[1]
    x_at = lax.axis_index("x")

    def own_half(w):
        return lax.dynamic_slice_in_dim(w, x_at * half, half, 0)

    spare = -(rank + 2 * states) % 128
    wide = rank + 2 * states + spare
    vectors = jnp.concatenate(
        [
            own_half(conv_taps),
            own_half(conv_offset)[:, None],
            own_half(step_bias)[:, None],
            own_half(skip_gain)[:, None],
            own_half(decay_log),
        ],
        axis=1,
    ).T
    vectors = jnp.pad(vectors, ((0, -vectors.shape[0] % 32), (0, 0)))
    weight_in = in_weight
    if half % 128:
        columns = lax.dynamic_index_in_dim(
            in_weight.reshape(in_rows, 2, z_size, 4, 2, half), x_at, 4, keepdims=False
        )
        weight_in = columns.transpose(1, 3, 0, 2, 4).reshape(2, 4, in_rows, chans)
    (
        all_normed,
        all_cot,
        w_conv,
        w_gate,
        w_out,
        w_mats,
        keep,
        conv_in,
        x,
        dt,
        pre,
        vectors,
        gains,
        selection,
    ) = front(
        z_size,
        taps,
        rank,
        tokens,
        norm_gain.reshape(1, -1),
        doc_ids,
        vectors,
        cotangent,
        weight_in,
        out_weight,
        select_weight,
        step_weight,
    )
    selection = selection.reshape(length * seqs, wide)

    hist, last, back_scan, back_gate_in, out_part, grad_out, grad_gate, w_gate, _ = scan_forward(
        z_size, rank, states, taps + 2, dt, x, selection, keep, all_normed, all_cot, w_gate, w_out, vectors
    )
    layer_sum = lax.psum_scatter(
        out_part.reshape(-1, width), PLANE, scatter_dimension=0, tiled=True
    )
    back_x, part, da, g_step, g_bias, g_skip, gate_fin, out_fin = scan_backward(
        z_size,
        rank,
        taps + 2,
        dt,
        x,
        back_scan,
        pre,
        selection,
        keep,
        hist,
        last,
        vectors,
        w_mats,
        grad_gate.reshape(z_size, -1, chans),
        grad_out.reshape(z_size, half, width),
    )
    tokens_grad, g_in_gate, g_in_conv, g_out, g_mats, g_vectors, g_gain = last_part(
        z_size,
        taps,
        part.reshape(4, 2, length, wide),
        keep,
        w_mats,
        vectors,
        gate_fin,
        out_fin,
        grad_out.reshape(z_size, half, width),
        da,
        g_step,
        g_bias,
        g_skip,
        tokens,
        cotangent,
        gains,
        back_x,
        conv_in,
        all_normed,
        w_conv,
        w_gate,
        back_gate_in,
    )
    if rh_size > 1:
        g_mats, g_vectors, g_in_gate, g_in_conv, g_out, g_gain = lax.psum(
            tuple(
                v.astype(F32) for v in (g_mats, g_vectors, g_in_gate, g_in_conv, g_out, g_gain)
            ),
            "rh",
        )
    layer_out, g_in, g_taps, g_offset, g_select, g_step, g_bias, g_decay, g_skip, g_out = close(
        taps, states, rank + 2 * states, tokens, layer_sum, g_mats, g_vectors, g_out, g_in_gate, g_in_conv
    )
    return (
        layer_out,
        tokens_grad,
        g_gain[0],
        g_in,
        g_taps,
        g_offset[0],
        g_select,
        g_step,
        g_bias[0],
        g_decay,
        g_skip[0],
        g_out,
    )


def solution(mesh):
    replicas = mesh.shape["replica"]
    shares = mesh.shape["fsdp"]
    grid = Mesh(
        mesh.devices.reshape(replicas // 2, 2, shares // 4, 2, 2), ("rh", "x", "z", "y", "c")
    )
    tok = ("rh", "x", "z", "y", "c")
    own = ("z", "y", "c")
    return jax.shard_map(
        shards,
        mesh=grid,
        in_specs=(
            P(tok, None),
            P(tok, None),
            P(own),
            P(own, None),
            P(own, None),
            P(own),
            P(own, None),
            P(own, None),
            P(own),
            P(own, None),
            P(own),
            P(own, None),
            P(tok, None),
        ),
        out_specs=(
            P(tok, None),
            P(tok, None),
            P(own),
            P(own, None),
            P(own, None),
            P(own),
            P(own, None),
            P(own, None),
            P(own),
            P(own, None),
            P(own),
            P(own, None),
        ),
        check_vma=False,
    )
```

```python
import functools

import jax
import jax.numpy as jnp
import numpy as np
from jax import lax
from jax.experimental import pallas as pl
from jax.experimental.pallas import tpu as pltpu
from jax.sharding import Mesh
from jax.sharding import PartitionSpec as P

F32 = jnp.float32
BF16 = jnp.bfloat16
epsilon = 1e-05
PLANE = ("x", "y", "c")
BIG = 1e30
STEPS = 32
COLUMNS = 512
INNER = 4
BACK_INNER = 8
TOGETHER = 4
LOG2E = 1.4426950408889634


def dot(a, b, dims):
    return lax.dot_general(a, b, (dims, ((), ())), preferred_element_type=F32)


def dot_nn(a, b):
    return dot(a, b, ((1,), (0,)))


def dot_tn(a, b):
    return dot(a, b, ((0,), (0,)))


def dot_nt(a, b):
    return dot(a, b, ((1,), (1,)))


def busy(micros):
    return pl.CostEstimate(flops=micros * 10**9, bytes_accessed=micros * 10**6, transcendentals=0)


MESH = pl.DeviceIdType.MESH
RING = 4


def place():
    return {a: lax.axis_index(a) for a in ("x", "z", "y", "c")}


def ring_chip(p):
    y = p // 2
    return (p + y) % 2, y


def ring_at(x, y):
    return 2 * y + (x + y) % 2


def share_at(f):
    return {"z": f // 4, "y": f // 2 % 2, "c": f % 2}


def remote(src, dst, send, recv, device):
    return pltpu.make_async_remote_copy(
        src_ref=src, dst_ref=dst, send_sem=send, recv_sem=recv, device_id=device, device_id_type=MESH
    )


def greet(devices):
    barrier = pltpu.get_barrier_semaphore()
    for device in devices:
        pl.semaphore_signal(barrier, inc=1, device_id=device, device_id_type=MESH)
    pl.semaphore_wait(barrier, len(devices))


def plane_others(me):
    out = []
    for dx in range(2):
        for dy in range(2):
            for dc in range(2):
                if dx + dy + dc:
                    out.append(
                        {"x": (me["x"] + dx) % 2, "y": (me["y"] + dy) % 2, "c": (me["c"] + dc) % 2}
                    )
    return out


def share_others(me, shares):
    f = me["z"] * 4 + me["y"] * 2 + me["c"]
    return [share_at((f + k) % shares) for k in range(1, shares)]


def z_only(me, shares):
    f = me["c"] + 2 * me["y"]
    out = []
    for dz in range(1, shares // 4):
        for k in range(4):
            out.append(
                {
                    "z": (me["z"] + dz) % (shares // 4),
                    "y": (f + k) % 4 // 2,
                    "c": (f + k) % 2,
                }
            )
    return out


def z_line(z, z_size, pieces, sems):
    up_s, up_r, down_s, down_r = sems

    def up(k):
        return [
            remote(p(z - k), p(z - k), up_s.at[k, j], up_r.at[k, j], {"z": z + 1})
            for j, p in enumerate(pieces)
        ]

    def down(k):
        return [
            remote(p(z + k), p(z + k), down_s.at[k, j], down_r.at[k, j], {"z": z - 1})
            for j, p in enumerate(pieces)
        ]

    def start(k):
        @pl.when((z < z_size - 1) & (z >= k))
        def _():
            for copy in up(k):
                copy.start()

        @pl.when((z > 0) & (z + k < z_size))
        def _():
            for copy in down(k):
                copy.start()

    def arrive(k):
        @pl.when(z > k)
        def _():
            for copy in up(k):
                copy.wait_recv()

        @pl.when(z + k < z_size - 1)
        def _():
            for copy in down(k):
                copy.wait_recv()

    def sent(k):
        @pl.when((z < z_size - 1) & (z >= k))
        def _():
            for copy in up(k):
                copy.wait_send()

        @pl.when((z > 0) & (z + k < z_size))
        def _():
            for copy in down(k):
                copy.wait_send()

    return start, arrive, sent


class Ring:
    def __init__(self, me, blocks, own, ring_send, ring_recv, sib_send, sib_recv):
        self.me, self.blocks, self.own = me, blocks, own
        self.sems = ring_send, ring_recv, sib_send, sib_recv
        self.at = ring_at(me["x"], me["y"])
        self.step = 1 + 2 * me["c"]
        nx, ny = ring_chip((self.at + self.step) % RING)
        self.following = {"x": nx, "y": ny}
        self.sibling = {"c": 1 - me["c"]}
        self.half = blocks.shape[1] // 2

    def slot(self, k):
        ox, oy = ring_chip((self.at + (RING - self.step) * k) % RING)
        return ox * 4 + oy * 2 + self.me["c"]

    def hop(self, k):
        out = []
        for p in range(2):
            rows = pl.ds(p * self.half, self.half)
            dst = self.blocks.at[self.slot(k), rows]
            src = self.own.at[rows] if k == 0 and self.own is not None else dst
            out.append(remote(src, dst, self.sems[0].at[k, p], self.sems[1].at[k, p], self.following))
        return out

    def cross(self, k):
        dst = self.blocks.at[self.slot(k)]
        src = self.own if k == 0 and self.own is not None else dst
        return remote(src, dst, self.sems[2].at[k], self.sems[3].at[k], self.sibling)

    def start(self, k):
        if k < RING - 1:
            for copy in self.hop(k):
                copy.start()
        self.cross(k).start()

    def arrive(self, k):
        for copy in self.hop(k):
            copy.wait_recv()

    def sent(self, k):
        if k < RING - 1:
            for copy in self.hop(k):
                copy.wait_send()
        self.cross(k).wait()


def sigmoid(v):
    return 0.5 + 0.5 * jnp.tanh(0.5 * v)


def softplus(v):
    e = jnp.exp(-jnp.abs(v))
    small = e * (1.0 - e * (0.5 - e * (1.0 / 3.0)))
    return jnp.maximum(v, 0.0) + jnp.where(e < 1e-3, small, jnp.log(1.0 + e))


def front_kernel(
    z_size,
    taps,
    rank,
    tokens_ref,
    gain_ref,
    ids_ref,
    rows_ref,
    cot_ref,
    in_ref,
    out_ref,
    select_ref,
    step_ref,
    normed_hbm,
    cot_all,
    conv_hbm,
    gate_all,
    out_all,
    mats_hbm,
    keep_hbm,
    cin_hbm,
    x_hbm,
    dt_hbm,
    pre_hbm,
    params,
    gain_all,
    selection,
    normed_all,
    conv_w,
    mats,
    rows_all,
    gain_got,
    ids_all,
    proj,
    cin,
    xs,
    picked,
    part,
    dts,
    pres,
    keep,
    first,
    from_sib,
    stage,
    got,
    local_sem,
    own_sem,
    gain_send,
    gain_recv,
    ids_send,
    ids_recv,
    conv_send,
    conv_recv,
    gate_send,
    gate_recv,
    ring_send,
    ring_recv,
    sib_send,
    sib_recv,
    cot_ring_send,
    cot_ring_recv,
    cot_sib_send,
    cot_sib_recv,
    a_us,
    a_ur,
    a_ds,
    a_dr,
    m_us,
    m_ur,
    m_ds,
    m_dr,
    b_us,
    b_ur,
    b_ds,
    b_dr,
    sw_s,
    sw_r,
    rs_s,
    rs_r,
    ag_s,
    ag_r,
    fw_s,
    fw_r,
):
    me = place()
    x, y, z, c = me["x"], me["y"], me["z"], me["c"]
    shares = z_size * 4
    share = z * 4 + y * 2 + c
    corner = y * 2 + c
    seq = x * 4 + y * 2 + c
    sibling = {"c": 1 - c}
    length, width = tokens_ref.shape
    chans = conv_w.shape[1]
    rows_in = width // shares
    half = chans // z_size
    hops = z_size - 1
    branch = 8 * chans
    greet(plane_others(me) + z_only(me, shares))

    def rows_at(ref, index, count):
        return ref.at[pl.ds(pl.multiple_of(index * count, count), count)]

    def pieces(first, dst, to):
        rows = rows_at(dst, share, rows_in)
        if len(in_ref.shape) == 4:
            return [(in_ref.at[1 if first else 0, to], rows)]
        out = []
        for zz in range(z_size):
            col = first + (zz * 4 + to) * 2 * half + x * half
            src = in_ref.at[:, pl.ds(pl.multiple_of(col, half), half)]
            out.append((src, rows.at[:, pl.ds(zz * half, half)]))
        return out

    def corner_sends(first, dst, send, recv):
        out = []
        for k in range(1, 4):
            to = (corner + k) % 4
            for i, (src, there) in enumerate(pieces(first, dst, to)):
                out.append(
                    remote(
                        src, there, send.at[k - 1, i], recv.at[k - 1, i], {"y": to // 2, "c": to % 2}
                    )
                )
        return out

    gain_got[share] = jnp.broadcast_to(gain_ref[...].astype(F32), gain_got.shape[1:])
    ids_all[seq] = jnp.broadcast_to(ids_ref[...], ids_all.shape[1:])
    swaps = corner_sends(0, conv_w, conv_send, conv_recv)
    gates = corner_sends(branch, gate_all, gate_send, gate_recv)
    for copy in swaps:
        copy.start()
    gains = [
        remote(gain_got.at[share], gain_got.at[share], gain_send.at[k], gain_recv.at[k], device)
        for k, device in enumerate(share_others(me, shares))
    ]
    for copy in gains:
        copy.start()
    locals_ = [
        pltpu.make_async_copy(
            out_ref.at[pl.ds(pl.multiple_of(x * half, half), half)], rows_at(out_all, z, half), local_sem.at[3]
        ),
        pltpu.make_async_copy(cot_ref, cot_all.at[seq], local_sem.at[4]),
    ]
    conv_own = [
        pltpu.make_async_copy(src, there, own_sem.at[0, i])
        for i, (src, there) in enumerate(pieces(0, conv_w, corner))
    ]
    for i, (src, there) in enumerate(pieces(branch, gate_all, corner)):
        locals_.append(pltpu.make_async_copy(src, there, own_sem.at[1, i]))
    for copy in conv_own + locals_:
        copy.start()
    ids_copies = [
        remote(ids_all.at[seq], ids_all.at[seq], ids_send.at[k], ids_recv.at[k], device)
        for k, device in enumerate(plane_others(me))
    ]
    for copy in ids_copies:
        copy.start()
    rows_all[z] = rows_ref[...]
    mine_rows = pl.ds(pl.multiple_of(x * half, half), half)
    at_rows = pl.ds(pl.multiple_of(z * half, half), half)
    wide = mats.shape[1] - rank
    mats[at_rows, :wide] = jnp.concatenate(
        [
            select_ref[mine_rows, :],
            jnp.zeros((half, wide - select_ref.shape[1]), BF16),
        ],
        axis=1,
    )
    mats[at_rows, wide:] = step_ref[mine_rows, :]

    values = tokens_ref[...].astype(F32)
    rstd = lax.rsqrt(jnp.mean(values * values, axis=-1, keepdims=True) + epsilon)
    for copy in gains:
        copy.wait()
    piece = gain_ref.shape[1]
    for f in range(shares):
        cols = pl.ds(f * piece, piece)
        normed = tokens_ref[:, cols].astype(F32) * rstd * gain_got[f, 0:1, :]
        normed_all[seq, :, cols] = normed.astype(BF16)
    for f in range(shares):
        gain_all[:, f * piece : (f + 1) * piece] = gain_got[f]

    ring = Ring(me, normed_all, None, ring_send, ring_recv, sib_send, sib_recv)
    cot_ring = Ring(me, cot_all, cot_ref, cot_ring_send, cot_ring_recv, cot_sib_send, cot_sib_recv)
    ring.start(0)
    for copy in swaps:
        copy.wait()
    for copy in conv_own:
        copy.wait()
    a_start, a_arrive, a_sent = z_line(
        z,
        z_size,
        [
            lambda k: rows_at(conv_w, k, 4 * rows_in),
            lambda k: rows_all.at[k],
        ],
        (a_us, a_ur, a_ds, a_dr),
    )
    m_start, m_arrive, m_sent = z_line(
        z, z_size, [lambda k: rows_at(mats, k, half)], (m_us, m_ur, m_ds, m_dr)
    )
    b_start, b_arrive, b_sent = z_line(
        z,
        z_size,
        [lambda k: rows_at(gate_all, k, 4 * rows_in), lambda k: rows_at(out_all, k, half)],
        (b_us, b_ur, b_ds, b_dr),
    )
    a_start(0)
    for copy in gates:
        copy.start()

    for copy in ids_copies:
        copy.wait()
    ids = jnp.concatenate([ids_all[s, 0:1, :] for s in range(8)], axis=0).astype(F32)
    before = pltpu.roll(ids, 1, 1)
    lane = lax.broadcasted_iota(jnp.int32, ids.shape, 1)
    same = jnp.where((ids == before) & (lane > 0), 1.0, 0.0)
    for t in range(length):
        keep[t] = jnp.broadcast_to(same[:, t : t + 1], (8, 128))
    keep_copy = pltpu.make_async_copy(keep, keep_hbm, local_sem.at[5])
    keep_copy.start()

    for k in range(max(hops, RING - 1)):
        if k < hops:
            a_arrive(k)
            if k + 1 < hops:
                a_start(k + 1)
            if k:
                m_arrive(k - 1)
            m_start(k)
        if k < RING - 1:
            ring.arrive(k)
            ring.start(k + 1)
        if k == RING - 2:
            cot_ring.start(0)
    for copy in gates + locals_:
        copy.wait()
    b_start(0)
    for k in range(RING):
        ring.sent(k)
    outs = [
        pltpu.make_async_copy(normed_all, normed_hbm, local_sem.at[6]),
        pltpu.make_async_copy(conv_w, conv_hbm, local_sem.at[7]),
    ]
    for copy in outs:
        copy.start()
    for zz in range(z_size):
        params[:, zz * half : (zz + 1) * half] = rows_all[zz].astype(F32)

    def project(s, carry):
        proj[s] = dot_nn(normed_all[s], conv_w[...])
        return carry

    lax.fori_loop(0, 8, project, 0)
    m_arrive(hops - 1)

    cin[0:3] = jnp.zeros((3, 8, chans), F32)
    block = 32
    fine = 4

    def turn(i, carry):
        t0 = pl.multiple_of(i * block, block)
        cin[pl.ds(3 + t0, block)] = jnp.swapaxes(proj[:, pl.ds(t0, block), :], 0, 1)
        return carry

    lax.fori_loop(0, length // block, turn, 0)
    cot_ring.arrive(0)
    cot_ring.start(1)

    def convolve(i, carry):
        t0 = i * fine
        for g in range(chans // 128):
            lanes = pl.ds(g * 128, 128)
            tap = [jnp.broadcast_to(params[taps - 1 - j : taps - j, lanes], (8, 128)) for j in range(taps)]
            offset = jnp.broadcast_to(params[taps : taps + 1, lanes], (8, 128))
            chosen = []
            for j in range(fine):
                t = t0 + j
                total = tap[3] * cin[t, :, lanes] * keep[jnp.maximum(t - 2, 0)]
                total = (total + tap[2] * cin[t + 1, :, lanes]) * keep[jnp.maximum(t - 1, 0)]
                total = (total + tap[1] * cin[t + 2, :, lanes]) * keep[t]
                v = total + tap[0] * cin[t + 3, :, lanes] + offset
                chosen.append((v * sigmoid(v)).astype(BF16))
                xs[t, :, lanes] = chosen[-1].astype(F32)
            rows = pl.ds(pl.multiple_of(t0 * 8, fine * 8), fine * 8)
            picked[rows, lanes] = jnp.concatenate(chosen, axis=0)
        return carry

    lax.fori_loop(0, length // fine, convolve, 0)
    outs += [
        pltpu.make_async_copy(mats, mats_hbm, local_sem.at[8]),
        pltpu.make_async_copy(cin.at[pl.ds(3, length)], cin_hbm, local_sem.at[9]),
        pltpu.make_async_copy(xs, x_hbm, local_sem.at[10]),
    ]
    for copy in outs[2:]:
        copy.start()

    wide = part.shape[3]

    def select(b, carry):
        rows = pl.ds(pl.multiple_of(b * length, length), length)
        part[b // 2, b % 2] = dot_nn(picked[rows, :], mats[:, :wide])
        return carry

    lax.fori_loop(0, 8, select, 0)
    first[...] = part[:, 1 - c].astype(BF16)
    swap = remote(first, from_sib, sw_s.at[0], sw_r.at[0], sibling)
    swap.start()
    swap.wait()
    mine = x * 2 + y
    chips = [((x + d // 2) % 2, (y + d % 2) % 2) for d in (1, 2, 3)]
    sends = []
    for k in (2, 1, 0):
        ox, oy = chips[k]
        j = ox * 2 + oy
        stage[k] = (part[j, c] + from_sib[j].astype(F32)).astype(BF16)
        copy = remote(stage.at[k], got.at[k], rs_s.at[k], rs_r.at[k], {"x": ox, "y": oy})
        copy.start()
        sends.append(copy)
    total = part[mine, c] + from_sib[mine].astype(F32)
    for copy in sends:
        copy.wait()
    for k in range(3):
        total = total + got[k].astype(F32)
    selection[mine, c] = total.astype(BF16)
    here = selection.at[mine, c]
    spreads = []
    for k in (2, 1, 0):
        ox, oy = chips[k]
        copy = remote(here, here, ag_s.at[k], ag_r.at[k], {"x": ox, "y": oy})
        copy.start()
        spreads.append((k, copy))
    forwards = [remote(here, here, fw_s.at[3], fw_r.at[3], sibling)]
    forwards[0].start()
    b_arrive(0)
    if hops > 2:
        b_start(1)
    cot_ring.arrive(1)
    for k, copy in reversed(spreads):
        copy.wait_recv()
        ox, oy = chips[k]
        there = selection.at[ox * 2 + oy, c]
        forwards.append(remote(there, there, fw_s.at[k], fw_r.at[k], sibling))
        forwards[-1].start()
    for _, copy in spreads:
        copy.wait_send()
    for copy in forwards:
        copy.wait()
    cot_ring.start(2)

    bias = params[taps + 1 : taps + 2, :]

    def steps(i, carry):
        rows = 64
        per = length // rows
        b = i // per
        at = pl.ds(pl.multiple_of((i % per) * rows, rows), rows)
        v = dot_nt(selection[b // 2, b % 2, at, :rank], mats[:, wide : wide + rank]) + bias
        t = pl.ds(i * (rows // 8), rows // 8)
        pres[t] = v.reshape(rows // 8, 8, chans)
        dts[t] = softplus(v).reshape(rows // 8, 8, chans)
        return carry

    lax.fori_loop(0, length * 8 // 64, steps, 0)
    outs += [
        pltpu.make_async_copy(dts, dt_hbm, local_sem.at[11]),
        pltpu.make_async_copy(pres, pre_hbm, local_sem.at[12]),
    ]
    for copy in outs[5:]:
        copy.start()

    for k in range(1, hops - 1):
        b_arrive(k)
        if k + 1 < hops - 1:
            b_start(k + 1)
    cot_ring.arrive(2)
    cot_ring.start(3)
    for k in range(RING):
        cot_ring.sent(k)
    for k in range(hops):
        a_sent(k)
        m_sent(k)
    for k in range(hops - 1):
        b_sent(k)
    for copy in outs + [keep_copy]:
        copy.wait()


def front(z_size, taps, rank, tokens, gain, ids, rows, cot, weight_in, out, select, step):
    length, width = tokens.shape
    shares = z_size * 4
    half = rows.shape[1]
    chans = half * z_size
    wide = select.shape[1] + -select.shape[1] % 128
    cuts = 1 if weight_in.ndim == 4 else z_size
    any_space = pl.BlockSpec(memory_space=pl.ANY)
    vmem = pl.BlockSpec(memory_space=pltpu.VMEM)
    dma = pltpu.SemaphoreType.DMA
    hops = z_size - 1
    shape = jax.ShapeDtypeStruct
    everyone = (8,) + tokens.shape
    per_token = (length, 8, chans)
    block = (length, wide)
    return pl.pallas_call(
        functools.partial(front_kernel, z_size, taps, rank),
        in_specs=[vmem] * 5 + [any_space] + [vmem] * 3,
        out_specs=[any_space] * 11 + [vmem] * 3,
        out_shape=[
            shape(everyone, BF16),
            shape(everyone, BF16),
            shape((width, chans), BF16),
            shape((width, chans), BF16),
            shape((chans, width), BF16),
            shape((chans, wide + rank), BF16),
            shape((length, 8, 128), F32),
            shape(per_token, F32),
            shape(per_token, F32),
            shape(per_token, F32),
            shape(per_token, F32),
            shape((rows.shape[0], chans), F32),
            shape((8, width), F32),
            shape((4, 2) + block, BF16),
        ],
        scratch_shapes=[
            pltpu.VMEM(everyone, BF16),
            pltpu.VMEM((width, chans), BF16),
            pltpu.VMEM((chans, wide + rank), BF16),
            pltpu.VMEM((z_size,) + rows.shape, BF16),
            pltpu.VMEM((shares, 8, gain.shape[1]), F32),
            pltpu.VMEM((8, 8, length), ids.dtype),
            pltpu.VMEM((8, length, chans), F32),
            pltpu.VMEM((length + 3, 8, chans), F32),
            pltpu.VMEM(per_token, F32),
            pltpu.VMEM((length * 8, chans), BF16),
            pltpu.VMEM((4, 2) + block, F32),
            pltpu.VMEM(per_token, F32),
            pltpu.VMEM(per_token, F32),
            pltpu.VMEM((length, 8, 128), F32),
            pltpu.VMEM((4,) + block, BF16),
            pltpu.VMEM((4,) + block, BF16),
            pltpu.VMEM((3,) + block, BF16),
            pltpu.VMEM((3,) + block, BF16),
            dma((13,)),
            dma((2, cuts)),
            dma((shares - 1,)),
            dma((shares - 1,)),
            dma((7,)),
            dma((7,)),
        ]
        + [dma((3, cuts))] * 4
        + [dma((RING - 1, 2)), dma((RING - 1, 2)), dma((RING,)), dma((RING,))] * 2
        + [dma((hops, 2))] * 4
        + [dma((hops, 1))] * 4
        + [dma((hops, 2))] * 4
        + [dma((1,))] * 2
        + [dma((3,))] * 4
        + [dma((4,))] * 2,
        cost_estimate=busy(120),
        compiler_params=pltpu.CompilerParams(
            collective_id=0, has_side_effects=True, vmem_limit_bytes=60 << 20
        ),
    )(tokens, gain, ids, rows, cot, weight_in, out, select, step)


def add_rows(dst, srcs, rows):
    count = dst.shape[0] // rows

    def body(i, carry):
        at = pl.ds(pl.multiple_of(i * rows, rows), rows)
        total = srcs[0][at].astype(F32)
        for src in srcs[1:]:
            total = total + src[at].astype(F32)
        dst[at] = total.astype(dst.dtype)
        return carry

    lax.fori_loop(0, count, body, 0)


def fill_rates(rate_ref, params_ref, first):
    states = rate_ref.shape[0]
    rows = -LOG2E * jnp.exp(params_ref[first : first + states, :])
    for n in range(states):
        rate_ref[n] = jnp.broadcast_to(rows[n : n + 1, :], rate_ref.shape[1:])


def forward_kernel(
    z_size,
    chunks,
    states,
    rank,
    skip_row,
    dt_ref,
    x_ref,
    sel_ref,
    keep_ref,
    normed_ref,
    cot_ref,
    normed_col,
    cot_col,
    params_ref,
    gate_given,
    out_given,
    hist_ref,
    last_ref,
    ds_ref,
    bgi_ref,
    part_ref,
    gout_ref,
    ggate_ref,
    gate_all,
    out_all,
    rate_ref,
    h_ref,
    bc_ref,
    y_ref,
    ys_ref,
    gate_ref,
    bg_ref,
    gated_ref,
    gated_all,
    bgi_all,
    gate_w_ref,
    out_w_ref,
    load_sem,
    up_s,
    up_r,
    down_s,
    down_r,
):
    step = pl.program_id(0)
    me = place()
    z = me["z"]
    hops = z_size - 1
    slab_rows = gate_all.shape[0] // z_size
    half = out_all.shape[0] // z_size
    line_start, line_arrive, line_sent = z_line(
        z,
        z_size,
        [
            lambda k: gate_all.at[pl.ds(pl.multiple_of(k * slab_rows, slab_rows), slab_rows)],
            lambda k: out_all.at[pl.ds(pl.multiple_of(k * half, half), half)],
        ],
        (up_s, up_r, down_s, down_r),
    )

    @pl.when(step == 0)
    def _():
        greet([{"z": (z + 1) % z_size}, {"z": (z + z_size - 1) % z_size}])
        line_start(hops - 1)
        fill_rates(rate_ref, params_ref, skip_row + 1)
        h_ref[...] = jnp.zeros_like(h_ref)

    steps, seqs, width = dt_ref.shape
    groups = width // 128
    rows = steps * seqs
    @pl.when(step < chunks)
    def _():
        bc_ref[...] = sel_ref[:, rank:].astype(F32).reshape(bc_ref.shape)

        def body(tb, carry):
            t0 = tb * INNER
            bc = [bc_ref[t0 + i] for i in range(INNER)]
            off = [(1.0 - keep_ref[t0 + i]) * BIG for i in range(INNER)]
            for g in range(groups):
                lanes = pl.ds(g * 128, 128)
                dt = [dt_ref[t0 + i, :, lanes] for i in range(INNER)]
                dtm = [dt[i] + off[i] for i in range(INNER)]
                u = [dt[i] * x_ref[t0 + i, :, lanes] for i in range(INNER)]
                y = [None] * INNER
                for n in range(states):
                    h = h_ref[n, :, lanes]
                    rate = rate_ref[n, :, lanes]
                    before = []
                    for i in range(INNER):
                        before.append(h)
                        a = jnp.exp2(dtm[i] * rate)
                        h = a * h + u[i] * bc[i][:, n : n + 1]
                        term = h * bc[i][:, states + n : states + n + 1]
                        y[i] = term if y[i] is None else y[i] + term
                    for i in range(0, INNER, 2):
                        pair = jnp.concatenate(before[i : i + 2], axis=0).astype(BF16)
                        hist_ref[t0 // 2 + i // 2, n, :, lanes] = pair
                    h_ref[n, :, lanes] = h
                skip = params_ref[skip_row : skip_row + 1, lanes]
                for i in range(INNER):
                    y_ref[step * steps + t0 + i, :, lanes] = y[i] + skip * x_ref[t0 + i, :, lanes]
            return carry

        lax.fori_loop(0, steps // INNER, body, 0)
        last_ref[...] = h_ref[...]

    @pl.when(step == chunks)
    def _():
        line_arrive(hops - 1)
        line_sent(hops - 1)
        loads = [
            pltpu.make_async_copy(gate_all, gate_w_ref, load_sem.at[0]),
            pltpu.make_async_copy(out_all, out_w_ref, load_sem.at[1]),
        ]
        for copy in loads:
            copy.start()
        for copy in loads:
            copy.wait()

    @pl.when((step >= chunks) & (step < 2 * chunks))
    def _():
        normed = normed_ref[...].reshape(rows, normed_ref.shape[2])
        cot = cot_ref[...].reshape(rows, cot_ref.shape[2])
        gate_ref[...] = dot_nn(normed, gate_w_ref[...])
        bg_ref[...] = dot_nt(cot, out_w_ref[...]).astype(BF16).astype(F32)
        y = y_ref[pl.ds((step - chunks) * steps, steps)]
        ys_ref[...] = jnp.swapaxes(y, 0, 1).reshape(rows, width)
        fine = 16

        def gating(i, carry):
            r = pl.ds(pl.multiple_of(i * fine, fine), fine)
            v = gate_ref[r, :]
            bg = bg_ref[r, :]
            y = ys_ref[r, :]
            s = sigmoid(v)
            gate = v * s
            gated_ref[r, :] = (y * gate).astype(BF16)
            bg_ref[r, :] = bg * gate
            gate_ref[r, :] = bg * y * (s + gate * (1.0 - s))
            return carry

        lax.fori_loop(0, rows // fine, gating, 0)
        ds_ref[...] = jnp.swapaxes(bg_ref[...].reshape(seqs, steps, width), 0, 1)
        bgi = gate_ref[...].astype(BF16).reshape(bgi_ref.shape)
        bgi_ref[...] = bgi
        gated = gated_ref[...]
        part_ref[...] = dot_nn(gated, out_w_ref[...]).astype(BF16).reshape(part_ref.shape)
        at = pl.ds(pl.multiple_of((step - chunks) * steps, steps), steps)
        gated_all[:, at, :] = gated.reshape(bgi_ref.shape)
        bgi_all[:, at, :] = bgi

    @pl.when(step >= 2 * chunks)
    def _():
        tall = (gated_all.shape[0] * gated_all.shape[1], width)
        cols = (tall[0], normed_col.shape[2])
        gout_ref[...] = dot_tn(gated_all[...].reshape(tall), cot_col[...].reshape(cols)).astype(BF16)
        ggate_ref[...] = dot_tn(normed_col[...].reshape(cols), bgi_all[...].reshape(tall)).astype(BF16)


def scan_forward(
    z_size, rank, states, skip_row, dt, x, selection, keep, normed, cot, gate_w, out_w, params
):
    length, seqs, width = dt.shape
    model = normed.shape[2]
    wide = selection.shape[1]
    chunks = length // STEPS
    early = lambda i: jnp.minimum(i, chunks - 1)
    late = lambda i: jnp.clip(i - chunks, 0, chunks - 1)
    pieces = model // COLUMNS
    last_of = lambda i: jnp.maximum(i - 2 * chunks, 0)
    column = pl.BlockSpec((seqs, length, COLUMNS), lambda i: (0, 0, last_of(i)))
    block = lambda *tail: pl.BlockSpec((STEPS,) + tail, lambda i: (early(i),) + (0,) * len(tail))
    across = lambda n: pl.BlockSpec((seqs, STEPS, n), lambda i: (0, late(i), 0))
    any_space = pl.BlockSpec(memory_space=pl.ANY)
    dma = pltpu.SemaphoreType.DMA
    hops = z_size - 1
    whole = lambda *dims: pl.BlockSpec(dims, lambda i: (0,) * len(dims))
    rows = STEPS * seqs
    shape = jax.ShapeDtypeStruct
    return pl.pallas_call(
        functools.partial(forward_kernel, z_size, chunks, states, rank, skip_row),
        grid=(2 * chunks + pieces,),
        in_specs=[
            block(seqs, width),
            block(seqs, width),
            pl.BlockSpec((rows, wide), lambda i: (early(i), 0)),
            block(seqs, 128),
            across(model),
            across(model),
            column,
            column,
            whole(*params.shape),
            any_space,
            any_space,
        ],
        out_specs=[
            pl.BlockSpec((STEPS // 2, states, 2 * seqs, width), lambda i: (early(i), 0, 0, 0)),
            whole(states, seqs, width),
            pl.BlockSpec((STEPS, seqs, width), lambda i: (late(i), 0, 0)),
            across(width),
            across(model),
            pl.BlockSpec((width, COLUMNS), lambda i: (0, last_of(i))),
            pl.BlockSpec((COLUMNS, width), lambda i: (last_of(i), 0)),
            any_space,
            any_space,
        ],
        out_shape=[
            shape((length // 2, states, 2 * seqs, width), BF16),
            shape((states, seqs, width), F32),
            shape(dt.shape, F32),
            shape((seqs, length, width), BF16),
            shape((seqs, length, model), BF16),
            shape((width, model), BF16),
            shape((model, width), BF16),
            shape(gate_w.shape, BF16),
            shape(out_w.shape, BF16),
        ],
        input_output_aliases={9: 7, 10: 8},
        scratch_shapes=[
            pltpu.VMEM((states, seqs, width), F32),
            pltpu.VMEM((states, seqs, width), F32),
            pltpu.VMEM((STEPS, seqs, wide - rank), F32),
            pltpu.VMEM((length, seqs, width), F32),
            pltpu.VMEM((rows, width), F32),
            pltpu.VMEM((rows, width), F32),
            pltpu.VMEM((rows, width), F32),
            pltpu.VMEM((rows, width), BF16),
            pltpu.VMEM((seqs, length, width), BF16),
            pltpu.VMEM((seqs, length, width), BF16),
            pltpu.VMEM(gate_w.shape, BF16),
            pltpu.VMEM(out_w.shape, BF16),
            dma((2,)),
        ]
        + [dma((hops, 2))] * 4,
        cost_estimate=busy(60),
        compiler_params=pltpu.CompilerParams(
            collective_id=5, has_side_effects=True, vmem_limit_bytes=60 << 20
        ),
    )(dt, x, selection, keep, normed, cot, normed, cot, params, gate_w, out_w)


def z_sums(z, z_size, owns, ups, downs, sems, blocks):
    up_s, up_r, down_s, down_r = sems

    def up_copy(k, j, own):
        src = owns[j].at[z_size - 1 - k] if own else ups[j].at[k]
        return remote(src, ups[j].at[k], up_s.at[k, j], up_r.at[k, j], {"z": z + 1})

    def down_copy(k, j, own):
        src = owns[j].at[k] if own else downs[j].at[k]
        return remote(src, downs[j].at[k], down_s.at[k, j], down_r.at[k, j], {"z": z - 1})

    def line(tau, j):
        k = tau - z
        high = z_size - 1 - k

        @pl.when((k >= 0) & (z < high) & (z > 0))
        def _():
            up_copy(k, j, False).wait_recv()
            add_rows(ups[j].at[k], [owns[j].at[high], ups[j].at[k]], blocks[j])
            up_copy(k, j, False).start()

        @pl.when((k >= 0) & (z < high) & (z == 0))
        def _():
            up_copy(k, j, True).start()

        m = tau - (z_size - 1 - z)

        @pl.when((m >= 0) & (z > m) & (z < z_size - 1))
        def _():
            down_copy(m, j, False).wait_recv()
            add_rows(downs[j].at[m], [owns[j].at[m], downs[j].at[m]], blocks[j])
            down_copy(m, j, False).start()

        @pl.when((m >= 0) & (z > m) & (z == z_size - 1))
        def _():
            down_copy(m, j, True).start()

    def settle(j, dst):
        low = z
        high = z_size - 1 - z

        @pl.when(z == 0)
        def _():
            down_copy(low, j, False).wait_recv()
            add_rows(dst, [owns[j].at[z], downs[j].at[low]], blocks[j])

        @pl.when(z == z_size - 1)
        def _():
            up_copy(high, j, False).wait_recv()
            add_rows(dst, [owns[j].at[z], ups[j].at[high]], blocks[j])

        @pl.when((z > 0) & (z < z_size - 1))
        def _():
            down_copy(low, j, False).wait_recv()
            up_copy(high, j, False).wait_recv()
            add_rows(dst, [owns[j].at[z], downs[j].at[low], ups[j].at[high]], blocks[j])

    def sent(j):
        for k in range(z_size - 1):

            @pl.when(z < z_size - 1 - k)
            def _():
                up_copy(k, j, False).wait_send()

            @pl.when(z > k)
            def _():
                down_copy(k, j, False).wait_send()

    return line, settle, sent


def backward_kernel(
    chunks_all,
    z_size,
    states,
    rank,
    skip_row,
    dt_ref,
    x_ref,
    ds_ref,
    pre_ref,
    sel_ref,
    keep_ref,
    hist_ref,
    last_ref,
    ones_ref,
    params_ref,
    step_w_ref,
    gate_hbm,
    out_hbm,
    bx_ref,
    part_ref,
    da_ref,
    gstep_ref,
    bias_ref,
    skip_ref,
    gate_fin,
    out_fin,
    rate_ref,
    ag_ref,
    h_ref,
    p_ref,
    bc_ref,
    bp_ref,
    gate_own,
    out_own,
    gate_up,
    out_up,
    gate_down,
    out_down,
    local_sem,
    up_s,
    up_r,
    down_s,
    down_r,
):
    chunk = pl.program_id(0)
    chunks = pl.num_programs(0)
    me = place()
    z = me["z"]
    hops = z_size - 1
    line, settle, sent = z_sums(
        z,
        z_size,
        (gate_own, out_own),
        (gate_up, out_up),
        (gate_down, out_down),
        (up_s, up_r, down_s, down_r),
        (64, 16),
    )

    @pl.when(chunk == 0)
    def _():
        greet([{"z": (z + 1) % z_size}, {"z": (z + z_size - 1) % z_size}])
        early = pl.ds(0, out_own.shape[2])
        loads = [
            pltpu.make_async_copy(gate_hbm, gate_own, local_sem.at[0]),
            pltpu.make_async_copy(out_hbm.at[:, :, early], out_own, local_sem.at[1]),
        ]
        for copy in loads:
            copy.start()
        fill_rates(rate_ref, params_ref, skip_row + 1)
        ag_ref[...] = jnp.zeros_like(ag_ref)
        da_ref[...] = jnp.zeros_like(da_ref)
        gstep_ref[...] = jnp.zeros_like(gstep_ref)
        bias_ref[...] = jnp.zeros_like(bias_ref)
        skip_ref[...] = jnp.zeros_like(skip_ref)
        h_ref[...] = last_ref[...]
        for copy in loads:
            copy.wait()

    for tau in range(hops):

        @pl.when(chunk == -(-tau * (chunks_all - 1) // hops))
        def _():
            line(tau, 0)
            line(tau, 1)

    steps, seqs, width = dt_ref.shape
    groups = width // 128
    blocks = steps // BACK_INNER
    bc_ref[...] = sel_ref[:, rank:].astype(F32).reshape(bc_ref.shape)

    inner = BACK_INNER

    def body(back, carry):
        t0 = (blocks - 1 - back) * inner
        rows = pl.ds(pl.multiple_of(t0 * seqs, inner * seqs), inner * seqs)
        bc = [bc_ref[t0 + i] for i in range(inner)]
        off = [(1.0 - keep_ref[t0 + i]) * BIG for i in range(inner)]
        for g0 in range(0, groups, TOGETHER):
            lanes = [pl.ds((g0 + q) * 128, 128) for q in range(TOGETHER)]
            each = [(q, i) for q in range(TOGETHER) for i in range(inner)]
            dt = {(q, i): dt_ref[t0 + i, :, lanes[q]] for q, i in each}
            dtm = {(q, i): dt[q, i] + off[i] for q, i in each}
            ds = {(q, i): ds_ref[t0 + i, :, lanes[q]] for q, i in each}
            u = {(q, i): dt[q, i] * x_ref[t0 + i, :, lanes[q]] for q, i in each}
            s1 = {}
            s2 = {}
            for n in range(states):
                pb = [None] * inner
                pc = [None] * inner
                for q in range(TOGETHER):
                    ag = ag_ref[n, :, lanes[q]]
                    h = h_ref[n, :, lanes[q]]
                    rate = rate_ref[n, :, lanes[q]]
                    da = da_ref[n, :, lanes[q]]
                    before = []
                    for i in range(0, inner, 2):
                        pair = hist_ref[t0 // 2 + i // 2, n, :, lanes[q]].astype(F32)
                        before += [pair[:seqs], pair[seqs:]]
                    for i in reversed(range(inner)):
                        prev = before[i]
                        a = jnp.exp2(dtm[q, i] * rate)
                        adj = ds[q, i] * bc[i][:, states + n : states + n + 1] + ag
                        c_term = ds[q, i] * h
                        b_term = adj * u[q, i]
                        pc[i] = c_term if q == 0 else pc[i] + c_term
                        pb[i] = b_term if q == 0 else pb[i] + b_term
                        ag = a * adj
                        w = ag * prev
                        rw = rate * w
                        gb = adj * bc[i][:, n : n + 1]
                        s1[q, i] = rw if n == 0 else s1[q, i] + rw
                        s2[q, i] = gb if n == 0 else s2[q, i] + gb
                        da = da + dt[q, i] * w
                        h = prev
                    ag_ref[n, :, lanes[q]] = ag
                    h_ref[n, :, lanes[q]] = h
                    da_ref[n, :, lanes[q]] = da
                cols = pl.ds(n * 128, 128)
                p_ref[0, g0 // TOGETHER, rows, cols] = jnp.concatenate(pb, axis=0).astype(BF16)
                p_ref[1, g0 // TOGETHER, rows, cols] = jnp.concatenate(pc, axis=0).astype(BF16)
            for q in range(TOGETHER):
                skip = params_ref[skip_row : skip_row + 1, lanes[q]]
                bias = bias_ref[:, lanes[q]]
                direct = skip_ref[:, lanes[q]]
                low = []
                for i in range(inner):
                    x = x_ref[t0 + i, :, lanes[q]]
                    bx_ref[t0 + i, :, lanes[q]] = dt[q, i] * s2[q, i] + skip * ds[q, i]
                    back_step = s1[q, i] * (1.0 / LOG2E) + x * s2[q, i]
                    back_pre = back_step / (1.0 + jnp.exp(-pre_ref[t0 + i, :, lanes[q]]))
                    low.append(back_pre)
                    bias = bias + back_pre
                    direct = direct + ds[q, i] * x
                bias_ref[:, lanes[q]] = bias
                skip_ref[:, lanes[q]] = direct
                bp_ref[rows, lanes[q]] = jnp.concatenate(low, axis=0).astype(BF16)
        return carry

    lax.fori_loop(0, blocks, body, 0)
    span = states * 128
    sets = groups // TOGETHER
    folded = dot_nn(p_ref[...].reshape(2 * sets * steps * seqs, span), ones_ref[...])
    folded = folded.reshape(2, sets, steps * seqs, 128)
    in_sum = folded[0, 0]
    out_sum = folded[1, 0]
    for g in range(1, sets):
        in_sum = in_sum + folded[0, g]
        out_sum = out_sum + folded[1, g]
    part_ref[:, rank:] = (in_sum + pltpu.roll(out_sum, states, 1)).astype(BF16)
    part_ref[:, :rank] = dot_nn(bp_ref[...], step_w_ref[...]).astype(BF16)
    gstep_ref[...] += dot_tn(bp_ref[...], sel_ref[:, :rank])

    @pl.when(chunk == chunks - 1)
    def _():
        settle(0, gate_fin)
        settle(1, out_fin)
        sent(0)
        sent(1)


def scan_backward(
    z_size, rank, skip_row, dt, x, ds, pre, selection, keep, hist, last, params, step_w, gate, out
):
    length, seqs, width = dt.shape
    states = last.shape[0]
    chunks = length // STEPS
    wide = selection.shape[1]
    rows = STEPS * seqs
    block = lambda *tail: pl.BlockSpec((STEPS,) + tail, lambda i: (chunks - 1 - i,) + (0,) * len(tail))
    flat = lambda n: pl.BlockSpec((rows, n), lambda i: (chunks - 1 - i, 0))
    whole = lambda *dims: pl.BlockSpec(dims, lambda i: (0,) * len(dims))
    any_space = pl.BlockSpec(memory_space=pl.ANY)
    span = states * 128
    ones = jnp.asarray((np.arange(span)[:, None] // 128 == np.arange(128)[None, :]).astype(np.float32), BF16)
    hops = z_size - 1
    gate_shape = gate.shape[1:]
    out_shape = (out.shape[1], out.shape[2] // 2)
    shape = jax.ShapeDtypeStruct
    dma = pltpu.SemaphoreType.DMA
    return pl.pallas_call(
        functools.partial(backward_kernel, chunks, z_size, states, rank, skip_row),
        grid=(chunks,),
        in_specs=[
            block(seqs, width),
            block(seqs, width),
            block(seqs, width),
            block(seqs, width),
            flat(wide),
            block(seqs, 128),
            pl.BlockSpec((STEPS // 2, states, 2 * seqs, width), lambda i: (chunks - 1 - i, 0, 0, 0)),
            whole(states, seqs, width),
            whole(span, 128),
            whole(*params.shape),
            pl.BlockSpec((width, rank), lambda i: (0, wide // rank)),
            any_space,
            any_space,
        ],
        out_specs=[
            block(seqs, width),
            flat(wide),
            whole(states, seqs, width),
            whole(width, rank),
            whole(seqs, width),
            whole(seqs, width),
            whole(*gate_shape),
            whole(*out_shape),
        ],
        out_shape=[
            shape(dt.shape, F32),
            shape((length * seqs, wide), BF16),
            shape((states, seqs, width), F32),
            shape((width, rank), F32),
            shape((seqs, width), F32),
            shape((seqs, width), F32),
            shape(gate_shape, BF16),
            shape(out_shape, BF16),
        ],
        scratch_shapes=[
            pltpu.VMEM((states, seqs, width), F32),
            pltpu.VMEM((states, seqs, width), F32),
            pltpu.VMEM((states, seqs, width), F32),
            pltpu.VMEM((2, width // 128 // TOGETHER, rows, span), BF16),
            pltpu.VMEM((STEPS, seqs, wide - rank), F32),
            pltpu.VMEM((rows, width), BF16),
            pltpu.VMEM(gate.shape, BF16),
            pltpu.VMEM(out.shape[:1] + out_shape, BF16),
            pltpu.VMEM((hops,) + gate_shape, BF16),
            pltpu.VMEM((hops,) + out_shape, BF16),
            pltpu.VMEM((hops,) + gate_shape, BF16),
            pltpu.VMEM((hops,) + out_shape, BF16),
            dma((2,)),
            dma((hops, 2)),
            dma((hops, 2)),
            dma((hops, 2)),
            dma((hops, 2)),
        ],
        cost_estimate=busy(80),
        compiler_params=pltpu.CompilerParams(
            collective_id=4, has_side_effects=True, vmem_limit_bytes=62 << 20
        ),
    )(dt, x, ds, pre, selection, keep, hist, last, ones, params, step_w, gate, out)


def last_kernel(
    z_size,
    taps,
    part_ref,
    keep_ref,
    mats_ref,
    params_ref,
    gate_fin,
    out_fin,
    da_ref,
    gstep_ref,
    bias_ref,
    skip_ref,
    tokens_ref,
    cot_ref,
    gain_ref,
    bx_hbm,
    cin_hbm,
    normed_hbm,
    conv_hbm,
    gate_hbm,
    bgi_hbm,
    gout_hbm,
    tgrad_ref,
    both_gate,
    both_conv,
    out_ref,
    small_out,
    vec_out,
    gain_out,
    chosen,
    from_sib,
    stage,
    got,
    bx,
    cin,
    picked,
    conv_w,
    gate_w,
    bgi,
    turned,
    bci,
    gsel,
    sums,
    columns,
    own_back,
    sib_stage,
    sib_back,
    ring_got,
    own_small,
    own_vec,
    own_conv,
    up_small,
    up_vec,
    up_conv,
    down_small,
    down_vec,
    down_conv,
    own_out,
    up_out,
    down_out,
    fin_conv,
    gain_parts,
    gain_got,
    gain_half,
    gain_pair,
    local_sem,
    column_sem,
    sw_s,
    sw_r,
    rs_s,
    rs_r,
    ag_s,
    ag_r,
    fw_s,
    fw_r,
    sib_send,
    sib_recv,
    ring_send,
    ring_recv,
    up_send,
    up_recv,
    down_send,
    down_recv,
    out_us,
    out_ur,
    out_ds,
    out_dr,
    swap_send,
    swap_recv,
    x_send,
    x_recv,
    gain_send,
    gain_recv,
):
    me = place()
    x, y, z, c = me["x"], me["y"], me["z"], me["c"]
    shares = z_size * 4
    share = z * 4 + y * 2 + c
    corner = y * 2 + c
    sibling = {"c": 1 - c}
    over_x = {"x": 1 - x}
    length, width = tokens_ref.shape
    chans = bx.shape[2]
    rows_in = both_gate.shape[2]
    half = own_out.shape[1]
    hops = z_size - 1
    wide = part_ref.shape[3]
    out_line, out_settle, out_sent = z_sums(
        z, z_size, (own_out,), (up_out,), (down_out,), (out_us, out_ur, out_ds, out_dr), (16,)
    )
    greet(plane_others(me) + z_only(me, shares))

    loads = [
        pltpu.make_async_copy(src, dst, local_sem.at[i])
        for i, (src, dst) in enumerate(
            [
                (cin_hbm, cin.at[pl.ds(3, length)]),
                (bx_hbm, bx.at[pl.ds(0, length)]),
                (bgi_hbm, bgi),
                (conv_hbm, conv_w),
                (gate_hbm, gate_w),
            ]
        )
    ]
    later = pl.ds(own_out.shape[2], own_out.shape[2])
    out_load = pltpu.make_async_copy(gout_hbm.at[:, :, later], own_out, local_sem.at[6])
    out_load.start()

    fine = 4
    block = length // 8

    def taps_of(lanes):
        return [
            jnp.broadcast_to(params_ref[taps - 1 - j : taps - j, lanes], (8, 128)) for j in range(taps)
        ]

    def activate(b, carry):
        t0 = b * block

        def convolve(i, carry):
            for g in range(chans // 128):
                lanes = pl.ds(g * 128, 128)
                tap = taps_of(lanes)
                offset = jnp.broadcast_to(params_ref[taps : taps + 1, lanes], (8, 128))
                taken = []
                slopes = []
                for j in range(fine):
                    t = t0 + i * fine + j
                    total = tap[3] * cin[t, :, lanes] * keep_ref[jnp.maximum(t - 2, 0)]
                    total = (total + tap[2] * cin[t + 1, :, lanes]) * keep_ref[jnp.maximum(t - 1, 0)]
                    total = (total + tap[1] * cin[t + 2, :, lanes]) * keep_ref[t]
                    v = total + tap[0] * cin[t + 3, :, lanes] + offset
                    s = sigmoid(v)
                    silu = v * s
                    taken.append(silu)
                    slopes.append(s + silu * (1.0 - s))
                rows = pl.ds(pl.multiple_of(i * fine * 8, fine * 8), fine * 8)
                picked[b, rows, lanes] = jnp.concatenate(taken, axis=0).astype(BF16)
                bci[b, rows, lanes] = jnp.concatenate(slopes, axis=0).astype(BF16)
            return carry

        lax.fori_loop(0, block // fine, convolve, 0)
        return carry

    swap = remote(part_ref.at[:, 1 - c], from_sib, sw_s.at[0], sw_r.at[0], sibling)
    swap.start()
    for copy in loads:
        copy.start()
    out_load.wait()
    out_line(0, 0)
    cin[0:3] = jnp.zeros((3, 8, chans), F32)
    bx[length : length + 3] = jnp.zeros((3, 8, chans), F32)
    sums[...] = jnp.zeros_like(sums)
    gsel[...] = jnp.zeros_like(gsel)
    swap.wait()
    mine = x * 2 + y
    chips = [((x + d // 2) % 2, (y + d % 2) % 2) for d in (1, 2, 3)]
    sends = []
    for k in (2, 1, 0):
        ox, oy = chips[k]
        j = ox * 2 + oy
        stage[k] = (part_ref[j, c].astype(F32) + from_sib[j].astype(F32)).astype(BF16)
        copy = remote(stage.at[k], got.at[k], rs_s.at[k], rs_r.at[k], {"x": ox, "y": oy})
        copy.start()
        sends.append(copy)
    loads[0].wait()
    lax.fori_loop(0, 8, activate, 0)
    total = part_ref[mine, c].astype(F32) + from_sib[mine].astype(F32)
    if hops > 1:
        out_line(1, 0)
    for copy in sends:
        copy.wait()
    for k in range(3):
        total = total + got[k].astype(F32)
    chosen[mine, c] = total.astype(BF16)
    here = chosen.at[mine, c]
    spreads = []
    for k in (2, 1, 0):
        ox, oy = chips[k]
        copy = remote(here, here, ag_s.at[k], ag_r.at[k], {"x": ox, "y": oy})
        copy.start()
        spreads.append((k, copy))
    forwards = [remote(here, here, fw_s.at[3], fw_r.at[3], sibling)]
    forwards[0].start()

    def corner_sends(src, dst, index):
        out = []
        for e in range(1, 8):
            to = (corner + e % 4) % 4
            out.append(
                remote(
                    src.at[pl.ds(pl.multiple_of(to * rows_in, rows_in), rows_in)],
                    dst.at[x, corner],
                    swap_send.at[index, e - 1],
                    swap_recv.at[index, e - 1],
                    {"x": (x + e // 4) % 2, "y": to // 2, "c": to % 2},
                )
            )
        return out

    gate_swaps = corner_sends(gate_fin, both_gate, 0)
    conv_swaps = corner_sends(fin_conv, both_conv, 1)
    both_gate[x, corner] = gate_fin[pl.ds(pl.multiple_of(corner * rows_in, rows_in), rows_in)]
    out_ref[x, :, : own_out.shape[2]] = out_fin[...]
    out_x = remote(out_ref.at[x], out_ref.at[x], x_send.at[0], x_recv.at[0], over_x)
    for k, copy in reversed(spreads):
        copy.wait_recv()
        ox, oy = chips[k]
        there = chosen.at[ox * 2 + oy, c]
        forwards.append(remote(there, there, fw_s.at[k], fw_r.at[k], sibling))
        forwards[-1].start()
    for copy in loads[1:]:
        copy.wait()
    for _, copy in spreads:
        copy.wait_send()
    for copy in forwards:
        copy.wait()
    for copy in gate_swaps:
        copy.start()
    for tau in range(2, hops):
        out_line(tau, 0)

    def select(b, carry):
        back = chosen[b // 2, b % 2]
        t0 = b * block
        bx[pl.ds(t0, block)] += dot_nt(back, mats_ref[:, :wide]).reshape(block, 8, chans)

        def convolve(i, carry):
            for g in range(chans // 128):
                lanes = pl.ds(g * 128, 128)
                acc = [sums[r, :, lanes] for r in range(taps + 1)]
                slopes = bci[b, pl.ds(pl.multiple_of(i * fine * 8, fine * 8), fine * 8), lanes].astype(F32)
                for j in range(fine):
                    t = t0 + i * fine + j
                    k0 = keep_ref[t]
                    k1 = k0 * keep_ref[jnp.maximum(t - 1, 0)]
                    k2 = k1 * keep_ref[jnp.maximum(t - 2, 0)]
                    back = bx[t, :, lanes] * slopes[j * 8 : (j + 1) * 8]
                    bx[t, :, lanes] = back
                    acc[0] = acc[0] + back * cin[t + 3, :, lanes]
                    acc[1] = acc[1] + back * (cin[t + 2, :, lanes] * k0)
                    acc[2] = acc[2] + back * (cin[t + 1, :, lanes] * k1)
                    acc[3] = acc[3] + back * (cin[t, :, lanes] * k2)
                    acc[4] = acc[4] + back
                for r in range(taps + 1):
                    sums[r, :, lanes] = acc[r]
            return carry

        lax.fori_loop(0, block // fine, convolve, 0)
        gsel[...] += dot_tn(picked[b], back)
        return carry

    lax.fori_loop(0, 8, select, 0)

    def unfold(b, carry):
        t0 = b * block

        def convolve(i, carry):
            for g in range(chans // 128):
                lanes = pl.ds(g * 128, 128)
                tap = taps_of(lanes)
                for j in range(fine):
                    t = t0 + i * fine + j
                    total = tap[3] * bx[t + 3, :, lanes] * keep_ref[jnp.minimum(t + 3, length - 1)]
                    total = (total + tap[2] * bx[t + 2, :, lanes]) * keep_ref[
                        jnp.minimum(t + 2, length - 1)
                    ]
                    total = (total + tap[1] * bx[t + 1, :, lanes]) * keep_ref[
                        jnp.minimum(t + 1, length - 1)
                    ]
                    turned[i * fine + j, :, lanes] = total + tap[0] * bx[t, :, lanes]
            return carry

        lax.fori_loop(0, block // fine, convolve, 0)
        bci[:, pl.ds(pl.multiple_of(t0, block), block), :] = jnp.swapaxes(turned[...], 0, 1).astype(BF16)
        return carry

    def column(i, slot):
        zz = jnp.where(z * 2 < z_size, z_size - 1 - i, i)
        cols = pl.ds(pl.multiple_of(zz * 4 * rows_in, 4 * rows_in), 4 * rows_in)
        return zz, pltpu.make_async_copy(normed_hbm.at[:, :, cols], columns.at[slot], column_sem.at[slot])

    column(0, 0)[1].start()
    out_settle(0, out_ref.at[x, :, later])
    out_x.start()
    lax.fori_loop(0, 8, unfold, 0)

    owns = (own_small, own_vec, own_conv)
    line, settle, sent = z_sums(
        z,
        z_size,
        owns,
        (up_small, up_vec, up_conv),
        (down_small, down_vec, down_conv),
        (up_send, up_recv, down_send, down_recv),
        (16, 16, 64),
    )

    rates = -jnp.exp(params_ref[taps + 3 : taps + 3 + da_ref.shape[0], :])
    vectors = (
        [jnp.sum(sums[taps - 1 - r], axis=0, keepdims=True) for r in range(taps)]
        + [
            jnp.sum(sums[taps], axis=0, keepdims=True),
            jnp.sum(bias_ref[...], axis=0, keepdims=True),
            jnp.sum(skip_ref[...], axis=0, keepdims=True),
        ]
        + [jnp.sum(da_ref[...], axis=1) * rates]
    )
    used = taps + 3 + da_ref.shape[0]
    vectors = jnp.concatenate(
        vectors + [jnp.zeros((own_vec.shape[1] - used, chans), F32)], axis=0
    ).astype(BF16)
    for zz in range(z_size):
        own_vec[zz] = vectors[:, zz * half : (zz + 1) * half]
        own_small[zz, :, :wide] = gsel[zz * half : (zz + 1) * half, :].astype(BF16)
        own_small[zz, :, wide:] = gstep_ref[zz * half : (zz + 1) * half, :].astype(BF16)

    at = ring_at(x, y)
    step = 1 + 2 * c
    sib_step = 3 - 2 * c
    nx, ny = ring_chip((at + step) % RING)
    following = {"x": nx, "y": ny}

    def grad_column(i):
        slot = i % 2
        zz, copy = column(i, slot)
        copy.wait()
        if i + 1 < z_size:
            column(i + 1, 1 - slot)[1].start()
        tall = columns[slot].reshape(8 * length, 4 * rows_in)
        own_conv[zz] = dot_tn(tall, bci[...].reshape(8 * length, chans)).astype(BF16)

    def back_block(dst, p, core):
        cx, cy = ring_chip(p % RING)
        s = cx * 4 + cy * 2 + core

        def cols(i, carry):
            n = pl.ds(pl.multiple_of(i * 512, 512), 512)
            total = dot_nt(bci[s], conv_w[n, :]) + dot_nt(bgi[s], gate_w[n, :])
            dst[:, n] = total.astype(BF16)
            return carry

        lax.fori_loop(0, width // 512, cols, 0)

    def cross(k):
        slot = k % 2
        return remote(sib_stage.at[slot], sib_back.at[k], sib_send.at[k], sib_recv.at[k], sibling)

    def ring(k, p):
        r = pl.ds(p * (length // 2), length // 2)
        return remote(
            own_back.at[k, r], ring_got.at[k, r], ring_send.at[k, p], ring_recv.at[k, p], following
        )

    def blocks_for(k):
        if k >= 2:
            cross(k - 2).wait_send()
        back_block(sib_stage.at[k % 2], at + sib_step * (RING - 1 - k), 1 - c)
        cross(k).start()
        back_block(own_back.at[k], at + step * (RING - 1 - k), c)

    def ring_step(k):
        cross(k).wait_recv()
        srcs = [own_back.at[k], sib_back.at[k]]
        if k:
            for p in range(2):
                ring(k - 1, p).wait_recv()
            srcs.append(ring_got.at[k - 1])
        add_rows(own_back.at[k], srcs, 16)
        for p in range(2):
            ring(k, p).start()

    def ring_end():
        last = RING - 1
        cross(last).wait_recv()
        for p in range(2):
            ring(last - 1, p).wait_recv()
        rows = 16

        def body(i, total):
            r = pl.ds(pl.multiple_of(i * rows, rows), rows)
            back = (
                own_back[last, r].astype(F32)
                + sib_back[last, r].astype(F32)
                + ring_got[last - 1, r].astype(F32)
            )
            values = tokens_ref[r].astype(F32)
            rstd = lax.rsqrt(jnp.mean(values * values, axis=-1, keepdims=True) + epsilon)
            scaled = back * gain_ref[0:1, :]
            inner = jnp.mean(scaled * values, axis=-1, keepdims=True)
            grad = cot_ref[r].astype(F32) + rstd * scaled - values * (rstd * rstd * rstd * inner)
            tgrad_ref[r] = grad.astype(BF16)
            terms = back * values * rstd
            return total + terms[:8] + terms[8:]

        total = lax.fori_loop(0, length // rows, body, jnp.zeros((8, width), F32))
        total = jnp.broadcast_to(jnp.sum(total, axis=0, keepdims=True), (8, width))
        piece = gain_parts.shape[2]
        for f in range(shares):
            gain_parts[f] = total[:, f * piece : (f + 1) * piece]
        gain_got[share] = gain_parts[share]

    gains = []
    for k in range(1, shares):
        f = (share + k) % shares
        gains.append(
            remote(
                gain_parts.at[f], gain_got.at[share], gain_send.at[k - 1], gain_recv.at[k - 1], share_at(f)
            )
        )

    def lines(tau):
        for j in (2, 0, 1):
            line(tau, j)

    blocks_for(0)
    ring_step(0)
    grad_column(0)
    lines(0)
    for i in range(1, z_size):
        grad_column(i)
    blocks_for(1)
    ring_step(1)
    blocks_for(2)
    lines(1)
    blocks_for(3)
    ring_step(2)
    for tau in range(2, hops):
        lines(tau)

    settle(2, fin_conv)
    for copy in conv_swaps:
        copy.start()
    ring_end()
    for copy in gains:
        copy.start()
    both_conv[x, corner] = fin_conv[pl.ds(pl.multiple_of(corner * rows_in, rows_in), rows_in)]
    settle(0, small_out.at[x])
    settle(1, vec_out.at[x])
    small_x = remote(small_out.at[x], small_out.at[x], x_send.at[2], x_recv.at[2], over_x)
    vec_x = remote(vec_out.at[x], vec_out.at[x], x_send.at[3], x_recv.at[3], over_x)
    small_x.start()
    vec_x.start()

    for copy in gains:
        copy.wait()
    gain_half[...] = jnp.sum(gain_got[...], axis=0)
    gain_x = remote(gain_half, gain_pair, x_send.at[5], x_recv.at[5], over_x)
    gain_x.start()
    for copy in gate_swaps:
        copy.wait()
    gain_x.wait()
    gain_out[...] = gain_half[...] + gain_pair[...]
    for copy in conv_swaps:
        copy.wait()
    for copy in (out_x, small_x, vec_x):
        copy.wait()
    for j in range(3):
        sent(j)
    out_sent(0)
    for k in range(RING - 1):
        for p in range(2):
            ring(k, p).wait_send()
    for k in range(2, RING):
        cross(k).wait_send()


def last_part(
    z_size,
    taps,
    part,
    keep,
    mats,
    params,
    gate_fin,
    out_fin,
    gout,
    da,
    gstep,
    bias,
    skip,
    tokens,
    cot,
    gain,
    bx,
    cin,
    normed,
    conv,
    gate,
    bgi,
):
    length, width = tokens.shape
    chans = bx.shape[2]
    shares = z_size * 4
    hops = z_size - 1
    rows_in = gate_fin.shape[0] // 4
    half = gout.shape[1]
    wide = part.shape[3]
    any_space = pl.BlockSpec(memory_space=pl.ANY)
    vmem = pl.BlockSpec(memory_space=pltpu.VMEM)
    dma = pltpu.SemaphoreType.DMA
    shape = jax.ShapeDtypeStruct
    block = (length, width)
    slabs = [(half, mats.shape[1]), (params.shape[0], half), (4 * rows_in, chans)]
    bufs = lambda n: [pltpu.VMEM((n,) + s, BF16) for s in slabs]
    both = shape((2, 4, rows_in, chans), BF16)
    piece = (8, width // shares)
    few = (length, wide)
    late_out = (half, width // 2)
    return pl.pallas_call(
        functools.partial(last_kernel, z_size, taps),
        in_specs=[vmem] * 13 + [any_space] * 7,
        out_specs=[vmem] * 7,
        out_shape=[
            shape(tokens.shape, BF16),
            both,
            both,
            shape((2,) + gout.shape[1:], BF16),
            shape((2,) + slabs[0], BF16),
            shape((2,) + slabs[1], BF16),
            shape(piece, F32),
        ],
        scratch_shapes=[
            pltpu.VMEM((4, 2) + few, BF16),
            pltpu.VMEM((4,) + few, BF16),
            pltpu.VMEM((3,) + few, BF16),
            pltpu.VMEM((3,) + few, BF16),
            pltpu.VMEM((length + 3, 8, chans), F32),
            pltpu.VMEM((length + 3, 8, chans), F32),
            pltpu.VMEM((8, length, chans), BF16),
            pltpu.VMEM(conv.shape, BF16),
            pltpu.VMEM(gate.shape, BF16),
            pltpu.VMEM(bgi.shape, BF16),
            pltpu.VMEM((length // 8, 8, chans), F32),
            pltpu.VMEM(bgi.shape, BF16),
            pltpu.VMEM((chans, wide), F32),
            pltpu.VMEM((taps + 1, 8, chans), F32),
            pltpu.VMEM((2, 8, length, 4 * rows_in), BF16),
            pltpu.VMEM((RING,) + block, BF16),
            pltpu.VMEM((2,) + block, BF16),
            pltpu.VMEM((RING,) + block, BF16),
            pltpu.VMEM((RING - 1,) + block, BF16),
        ]
        + bufs(z_size)
        + bufs(hops)
        + bufs(hops)
        + [
            pltpu.VMEM((z_size,) + late_out, BF16),
            pltpu.VMEM((hops,) + late_out, BF16),
            pltpu.VMEM((hops,) + late_out, BF16),
            pltpu.VMEM(slabs[2], BF16),
            pltpu.VMEM((shares,) + piece, F32),
            pltpu.VMEM((shares,) + piece, F32),
            pltpu.VMEM(piece, F32),
            pltpu.VMEM(piece, F32),
            dma((7,)),
            dma((2,)),
            dma((1,)),
            dma((1,)),
        ]
        + [dma((3,))] * 4
        + [dma((4,))] * 2
        + [dma((RING,))] * 2
        + [dma((RING - 1, 2))] * 2
        + [dma((hops, 3))] * 4
        + [dma((hops, 1))] * 4
        + [dma((2, 7))] * 2
        + [dma((6,))] * 2
        + [dma((shares - 1,))] * 2,
        cost_estimate=busy(120),
        compiler_params=pltpu.CompilerParams(
            collective_id=3, has_side_effects=True, vmem_limit_bytes=63 << 20
        ),
    )(
        part,
        keep,
        mats,
        params,
        gate_fin,
        out_fin,
        da,
        gstep,
        bias,
        skip,
        tokens,
        cot,
        gain,
        bx,
        cin,
        normed,
        conv,
        gate,
        bgi,
        gout,
    )


def close_kernel(
    taps,
    wide,
    tokens_ref,
    sum_ref,
    mats_ref,
    vec_ref,
    weight_ref,
    gate_ref,
    conv_ref,
    layer_ref,
    in_ref,
    taps_ref,
    offset_ref,
    select_ref,
    step_ref,
    bias_ref,
    decay_ref,
    skip_ref,
    out_ref,
):
    layer_ref[...] = (tokens_ref[...].astype(F32) + sum_ref[...].astype(F32)).astype(BF16)
    half = mats_ref.shape[1]
    for xx in range(2):
        rows = pl.ds(xx * half, half)
        select_ref[rows, :] = mats_ref[xx, :, : select_ref.shape[1]].astype(F32)
        step_ref[rows, :] = mats_ref[xx, :, wide:].astype(F32)
        out_ref[rows, :] = weight_ref[xx].astype(F32)
    z_size = conv_ref.shape[3] // half
    for first, both in ((0, conv_ref), (in_ref.shape[1] // 2, gate_ref)):
        for zz in range(z_size):
            for j in range(4):
                for xx in range(2):
                    col = first + (zz * 4 + j) * 2 * half + xx * half
                    in_ref[:, col : col + half] = both[xx, j, :, zz * half : (zz + 1) * half].astype(F32)
    vectors = jnp.concatenate([vec_ref[0].astype(F32), vec_ref[1].astype(F32)], axis=1)
    offset_ref[...] = vectors[taps : taps + 1, :]
    bias_ref[...] = vectors[taps + 1 : taps + 2, :]
    skip_ref[...] = vectors[taps + 2 : taps + 3, :]
    tall = vectors.T
    taps_ref[...] = tall[:, :taps]
    decay_ref[...] = tall[:, taps + 3 : taps + 3 + decay_ref.shape[1]]


def close(taps, states, select_width, tokens, layer_sum, mats, vectors, weight, gate, conv):
    rows = 2 * mats.shape[1]
    wide = select_width + -select_width % 128
    rank = mats.shape[2] - wide
    vmem = pl.BlockSpec(memory_space=pltpu.VMEM)
    shape = jax.ShapeDtypeStruct
    return pl.pallas_call(
        functools.partial(close_kernel, taps, wide),
        in_specs=[vmem] * 7,
        out_specs=[vmem] * 10,
        out_shape=[
            shape(tokens.shape, BF16),
            shape((gate.shape[2], 16 * gate.shape[3]), F32),
            shape((rows, taps), F32),
            shape((1, rows), F32),
            shape((rows, select_width), F32),
            shape((rows, rank), F32),
            shape((1, rows), F32),
            shape((rows, states), F32),
            shape((1, rows), F32),
            shape((rows, weight.shape[2]), F32),
        ],
        compiler_params=pltpu.CompilerParams(vmem_limit_bytes=60 << 20),
    )(tokens, layer_sum, mats, vectors, weight, gate, conv)


def shards(
    tokens,
    doc_ids,
    norm_gain,
    in_weight,
    conv_taps,
    conv_offset,
    select_weight,
    step_weight,
    step_bias,
    decay_log,
    skip_gain,
    out_weight,
    cotangent,
):
    z_size = lax.axis_size("z")
    rh_size = lax.axis_size("rh")
    seqs = 8
    length = doc_ids.shape[1]
    width = tokens.shape[1]
    in_rows = in_weight.shape[0]
    rows = out_weight.shape[0]
    half = rows // 2
    chans = half * z_size
    taps = conv_taps.shape[1]
    rank = step_weight.shape[1]
    states = decay_log.shape[1]
    x_at = lax.axis_index("x")

    def own_half(w):
        return lax.dynamic_slice_in_dim(w, x_at * half, half, 0)

    spare = -(rank + 2 * states) % 128
    wide = rank + 2 * states + spare
    vectors = jnp.concatenate(
        [
            own_half(conv_taps),
            own_half(conv_offset)[:, None],
            own_half(step_bias)[:, None],
            own_half(skip_gain)[:, None],
            own_half(decay_log),
        ],
        axis=1,
    ).T
    vectors = jnp.pad(vectors, ((0, -vectors.shape[0] % 32), (0, 0)))
    weight_in = in_weight
    if half % 128:
        columns = lax.dynamic_index_in_dim(
            in_weight.reshape(in_rows, 2, z_size, 4, 2, half), x_at, 4, keepdims=False
        )
        weight_in = columns.transpose(1, 3, 0, 2, 4).reshape(2, 4, in_rows, chans)
    (
        all_normed,
        all_cot,
        w_conv,
        w_gate,
        w_out,
        w_mats,
        keep,
        conv_in,
        x,
        dt,
        pre,
        vectors,
        gains,
        selection,
    ) = front(
        z_size,
        taps,
        rank,
        tokens,
        norm_gain.reshape(1, -1),
        doc_ids,
        vectors,
        cotangent,
        weight_in,
        out_weight,
        select_weight,
        step_weight,
    )
    selection = selection.reshape(length * seqs, wide)

    hist, last, back_scan, back_gate_in, out_part, grad_out, grad_gate, w_gate, _ = scan_forward(
        z_size, rank, states, taps + 2, dt, x, selection, keep, all_normed, all_cot, w_gate, w_out, vectors
    )
    layer_sum = lax.psum_scatter(
        out_part.reshape(-1, width), PLANE, scatter_dimension=0, tiled=True
    )
    back_x, part, da, g_step, g_bias, g_skip, gate_fin, out_fin = scan_backward(
        z_size,
        rank,
        taps + 2,
        dt,
        x,
        back_scan,
        pre,
        selection,
        keep,
        hist,
        last,
        vectors,
        w_mats,
        grad_gate.reshape(z_size, -1, chans),
        grad_out.reshape(z_size, half, width),
    )
    tokens_grad, g_in_gate, g_in_conv, g_out, g_mats, g_vectors, g_gain = last_part(
        z_size,
        taps,
        part.reshape(4, 2, length, wide),
        keep,
        w_mats,
        vectors,
        gate_fin,
        out_fin,
        grad_out.reshape(z_size, half, width),
        da,
        g_step,
        g_bias,
        g_skip,
        tokens,
        cotangent,
        gains,
        back_x,
        conv_in,
        all_normed,
        w_conv,
        w_gate,
        back_gate_in,
    )
    if rh_size > 1:
        g_mats, g_vectors, g_in_gate, g_in_conv, g_out, g_gain = lax.psum(
            tuple(
                v.astype(F32) for v in (g_mats, g_vectors, g_in_gate, g_in_conv, g_out, g_gain)
            ),
            "rh",
        )
    layer_out, g_in, g_taps, g_offset, g_select, g_step, g_bias, g_decay, g_skip, g_out = close(
        taps, states, rank + 2 * states, tokens, layer_sum, g_mats, g_vectors, g_out, g_in_gate, g_in_conv
    )
    return (
        layer_out,
        tokens_grad,
        g_gain[0],
        g_in,
        g_taps,
        g_offset[0],
        g_select,
        g_step,
        g_bias[0],
        g_decay,
        g_skip[0],
        g_out,
    )


def solution(mesh):
    replicas = mesh.shape["replica"]
    shares = mesh.shape["fsdp"]
    grid = Mesh(
        mesh.devices.reshape(replicas // 2, 2, shares // 4, 2, 2), ("rh", "x", "z", "y", "c")
    )
    tok = ("rh", "x", "z", "y", "c")
    own = ("z", "y", "c")
    return jax.shard_map(
        shards,
        mesh=grid,
        in_specs=(
            P(tok, None),
            P(tok, None),
            P(own),
            P(own, None),
            P(own, None),
            P(own),
            P(own, None),
            P(own, None),
            P(own),
            P(own, None),
            P(own),
            P(own, None),
            P(tok, None),
        ),
        out_specs=(
            P(tok, None),
            P(tok, None),
            P(own),
            P(own, None),
            P(own, None),
            P(own),
            P(own, None),
            P(own, None),
            P(own),
            P(own, None),
            P(own),
            P(own, None),
        ),
        check_vma=False,
    )
```
